32 devices in a mesh: dp: 8 (over y, x, core), mp: 4 (over z).
Axes of the slice: x: 2, y: 2, z: 4, core: 2. Of those that a mesh axis runs over, the one named last changes fastest.
Arguments:
- tokens: bfloat16 [6144, 768], P(('dp', 'mp')), may hold values from -6 to 6
- cotangent: bfloat16 [6144, 768], P(('dp', 'mp')), may hold values from -6 to 6
- lengths: int32 [8, 4], P('dp'), may hold values from 1 to 512, 768 in all within a row
- routes: int32 [6144], P(('dp', 'mp')), may hold values from 0 to 7, as said below
- slot_place: int32 [6144], P(('dp', 'mp')), may hold values from 0 to 29, as said below
- norm_in: float32 [2, 768], replicated, may hold values from 0.5 to 1.5
- w_in: bfloat16 [2, 2, 768, 1536], P(None, None, None, 'mp'), may hold values from -0.21875 to 0.21875
- conv_w: float32 [2, 4, 1536], P(None, None, 'mp'), may hold values from -3 to 3
- conv_b: float32 [2, 1536], P(None, 'mp'), may hold values from -3 to 3
- x_proj: bfloat16 [2, 1536, 80], P(None, 'mp'), may hold values from -0.15625 to 0.15625
- dt_proj: bfloat16 [2, 48, 1536], P(None, None, 'mp'), may hold values from -0.875 to 0.875
- dt_bias: float32 [2, 1536], P(None, 'mp'), may hold values from -4 to 2
- a_log: float32 [2, 16, 1536], P(None, None, 'mp'), may hold values from 0 to 2.77
- d_skip: float32 [2, 1536], P(None, 'mp'), may hold values from 0.5 to 1.5
- w_out: bfloat16 [2, 1536, 768], P(None, 'mp'), may hold values from -0.3125 to 0.3125
- norm_moe: float32 [2, 768], replicated, may hold values from 0.5 to 1.5
- router: float32 [2, 768, 8], replicated, may hold values from -0.15625 to 0.15625
- w_up: bfloat16 [2, 8, 768, 3072], P(None, 'dp', None, 'mp'), may hold values from -0.21875 to 0.21875
- w_down: bfloat16 [2, 8, 3072, 768], P(None, 'dp', 'mp'), may hold values from -0.875 to 0.875
Outputs:
- result: float32 [6144, 768], P(('dp', 'mp'))
- d_tokens: float32 [6144, 768], P(('dp', 'mp'))
- d_norm_in: float32 [2, 768], replicated
- d_w_in: float32 [2, 2, 768, 1536], P(None, None, None, 'mp')
- d_conv_w: float32 [2, 4, 1536], P(None, None, 'mp')
- d_conv_b: float32 [2, 1536], P(None, 'mp')
- d_x_proj: float32 [2, 1536, 80], P(None, 'mp')
- d_dt_proj: float32 [2, 48, 1536], P(None, None, 'mp')
- d_dt_bias: float32 [2, 1536], P(None, 'mp')
- d_a_log: float32 [2, 16, 1536], P(None, None, 'mp')
- d_d_skip: float32 [2, 1536], P(None, 'mp')
- d_w_out: float32 [2, 1536, 768], P(None, 'mp')
- d_norm_moe: float32 [2, 768], replicated
- d_router: float32 [2, 768, 8], replicated
- d_w_up: float32 [2, 8, 768, 3072], P(None, 'dp', None, 'mp')
- d_w_down: float32 [2, 8, 3072, 768], P(None, 'dp', 'mp')
The draws below stay inside these ranges and needn't reach their ends.
Inputs may be any that keep to these rules, and one draw needn't show every extreme that they name: `routes`: in each aligned block of 192 rows (the rows of one device) no expert is named more than 30 times, and one expert, the same in every block, exactly 30 times. `slot_place`: among the tokens of one block of 192 rows with one expert, the slots are 0, 1, 2, ... each once. `lengths`: each row sums to 768.
All inputs are finite; a program needn't handle non-finite values.
Results may differ from the reference program's by a relative error of at most 0.03.
Values may be sent and summed in bfloat16 or wider, within the bound.
A program may use at most 192 MiB of HBM per device.

```python
import math
import jax
import jax.numpy as jnp
import numpy as np
from jax import lax

D = 768
E = 1536
STATE = 16
DT_RANK = 48
CONV = 4
FF = 3072
LAYERS = 2
SCAN_LEN = 64
SEQS = 4
TOK_DEV = 768
EXPERTS = 8
BLK = 192
CAP = 30
MAXLEN = 512
PROJ = 80
TOKENS = 6144
N_DP = 8
N_MP = 4


def route_table(key):
    blocks = N_DP * N_MP
    total_slots = EXPERTS * CAP
    key_favor, key_full, key_score, key_shuffle = jax.random.split(key, 4)
    favor = jax.random.randint(key_favor, (EXPERTS,), 1, 9)
    favored = jax.random.randint(key_full, (), 0, EXPERTS)
    position = jnp.arange(total_slots, dtype=jnp.int32)
    owning = position // CAP
    drawn = jax.random.randint(key_score, (blocks, total_slots), 0, 32768)
    scores = drawn * favor[owning][None, :] * total_slots + position[None, :]
    scores = scores + (owning == favored).astype(jnp.int32)[None, :] * (1 << 30)
    _, chosen = lax.top_k(scores, BLK)
    shuffle = jax.vmap(lambda one_key: jax.random.permutation(one_key, BLK))(jax.random.split(key_shuffle, blocks))
    chosen = jnp.take_along_axis(chosen, shuffle, axis=1)
    occupied = jnp.zeros((blocks, total_slots), jnp.int32).at[jnp.arange(blocks)[:, None], chosen].set(1)
    ranks_in = (jnp.cumsum(occupied.reshape(blocks, EXPERTS, CAP), axis=2) - 1).reshape(blocks, total_slots)
    slot_index = jnp.take_along_axis(ranks_in, chosen, axis=1)
    return ((chosen // CAP).reshape(-1).astype(jnp.int32), slot_index.reshape(-1).astype(jnp.int32))


def draw_routes(key, part):
    expert_ids, _ = route_table(key)
    return expert_ids


def draw_slot_place(key, part):
    _, slot_index = route_table(key)
    return slot_index


def block_scale(stream_key, dims, cuts, smallest, largest):
    level, own = 1.0, jax.random.fold_in(stream_key, 6)
    for dim, parts in cuts:
        draws = jnp.exp(jax.random.uniform(jax.random.fold_in(own, dim), (parts,), jnp.float32, smallest / len(cuts), largest / len(cuts)))
        level = level * jnp.repeat(draws, dims[dim] // parts).reshape([-1 if axis == dim else 1 for axis in range(len(dims))])
    return level


def profile(count, total, bound, slope):
    loads = [(1 << 20) // math.isqrt(grade ** slope) + 1 for grade in range(2, count + 1)]
    rest, holding = total - bound - (count - 1), [1] * (count - 1)
    while rest > 0:
        free = [i for i in range(count - 1) if holding[i] < bound]
        pool, budget = sum([loads[i] for i in free]), rest
        for i in free:
            addition = min(bound - holding[i], max(1, budget * loads[i] // pool), rest)
            holding[i] = holding[i] + addition
            rest = rest - addition
    return np.array([bound] + holding)


def uneven(stream_key, amount, total, bound, slope):
    if amount == 2:
        one = jax.random.randint(stream_key, (), max(1, total - bound), min(bound, total - 1) + 1)
        return jnp.stack([one, total - one])
    sizes = jnp.asarray(profile(amount, total, bound, slope), jnp.int32)
    pairs = (amount - 1) // 2
    giver, sink = sizes[1:1 + 2 * pairs:2], sizes[2:2 + 2 * pairs:2]
    room = jnp.minimum(giver - 1, bound - sink)
    moved = jax.random.randint(jax.random.fold_in(stream_key, 1), (pairs,), 0, 1 << 20) % (room + 1)
    sizes = sizes.at[1:1 + 2 * pairs:2].set(giver - moved).at[2:2 + 2 * pairs:2].set(sink + moved)
    return sizes[jax.random.permutation(jax.random.fold_in(stream_key, 2), amount)]


def centred(own_key, shape, deviation, bound, pieces=(), kind=jnp.bfloat16):
    loudness = block_scale(own_key, shape, pieces, -0.22, 0.18) if pieces else 1.0
    array = jax.random.normal(own_key, shape, jnp.float32) * deviation * loudness
    return jnp.minimum(jnp.maximum(array, -bound), bound).astype(kind)


def setup_inputs(seed: int = 0) -> dict:
    key_list = jax.random.split(jax.random.key(seed), 20)
    return {
        "tokens": centred(key_list[0], (TOKENS, D), 1.0, 6.0, ((0, 32),)),
        "cotangent": centred(key_list[1], (TOKENS, D), 1.0, 6.0, ((0, 32),)),
        "lengths": jax.vmap(lambda own: uneven(own, SEQS, TOK_DEV, MAXLEN, 2))(jax.random.split(key_list[2], N_DP)).reshape((N_DP, SEQS)).astype(jnp.int32),
        "routes": draw_routes(jax.random.fold_in(key_list[19], 71), 0),
        "slot_place": draw_slot_place(jax.random.fold_in(key_list[19], 71), 0),
        "norm_in": jnp.clip(1.0 + 0.1 * jax.random.normal(key_list[5], (LAYERS, D), jnp.float32), 0.5, 1.5),
        "w_in": centred(key_list[6], (LAYERS, 2, D, E), D ** -0.5, 0.21875, ((3, 4),)),
        "conv_w": centred(key_list[7], (LAYERS, CONV, E), CONV ** -0.5, 3.0, ((2, 4),), jnp.float32),
        "conv_b": centred(key_list[8], (LAYERS, E), 0.5, 3.0, ((1, 4),), jnp.float32),
        "x_proj": centred(key_list[9], (LAYERS, E, PROJ), E ** -0.5, 0.15625, ((1, 4),)),
        "dt_proj": centred(key_list[10], (LAYERS, DT_RANK, E), DT_RANK ** -0.5, 0.875, ((2, 4),)),
        "dt_bias": jnp.clip(-4.0 + 6.0 * jax.random.uniform(key_list[11], (LAYERS, E), jnp.float32) ** block_scale(key_list[11], (LAYERS, E), ((1, 4),), -0.2, 0.2), -4.0, 2.0),
        "a_log": jnp.clip(2.77 * jax.random.uniform(key_list[12], (LAYERS, STATE, E), jnp.float32) ** block_scale(key_list[12], (LAYERS, STATE, E), ((2, 4),), -0.2, 0.2), 0.0, 2.77),
        "d_skip": jnp.clip(1.0 + 0.1 * jax.random.normal(key_list[13], (LAYERS, E), jnp.float32), 0.5, 1.5),
        "w_out": centred(key_list[14], (LAYERS, E, D), (E // 4) ** -0.5, 0.3125, ((1, 4),)),
        "norm_moe": jnp.clip(1.0 + 0.1 * jax.random.normal(key_list[15], (LAYERS, D), jnp.float32), 0.5, 1.5),
        "router": centred(key_list[16], (LAYERS, D, EXPERTS), (2 * D) ** -0.5, 0.15625, (), jnp.float32),
        "w_up": centred(key_list[17], (LAYERS, EXPERTS, D, FF), D ** -0.5, 0.21875, ((1, 8), (3, 4))),
        "w_down": centred(key_list[18], (LAYERS, EXPERTS, FF, D), (max(1, FF // (EXPERTS * EXPERTS))) ** -0.5, 0.875, ((1, 8), (2, 4))),
    }


@jax.custom_vjp
def low(v):
    return lax.optimization_barrier(v.astype(jnp.bfloat16)).astype(jnp.float32)

@jax.custom_vjp
def low_back(v):
    return v

def low_keep(v):
    return (low(v), None)

def low_pass(kept, grad):
    return (grad,)

def back_keep(v):
    return (v, None)

def back_low(kept, grad):
    return (low(grad),)
low.defvjp(low_keep, low_pass)
low_back.defvjp(back_keep, back_low)
highest = lax.Precision.HIGHEST
epsilon = 1e-05
dt_most = 0.05

def rms_scale(values, gain):
    return values * lax.rsqrt(lax.optimization_barrier(jnp.mean(values * values, axis=-1, keepdims=True)) + epsilon) * gain

def row_layout(seq_lengths, row_total):
    seq_ends = jnp.cumsum(seq_lengths).astype(jnp.int32)
    seq_starts = (seq_ends - seq_lengths).astype(jnp.int32)
    position = jnp.arange(row_total, dtype=jnp.int32)
    segment = lax.optimization_barrier(jnp.sum((position[:, None] >= seq_ends[None, :]).astype(jnp.int32), axis=1)).astype(jnp.int32)
    restart = jnp.any(position[:, None] == seq_starts[None, :], axis=1)
    return (segment, restart)

def causal_conv(conv_in, taps, bias, segment):
    summed_taps = bias[None, :] + taps[CONV - 1][None, :] * conv_in
    for offset in range(1, CONV):
        shifted = jnp.concatenate([jnp.zeros((offset, conv_in.shape[1]), conv_in.dtype), conv_in[:-offset]], axis=0)
        seg_shift = jnp.concatenate([jnp.full((offset,), -1, jnp.int32), segment[:-offset]]).astype(jnp.int32)
        usable = (seg_shift == segment).astype(conv_in.dtype)
        summed_taps = summed_taps + taps[CONV - 1 - offset][None, :] * shifted * usable[:, None]
    return jax.nn.silu(summed_taps)

def scan_block(carried, block_in, decay_rate):
    step_size, drive_in, in_mat, out_mat, restart, skipped = block_in
    block_len = step_size.shape[0]
    lower = (jnp.arange(block_len, dtype=jnp.int32)[:, None] >= jnp.arange(block_len, dtype=jnp.int32)[None, :]).astype(step_size.dtype)
    cum_step = jnp.dot(lower, step_size, precision=highest)
    log_decay = decay_rate[None] * cum_step[:, None, :]
    count_reset = jnp.dot(lower, restart, precision=highest)
    joined = lower * (count_reset[:, None] == count_reset[None, :]).astype(step_size.dtype)
    drive = drive_in[:, None, :] * in_mat[:, :, None]
    weighted = jnp.dot(joined, (jnp.exp(-log_decay) * drive).reshape(block_len, -1), precision=highest).reshape(log_decay.shape)
    fresh = (count_reset == 0).astype(step_size.dtype)
    states = jnp.exp(log_decay) * (weighted + fresh[:, None, None] * carried[None])
    outputs = jnp.einsum('cn,cne->ce', out_mat, states, precision=highest) + skipped
    return (states[-1], outputs)

def selective(conv_out, gate_in, projected, dt_weight, dt_shift, log_rate, skip, restart):
    row_total, channels = conv_out.shape
    dt_low = projected[:, :DT_RANK]
    in_mat = projected[:, DT_RANK:DT_RANK + STATE]
    out_mat = projected[:, DT_RANK + STATE:]
    step_size = dt_most * jax.nn.sigmoid(jnp.dot(dt_low, dt_weight, precision=highest) + dt_shift)
    decay_rate = -jnp.exp(log_rate)
    blocks = row_total // SCAN_LEN

    def into_blocks(values):
        return values.reshape((blocks, SCAN_LEN) + values.shape[1:])

    def block_step(carried, block_in):
        return scan_block(carried, block_in, decay_rate)
    _, outputs = lax.scan(jax.checkpoint(block_step), jnp.zeros((STATE, channels), conv_out.dtype), (into_blocks(step_size), into_blocks(step_size * conv_out), into_blocks(in_mat), into_blocks(out_mat), into_blocks(restart), into_blocks(skip[None, :] * conv_out)))
    return outputs.reshape(row_total, channels) * jax.nn.silu(gate_in)

def mamba_row(row_in, seq_lengths, gain, weight_in, taps, bias, weight_proj, dt_weight, dt_shift, log_rate, skip, weight_out):
    segment, restart = row_layout(seq_lengths, row_in.shape[0])
    normed = low(rms_scale(row_in, gain))
    paired = low_back(jnp.einsum('td,kde->kte', normed, weight_in, precision=highest))
    conv_out = causal_conv(paired[0], taps, bias, segment)
    projected = jnp.dot(conv_out, weight_proj, precision=highest)
    gated = selective(conv_out, paired[1], projected, dt_weight, dt_shift, log_rate, skip, restart.astype(row_in.dtype))
    return jnp.dot(low(gated), weight_out, precision=highest)

def forward(tokens, norm_in, w_in, conv_w, conv_b, x_proj, dt_proj, dt_bias, a_log, d_skip, w_out, norm_moe, router, w_up, w_down, lengths, routes, slot_place):
    activation = tokens
    block_of = (jnp.arange(TOKENS, dtype=jnp.int32) // BLK).astype(jnp.int32)
    choose = (routes[:, None] == jnp.arange(EXPERTS, dtype=jnp.int32)[None, :]).astype(tokens.dtype)
    for layer_index in range(LAYERS):
        layer_weights = (norm_in[layer_index], w_in[layer_index], conv_w[layer_index], conv_b[layer_index], x_proj[layer_index], dt_proj[layer_index], dt_bias[layer_index], a_log[layer_index], d_skip[layer_index], w_out[layer_index])

        def row_step(carried, row_item, layer_weights=layer_weights):
            return (carried, jax.checkpoint(mamba_row)(row_item[0], row_item[1], *layer_weights))
        _, mixed = lax.scan(row_step, None, (activation.reshape(N_DP, TOK_DEV, D), lengths))
        middle = activation + low_back(mixed.reshape(TOKENS, D))
        normed = rms_scale(middle, norm_moe[layer_index])
        chance = jax.nn.softmax(jnp.dot(normed, router[layer_index], precision=highest), axis=-1)
        gate_value = lax.optimization_barrier(jnp.sum(chance * choose, axis=1))
        buffer = jnp.zeros((EXPERTS, N_DP * N_MP, CAP, D), tokens.dtype).at[routes, block_of, slot_place].set(low(normed))
        buffer = low_back(buffer).reshape(EXPERTS, N_DP * N_MP * CAP, D)

        def expert(expert_item):
            slot_rows, first_mat, second_mat = expert_item
            hidden = low_back(jnp.dot(slot_rows, first_mat, precision=highest))
            return low_back(low(jnp.dot(low(jax.nn.gelu(hidden)), second_mat, precision=highest)))
        returned = lax.map(jax.checkpoint(expert), (buffer, w_up[layer_index], w_down[layer_index]))
        picked = returned.reshape(EXPERTS, N_DP * N_MP, CAP, D)[routes, block_of, slot_place]
        activation = middle + gate_value[:, None] * picked
    return activation

def reference(tokens, cotangent, lengths, routes, slot_place, norm_in, w_in, conv_w, conv_b, x_proj, dt_proj, dt_bias, a_log, d_skip, w_out, norm_moe, router, w_up, w_down):
    floats = [value.astype(jnp.float32) for value in (tokens, norm_in, w_in, conv_w, conv_b, x_proj, dt_proj, dt_bias, a_log, d_skip, w_out, norm_moe, router, w_up, w_down)]

    def whole_model(*params):
        return forward(*params, lengths, routes, slot_place)
    result, pull_back = jax.vjp(whole_model, *floats)
    grads = pull_back(cotangent.astype(jnp.float32))
    return (result, grads[0], grads[1], grads[2], grads[3], grads[4], grads[5], grads[6], grads[7], grads[8], grads[9], grads[10], grads[11], grads[12], grads[13], grads[14])
```

```python
import functools
import jax
import jax.numpy as jnp
from jax import lax
from jax.experimental import pallas as pl
from jax.experimental.pallas import tpu as pltpu
from jax.sharding import PartitionSpec as P

STATE = 16
DT_RANK = 48
LANES = 128
CHUNK = 128
LOG2E = 1.4426950408889634
RESET = 1.0e6
CONV = 4
dt_most = 0.05
epsilon = 1e-05
highest = lax.Precision.HIGHEST
F32, BF16 = jnp.float32, jnp.bfloat16


def sigmoid(v):
    return 1.0 / (1.0 + jnp.exp(-v))


def dot(a, b):
    return jnp.dot(a, b, preferred_element_type=F32)


def dot_nt(a, b):
    return lax.dot_general(a, b, (((1,), (1,)), ((), ())), preferred_element_type=F32)


def dot_tn(a, b):
    return lax.dot_general(a, b, (((0,), (0,)), ((), ())), preferred_element_type=F32)


def spread_matrix(first):
    rows = lax.broadcasted_iota(jnp.int32, (LANES, STATE * LANES), 0)
    cols = lax.broadcasted_iota(jnp.int32, (LANES, STATE * LANES), 1)
    return (rows == first + cols // LANES).astype(BF16)


def put(ref, value):
    for j in range(ref.shape[0]):
        ref[j] = value[:, j * LANES : (j + 1) * LANES]


def spread_rows(proj, spread, out_ref):
    wide = dot(proj, spread)
    for n in range(STATE):
        out_ref[pl.ds(n, CHUNK, stride=STATE), :] = wide[:, n * LANES : (n + 1) * LANES]


def scan_fwd_kernel(xs_ref, zg_ref, proj_ref, rst_ref, dtw_ref, dtb_ref, alog_ref, skip_ref, sb_ref, sc_ref,
                    gated_ref, ys_ref, hck_ref,
                    h_ref, dm_ref, dx_ref, bx_ref, cx_ref, yq_ref):
    groups = xs_ref.shape[1] // LANES

    @pl.when(pl.program_id(0) == 0)
    def _():
        h_ref[...] = jnp.zeros_like(h_ref)

    hck_ref[0] = h_ref[...]
    proj = proj_ref[...]
    xs = xs_ref[...]
    delta = dt_most * sigmoid(dot(proj, dtw_ref[...]) + dtb_ref[...])
    put(dm_ref, delta + RESET * rst_ref[...])
    put(dx_ref, delta * xs)
    spread_rows(proj, sb_ref[...], bx_ref)
    spread_rows(proj, sc_ref[...], cx_ref)
    rate = -LOG2E * jnp.exp(alog_ref[...])
    rates = [rate[:, j * LANES : (j + 1) * LANES] for j in range(groups)]

    def step(g, hs):
        hs = list(hs)
        t0 = pl.multiple_of(g * 8, 8)
        for i in range(8):
            t = t0 + i
            r0 = pl.multiple_of(t * STATE, STATE)
            b = bx_ref[pl.ds(r0, STATE), :]
            c = cx_ref[pl.ds(r0, STATE), :]
            q0 = pl.multiple_of(t * 8, 8)
            for j in range(groups):
                lanes = slice(j * LANES, (j + 1) * LANES)
                dec = jnp.exp2(dm_ref[j, pl.ds(t, 1), :] * rates[j])
                hs[j] = dec * hs[j] + dx_ref[j, pl.ds(t, 1), :] * b
                q = c * hs[j]
                yq_ref[j, pl.ds(q0, 8), :] = q[:8] + q[8:]
        return tuple(hs)

    hs = lax.fori_loop(0, CHUNK // 8, step, tuple(h_ref[:, j * LANES : (j + 1) * LANES] for j in range(groups)))
    for j in range(groups):
        h_ref[:, j * LANES : (j + 1) * LANES] = hs[j]
    zg = zg_ref[...]
    for j in range(groups):
        lanes = slice(j * LANES, (j + 1) * LANES)
        y = skip_ref[:, lanes] * xs[:, lanes]
        for k in range(8):
            y = y + yq_ref[j, pl.ds(k, CHUNK, stride=8), :]
        ys_ref[:, lanes] = y
        z = zg[:, lanes]
        gated_ref[:, lanes] = (y * z * sigmoid(z)).astype(BF16)


def scan_fwd(xs, zg, proj, restart, dtw, dtb, alog, skip, sb, sc):
    rows, ch = xs.shape
    steps = rows // CHUNK
    row = lambda w: pl.BlockSpec((CHUNK, w), lambda i: (i, 0))
    full = lambda s: pl.BlockSpec(s, lambda i: (0,) * len(s))
    return pl.pallas_call(
        scan_fwd_kernel,
        grid=(steps,),
        out_shape=[
            jax.ShapeDtypeStruct((rows, ch), BF16),
            jax.ShapeDtypeStruct((rows, ch), F32),
            jax.ShapeDtypeStruct((steps, STATE, ch), F32),
        ],
        in_specs=[row(ch), row(ch), row(LANES), row(1), full((LANES, ch)), full((1, ch)), full((STATE, ch)), full((1, ch)),
                  full((LANES, STATE * LANES)), full((LANES, STATE * LANES))],
        out_specs=[row(ch), row(ch), pl.BlockSpec((1, STATE, ch), lambda i: (i, 0, 0))],
        scratch_shapes=[
            pltpu.VMEM((STATE, ch), F32),
            pltpu.VMEM((ch // LANES, CHUNK, LANES), F32),
            pltpu.VMEM((ch // LANES, CHUNK, LANES), F32),
            pltpu.VMEM((CHUNK * STATE, LANES), F32),
            pltpu.VMEM((CHUNK * STATE, LANES), F32),
            pltpu.VMEM((ch // LANES, CHUNK * 8, LANES), F32),
        ],
        compiler_params=pltpu.CompilerParams(vmem_limit_bytes=48 << 20),
        name="scan_fwd",
    )(xs, zg, proj, restart, dtw, dtb, alog, skip, sb, sc)


def scan_bwd_kernel(xs_ref, zg_ref, proj_ref, rst_ref, ys_ref, gg_ref, hck_ref, dtw_ref, dtb_ref, alog_ref, skip_ref,
                    sb_ref, sc_ref,
                    gxs_ref, gzg_ref, gproj_ref, gdtw_ref, gdtb_ref, galog_ref, gskip_ref,
                    a_ref, dm_ref, dx_ref, dl_ref, gy_ref, bx_ref, cx_ref, h_ref, dec_ref, pq_ref, gq_ref, gb_ref, gc_ref):
    groups = xs_ref.shape[1] // LANES
    cols = [slice(j * LANES, (j + 1) * LANES) for j in range(groups)]

    @pl.when(pl.program_id(0) == 0)
    def _():
        a_ref[...] = jnp.zeros_like(a_ref)
        gdtw_ref[...] = jnp.zeros_like(gdtw_ref)
        gdtb_ref[...] = jnp.zeros_like(gdtb_ref)
        galog_ref[...] = jnp.zeros_like(galog_ref)
        gskip_ref[...] = jnp.zeros_like(gskip_ref)

    proj = proj_ref[...]
    xs = xs_ref[...]
    delta = dt_most * sigmoid(dot(proj, dtw_ref[...]) + dtb_ref[...])
    put(dl_ref, delta)
    put(dm_ref, delta + RESET * rst_ref[...])
    put(dx_ref, delta * xs)
    zg = zg_ref[...]
    sz = sigmoid(zg)
    gg = gg_ref[...]
    gy = gg * (zg * sz)
    put(gy_ref, gy)
    gzg_ref[...] = gg * ys_ref[...] * (sz * (1.0 + zg * (1.0 - sz)))
    gskip_ref[...] += jnp.sum(gy * xs, axis=0, keepdims=True)
    spread_rows(proj, sb_ref[...], bx_ref)
    spread_rows(proj, sc_ref[...], cx_ref)
    rate = -jnp.exp(alog_ref[...])
    rates2 = [LOG2E * rate[:, c] for c in cols]
    rates = [rate[:, c] for c in cols]

    for j in range(groups):
        h_ref[j, :STATE, :] = hck_ref[0][:, cols[j]]

    def again(g, hs):
        hs = list(hs)
        t0 = pl.multiple_of(g * 8, 8)
        for i in range(8):
            t = t0 + i
            r0 = pl.multiple_of(t * STATE, STATE)
            r1 = pl.multiple_of(t * STATE + STATE, STATE)
            b = bx_ref[pl.ds(r0, STATE), :]
            for j in range(groups):
                dec = jnp.exp2(dm_ref[j, pl.ds(t, 1), :] * rates2[j])
                hs[j] = dec * hs[j] + dx_ref[j, pl.ds(t, 1), :] * b
                dec_ref[j, pl.ds(r0, STATE), :] = dec
                h_ref[j, pl.ds(r1, STATE), :] = hs[j]
        return tuple(hs)

    last = lax.fori_loop(0, CHUNK // 8, again, tuple(hck_ref[0][:, c] for c in cols))

    def back(g, carry):
        carry = [list(c) for c in carry]
        aa, hs, acc = carry
        t0 = pl.multiple_of(CHUNK - 8 - g * 8, 8)
        for i in reversed(range(8)):
            t = t0 + i
            r0 = pl.multiple_of(t * STATE, STATE)
            q0 = pl.multiple_of(t * 8, 8)
            b = bx_ref[pl.ds(r0, STATE), :]
            c = cx_ref[pl.ds(r0, STATE), :]
            gb, gc = None, None
            for j in range(groups):
                gyj = gy_ref[j, pl.ds(t, 1), :]
                a = c * gyj + aa[j]
                dec = dec_ref[j, pl.ds(r0, STATE), :]
                before = h_ref[j, pl.ds(r0, STATE), :]
                carry_a = dec * a
                p = carry_a * before * rates[j]
                ab = a * b
                pq_ref[j, pl.ds(q0, 8), :] = p[:8] + p[8:]
                gq_ref[j, pl.ds(q0, 8), :] = ab[:8] + ab[8:]
                acc[j] = acc[j] + p * dl_ref[j, pl.ds(t, 1), :]
                gbj = a * dx_ref[j, pl.ds(t, 1), :]
                gcj = gyj * hs[j]
                gb = gbj if gb is None else gb + gbj
                gc = gcj if gc is None else gc + gcj
                aa[j] = carry_a
                hs[j] = before
            gb_ref[pl.ds(r0, STATE), :] = gb
            gc_ref[pl.ds(r0, STATE), :] = gc
        return tuple(tuple(c) for c in carry)

    aa, _, acc = lax.fori_loop(
        0, CHUNK // 8, back,
        (tuple(a_ref[:, c] for c in cols), last, tuple(jnp.zeros((STATE, LANES), F32) for _ in cols)))
    for j in range(groups):
        a_ref[:, cols[j]] = aa[j]
        galog_ref[:, cols[j]] += acc[j]

    skip = skip_ref[...]
    gdts = []
    for j in range(groups):
        psum = pq_ref[j, pl.ds(0, CHUNK, stride=8), :]
        gsum = gq_ref[j, pl.ds(0, CHUNK, stride=8), :]
        for k in range(1, 8):
            psum = psum + pq_ref[j, pl.ds(k, CHUNK, stride=8), :]
            gsum = gsum + gq_ref[j, pl.ds(k, CHUNK, stride=8), :]
        dl = delta[:, cols[j]]
        gdelta = psum + xs[:, cols[j]] * gsum
        gxs_ref[:, cols[j]] = dl * gsum + skip[:, cols[j]] * gy[:, cols[j]]
        gdts.append(gdelta * dl * (1.0 - dl * (1.0 / dt_most)))
    gdt = jnp.concatenate(gdts, axis=1)
    gdtb_ref[...] += jnp.sum(gdt, axis=0, keepdims=True)
    gdt_low = gdt.astype(BF16)
    gdtw_ref[...] += dot_tn(proj, gdt_low)
    gp = dot_nt(gdt_low, dtw_ref[...])
    wide_b = jnp.concatenate([gb_ref[pl.ds(n, CHUNK, stride=STATE), :].astype(BF16) for n in range(STATE)], axis=1)
    gp = gp + dot_nt(wide_b, sb_ref[...])
    wide_c = jnp.concatenate([gc_ref[pl.ds(n, CHUNK, stride=STATE), :].astype(BF16) for n in range(STATE)], axis=1)
    gproj_ref[...] = gp + dot_nt(wide_c, sc_ref[...])


def scan_bwd(xs, zg, proj, restart, ys, gg, hck, dtw, dtb, alog, skip, sb, sc):
    rows, ch = xs.shape
    steps = rows // CHUNK
    row = lambda w: pl.BlockSpec((CHUNK, w), lambda i: (steps - 1 - i, 0))
    full = lambda s: pl.BlockSpec(s, lambda i: (0,) * len(s))
    big = lambda: pltpu.VMEM((CHUNK * STATE, LANES), F32)
    g = ch // LANES
    return pl.pallas_call(
        scan_bwd_kernel,
        grid=(steps,),
        out_shape=[
            jax.ShapeDtypeStruct((rows, ch), F32),
            jax.ShapeDtypeStruct((rows, ch), F32),
            jax.ShapeDtypeStruct((rows, LANES), F32),
            jax.ShapeDtypeStruct((LANES, ch), F32),
            jax.ShapeDtypeStruct((1, ch), F32),
            jax.ShapeDtypeStruct((STATE, ch), F32),
            jax.ShapeDtypeStruct((1, ch), F32),
        ],
        in_specs=[row(ch), row(ch), row(LANES), row(1), row(ch), row(ch),
                  pl.BlockSpec((1, STATE, ch), lambda i: (steps - 1 - i, 0, 0)),
                  full((LANES, ch)), full((1, ch)), full((STATE, ch)), full((1, ch)),
                  full((LANES, STATE * LANES)), full((LANES, STATE * LANES))],
        out_specs=[row(ch), row(ch), row(LANES), full((LANES, ch)), full((1, ch)), full((STATE, ch)), full((1, ch))],
        scratch_shapes=[
            pltpu.VMEM((STATE, ch), F32),
            pltpu.VMEM((ch // LANES, CHUNK, LANES), F32),
            pltpu.VMEM((ch // LANES, CHUNK, LANES), F32),
            pltpu.VMEM((ch // LANES, CHUNK, LANES), F32),
            pltpu.VMEM((ch // LANES, CHUNK, LANES), F32),
            big(), big(),
            pltpu.VMEM((g, CHUNK * STATE + STATE, LANES), F32),
            pltpu.VMEM((g, CHUNK * STATE, LANES), F32),
            pltpu.VMEM((g, CHUNK * 8, LANES), F32),
            pltpu.VMEM((g, CHUNK * 8, LANES), F32),
            big(), big(),
        ],
        compiler_params=pltpu.CompilerParams(vmem_limit_bytes=48 << 20),
        name="scan_bwd",
    )(xs, zg, proj, restart, ys, gg, hck, dtw, dtb, alog, skip, sb, sc)


def rms_inverse(values):
    return lax.rsqrt(jnp.mean(values * values, axis=-1, keepdims=True) + epsilon)


def norm_back(values, inverse, gain, grad):
    scaled = grad * gain
    pulled = inverse * scaled - values * (inverse**3) * jnp.mean(scaled * values, axis=-1, keepdims=True)
    return pulled, jnp.sum(grad * values * inverse, axis=0)


def row_layout(seq_lengths, row_total):
    seq_ends = jnp.cumsum(seq_lengths)
    seq_starts = seq_ends - seq_lengths
    position = jnp.arange(row_total, dtype=jnp.int32)
    segment = jnp.sum((position[:, None] >= seq_ends[None, :]).astype(jnp.int32), axis=1)
    restart = jnp.any(position[:, None] == seq_starts[None, :], axis=1)
    return (segment, restart)


def causal_conv(conv_in, taps, bias, segment):
    summed_taps = bias[None, :] + taps[CONV - 1][None, :] * conv_in
    for offset in range(1, CONV):
        shifted = jnp.concatenate(
            [jnp.zeros((offset, conv_in.shape[1]), conv_in.dtype), conv_in[:-offset]], axis=0
        )
        seg_shift = jnp.concatenate([jnp.full((offset,), -1, jnp.int32), segment[:-offset]])
        usable = (seg_shift == segment).astype(conv_in.dtype)
        summed_taps = summed_taps + taps[CONV - 1 - offset][None, :] * shifted * usable[:, None]
    return jax.nn.silu(summed_taps)


def gather_rows(values):
    return lax.all_gather(values, "mp", axis=0, tiled=True)


def scatter_rows(values):
    return lax.psum_scatter(values.astype(BF16), "mp", scatter_dimension=0, tiled=True).astype(F32)


def sum_over_channels(values):
    return lax.psum(values.astype(BF16), "mp")


def to_experts(buffer, lanes):
    experts_slots, width = buffer.shape
    capacity = experts_slots // lax.axis_size("dp")
    copies = jnp.broadcast_to(
        buffer.reshape(-1, 1, capacity, width), (lax.axis_size("dp"), lanes, capacity, width)
    ).reshape(-1, capacity, width)
    arrived = lax.all_to_all(copies, ("dp", "mp"), split_axis=0, concat_axis=0, tiled=True)
    return arrived.reshape(-1, width)


def from_experts(partial_out, lanes):
    rows, width = partial_out.shape
    capacity = rows // (lanes * lax.axis_size("dp"))
    arrived = lax.all_to_all(
        partial_out.reshape(-1, capacity, width).astype(BF16),
        ("dp", "mp"),
        split_axis=0,
        concat_axis=0,
        tiled=True,
    ).astype(F32)
    return jnp.sum(arrived.reshape(-1, lanes, capacity, width), axis=1).astype(BF16).reshape(-1, width)


def on_device(
    tokens, cotangent, lengths, routes, slot_place, norm_in, w_in, conv_w, conv_b, x_proj, dt_proj, dt_bias,
    a_log, d_skip, w_out, norm_moe, router, w_up, w_down,
):
    layers = norm_in.shape[0]
    rows_here, width = tokens.shape
    lanes = lax.axis_size("mp")
    row_total = rows_here * lanes
    experts = router.shape[2]
    capacity = max(2, (5 * rows_here + 4 * experts - 1) // (4 * experts))
    padded = (capacity + 15) // 16 * 16
    segment, restart_flag = row_layout(lengths[0], row_total)
    restart = restart_flag.astype(F32)[:, None]
    chosen = routes[:, None] == jnp.arange(experts, dtype=jnp.int32)[None, :]
    choose = chosen.astype(F32)
    place = routes * padded + slot_place
    pick = (place[:, None] == jnp.arange(experts * padded, dtype=jnp.int32)[None, :]).astype(BF16)
    spread_b, spread_c = spread_matrix(DT_RANK), spread_matrix(DT_RANK + STATE)
    proj_pad = ((0, 0), (0, 0), (0, LANES - x_proj.shape[2]))
    x_proj = jnp.pad(x_proj, proj_pad)
    dt_proj = jnp.pad(dt_proj, ((0, 0), (0, LANES - DT_RANK), (0, 0)))

    activation = tokens.astype(F32)
    stored = []
    for l in range(layers):
        inv_in = rms_inverse(activation)
        whole = gather_rows((activation * inv_in * norm_in[l]).astype(BF16))
        conv_in = dot(whole, w_in[l, 0])
        gate_in = dot(whole, w_in[l, 1])
        conv_out, conv_pull = jax.vjp(
            lambda v, taps, bias: causal_conv(v, taps, bias, segment), conv_in, conv_w[l], conv_b[l]
        )
        conv_low = conv_out.astype(BF16)
        proj = sum_over_channels(dot(conv_low, x_proj[l]))
        gated, ys, marks = scan_fwd(
            conv_out, gate_in, proj, restart, dt_proj[l], dt_bias[l : l + 1], a_log[l], d_skip[l : l + 1], spread_b, spread_c
        )
        middle = activation + scatter_rows(dot(gated, w_out[l]))
        inv_moe = rms_inverse(middle)
        normed = middle * inv_moe * norm_moe[l]
        chance = jax.nn.softmax(jnp.dot(normed, router[l], precision=highest), axis=-1)
        gate = jnp.sum(chance * choose, axis=1, keepdims=True)
        arrived = to_experts(dot_tn(pick, normed.astype(BF16)).astype(BF16), lanes)
        hidden = dot(arrived, w_up[l, 0])
        active = jax.nn.gelu(hidden).astype(BF16)
        picked = dot(pick, from_experts(dot(active, w_down[l, 0]), lanes))
        stored.append((activation, inv_in, whole, gate_in, conv_out, conv_low, conv_pull, proj, gated, ys, marks,
                       middle, inv_moe, normed, chance, gate, arrived, hidden, active, picked))
        activation = middle + gate * picked
    upstream = cotangent.astype(F32)
    collected = []
    for l in reversed(range(layers)):
        (before, inv_in, whole, gate_in, conv_out, conv_low, conv_pull, proj, gated, ys, marks,
         middle, inv_moe, normed, chance, gate, arrived, hidden, active, picked) = stored[l]
        slot_grad = to_experts(dot_tn(pick, (gate * upstream).astype(BF16)).astype(BF16), lanes)
        grad_down = dot_tn(active, slot_grad)
        grad_active = dot_nt(slot_grad, w_down[l, 0])
        _, gelu_pull = jax.vjp(jax.nn.gelu, hidden)
        grad_hidden = gelu_pull(grad_active)[0].astype(BF16)
        grad_up = dot_tn(arrived, grad_hidden)
        grad_normed = dot(pick, from_experts(dot_nt(grad_hidden, w_up[l, 0]), lanes))
        grad_gate = jnp.sum(upstream * picked, axis=1, keepdims=True)
        grad_logit = gate * grad_gate * (choose - chance)
        grad_router = lax.dot_general(normed, grad_logit, (((0,), (0,)), ((), ())), precision=highest)
        grad_normed = grad_normed + lax.dot_general(
            grad_logit, router[l], (((1,), (1,)), ((), ())), precision=highest
        )
        pulled, grad_norm_moe = norm_back(middle, inv_moe, norm_moe[l], grad_normed)
        grad_middle = upstream + pulled
        grad_whole = gather_rows(grad_middle.astype(BF16))
        grad_w_out = dot_tn(gated, grad_whole)
        grad_gated = dot_nt(grad_whole, w_out[l])
        grad_conv, grad_gate_in, grad_proj_part, grad_dtw, grad_dtb, grad_alog, grad_skip = scan_bwd(
            conv_out, gate_in, proj, restart, ys, grad_gated, marks, dt_proj[l], dt_bias[l : l + 1], a_log[l],
            d_skip[l : l + 1], spread_b, spread_c
        )
        grad_proj = sum_over_channels(grad_proj_part)
        grad_x_proj = dot_tn(conv_low, grad_proj)
        grad_conv_in, grad_taps, grad_bias = conv_pull(grad_conv + dot_nt(grad_proj, x_proj[l]))
        grad_xi, grad_zg = grad_conv_in.astype(BF16), grad_gate_in.astype(BF16)
        grad_w_in = jnp.stack([dot_tn(whole, grad_xi), dot_tn(whole, grad_zg)])
        grad_u = scatter_rows(dot_nt(grad_xi, w_in[l, 0]) + dot_nt(grad_zg, w_in[l, 1]))
        pulled, grad_norm_in = norm_back(before, inv_in, norm_in[l], grad_u)
        upstream = grad_middle + pulled
        summed = [
            lax.psum(value.astype(BF16), "dp").astype(F32)
            for value in (grad_w_in, grad_taps, grad_bias, grad_x_proj[:, : DT_RANK + 2 * STATE], grad_dtw[:DT_RANK],
                          grad_dtb[0], grad_alog, grad_skip[0], grad_w_out)
        ]
        shared = lax.psum((grad_norm_in, grad_norm_moe, grad_router), ("dp", "mp"))
        collected.append((summed, shared, grad_up, grad_down))
    collected = collected[::-1]

    def stacked(first, second):
        return jnp.stack([entry[first][second] for entry in collected])

    return (
        activation,
        upstream,
        stacked(1, 0),
        *(stacked(0, i) for i in range(9)),
        stacked(1, 1),
        stacked(1, 2),
        jnp.stack([entry[2][None] for entry in collected]),
        jnp.stack([entry[3][None] for entry in collected]),
    )


def solution(mesh):
    return jax.shard_map(
        on_device,
        mesh=mesh,
        in_specs=(
            P(("dp", "mp"), None),
            P(("dp", "mp"), None),
            P("dp", None),
            P(("dp", "mp")),
            P(("dp", "mp")),
            P(),
            P(None, None, None, "mp"),
            P(None, None, "mp"),
            P(None, "mp"),
            P(None, "mp", None),
            P(None, None, "mp"),
            P(None, "mp"),
            P(None, None, "mp"),
            P(None, "mp"),
            P(None, "mp", None),
            P(),
            P(),
            P(None, "dp", None, "mp"),
            P(None, "dp", "mp", None),
        ),
        out_specs=(
            P(("dp", "mp"), None),
            P(("dp", "mp"), None),
            P(),
            P(None, None, None, "mp"),
            P(None, None, "mp"),
            P(None, "mp"),
            P(None, "mp", None),
            P(None, None, "mp"),
            P(None, "mp"),
            P(None, None, "mp"),
            P(None, "mp"),
            P(None, "mp", None),
            P(),
            P(),
            P(None, "dp", None, "mp"),
            P(None, "dp", "mp", None),
        ),
        check_vma=False,
    )
```

```python
import functools
import jax
import jax.numpy as jnp
from jax import lax
from jax.experimental import pallas as pl
from jax.experimental.pallas import tpu as pltpu
from jax.sharding import PartitionSpec as P

STATE = 16
DT_RANK = 48
LANES = 128
CHUNK = 128
LOG2E = 1.4426950408889634
RESET = 1.0e6
PROJ = DT_RANK + 2 * STATE
CONV = 4
dt_most = 0.05
epsilon = 1e-05
highest = lax.Precision.HIGHEST
MESH = pl.DeviceIdType.MESH
F32, BF16 = jnp.float32, jnp.bfloat16


def sigmoid(v):
    return 1.0 / (1.0 + jnp.exp(-v))


def dot(a, b):
    return jnp.dot(a, b, preferred_element_type=F32)


def dot_nt(a, b):
    return lax.dot_general(a, b, (((1,), (1,)), ((), ())), preferred_element_type=F32)


def dot_tn(a, b):
    return lax.dot_general(a, b, (((0,), (0,)), ((), ())), preferred_element_type=F32)


def spread_matrix():
    rows = lax.broadcasted_iota(jnp.int32, (STATE, STATE * LANES), 0)
    cols = lax.broadcasted_iota(jnp.int32, (STATE, STATE * LANES), 1)
    return (rows == cols // LANES).astype(BF16)


def put(ref, value):
    for j in range(ref.shape[0]):
        ref[j] = value[:, j * LANES : (j + 1) * LANES]


def spread_rows(proj, spread, out_ref):
    wide = dot_tn(proj, spread)
    for n in range(STATE):
        out_ref[pl.ds(n, CHUNK, stride=STATE), :] = wide[:, n * LANES : (n + 1) * LANES]


def scan_fwd_kernel(l, xs_ref, zg_ref, proj_ref, since_ref, dtw_ref, dtb_ref, alog_ref, skip_ref, spread_ref,
                    gated_ref, ys_ref, hck_ref,
                    h_ref, dm_ref, dx_ref, bx_ref, cx_ref, yq_ref):
    groups = xs_ref.shape[1] // LANES

    @pl.when(pl.program_id(0) == 0)
    def _():
        h_ref[...] = jnp.zeros_like(h_ref)

    hck_ref[0] = h_ref[...]
    proj = proj_ref[...]
    xs = xs_ref[...]
    delta = dt_most * sigmoid(dot_tn(proj[:DT_RANK], dtw_ref[l]) + dtb_ref[l : l + 1, :])
    put(dm_ref, delta + RESET * (since_ref[...] == 0).astype(F32))
    put(dx_ref, delta * xs)
    spread_rows(proj[DT_RANK : DT_RANK + STATE], spread_ref[...], bx_ref)
    spread_rows(proj[DT_RANK + STATE :], spread_ref[...], cx_ref)
    rate = -LOG2E * jnp.exp(alog_ref[l])
    rates = [rate[:, j * LANES : (j + 1) * LANES] for j in range(groups)]

    def step(g, hs):
        hs = list(hs)
        t0 = pl.multiple_of(g * 8, 8)
        for i in range(8):
            t = t0 + i
            r0 = pl.multiple_of(t * STATE, STATE)
            b = bx_ref[pl.ds(r0, STATE), :]
            c = cx_ref[pl.ds(r0, STATE), :]
            q0 = pl.multiple_of(t * 8, 8)
            for j in range(groups):
                lanes = slice(j * LANES, (j + 1) * LANES)
                dec = jnp.exp2(dm_ref[j, pl.ds(t, 1), :] * rates[j])
                hs[j] = dec * hs[j] + dx_ref[j, pl.ds(t, 1), :] * b
                q = c * hs[j]
                yq_ref[j, pl.ds(q0, 8), :] = q[:8] + q[8:]
        return tuple(hs)

    hs = lax.fori_loop(0, CHUNK // 8, step, tuple(h_ref[:, j * LANES : (j + 1) * LANES] for j in range(groups)))
    for j in range(groups):
        h_ref[:, j * LANES : (j + 1) * LANES] = hs[j]
    zg = zg_ref[...]
    for j in range(groups):
        lanes = slice(j * LANES, (j + 1) * LANES)
        y = skip_ref[l : l + 1, lanes] * xs[:, lanes]
        for k in range(8):
            y = y + yq_ref[j, pl.ds(k, CHUNK, stride=8), :]
        ys_ref[:, lanes] = y
        z = zg[:, lanes]
        gated_ref[:, lanes] = (y * z * sigmoid(z)).astype(BF16)


def scan_fwd(l, xs, zg, proj, since, dtw, dtb, alog, skip, spread):
    rows, ch = xs.shape
    steps = rows // CHUNK
    row = lambda w: pl.BlockSpec((CHUNK, w), lambda i: (i, 0))
    full = lambda s: pl.BlockSpec(s, lambda i: (0,) * len(s))
    return pl.pallas_call(
        functools.partial(scan_fwd_kernel, l),
        grid=(steps,),
        out_shape=[
            jax.ShapeDtypeStruct((rows, ch), BF16),
            jax.ShapeDtypeStruct((rows, ch), F32),
            jax.ShapeDtypeStruct((steps, STATE, ch), F32),
        ],
        in_specs=[row(ch), row(ch), pl.BlockSpec((PROJ, CHUNK), lambda i: (0, i)), row(1)]
        + [full(v.shape) for v in (dtw, dtb, alog, skip, spread)],
        out_specs=[row(ch), row(ch), pl.BlockSpec((1, STATE, ch), lambda i: (i, 0, 0))],
        scratch_shapes=[
            pltpu.VMEM((STATE, ch), F32),
            pltpu.VMEM((ch // LANES, CHUNK, LANES), F32),
            pltpu.VMEM((ch // LANES, CHUNK, LANES), F32),
            pltpu.VMEM((CHUNK * STATE, LANES), F32),
            pltpu.VMEM((CHUNK * STATE, LANES), F32),
            pltpu.VMEM((ch // LANES, CHUNK * 8, LANES), F32),
        ],
        compiler_params=pltpu.CompilerParams(vmem_limit_bytes=48 << 20),
        name="scan_fwd",
    )(xs, zg, proj, since, dtw, dtb, alog, skip, spread)


def scan_bwd_kernel(l, xs_ref, zg_ref, proj_ref, since_ref, ys_ref, gg_ref, hck_ref, dtw_ref, dtb_ref, alog_ref, skip_ref, spread_ref,
                    gxs_ref, gzg_ref, gproj_ref, gdtw_ref, gdtb_ref, galog_ref, gskip_ref,
                    a_ref, dm_ref, dx_ref, dl_ref, gy_ref, bx_ref, cx_ref, h_ref, dec_ref, pq_ref, gq_ref, gb_ref, gc_ref):
    groups = xs_ref.shape[1] // LANES
    cols = [slice(j * LANES, (j + 1) * LANES) for j in range(groups)]

    @pl.when(pl.program_id(0) == 0)
    def _():
        a_ref[...] = jnp.zeros_like(a_ref)
        gdtw_ref[...] = jnp.zeros_like(gdtw_ref)
        gdtb_ref[...] = jnp.zeros_like(gdtb_ref)
        galog_ref[...] = jnp.zeros_like(galog_ref)
        gskip_ref[...] = jnp.zeros_like(gskip_ref)

    proj = proj_ref[...]
    xs = xs_ref[...]
    delta = dt_most * sigmoid(dot_tn(proj[:DT_RANK], dtw_ref[l]) + dtb_ref[l : l + 1, :])
    put(dl_ref, delta)
    put(dm_ref, delta + RESET * (since_ref[...] == 0).astype(F32))
    put(dx_ref, delta * xs)
    zg = zg_ref[...]
    sz = sigmoid(zg)
    gg = gg_ref[...]
    gy = gg * (zg * sz)
    put(gy_ref, gy)
    gzg_ref[...] = (gg * ys_ref[...] * (sz * (1.0 + zg * (1.0 - sz)))).astype(BF16)
    gskip_ref[...] += jnp.sum(gy * xs, axis=0, keepdims=True)
    spread_rows(proj[DT_RANK : DT_RANK + STATE], spread_ref[...], bx_ref)
    spread_rows(proj[DT_RANK + STATE :], spread_ref[...], cx_ref)
    rate = -jnp.exp(alog_ref[l])
    rates2 = [LOG2E * rate[:, c] for c in cols]
    rates = [rate[:, c] for c in cols]

    for j in range(groups):
        h_ref[j, :STATE, :] = hck_ref[0][:, cols[j]]

    def again(g, hs):
        hs = list(hs)
        t0 = pl.multiple_of(g * 8, 8)
        for i in range(8):
            t = t0 + i
            r0 = pl.multiple_of(t * STATE, STATE)
            r1 = pl.multiple_of(t * STATE + STATE, STATE)
            b = bx_ref[pl.ds(r0, STATE), :]
            for j in range(groups):
                dec = jnp.exp2(dm_ref[j, pl.ds(t, 1), :] * rates2[j])
                hs[j] = dec * hs[j] + dx_ref[j, pl.ds(t, 1), :] * b
                dec_ref[j, pl.ds(r0, STATE), :] = dec
                h_ref[j, pl.ds(r1, STATE), :] = hs[j]
        return tuple(hs)

    last = lax.fori_loop(0, CHUNK // 8, again, tuple(hck_ref[0][:, c] for c in cols))

    def back(g, carry):
        carry = [list(c) for c in carry]
        aa, hs, acc = carry
        t0 = pl.multiple_of(CHUNK - 8 - g * 8, 8)
        for i in reversed(range(8)):
            t = t0 + i
            r0 = pl.multiple_of(t * STATE, STATE)
            q0 = pl.multiple_of(t * 8, 8)
            b = bx_ref[pl.ds(r0, STATE), :]
            c = cx_ref[pl.ds(r0, STATE), :]
            gb, gc = None, None
            for j in range(groups):
                gyj = gy_ref[j, pl.ds(t, 1), :]
                a = c * gyj + aa[j]
                dec = dec_ref[j, pl.ds(r0, STATE), :]
                before = h_ref[j, pl.ds(r0, STATE), :]
                carry_a = dec * a
                p = carry_a * before * rates[j]
                ab = a * b
                pq_ref[j, pl.ds(q0, 8), :] = p[:8] + p[8:]
                gq_ref[j, pl.ds(q0, 8), :] = ab[:8] + ab[8:]
                acc[j] = acc[j] + p * dl_ref[j, pl.ds(t, 1), :]
                gbj = a * dx_ref[j, pl.ds(t, 1), :]
                gcj = gyj * hs[j]
                gb = gbj if gb is None else gb + gbj
                gc = gcj if gc is None else gc + gcj
                aa[j] = carry_a
                hs[j] = before
            gb_ref[pl.ds(r0, STATE), :] = gb
            gc_ref[pl.ds(r0, STATE), :] = gc
        return tuple(tuple(c) for c in carry)

    aa, _, acc = lax.fori_loop(
        0, CHUNK // 8, back,
        (tuple(a_ref[:, c] for c in cols), last, tuple(jnp.zeros((STATE, LANES), F32) for _ in cols)))
    for j in range(groups):
        a_ref[:, cols[j]] = aa[j]
        galog_ref[:, cols[j]] += acc[j]

    skip = skip_ref[l : l + 1, :]
    gdts = []
    for j in range(groups):
        psum = pq_ref[j, pl.ds(0, CHUNK, stride=8), :]
        gsum = gq_ref[j, pl.ds(0, CHUNK, stride=8), :]
        for k in range(1, 8):
            psum = psum + pq_ref[j, pl.ds(k, CHUNK, stride=8), :]
            gsum = gsum + gq_ref[j, pl.ds(k, CHUNK, stride=8), :]
        dl = delta[:, cols[j]]
        gdelta = psum + xs[:, cols[j]] * gsum
        gxs_ref[:, cols[j]] = dl * gsum + skip[:, cols[j]] * gy[:, cols[j]]
        gdts.append(gdelta * dl * (1.0 - dl * (1.0 / dt_most)))
    gdt = jnp.concatenate(gdts, axis=1)
    gdtb_ref[...] += jnp.sum(gdt, axis=0, keepdims=True)
    gdt_low = gdt.astype(BF16)
    gdtw_ref[...] += dot(proj[:DT_RANK], gdt_low)
    gproj_ref[:DT_RANK, :] = dot_nt(dtw_ref[l], gdt_low)
    wide_b = jnp.concatenate([gb_ref[pl.ds(n, CHUNK, stride=STATE), :].astype(BF16) for n in range(STATE)], axis=1)
    gproj_ref[DT_RANK : DT_RANK + STATE, :] = dot_nt(spread_ref[...], wide_b)
    wide_c = jnp.concatenate([gc_ref[pl.ds(n, CHUNK, stride=STATE), :].astype(BF16) for n in range(STATE)], axis=1)
    gproj_ref[DT_RANK + STATE :, :] = dot_nt(spread_ref[...], wide_c)


def scan_bwd(l, xs, zg, proj, since, ys, gg, hck, dtw, dtb, alog, skip, spread):
    rows, ch = xs.shape
    steps = rows // CHUNK
    row = lambda w: pl.BlockSpec((CHUNK, w), lambda i: (steps - 1 - i, 0))
    full = lambda s: pl.BlockSpec(s, lambda i: (0,) * len(s))
    big = lambda: pltpu.VMEM((CHUNK * STATE, LANES), F32)
    g = ch // LANES
    return pl.pallas_call(
        functools.partial(scan_bwd_kernel, l),
        grid=(steps,),
        out_shape=[
            jax.ShapeDtypeStruct((rows, ch), F32),
            jax.ShapeDtypeStruct((rows, ch), BF16),
            jax.ShapeDtypeStruct((PROJ, rows), F32),
            jax.ShapeDtypeStruct((DT_RANK, ch), F32),
            jax.ShapeDtypeStruct((1, ch), F32),
            jax.ShapeDtypeStruct((STATE, ch), F32),
            jax.ShapeDtypeStruct((1, ch), F32),
        ],
        in_specs=[row(ch), row(ch), pl.BlockSpec((PROJ, CHUNK), lambda i: (0, steps - 1 - i)), row(1), row(ch), row(ch),
                  pl.BlockSpec((1, STATE, ch), lambda i: (steps - 1 - i, 0, 0))]
        + [full(v.shape) for v in (dtw, dtb, alog, skip, spread)],
        out_specs=[row(ch), row(ch), pl.BlockSpec((PROJ, CHUNK), lambda i: (0, steps - 1 - i)), full((DT_RANK, ch)), full((1, ch)), full((STATE, ch)), full((1, ch))],
        scratch_shapes=[
            pltpu.VMEM((STATE, ch), F32),
            pltpu.VMEM((ch // LANES, CHUNK, LANES), F32),
            pltpu.VMEM((ch // LANES, CHUNK, LANES), F32),
            pltpu.VMEM((ch // LANES, CHUNK, LANES), F32),
            pltpu.VMEM((ch // LANES, CHUNK, LANES), F32),
            big(), big(),
            pltpu.VMEM((g, CHUNK * STATE + STATE, LANES), F32),
            pltpu.VMEM((g, CHUNK * STATE, LANES), F32),
            pltpu.VMEM((g, CHUNK * 8, LANES), F32),
            pltpu.VMEM((g, CHUNK * 8, LANES), F32),
            big(), big(),
        ],
        compiler_params=pltpu.CompilerParams(vmem_limit_bytes=48 << 20),
        name="scan_bwd",
    )(xs, zg, proj, since, ys, gg, hck, dtw, dtb, alog, skip, spread)


def rms_inverse(values):
    return lax.rsqrt(jnp.mean(values * values, axis=-1, keepdims=True) + epsilon)


def norm_back(values, inverse, gain, grad):
    scaled = grad * gain
    pulled = inverse * scaled - values * (inverse * inverse * inverse) * jnp.mean(scaled * values, axis=-1, keepdims=True)
    return pulled, jnp.sum(grad * values * inverse, axis=0, keepdims=True)


GELU_A, GELU_B = 0.7978845608028654, 0.044715


def gelu(v):
    return 0.5 * v * (1.0 + jnp.tanh(GELU_A * (v + GELU_B * v * v * v)))


def gelu_slope(v):
    square = v * v
    t = jnp.tanh(GELU_A * v * (1.0 + GELU_B * square))
    return 0.5 * (1.0 + t) + 0.5 * v * (1.0 - t * t) * GELU_A * (1.0 + 3.0 * GELU_B * square)


def by_lane(m, values):
    picked = jnp.int32(values[0])
    for k in range(1, len(values)):
        picked = jnp.where(m == k, jnp.int32(values[k]), picked)
    return picked


def nearest_first(m, lanes):
    orders = [sorted((s for s in range(lanes) if s != k), key=lambda s: (abs(s - k), s)) for k in range(lanes)]
    return [by_lane(m, [order[i] for order in orders]) for i in range(lanes - 1)]


def chain_order(m, lanes):
    def due(k, s):
        return (lanes - 1 - s) + k if s > k else s + (lanes - 1 - k)

    orders = [sorted((s for s in range(lanes) if s != k), key=lambda s: (due(k, s), s)) for k in range(lanes)]
    return [by_lane(m, [order[i] for order in orders]) for i in range(lanes - 1)]


def greet(d, m, lanes, peers, across):
    barrier = pltpu.get_barrier_semaphore()
    if across:
        for k in range(1, lanes):
            pl.semaphore_signal(barrier, inc=1, device_id=(d, lax.rem(m + k, lanes)), device_id_type=MESH)
        for k in range(1, peers):
            pl.semaphore_signal(barrier, inc=1, device_id=(lax.rem(d + k, peers), m), device_id_type=MESH)
        pl.semaphore_wait(barrier, lanes + peers - 2)
    else:

        @pl.when(m > 0)
        def _():
            pl.semaphore_signal(barrier, inc=1, device_id=(d, m - 1), device_id_type=MESH)

        @pl.when(m < lanes - 1)
        def _():
            pl.semaphore_signal(barrier, inc=1, device_id=(d, m + 1), device_id_type=MESH)

        pl.semaphore_wait(barrier, jnp.where(m > 0, 1, 0) + jnp.where(m < lanes - 1, 1, 0))


class LineGather:
    def __init__(self, buf, send, recv, d, m, lanes):
        self.buf, self.send, self.recv, self.d, self.m, self.lanes = buf, send, recv, d, m, lanes
        self.order = nearest_first(m, lanes)

    def copy(self, s, up):
        return pltpu.make_async_remote_copy(
            src_ref=self.buf.at[s], dst_ref=self.buf.at[s], send_sem=self.send.at[0 if up else 1, s],
            recv_sem=self.recv.at[s], device_id=(self.d, self.m + 1 if up else self.m - 1), device_id_type=MESH,
        )

    def start(self):
        @pl.when(self.m < self.lanes - 1)
        def _():
            self.copy(self.m, True).start()

        @pl.when(self.m > 0)
        def _():
            self.copy(self.m, False).start()

    def arrive(self, i):
        s, m = self.order[i], self.m
        self.copy(s, True).wait_recv()

        @pl.when((s < m) & (m < self.lanes - 1))
        def _():
            self.copy(s, True).start()

        @pl.when((s > m) & (m > 0))
        def _():
            self.copy(s, False).start()

        return s

    def finish(self):
        for s in range(self.lanes):

            @pl.when((s <= self.m) & (self.m < self.lanes - 1))
            def _():
                self.copy(s, True).wait_send()

            @pl.when((s >= self.m) & (self.m > 0))
            def _():
                self.copy(s, False).wait_send()


class LineReduce:
    def __init__(self, stage, inbox, send, recv, d, m, lanes):
        self.stage, self.inbox, self.send, self.recv = stage, inbox, send, recv
        self.d, self.m, self.lanes = d, m, lanes
        self.order = chain_order(m, lanes)

    def copy(self, s):
        up = s > self.m
        side = jnp.where(up, 0, 1)
        return pltpu.make_async_remote_copy(
            src_ref=self.stage.at[s], dst_ref=self.inbox.at[side, s], send_sem=self.send.at[s],
            recv_sem=self.recv.at[side, s], device_id=(self.d, jnp.where(up, self.m + 1, self.m - 1)), device_id_type=MESH,
        )

    def push(self, s, term):
        up = s > self.m
        side = jnp.where(up, 0, 1)
        has_more = jnp.where(up, self.m, self.lanes - 1 - self.m) > 0

        @pl.when(has_more)
        def _():
            self.copy(s).wait_recv()
            self.stage[s] = (term + self.inbox[side, s].astype(F32)).astype(BF16)

        @pl.when(jnp.logical_not(has_more))
        def _():
            self.stage[s] = term.astype(BF16)

        self.copy(s).start()

    def total(self, own_ref):
        m = self.m

        def wait(side):
            pltpu.make_async_remote_copy(
                src_ref=self.stage.at[m], dst_ref=self.inbox.at[side, m], send_sem=self.send.at[m],
                recv_sem=self.recv.at[side, m], device_id=(self.d, m), device_id_type=MESH,
            ).wait_recv()

        @pl.when(m > 0)
        def _():
            wait(0)
            own_ref[...] += self.inbox[0, m].astype(F32)

        @pl.when(m < self.lanes - 1)
        def _():
            wait(1)
            own_ref[...] += self.inbox[1, m].astype(F32)

    def finish(self):
        for s in self.order:
            self.copy(s).wait_send()


PARTS = 2


def line_sum(part, stage, inbox, send, recv, out, d, m, lanes, between=lambda: None):
    width = part.shape[1] // PARTS

    def copy(side, b):
        return pltpu.make_async_remote_copy(
            src_ref=stage.at[side, b], dst_ref=inbox.at[side, b], send_sem=send.at[side, b], recv_sem=recv.at[side, b],
            device_id=(d, m + 1 if side == 0 else m - 1), device_id_type=MESH,
        )

    def step(side, b):
        has_source = m > 0 if side == 0 else m < lanes - 1
        has_target = m < lanes - 1 if side == 0 else m > 0
        cols = slice(b * width, (b + 1) * width)

        @pl.when(has_source)
        def _():
            copy(side, b).wait_recv()

        @pl.when(jnp.logical_not(has_source))
        def _():
            inbox[side, b] = jnp.zeros(inbox.shape[2:], BF16)

        @pl.when(has_target)
        def _():
            stage[side, b] = (part[:, cols] + inbox[side, b].astype(F32)).astype(BF16)
            copy(side, b).start()

    low = 2 * m < lanes

    def both(first):
        def run(side):
            for b in range(PARTS):
                step(side, b)

        @pl.when(low)
        def _():
            run(0 if first else 1)

        @pl.when(jnp.logical_not(low))
        def _():
            run(1 if first else 0)

    both(True)
    between()
    both(False)
    for b in range(PARTS):
        cols = slice(b * width, (b + 1) * width)
        out[:, cols] = (part[:, cols] + inbox[0, b].astype(F32) + inbox[1, b].astype(F32)).astype(BF16)

    def finish():
        for b in range(PARTS):

            @pl.when(m < lanes - 1)
            def _():
                copy(0, b).wait_send()

            @pl.when(m > 0)
            def _():
                copy(1, b).wait_send()

    return finish


def vmem(count):
    return [pl.BlockSpec(memory_space=pltpu.VMEM)] * count


def f32(*shape):
    return jax.ShapeDtypeStruct(shape, F32)


def bf16(*shape):
    return jax.ShapeDtypeStruct(shape, BF16)


def dma(*shape):
    return pltpu.SemaphoreType.DMA(shape)


def hbm(count):
    return [pl.BlockSpec(memory_space=pl.ANY)] * count


def fetch(pairs, sem):
    copies = [pltpu.make_async_copy(src, dst, sem.at[i]) for i, (src, dst) in enumerate(pairs)]
    for copy in copies:
        copy.start()
    return copies


def params(cid):
    return pltpu.CompilerParams(collective_id=cid, has_side_effects=True, vmem_limit_bytes=56 << 20)


CONV_ROWS = 128
HEAD = 8


def conv_window(padded_ref, since_ref, taps, bias, base):
    window = padded_ref[pl.ds(base, CONV_ROWS + HEAD), :]
    since = since_ref[pl.ds(base, CONV_ROWS), :]
    shifted = [window[HEAD:]]
    for j in range(1, CONV):
        shifted.append(window[HEAD - j : HEAD - j + CONV_ROWS] * (since >= j).astype(F32))
    pre = bias
    for j in range(CONV):
        pre = pre + taps[CONV - 1 - j : CONV - j, :] * shifted[j]
    return pre, shifted


def in_kernel(l, lanes, act_ref, gain_ref, taps_ref, bias_ref, since_ref, xp_ref, win_hbm,
              whole_ref, conv_ref, gate_ref, xs_ref, proj_ref,
              win_ref, part_ref, stage_ref, inbox_ref, gsend, grecv, psend, precv, wsem):
    d, m = lax.axis_index("dp"), lax.axis_index("mp")
    rows = act_ref.shape[0]
    (weights,) = fetch([(win_hbm.at[l], win_ref)], wsem)
    greet(d, m, lanes, 0, False)
    act = act_ref[...].astype(F32)
    whole_ref[m] = (act * rms_inverse(act) * gain_ref[l : l + 1, :]).astype(BF16)
    gather = LineGather(whole_ref, gsend, grecv, d, m, lanes)
    gather.start()
    conv_ref[:HEAD, :] = jnp.zeros((HEAD, conv_ref.shape[1]), F32)
    weights.wait()

    def project(s):
        u = whole_ref[s]
        conv_ref[pl.ds(pl.multiple_of(s * rows + HEAD, 8), rows), :] = dot(u, win_ref[0])
        gate_ref[pl.ds(pl.multiple_of(s * rows, 8), rows), :] = dot(u, win_ref[1])

    project(m)
    for i in range(lanes - 1):
        project(gather.arrive(i))
    taps, bias = taps_ref[l], bias_ref[l : l + 1, :]

    def conv_step(c, carry):
        base = pl.multiple_of(c * CONV_ROWS, CONV_ROWS)
        pre, _ = conv_window(conv_ref, since_ref, taps, bias, base)
        xs = pre * sigmoid(pre)
        xs_ref[pl.ds(base, CONV_ROWS), :] = xs
        part_ref[:, pl.ds(base, CONV_ROWS)] = dot_nt(xp_ref[l], xs.astype(BF16))
        return carry

    lax.fori_loop(0, lanes * rows // CONV_ROWS, conv_step, 0)
    finish = line_sum(part_ref, stage_ref, inbox_ref, psend, precv, proj_ref, d, m, lanes)
    gather.finish()
    finish()


def in_block(l, lanes, act, gain, taps, bias, since, xp, win):
    rows, width = act.shape
    ch, total = win.shape[3], rows * lanes
    return pl.pallas_call(
        functools.partial(in_kernel, l, lanes),
        out_shape=[bf16(lanes, rows, width), f32(total + HEAD, ch), f32(total, ch), f32(total, ch), bf16(PROJ, total)],
        in_specs=vmem(6) + hbm(1),
        out_specs=vmem(5),
        scratch_shapes=[
            pltpu.VMEM(win.shape[1:], BF16),
            pltpu.VMEM((PROJ, total), F32),
            pltpu.VMEM((2, PARTS, PROJ, total // PARTS), BF16),
            pltpu.VMEM((2, PARTS, PROJ, total // PARTS), BF16),
            dma(2, lanes), dma(lanes), dma(2, PARTS), dma(2, PARTS), dma(1),
        ],
        compiler_params=params(l),
        name="mamba_in",
    )(act, gain, taps, bias, since, xp, win)


class Experts:
    def __init__(self, d, m, lanes, peers, rows_ref, into_ref, pack_ref, slots_ref, part_ref, back_ref, stage_ref, inbox_ref,
                 gsend, grecv, dsend, drecv, bsend, brecv, rsend, rrecv):
        self.d, self.m, self.lanes, self.peers = d, m, lanes, peers
        self.rows, self.into = rows_ref, into_ref
        self.pack, self.slots, self.part, self.back, self.stage, self.inbox = pack_ref, slots_ref, part_ref, back_ref, stage_ref, inbox_ref
        self.dsend, self.drecv, self.bsend, self.brecv, self.rsend, self.rrecv = dsend, drecv, bsend, brecv, rsend, rrecv
        self.cap = pack_ref.shape[1] // peers
        self.gather = LineGather(rows_ref, gsend, grecv, d, m, lanes)

    def at(self, e):
        return pl.ds(pl.multiple_of(e * self.cap, self.cap), self.cap)

    def hop(self, src, dst, send, recv, s, k):
        other = lax.rem(self.d + k, self.peers)
        return pltpu.make_async_remote_copy(
            src_ref=src.at[s, self.at(other)], dst_ref=dst.at[s, self.at(self.d)], send_sem=send.at[s, k - 1],
            recv_sem=recv.at[s, k - 1], device_id=(other, self.m), device_id_type=MESH,
        )

    def across(self, src, dst, send, recv, s):
        for k in range(1, self.peers):
            self.hop(src, dst, send, recv, s, k).start()
        dst[s, self.at(self.d)] = src[s, self.at(self.d)]

    def dispatch(self, s):
        self.pack[s] = dot(self.into[s], self.rows[s]).astype(BF16)
        self.across(self.pack, self.slots, self.dsend, self.drecv, s)

    def answer(self, s, expert):
        for k in range(1, self.peers):
            self.hop(self.pack, self.slots, self.dsend, self.drecv, s, k).wait_recv()
        self.part[s] = expert(s)
        self.across(self.part, self.back, self.bsend, self.brecv, s)

    def home(self, s):
        return pltpu.make_async_remote_copy(
            src_ref=self.stage.at[s], dst_ref=self.inbox.at[self.m], send_sem=self.rsend.at[s], recv_sem=self.rrecv.at[self.m],
            device_id=(self.d, s), device_id_type=MESH,
        )

    def combine(self, s):
        for k in range(1, self.peers):
            self.hop(self.part, self.back, self.bsend, self.brecv, s, k).wait_recv()
        return dot_tn(self.into[s], self.back[s])

    def combine_away(self, s):
        self.stage[s] = self.combine(s).astype(BF16)
        self.home(s).start()

    def run(self, expert, own_ref, meanwhile):
        order = [self.m]
        self.gather.start()
        self.dispatch(self.m)
        for i in range(self.lanes - 1):
            s = self.gather.arrive(i)
            self.dispatch(s)
            self.answer(order[-1], expert)
            if i == 1:
                own_ref[...] = self.combine(self.m)
            if i > 1:
                self.combine_away(order[-2])
            order.append(s)
        self.answer(order[-1], expert)
        self.combine_away(order[-2])
        self.combine_away(order[-1])
        meanwhile()
        for s in order[1:]:
            pltpu.make_async_remote_copy(
                src_ref=self.stage.at[s], dst_ref=self.inbox.at[s], send_sem=self.rsend.at[s], recv_sem=self.rrecv.at[s],
                device_id=(self.d, s), device_id_type=MESH,
            ).wait_recv()
            own_ref[...] += self.inbox[s].astype(F32)
        self.gather.finish()
        for s in order:
            for k in range(1, self.peers):
                self.hop(self.pack, self.slots, self.dsend, self.drecv, s, k).wait_send()
                self.hop(self.part, self.back, self.bsend, self.brecv, s, k).wait_send()
        for s in order[1:]:
            self.home(s).wait_send()


def expert_scratch(lanes, peers, rows, width, slots):
    return [
        pltpu.VMEM((lanes, rows, width), BF16),
        pltpu.VMEM((lanes, slots, width), BF16),
        pltpu.VMEM((lanes, slots, width), BF16),
        pltpu.VMEM((lanes, slots, width), BF16),
        pltpu.VMEM((lanes, rows, width), BF16),
        pltpu.VMEM((lanes, rows, width), BF16),
        pltpu.VMEM((rows, width), F32),
        dma(2, lanes), dma(lanes), dma(lanes, peers - 1), dma(lanes, peers - 1), dma(lanes, peers - 1), dma(lanes, peers - 1),
        dma(lanes), dma(lanes),
    ]


def mid_kernel(l, lanes, peers, experts, act_ref, gated_ref, gain_ref, router_ref, choose_ref, place_ref, wout_hbm, wup_hbm, wdown_hbm,
               middle_ref, chance_ref, into_ref, slots_ref, hidden_ref, active_ref, picked_ref, next_ref,
               rows_ref, pack_ref, part_ref, back_ref, stage_ref, inbox_ref, own_ref,
               gsend, grecv, dsend, drecv, bsend, brecv, rsend, rrecv, cstage_ref, cinbox_ref, csend, crecv,
               places_ref, isend, irecv, wout_ref, wup_ref, wdown_ref, wsem):
    d, m = lax.axis_index("dp"), lax.axis_index("mp")
    wout, wup, wdown = fetch([(wout_hbm.at[l], wout_ref), (wup_hbm.at[l, 0], wup_ref), (wdown_hbm.at[l, 0], wdown_ref)], wsem)
    greet(d, m, lanes, peers, True)
    places_ref[m] = place_ref[...]
    places = LineGather(places_ref, isend, irecv, d, m, lanes)
    places.start()
    reduce = LineReduce(cstage_ref, cinbox_ref, csend, crecv, d, m, lanes)
    wout.wait()
    for s in reduce.order:
        reduce.push(s, dot(gated_ref[s], wout_ref[...]))
    own_ref[...] = act_ref[...].astype(F32) + dot(gated_ref[m], wout_ref[...])
    slots = into_ref.shape[1]

    def spread_places(s):
        numbers = lax.broadcasted_iota(jnp.int32, (slots, into_ref.shape[2]), 0)
        into_ref[s] = (numbers == places_ref[s][:1, : into_ref.shape[2]]).astype(F32).astype(BF16)

    spread_places(m)
    for i in range(lanes - 1):
        spread_places(places.arrive(i))
    places.finish()
    wup.wait()
    wdown.wait()
    reduce.total(own_ref)
    middle = own_ref[...]
    middle_ref[...] = middle
    normed = middle * rms_inverse(middle) * gain_ref[l : l + 1, :]
    rows_ref[m] = normed.astype(BF16)
    moe = Experts(d, m, lanes, peers, rows_ref, into_ref, pack_ref, slots_ref, part_ref, back_ref, stage_ref, inbox_ref,
                  gsend, grecv, dsend, drecv, bsend, brecv, rsend, rrecv)

    def expert(s):
        hidden = dot(slots_ref[s], wup_ref[...])
        hidden_ref[s] = hidden.astype(BF16)
        active = gelu(hidden).astype(BF16)
        active_ref[s] = active
        return dot(active, wdown_ref[...]).astype(BF16)

    def meanwhile():
        reduce.finish()
        normed = middle_ref[...] * rms_inverse(middle_ref[...]) * gain_ref[l : l + 1, :]
        logits = jnp.dot(normed, router_ref[l], precision=highest, preferred_element_type=F32)
        valid = lax.broadcasted_iota(jnp.int32, logits.shape, 1) < experts
        logits = jnp.where(valid, logits, -1e30)
        raised = jnp.exp(logits - jnp.max(logits, axis=1, keepdims=True))
        chance_ref[...] = raised / jnp.sum(raised, axis=1, keepdims=True)

    moe.run(expert, own_ref, meanwhile)
    picked = own_ref[...].astype(BF16)
    picked_ref[...] = picked
    gate = jnp.sum(chance_ref[...] * choose_ref[...], axis=1, keepdims=True)
    next_ref[...] = middle_ref[...] + gate * picked.astype(F32)


def mid_block(l, lanes, peers, experts, padded, act, gated, gain, router, choose, place, wout, wup, wdown):
    rows, width = act.shape
    slots, ff = experts * padded, wup.shape[3]
    return pl.pallas_call(
        functools.partial(mid_kernel, l, lanes, peers, experts),
        out_shape=[f32(rows, width), f32(rows, LANES), bf16(lanes, slots, rows), bf16(lanes, slots, width), bf16(lanes, slots, ff),
                   bf16(lanes, slots, ff), bf16(rows, width), f32(rows, width)],
        in_specs=vmem(6) + hbm(3),
        out_specs=vmem(8),
        scratch_shapes=expert_scratch(lanes, peers, rows, width, slots)
        + [
            pltpu.VMEM((lanes, rows, width), BF16),
            pltpu.VMEM((2, lanes, rows, width), BF16),
            dma(lanes), dma(2, lanes),
            pltpu.VMEM((lanes, *place.shape), jnp.int32),
            dma(2, lanes), dma(lanes),
            pltpu.VMEM(wout.shape[1:], BF16), pltpu.VMEM(wup.shape[2:], BF16), pltpu.VMEM(wdown.shape[2:], BF16), dma(3),
        ],
        compiler_params=params(2 + l),
        name="mid_forward",
    )(act, gated, gain, router, choose, place, wout, wup, wdown)


def moe_back_kernel(l, lanes, peers, up_ref, chance_ref, choose_ref, picked_ref, middle_ref, gain_ref, router_ref, into_ref,
                    slots_ref, hidden_ref, active_ref, gated_ref, wout_hbm, wup_hbm, wdown_hbm,
                    gmid_ref, gup_ref, gdown_ref, ggated_ref, gwout_ref, gshare_ref,
                    rows_ref, pack_ref, part_ref, back_ref, stage_ref, inbox_ref, own_ref,
                    gsend, grecv, dsend, drecv, bsend, brecv, rsend, rrecv, sgrad_ref, ghid_ref, wide_ref, wsend, wrecv,
                    wout_ref, wup_ref, wdown_ref, wsem):
    d, m = lax.axis_index("dp"), lax.axis_index("mp")
    weights = fetch([(wdown_hbm.at[l, 0], wdown_ref), (wup_hbm.at[l, 0], wup_ref), (wout_hbm.at[l], wout_ref)], wsem)
    greet(d, m, lanes, peers, True)
    chance, choose = chance_ref[...], choose_ref[...]
    gate = jnp.sum(chance * choose, axis=1, keepdims=True)
    rows_ref[m] = (gate * up_ref[...].astype(F32)).astype(BF16)
    for weight in weights:
        weight.wait()
    moe = Experts(d, m, lanes, peers, rows_ref, into_ref, pack_ref, sgrad_ref, part_ref, back_ref, stage_ref, inbox_ref,
                  gsend, grecv, dsend, drecv, bsend, brecv, rsend, rrecv)

    def expert(s):
        grad_active = dot_nt(sgrad_ref[s], wdown_ref[...])
        grad_hidden = (grad_active * gelu_slope(hidden_ref[s].astype(F32))).astype(BF16)
        ghid_ref[s] = grad_hidden
        return dot_nt(grad_hidden, wup_ref[...]).astype(BF16)

    flat = lambda ref: ref[...].reshape(ref.shape[0] * ref.shape[1], ref.shape[2])

    def meanwhile():
        gdown_ref[...] = dot_tn(flat(active_ref), flat(sgrad_ref))
        gup_ref[...] = dot_tn(flat(slots_ref), flat(ghid_ref))

    moe.run(expert, own_ref, meanwhile)
    upstream, middle = up_ref[...].astype(F32), middle_ref[...]
    inverse = rms_inverse(middle)
    gain = gain_ref[l : l + 1, :]
    grad_gate = jnp.sum(upstream * picked_ref[...].astype(F32), axis=1, keepdims=True)
    grad_logit = gate * grad_gate * (choose - chance)
    grad_normed = own_ref[...].astype(BF16).astype(F32) + lax.dot_general(
        grad_logit, router_ref[l], (((1,), (1,)), ((), ())), precision=highest, preferred_element_type=F32)
    pulled, grad_gain = norm_back(middle, inverse, gain, grad_normed)
    grad_middle = upstream + pulled
    gmid_ref[...] = grad_middle
    wide_ref[m] = grad_middle.astype(BF16)
    gather = LineGather(wide_ref, wsend, wrecv, d, m, lanes)
    gather.start()
    grad_router = lax.dot_general(
        grad_logit, middle * inverse * gain, (((0,), (0,)), ((), ())), precision=highest, preferred_element_type=F32)
    experts = gshare_ref.shape[0] - 8
    gshare_ref[:experts, :] = grad_router[:experts]
    gshare_ref[experts:, :] = jnp.broadcast_to(grad_gain, (8, grad_gain.shape[1]))

    def gate_back(s):
        ggated_ref[s] = dot_nt(wide_ref[s], wout_ref[...])

    gate_back(m)
    for i in range(lanes - 1):
        gate_back(gather.arrive(i))
    gwout_ref[...] = dot_tn(flat(gated_ref), flat(wide_ref)).astype(BF16)
    gather.finish()


def moe_back(l, lanes, peers, experts, up, chance, choose, picked, middle, gain, router, into, slots, hidden, active, gated, wout, wup, wdown):
    rows, width = up.shape
    count, ff, ch = into.shape[1], wup.shape[3], wout.shape[1]
    return pl.pallas_call(
        functools.partial(moe_back_kernel, l, lanes, peers),
        out_shape=[f32(rows, width), f32(width, ff), f32(ff, width), f32(lanes, rows, ch), bf16(ch, width), f32(experts + 8, width)],
        in_specs=vmem(12) + hbm(3),
        out_specs=vmem(6),
        scratch_shapes=expert_scratch(lanes, peers, rows, width, count)
        + [
            pltpu.VMEM((lanes, count, width), BF16),
            pltpu.VMEM((lanes, count, ff), BF16),
            pltpu.VMEM((lanes, rows, width), BF16),
            dma(2, lanes), dma(lanes),
            pltpu.VMEM(wout.shape[1:], BF16), pltpu.VMEM(wup.shape[2:], BF16), pltpu.VMEM(wdown.shape[2:], BF16), dma(3),
        ],
        compiler_params=params(4 + l),
        name="moe_backward",
    )(up, chance, choose, picked, middle, gain, router, into, slots, hidden, active, gated, wout, wup, wdown)


class PlaneSum:
    def __init__(self, d, m, peers, mine, pair, half, inbox, result, psend, precv, csend, crecv, gsend, grecv):
        self.m, self.mine, self.pair, self.half, self.inbox, self.result = m, mine, pair, half, inbox, result
        self.psend, self.precv, self.csend, self.crecv, self.gsend, self.grecv = psend, precv, csend, crecv, gsend, grecv
        self.chips = peers // 2
        self.chip, self.core = lax.div(d, 2), lax.rem(d, 2)
        self.rows = mine.shape[0] // 2
        self.block = self.rows // self.chips

    def side(self, core):
        return pl.ds(pl.multiple_of(core * self.rows, 16), self.rows)

    def at(self, chip):
        return pl.ds(pl.multiple_of(chip * self.block, 16), self.block)

    def final(self, chip):
        return pl.ds(pl.multiple_of(self.core * self.rows + chip * self.block, 16), self.block)

    def swap(self, src, dst, i):
        return pltpu.make_async_remote_copy(
            src_ref=src, dst_ref=dst, send_sem=self.psend.at[i], recv_sem=self.precv.at[i],
            device_id=(self.chip * 2 + 1 - self.core, self.m), device_id_type=MESH)

    def first_swap(self):
        return self.swap(self.mine.at[self.side(1 - self.core)], self.pair, 0)

    def last_swap(self):
        return self.swap(self.result.at[self.side(self.core)], self.result.at[self.side(self.core)], 1)

    def other(self, k):
        return lax.rem(self.chip + k, self.chips)

    def scatter(self, k):
        return pltpu.make_async_remote_copy(
            src_ref=self.half.at[self.at(self.other(k))], dst_ref=self.inbox.at[k - 1], send_sem=self.csend.at[k - 1],
            recv_sem=self.crecv.at[k - 1], device_id=(self.other(k) * 2 + self.core, self.m), device_id_type=MESH)

    def gather(self, k):
        return pltpu.make_async_remote_copy(
            src_ref=self.result.at[self.final(self.chip)], dst_ref=self.result.at[self.final(self.chip)], send_sem=self.gsend.at[k - 1],
            recv_sem=self.grecv.at[k - 1], device_id=(self.other(k) * 2 + self.core, self.m), device_id_type=MESH)

    def begin(self):
        self.first_swap().start()

    def second(self):
        self.first_swap().wait_recv()
        self.half[...] = (self.mine[self.side(self.core)].astype(F32) + self.pair[...].astype(F32)).astype(BF16)
        for k in range(1, self.chips):
            self.scatter(k).start()

    def third(self):
        for k in range(1, self.chips):
            self.scatter(k).wait_recv()
        summed = self.half[self.at(self.chip)].astype(F32)
        for k in range(1, self.chips):
            summed = summed + self.inbox[k - 1].astype(F32)
        self.result[self.final(self.chip)] = summed.astype(BF16)
        for k in range(1, self.chips):
            self.gather(k).start()

    def fourth(self):
        for k in range(1, self.chips):
            self.gather(k).wait_recv()
        self.last_swap().start()

    def end(self):
        self.last_swap().wait_recv()

    def finish(self):
        self.first_swap().wait_send()
        self.last_swap().wait_send()
        for k in range(1, self.chips):
            self.scatter(k).wait_send()
            self.gather(k).wait_send()


def plane_scratch(peers, rows, width):
    return [
        pltpu.VMEM((rows, width), BF16),
        pltpu.VMEM((rows // 2, width), BF16),
        pltpu.VMEM((rows // 2, width), BF16),
        pltpu.VMEM((peers // 2 - 1, rows // peers, width), BF16),
        dma(2), dma(2), dma(peers // 2 - 1), dma(peers // 2 - 1), dma(peers // 2 - 1), dma(peers // 2 - 1),
    ]


def exchange(targets, buf, inbox, send, recv):
    copies = [
        pltpu.make_async_remote_copy(src_ref=buf, dst_ref=inbox.at[k], send_sem=send.at[k], recv_sem=recv.at[k],
                                     device_id=target, device_id_type=MESH)
        for k, target in enumerate(targets)
    ]
    for copy in copies:
        copy.start()

    def collect():
        total = buf[...].astype(F32)
        for k, copy in enumerate(copies):
            copy.wait()
            total = total + inbox[k].astype(F32)
        return total

    return collect


def early_rows(width, experts):
    sizes = [width, width, DT_RANK, STATE, 16, experts + 8, experts + 8]
    return [sum(sizes[:i]) for i in range(len(sizes) + 1)]


def late_rows(width):
    sizes = [width, PROJ, 16]
    return [sum(sizes[:i]) for i in range(len(sizes) + 1)]


def whole_blocks(rows, peers):
    return -(-rows // (16 * peers)) * 16 * peers


def in_back_kernel(l, lanes, peers, experts, gpart_ref, gxs_ref, gzg_ref, conv_ref, taps_ref, bias_ref, since_ref, xp_ref, xs_ref, whole_ref,
                   act_ref, gain_ref, gmid_ref, gwout_ref, gshare_ref, gdtw_ref, gdtb_ref, galog_ref, gskip_ref, prior_ref, win_hbm,
                   up_ref, early_ref, late_ref, share_ref, gnorm_ref,
                   stage_ref, inbox_ref, gproj_ref, gpre_ref, gxi_ref, gconv_ref, cstage_ref, cinbox_ref, own_ref, psend, precv, csend, crecv,
                   win_ref, wsem, zbuf_ref, zin_ref, zsend, zrecv, nbuf_ref, nin_ref, nsend, nrecv, nbuf2_ref, nin2_ref, nsend2, nrecv2,
                   *plane):
    d, m = lax.axis_index("dp"), lax.axis_index("mp")
    rows, width = act_ref.shape
    ch = gxs_ref.shape[1]
    total = rows * lanes
    (weights,) = fetch([(win_hbm.at[l], win_ref)], wsem)
    greet(d, m, lanes, peers, True)
    line = [(d, lax.rem(m + k, lanes)) for k in range(1, lanes)]
    half = len(plane) // 2
    emine, lmine = plane[0], plane[half]
    early = PlaneSum(d, m, peers, *plane[:4], early_ref, *plane[4:half])
    late = PlaneSum(d, m, peers, *plane[half : half + 4], late_ref, *plane[half + 4 :])
    whole = whole_ref[...].reshape(total, width)
    at = early_rows(width, experts)
    till = late_rows(width)

    def early_work():
        emine[at[0] : at[1], :] = dot_tn(whole, gzg_ref[...]).astype(BF16)
        for i in range(width // ch):
            emine[at[1] + i * ch : at[1] + (i + 1) * ch, :] = gwout_ref[:, i * ch : (i + 1) * ch]
            emine[at[5 + i] : at[6 + i], :] = gshare_ref[:, i * ch : (i + 1) * ch].astype(BF16)
        emine[at[2] : at[3], :] = gdtw_ref[...].astype(BF16)
        emine[at[3] : at[4], :] = galog_ref[...].astype(BF16)
        emine[at[4] : at[5], :] = jnp.concatenate([gdtb_ref[...], gskip_ref[...], jnp.zeros((14, ch), F32)], axis=0).astype(BF16)
        if at[7] < emine.shape[0]:
            emine[at[7] :, :] = jnp.zeros((emine.shape[0] - at[7], ch), BF16)
        early.begin()

    finish = line_sum(gpart_ref, stage_ref, inbox_ref, psend, precv, gproj_ref, d, m, lanes, early_work)
    taps, bias = taps_ref[l], bias_ref[l : l + 1, :]
    gconv_ref[...] = jnp.zeros_like(gconv_ref)
    gpre_ref[total:, :] = jnp.zeros((HEAD, ch), F32)

    def first(c, carry):
        base = pl.multiple_of(c * CONV_ROWS, CONV_ROWS)
        pre, shifted = conv_window(conv_ref, since_ref, taps, bias, base)
        sig = sigmoid(pre)
        grad = gxs_ref[pl.ds(base, CONV_ROWS), :] + dot_tn(gproj_ref[:, pl.ds(base, CONV_ROWS)], xp_ref[l])
        grad = grad * (sig * (1.0 + pre * (1.0 - sig)))
        gpre_ref[pl.ds(base, CONV_ROWS), :] = grad
        for j in range(CONV):
            gconv_ref[CONV - 1 - j : CONV - j, :] += jnp.sum(grad * shifted[j], axis=0, keepdims=True)
        gconv_ref[CONV : CONV + 1, :] += jnp.sum(grad, axis=0, keepdims=True)
        return carry

    lax.fori_loop(0, total // CONV_ROWS, first, 0)

    def second(c, carry):
        base = pl.multiple_of(c * CONV_ROWS, CONV_ROWS)
        window = gpre_ref[pl.ds(base, CONV_ROWS + HEAD), :]
        since = since_ref[pl.ds(base, CONV_ROWS + HEAD), :]
        grad = taps[CONV - 1 : CONV, :] * window[:CONV_ROWS]
        for j in range(1, CONV):
            grad = grad + taps[CONV - 1 - j : CONV - j, :] * (window * (since >= j).astype(F32))[j : j + CONV_ROWS]
        gxi_ref[pl.ds(base, CONV_ROWS), :] = grad.astype(BF16)
        return carry

    lax.fori_loop(0, total // CONV_ROWS, second, 0)
    weights.wait()
    reduce = LineReduce(cstage_ref, cinbox_ref, csend, crecv, d, m, lanes)

    def term(s):
        part = pl.ds(pl.multiple_of(s * rows, 16), rows)
        return dot_nt(gxi_ref[part, :], win_ref[0]) + dot_nt(gzg_ref[part, :], win_ref[1])

    reduce.push(reduce.order[0], term(reduce.order[0]))
    early.second()
    lmine[till[0] : till[1], :] = dot_tn(whole, gxi_ref[...]).astype(BF16)
    lmine[till[1] : till[2], :] = dot(gproj_ref[...], xs_ref[...].astype(BF16)).astype(BF16)
    lmine[till[2] : till[3], :] = gconv_ref[...].astype(BF16)
    if till[3] < lmine.shape[0]:
        lmine[till[3] :, :] = jnp.zeros((lmine.shape[0] - till[3], ch), BF16)
    late.begin()
    for s in reduce.order[1:]:
        reduce.push(s, term(s))
    own_ref[...] = term(m)
    late.second()
    early.third()
    late.third()
    early.fourth()
    early.end()
    zbuf_ref[...] = early_ref[at[5] : at[7], :]
    shared = exchange(line, zbuf_ref, zin_ref, zsend, zrecv)
    late.fourth()
    reduce.total(own_ref)
    act = act_ref[...].astype(F32)
    pulled, grad_gain = norm_back(act, rms_inverse(act), gain_ref[l : l + 1, :], own_ref[...])
    up_ref[...] = gmid_ref[...] + pulled
    late.end()
    if l == 0:
        both = jnp.concatenate([grad_gain, prior_ref[...]], axis=0)
        groups = width // LANES
        for g in range(groups):
            nbuf_ref[2 * g : 2 * g + 2, :] = both[:, g * LANES : (g + 1) * LANES]
        nbuf_ref[2 * groups :, :] = jnp.zeros((nbuf_ref.shape[0] - 2 * groups, LANES), F32)
        nbuf2_ref[...] = exchange([(lax.rem(d + k, peers), m) for k in range(1, peers)], nbuf_ref, nin_ref, nsend, nrecv)()
        summed = exchange(line, nbuf2_ref, nin2_ref, nsend2, nrecv2)()
        gnorm_ref[...] = jnp.concatenate([summed[2 * g : 2 * g + 2, :] for g in range(groups)], axis=1)
    else:
        gnorm_ref[...] = grad_gain
    share_ref[...] = shared()
    finish()
    reduce.finish()
    early.finish()
    late.finish()


def in_back(l, lanes, peers, experts, gpart, gxs, gzg, conv, taps, bias, since, xp, xs, whole, act, gain, gmid, gwout, gshare, gdtw, gdtb,
            galog, gskip, prior, win):
    rows, width = act.shape
    ch, total = win.shape[3], rows * lanes
    early = whole_blocks(early_rows(width, experts)[-1], peers)
    late = whole_blocks(late_rows(width)[-1], peers)
    shared = 2 * (experts + 8)
    small = -(-2 * (width // LANES) // 8) * 8
    return pl.pallas_call(
        functools.partial(in_back_kernel, l, lanes, peers, experts),
        out_shape=[f32(rows, width), bf16(early, ch), bf16(late, ch), f32(shared, ch), f32(2 if l == 0 else 1, width)],
        in_specs=vmem(20) + hbm(1),
        out_specs=vmem(5),
        scratch_shapes=[
            pltpu.VMEM((2, PARTS, PROJ, total // PARTS), BF16),
            pltpu.VMEM((2, PARTS, PROJ, total // PARTS), BF16),
            pltpu.VMEM((PROJ, total), BF16),
            pltpu.VMEM((total + HEAD, ch), F32),
            pltpu.VMEM((total, ch), BF16),
            pltpu.VMEM((16, ch), F32),
            pltpu.VMEM((lanes, rows, width), BF16),
            pltpu.VMEM((2, lanes, rows, width), BF16),
            pltpu.VMEM((rows, width), F32),
            dma(2, PARTS), dma(2, PARTS), dma(lanes), dma(2, lanes),
            pltpu.VMEM(win.shape[1:], BF16), dma(1),
            pltpu.VMEM((shared, ch), BF16), pltpu.VMEM((lanes - 1, shared, ch), BF16), dma(lanes - 1), dma(lanes - 1),
            pltpu.VMEM((small, LANES), F32), pltpu.VMEM((peers - 1, small, LANES), F32), dma(peers - 1), dma(peers - 1),
            pltpu.VMEM((small, LANES), F32), pltpu.VMEM((lanes - 1, small, LANES), F32), dma(lanes - 1), dma(lanes - 1),
        ]
        + plane_scratch(peers, early, ch)
        + plane_scratch(peers, late, ch),
        compiler_params=params(6 + l),
        name="mamba_in_backward",
    )(gpart, gxs, gzg, conv, taps, bias, since, xp, xs, whole, act, gain, gmid, gwout, gshare, gdtw, gdtb, galog, gskip, prior, win)


def on_device(
    tokens, cotangent, lengths, routes, slot_place, norm_in, w_in, conv_w, conv_b, x_proj, dt_proj, dt_bias,
    a_log, d_skip, w_out, norm_moe, router, w_up, w_down,
):
    layers = norm_in.shape[0]
    rows_here, width = tokens.shape
    lanes, peers = lax.axis_size("mp"), lax.axis_size("dp")
    total = rows_here * lanes
    channels = w_in.shape[3]
    experts = router.shape[2]
    capacity = max(2, (5 * rows_here + 4 * experts - 1) // (4 * experts))
    padded = (capacity + 15) // 16 * 16
    position = lax.broadcasted_iota(jnp.int32, (total + HEAD, 1), 0)
    since, first = position, 0
    for i in range(lengths.shape[1] - 1):
        first = first + lengths[0, i]
        since = jnp.where(position >= first, position - first, since)
    since = jnp.where(position < total, since, 0)
    choose = (routes[:, None] == jnp.arange(LANES, dtype=jnp.int32)[None, :]).astype(F32)
    place = jnp.pad(routes * padded + slot_place, (0, -rows_here % LANES))
    place = jnp.broadcast_to(place[None, :], (8, place.shape[0]))
    spread = spread_matrix()
    x_proj = jnp.swapaxes(x_proj, 1, 2)
    router = jnp.pad(router, ((0, 0), (0, 0), (0, LANES - experts)))

    activation = tokens
    stored = []
    for l in range(layers):
        whole, conv_in, gate_in, conv_out, proj = in_block(l, lanes, activation, norm_in, conv_w, conv_b, since, x_proj, w_in)
        gated, ys, marks = scan_fwd(l, conv_out, gate_in, proj, since, dt_proj, dt_bias, a_log, d_skip, spread)
        gated = gated.reshape(lanes, rows_here, channels)
        middle, chance, into, arrived, hidden, active, picked, following = mid_block(
            l, lanes, peers, experts, padded, activation, gated, norm_moe, router, choose, place, w_out, w_up, w_down)
        stored.append((activation, whole, conv_in, gate_in, conv_out, proj, gated, ys, marks, middle, chance, into, arrived, hidden, active, picked))
        activation = following
    upstream = cotangent
    collected = []
    grad_norm_in = jnp.zeros((1, width), F32)
    for l in reversed(range(layers)):
        before, whole, conv_in, gate_in, conv_out, proj, gated, ys, marks, middle, chance, into, arrived, hidden, active, picked = stored[l]
        grad_middle, grad_up, grad_down, grad_gated, grad_w_out, grad_share = moe_back(
            l, lanes, peers, experts, upstream, chance, choose, picked, middle, norm_moe, router, into, arrived, hidden, active, gated,
            w_out, w_up, w_down)
        grad_conv, grad_zg, grad_proj, grad_dtw, grad_dtb, grad_alog, grad_skip = scan_bwd(
            l, conv_out, gate_in, proj, since, ys, grad_gated.reshape(total, channels), marks, dt_proj, dt_bias, a_log, d_skip, spread)
        upstream, early, late, share, grad_norm_in = in_back(
            l, lanes, peers, experts, grad_proj, grad_conv, grad_zg, conv_in, conv_w, conv_b, since, x_proj, conv_out, whole,
            before, norm_in, grad_middle, grad_w_out, grad_share, grad_dtw, grad_dtb, grad_alog, grad_skip, grad_norm_in, w_in)
        collected.append((early, late, share, grad_up, grad_down))
    collected = collected[::-1]
    at, till = early_rows(width, experts), late_rows(width)

    def stacked(make):
        return jnp.stack([make(*entry).astype(F32) for entry in collected])

    def from_early(first, count):
        return stacked(lambda early, *rest: early[first : first + count])

    def from_late(first, count):
        return stacked(lambda early, late, *rest: late[first : first + count])

    def wide(rows, first, count):
        return jnp.concatenate([rows[first + i * count : first + (i + 1) * count] for i in range(width // channels)], axis=1)

    return (
        activation,
        upstream,
        grad_norm_in,
        stacked(lambda early, late, *rest: jnp.stack([late[till[0] : till[1]], early[at[0] : at[1]]])),
        from_late(till[2], CONV),
        from_late(till[2] + CONV, 1)[:, 0],
        jnp.swapaxes(from_late(till[1], PROJ), 1, 2),
        from_early(at[2], DT_RANK),
        from_early(at[4], 1)[:, 0],
        from_early(at[3], STATE),
        from_early(at[4] + 1, 1)[:, 0],
        stacked(lambda early, *rest: wide(early, at[1], channels)),
        stacked(lambda early, late, share, *rest: wide(share, 0, experts + 8)[experts]),
        stacked(lambda early, late, share, *rest: wide(share, 0, experts + 8)[:experts].T),
        jnp.stack([entry[3][None] for entry in collected]),
        jnp.stack([entry[4][None] for entry in collected]),
    )


def solution(mesh):
    return jax.shard_map(
        on_device,
        mesh=mesh,
        in_specs=(
            P(("dp", "mp"), None),
            P(("dp", "mp"), None),
            P("dp", None),
            P(("dp", "mp")),
            P(("dp", "mp")),
            P(),
            P(None, None, None, "mp"),
            P(None, None, "mp"),
            P(None, "mp"),
            P(None, "mp", None),
            P(None, None, "mp"),
            P(None, "mp"),
            P(None, None, "mp"),
            P(None, "mp"),
            P(None, "mp", None),
            P(),
            P(),
            P(None, "dp", None, "mp"),
            P(None, "dp", "mp", None),
        ),
        out_specs=(
            P(("dp", "mp"), None),
            P(("dp", "mp"), None),
            P(),
            P(None, None, None, "mp"),
            P(None, None, "mp"),
            P(None, "mp"),
            P(None, "mp", None),
            P(None, None, "mp"),
            P(None, "mp"),
            P(None, None, "mp"),
            P(None, "mp"),
            P(None, "mp", None),
            P(),
            P(),
            P(None, "dp", None, "mp"),
            P(None, "dp", "mp", None),
        ),
        check_vma=False,
    )
```

```python
import functools
import types

import jax
import jax.numpy as jnp
from jax import lax
from jax.experimental import pallas as pl
from jax.experimental.pallas import tpu as pltpu
from jax.sharding import PartitionSpec as P

STATE = 16
DT_RANK = 48
LANES = 128
CHUNK = 128
LOG2E = 1.4426950408889634
RESET = 1.0e6
PROJ = DT_RANK + 2 * STATE
CONV = 4
dt_most = 0.05
epsilon = 1e-05
highest = lax.Precision.HIGHEST
MESH = pl.DeviceIdType.MESH
F32, BF16 = jnp.float32, jnp.bfloat16


def sigmoid(v):
    return 1.0 / (1.0 + jnp.exp(-v))


def dot(a, b):
    return jnp.dot(a, b, preferred_element_type=F32)


def dot_nt(a, b):
    return lax.dot_general(a, b, (((1,), (1,)), ((), ())), preferred_element_type=F32)


def dot_tn(a, b):
    return lax.dot_general(a, b, (((0,), (0,)), ((), ())), preferred_element_type=F32)


def spread_matrix():
    rows = lax.broadcasted_iota(jnp.int32, (STATE, STATE * LANES), 0)
    cols = lax.broadcasted_iota(jnp.int32, (STATE, STATE * LANES), 1)
    return (rows == cols // LANES).astype(BF16)


def put(ref, value):
    for j in range(ref.shape[0]):
        ref[j] = value[:, j * LANES : (j + 1) * LANES]


def spread_rows(proj, spread, out_ref):
    wide = dot_tn(proj, spread)
    for n in range(STATE):
        out_ref[pl.ds(n, CHUNK, stride=STATE), :] = wide[:, n * LANES : (n + 1) * LANES]


def scan_fwd_kernel(l, xs_ref, zg_ref, proj_ref, since_ref, dtw_ref, dtb_ref, alog_ref, skip_ref, spread_ref,
                    gated_ref, ys_ref, hck_ref,
                    h_ref, dm_ref, dx_ref, bx_ref, cx_ref, yq_ref):
    groups = xs_ref.shape[1] // LANES

    @pl.when(pl.program_id(0) == 0)
    def _():
        h_ref[...] = jnp.zeros_like(h_ref)

    hck_ref[0] = h_ref[...]
    proj = proj_ref[...]
    xs = xs_ref[...]
    delta = dt_most * sigmoid(dot_tn(proj[:DT_RANK], dtw_ref[l]) + dtb_ref[l : l + 1, :])
    put(dm_ref, delta + RESET * (since_ref[...] == 0).astype(F32))
    put(dx_ref, delta * xs)
    spread_rows(proj[DT_RANK : DT_RANK + STATE], spread_ref[...], bx_ref)
    spread_rows(proj[DT_RANK + STATE :], spread_ref[...], cx_ref)
    rate = -LOG2E * jnp.exp(alog_ref[l])
    rates = [rate[:, j * LANES : (j + 1) * LANES] for j in range(groups)]

    def step(g, hs):
        hs = list(hs)
        t0 = pl.multiple_of(g * 8, 8)
        for i in range(8):
            t = t0 + i
            r0 = pl.multiple_of(t * STATE, STATE)
            b = bx_ref[pl.ds(r0, STATE), :]
            c = cx_ref[pl.ds(r0, STATE), :]
            q0 = pl.multiple_of(t * 8, 8)
            for j in range(groups):
                lanes = slice(j * LANES, (j + 1) * LANES)
                dec = jnp.exp2(dm_ref[j, pl.ds(t, 1), :] * rates[j])
                hs[j] = dec * hs[j] + dx_ref[j, pl.ds(t, 1), :] * b
                q = c * hs[j]
                yq_ref[j, pl.ds(q0, 8), :] = q[:8] + q[8:]
        return tuple(hs)

    hs = lax.fori_loop(0, CHUNK // 8, step, tuple(h_ref[:, j * LANES : (j + 1) * LANES] for j in range(groups)))
    for j in range(groups):
        h_ref[:, j * LANES : (j + 1) * LANES] = hs[j]
    zg = zg_ref[...]
    for j in range(groups):
        lanes = slice(j * LANES, (j + 1) * LANES)
        y = skip_ref[l : l + 1, lanes] * xs[:, lanes]
        for k in range(8):
            y = y + yq_ref[j, pl.ds(k, CHUNK, stride=8), :]
        ys_ref[:, lanes] = y
        z = zg[:, lanes]
        gated_ref[:, lanes] = (y * z * sigmoid(z)).astype(BF16)


def scan_fwd(l, xs, zg, proj, since, dtw, dtb, alog, skip, spread):
    rows, ch = xs.shape
    steps = rows // CHUNK
    row = lambda w: pl.BlockSpec((CHUNK, w), lambda i: (i, 0))
    full = lambda s: pl.BlockSpec(s, lambda i: (0,) * len(s))
    return pl.pallas_call(
        functools.partial(scan_fwd_kernel, l),
        grid=(steps,),
        out_shape=[
            jax.ShapeDtypeStruct((rows, ch), BF16),
            jax.ShapeDtypeStruct((rows, ch), F32),
            jax.ShapeDtypeStruct((steps, STATE, ch), F32),
        ],
        in_specs=[row(ch), row(ch), pl.BlockSpec((PROJ, CHUNK), lambda i: (0, i)), row(1)]
        + [full(v.shape) for v in (dtw, dtb, alog, skip, spread)],
        out_specs=[row(ch), row(ch), pl.BlockSpec((1, STATE, ch), lambda i: (i, 0, 0))],
        scratch_shapes=[
            pltpu.VMEM((STATE, ch), F32),
            pltpu.VMEM((ch // LANES, CHUNK, LANES), F32),
            pltpu.VMEM((ch // LANES, CHUNK, LANES), F32),
            pltpu.VMEM((CHUNK * STATE, LANES), F32),
            pltpu.VMEM((CHUNK * STATE, LANES), F32),
            pltpu.VMEM((ch // LANES, CHUNK * 8, LANES), F32),
        ],
        compiler_params=pltpu.CompilerParams(vmem_limit_bytes=60 << 20),
        name="scan_fwd",
    )(xs, zg, proj, since, dtw, dtb, alog, skip, spread)


def scan_bwd_kernel(l, xs_ref, zg_ref, proj_ref, since_ref, ys_ref, gg_ref, hck_ref, dtw_ref, dtb_ref, alog_ref, skip_ref, spread_ref,
                    gxs_ref, gzg_ref, gproj_ref, gdtw_ref, gdtb_ref, galog_ref, gskip_ref,
                    a_ref, dm_ref, dx_ref, dl_ref, gy_ref, bx_ref, cx_ref, h_ref, dec_ref, pq_ref, gq_ref, gb_ref, gc_ref):
    groups = xs_ref.shape[1] // LANES
    cols = [slice(j * LANES, (j + 1) * LANES) for j in range(groups)]

    @pl.when(pl.program_id(0) == 0)
    def _():
        a_ref[...] = jnp.zeros_like(a_ref)
        gdtw_ref[...] = jnp.zeros_like(gdtw_ref)
        gdtb_ref[...] = jnp.zeros_like(gdtb_ref)
        galog_ref[...] = jnp.zeros_like(galog_ref)
        gskip_ref[...] = jnp.zeros_like(gskip_ref)

    proj = proj_ref[...]
    xs = xs_ref[...]
    delta = dt_most * sigmoid(dot_tn(proj[:DT_RANK], dtw_ref[l]) + dtb_ref[l : l + 1, :])
    put(dl_ref, delta)
    put(dm_ref, delta + RESET * (since_ref[...] == 0).astype(F32))
    put(dx_ref, delta * xs)
    zg = zg_ref[...]
    sz = sigmoid(zg)
    gg = gg_ref[...]
    gy = gg * (zg * sz)
    put(gy_ref, gy)
    gzg_ref[...] = (gg * ys_ref[...] * (sz * (1.0 + zg * (1.0 - sz)))).astype(BF16)
    gskip_ref[...] += jnp.sum(gy * xs, axis=0, keepdims=True)
    spread_rows(proj[DT_RANK : DT_RANK + STATE], spread_ref[...], bx_ref)
    spread_rows(proj[DT_RANK + STATE :], spread_ref[...], cx_ref)
    rate = -jnp.exp(alog_ref[l])
    rates2 = [LOG2E * rate[:, c] for c in cols]
    rates = [rate[:, c] for c in cols]

    for j in range(groups):
        h_ref[j, :STATE, :] = hck_ref[0][:, cols[j]]

    def again(g, hs):
        hs = list(hs)
        t0 = pl.multiple_of(g * 8, 8)
        for i in range(8):
            t = t0 + i
            r0 = pl.multiple_of(t * STATE, STATE)
            r1 = pl.multiple_of(t * STATE + STATE, STATE)
            b = bx_ref[pl.ds(r0, STATE), :]
            for j in range(groups):
                dec = jnp.exp2(dm_ref[j, pl.ds(t, 1), :] * rates2[j])
                hs[j] = dec * hs[j] + dx_ref[j, pl.ds(t, 1), :] * b
                dec_ref[j, pl.ds(r0, STATE), :] = dec
                h_ref[j, pl.ds(r1, STATE), :] = hs[j]
        return tuple(hs)

    last = lax.fori_loop(0, CHUNK // 8, again, tuple(hck_ref[0][:, c] for c in cols))

    def back(g, carry):
        carry = [list(c) for c in carry]
        aa, hs, acc = carry
        t0 = pl.multiple_of(CHUNK - 8 - g * 8, 8)
        for i in reversed(range(8)):
            t = t0 + i
            r0 = pl.multiple_of(t * STATE, STATE)
            q0 = pl.multiple_of(t * 8, 8)
            b = bx_ref[pl.ds(r0, STATE), :]
            c = cx_ref[pl.ds(r0, STATE), :]
            gb, gc = None, None
            for j in range(groups):
                gyj = gy_ref[j, pl.ds(t, 1), :]
                a = c * gyj + aa[j]
                dec = dec_ref[j, pl.ds(r0, STATE), :]
                before = h_ref[j, pl.ds(r0, STATE), :]
                carry_a = dec * a
                p = carry_a * before * rates[j]
                ab = a * b
                pq_ref[j, pl.ds(q0, 8), :] = p[:8] + p[8:]
                gq_ref[j, pl.ds(q0, 8), :] = ab[:8] + ab[8:]
                acc[j] = acc[j] + p * dl_ref[j, pl.ds(t, 1), :]
                gbj = a * dx_ref[j, pl.ds(t, 1), :]
                gcj = gyj * hs[j]
                gb = gbj if gb is None else gb + gbj
                gc = gcj if gc is None else gc + gcj
                aa[j] = carry_a
                hs[j] = before
            gb_ref[pl.ds(r0, STATE), :] = gb
            gc_ref[pl.ds(r0, STATE), :] = gc
        return tuple(tuple(c) for c in carry)

    aa, _, acc = lax.fori_loop(
        0, CHUNK // 8, back,
        (tuple(a_ref[:, c] for c in cols), last, tuple(jnp.zeros((STATE, LANES), F32) for _ in cols)))
    for j in range(groups):
        a_ref[:, cols[j]] = aa[j]
        galog_ref[:, cols[j]] += acc[j]

    skip = skip_ref[l : l + 1, :]
    gdts = []
    for j in range(groups):
        psum = pq_ref[j, pl.ds(0, CHUNK, stride=8), :]
        gsum = gq_ref[j, pl.ds(0, CHUNK, stride=8), :]
        for k in range(1, 8):
            psum = psum + pq_ref[j, pl.ds(k, CHUNK, stride=8), :]
            gsum = gsum + gq_ref[j, pl.ds(k, CHUNK, stride=8), :]
        dl = delta[:, cols[j]]
        gdelta = psum + xs[:, cols[j]] * gsum
        gxs_ref[:, cols[j]] = dl * gsum + skip[:, cols[j]] * gy[:, cols[j]]
        gdts.append(gdelta * dl * (1.0 - dl * (1.0 / dt_most)))
    gdt = jnp.concatenate(gdts, axis=1)
    gdtb_ref[...] += jnp.sum(gdt, axis=0, keepdims=True)
    gdt_low = gdt.astype(BF16)
    gdtw_ref[...] += dot(proj[:DT_RANK], gdt_low)
    gproj_ref[:DT_RANK, :] = dot_nt(dtw_ref[l], gdt_low)
    wide_b = jnp.concatenate([gb_ref[pl.ds(n, CHUNK, stride=STATE), :].astype(BF16) for n in range(STATE)], axis=1)
    gproj_ref[DT_RANK : DT_RANK + STATE, :] = dot_nt(spread_ref[...], wide_b)
    wide_c = jnp.concatenate([gc_ref[pl.ds(n, CHUNK, stride=STATE), :].astype(BF16) for n in range(STATE)], axis=1)
    gproj_ref[DT_RANK + STATE :, :] = dot_nt(spread_ref[...], wide_c)


def scan_bwd(l, xs, zg, proj, since, ys, gg, hck, dtw, dtb, alog, skip, spread):
    rows, ch = xs.shape
    steps = rows // CHUNK
    row = lambda w: pl.BlockSpec((CHUNK, w), lambda i: (steps - 1 - i, 0))
    full = lambda s: pl.BlockSpec(s, lambda i: (0,) * len(s))
    big = lambda: pltpu.VMEM((CHUNK * STATE, LANES), F32)
    g = ch // LANES
    return pl.pallas_call(
        functools.partial(scan_bwd_kernel, l),
        grid=(steps,),
        out_shape=[
            jax.ShapeDtypeStruct((rows, ch), F32),
            jax.ShapeDtypeStruct((rows, ch), BF16),
            jax.ShapeDtypeStruct((PROJ, rows), F32),
            jax.ShapeDtypeStruct((DT_RANK, ch), F32),
            jax.ShapeDtypeStruct((1, ch), F32),
            jax.ShapeDtypeStruct((STATE, ch), F32),
            jax.ShapeDtypeStruct((1, ch), F32),
        ],
        in_specs=[row(ch), row(ch), pl.BlockSpec((PROJ, CHUNK), lambda i: (0, steps - 1 - i)), row(1), row(ch), row(ch),
                  pl.BlockSpec((1, STATE, ch), lambda i: (steps - 1 - i, 0, 0))]
        + [full(v.shape) for v in (dtw, dtb, alog, skip, spread)],
        out_specs=[row(ch), row(ch), pl.BlockSpec((PROJ, CHUNK), lambda i: (0, steps - 1 - i)), full((DT_RANK, ch)), full((1, ch)), full((STATE, ch)), full((1, ch))],
        scratch_shapes=[
            pltpu.VMEM((STATE, ch), F32),
            pltpu.VMEM((ch // LANES, CHUNK, LANES), F32),
            pltpu.VMEM((ch // LANES, CHUNK, LANES), F32),
            pltpu.VMEM((ch // LANES, CHUNK, LANES), F32),
            pltpu.VMEM((ch // LANES, CHUNK, LANES), F32),
            big(), big(),
            pltpu.VMEM((g, CHUNK * STATE + STATE, LANES), F32),
            pltpu.VMEM((g, CHUNK * STATE, LANES), F32),
            pltpu.VMEM((g, CHUNK * 8, LANES), F32),
            pltpu.VMEM((g, CHUNK * 8, LANES), F32),
            big(), big(),
        ],
        compiler_params=pltpu.CompilerParams(vmem_limit_bytes=60 << 20),
        name="scan_bwd",
    )(xs, zg, proj, since, ys, gg, hck, dtw, dtb, alog, skip, spread)


def rms_inverse(values):
    return lax.rsqrt(jnp.mean(values * values, axis=-1, keepdims=True) + epsilon)


def norm_back(values, inverse, gain, grad):
    scaled = grad * gain
    pulled = inverse * scaled - values * (inverse * inverse * inverse) * jnp.mean(scaled * values, axis=-1, keepdims=True)
    return pulled, jnp.sum(grad * values * inverse, axis=0, keepdims=True)


GELU_A, GELU_B = 0.7978845608028654, 0.044715


def gelu(v):
    return 0.5 * v * (1.0 + jnp.tanh(GELU_A * (v + GELU_B * v * v * v)))


def gelu_slope(v):
    square = v * v
    t = jnp.tanh(GELU_A * v * (1.0 + GELU_B * square))
    return 0.5 * (1.0 + t) + 0.5 * v * (1.0 - t * t) * GELU_A * (1.0 + 3.0 * GELU_B * square)


def by_lane(m, values):
    picked = jnp.int32(values[0])
    for k in range(1, len(values)):
        picked = jnp.where(m == k, jnp.int32(values[k]), picked)
    return picked


def nearest_first(m, lanes):
    orders = [sorted((s for s in range(lanes) if s != k), key=lambda s: (abs(s - k), s)) for k in range(lanes)]
    return [by_lane(m, [order[i] for order in orders]) for i in range(lanes - 1)]


def chain_order(m, lanes):
    def due(k, s):
        return (lanes - 1 - s) + k if s > k else s + (lanes - 1 - k)

    orders = [sorted((s for s in range(lanes) if s != k), key=lambda s: (due(k, s), s)) for k in range(lanes)]
    return [by_lane(m, [order[i] for order in orders]) for i in range(lanes - 1)]


def greet(d, m, lanes, peers, across):
    barrier = pltpu.get_barrier_semaphore()
    if across:
        for k in range(1, lanes):
            pl.semaphore_signal(barrier, inc=1, device_id=(d, lax.rem(m + k, lanes)), device_id_type=MESH)
        for k in range(1, peers):
            pl.semaphore_signal(barrier, inc=1, device_id=(lax.rem(d + k, peers), m), device_id_type=MESH)
        pl.semaphore_wait(barrier, lanes + peers - 2)
    else:

        @pl.when(m > 0)
        def _():
            pl.semaphore_signal(barrier, inc=1, device_id=(d, m - 1), device_id_type=MESH)

        @pl.when(m < lanes - 1)
        def _():
            pl.semaphore_signal(barrier, inc=1, device_id=(d, m + 1), device_id_type=MESH)

        pl.semaphore_wait(barrier, jnp.where(m > 0, 1, 0) + jnp.where(m < lanes - 1, 1, 0))


class LineGather:
    def __init__(self, buf, send, recv, d, m, lanes):
        self.buf, self.send, self.recv, self.d, self.m, self.lanes = buf, send, recv, d, m, lanes
        self.order = nearest_first(m, lanes)

    def copy(self, s, up):
        return pltpu.make_async_remote_copy(
            src_ref=self.buf.at[s], dst_ref=self.buf.at[s], send_sem=self.send.at[0 if up else 1, s],
            recv_sem=self.recv.at[s], device_id=(self.d, self.m + 1 if up else self.m - 1), device_id_type=MESH,
        )

    def start(self):
        @pl.when(self.m < self.lanes - 1)
        def _():
            self.copy(self.m, True).start()

        @pl.when(self.m > 0)
        def _():
            self.copy(self.m, False).start()

    def arrive(self, i):
        s, m = self.order[i], self.m
        self.copy(s, True).wait_recv()

        @pl.when((s < m) & (m < self.lanes - 1))
        def _():
            self.copy(s, True).start()

        @pl.when((s > m) & (m > 0))
        def _():
            self.copy(s, False).start()

        return s

    def finish(self):
        for s in range(self.lanes):

            @pl.when((s <= self.m) & (self.m < self.lanes - 1))
            def _():
                self.copy(s, True).wait_send()

            @pl.when((s >= self.m) & (self.m > 0))
            def _():
                self.copy(s, False).wait_send()


PIECES = 1


class LineReduce:
    def __init__(self, stage, inbox, send, recv, d, m, lanes):
        self.stage, self.inbox, self.send, self.recv = stage, inbox, send, recv
        self.d, self.m, self.lanes = d, m, lanes
        self.rows = stage.shape[1] // PIECES
        self.order = chain_order(m, lanes)
        self.middle = jnp.logical_and(m > 0, m < lanes - 1)
        self.at_end = jnp.logical_not(self.middle)

    def piece(self, p):
        return pl.ds(p * self.rows, self.rows)

    def copy(self, s, p):
        up = s > self.m
        side = jnp.where(up, 0, 1)
        return pltpu.make_async_remote_copy(
            src_ref=self.stage.at[s, self.piece(p)], dst_ref=self.inbox.at[side, s, self.piece(p)], send_sem=self.send.at[s, p],
            recv_sem=self.recv.at[side, s, p], device_id=(self.d, jnp.where(up, self.m + 1, self.m - 1)), device_id_type=MESH,
        )

    def push_first(self, s, term):
        self.stage[s] = term.astype(BF16)
        for p in range(PIECES):
            self.copy(s, p).start()

    def push_on(self, s, p, term):
        side = jnp.where(s > self.m, 0, 1)
        self.copy(s, p).wait_recv()
        self.stage[s, self.piece(p)] = (term + self.inbox[side, s, self.piece(p)].astype(F32)).astype(BF16)
        self.copy(s, p).start()

    def push(self, s, term):
        @pl.when(self.at_end)
        def _():
            self.push_first(s, term)

        @pl.when(self.middle)
        def _():
            for p in range(PIECES):
                self.push_on(s, p, term[p * self.rows : (p + 1) * self.rows])

    def total(self, own_ref):
        m = self.m

        def add(side):
            for p in range(PIECES):
                pltpu.make_async_remote_copy(
                    src_ref=self.stage.at[m, self.piece(p)], dst_ref=self.inbox.at[side, m, self.piece(p)], send_sem=self.send.at[m, p],
                    recv_sem=self.recv.at[side, m, p], device_id=(self.d, m), device_id_type=MESH,
                ).wait_recv()
            own_ref[...] += self.inbox[side, m].astype(F32)

        @pl.when(m > 0)
        def _():
            add(0)

        @pl.when(m < self.lanes - 1)
        def _():
            add(1)

    def finish(self):
        for s in self.order:
            for p in range(PIECES):
                self.copy(s, p).wait_send()


def reduce_scratch(lanes, rows, width):
    return [
        pltpu.VMEM((lanes, rows, width), BF16),
        pltpu.VMEM((2, lanes, rows, width), BF16),
        dma(lanes, PIECES), dma(2, lanes, PIECES),
    ]


PARTS = 2


def line_sum(part, stage, inbox, send, recv, out, d, m, lanes, between=lambda: None):
    width = part.shape[1] // PARTS

    def copy(side, b):
        return pltpu.make_async_remote_copy(
            src_ref=stage.at[side, b], dst_ref=inbox.at[side, b], send_sem=send.at[side, b], recv_sem=recv.at[side, b],
            device_id=(d, m + 1 if side == 0 else m - 1), device_id_type=MESH,
        )

    def step(side, b):
        has_source = m > 0 if side == 0 else m < lanes - 1
        has_target = m < lanes - 1 if side == 0 else m > 0
        cols = slice(b * width, (b + 1) * width)

        @pl.when(has_source)
        def _():
            copy(side, b).wait_recv()

        @pl.when(jnp.logical_not(has_source))
        def _():
            inbox[side, b] = jnp.zeros(inbox.shape[2:], BF16)

        @pl.when(has_target)
        def _():
            stage[side, b] = (part[:, cols] + inbox[side, b].astype(F32)).astype(BF16)
            copy(side, b).start()

    low = 2 * m < lanes

    def both(first):
        def run(side):
            for b in range(PARTS):
                step(side, b)

        @pl.when(low)
        def _():
            run(0 if first else 1)

        @pl.when(jnp.logical_not(low))
        def _():
            run(1 if first else 0)

    both(True)
    between()
    both(False)
    for b in range(PARTS):
        cols = slice(b * width, (b + 1) * width)
        out[:, cols] = (part[:, cols] + inbox[0, b].astype(F32) + inbox[1, b].astype(F32)).astype(BF16)

    def finish():
        for b in range(PARTS):

            @pl.when(m < lanes - 1)
            def _():
                copy(0, b).wait_send()

            @pl.when(m > 0)
            def _():
                copy(1, b).wait_send()

    return finish


def vmem(count):
    return [pl.BlockSpec(memory_space=pltpu.VMEM)] * count


def f32(*shape):
    return jax.ShapeDtypeStruct(shape, F32)


def bf16(*shape):
    return jax.ShapeDtypeStruct(shape, BF16)


def dma(*shape):
    return pltpu.SemaphoreType.DMA(shape)


def hbm(count):
    return [pl.BlockSpec(memory_space=pl.ANY)] * count


def fetch(pairs, sem):
    copies = [pltpu.make_async_copy(src, dst, sem.at[i]) for i, (src, dst) in enumerate(pairs)]
    for copy in copies:
        copy.start()
    return copies


def params(cid, limit=58):
    return pltpu.CompilerParams(collective_id=cid, has_side_effects=True, vmem_limit_bytes=limit << 20)


CONV_ROWS = 128
HEAD = 8


def conv_window(padded_ref, since_ref, taps, bias, base):
    window = padded_ref[pl.ds(base, CONV_ROWS + HEAD), :]
    since = since_ref[pl.ds(base, CONV_ROWS), :]
    shifted = [window[HEAD:]]
    for j in range(1, CONV):
        shifted.append(window[HEAD - j : HEAD - j + CONV_ROWS] * (since >= j).astype(F32))
    pre = bias
    for j in range(CONV):
        pre = pre + taps[CONV - 1 - j : CONV - j, :] * shifted[j]
    return pre, shifted


class Experts:
    def __init__(self, d, m, lanes, peers, into_ref, rows_ref, pack_ref, slots_ref, part_ref, back_ref, stage_ref, inbox_ref,
                 gsend, grecv, dsend, drecv, bsend, brecv, rsend, rrecv):
        self.d, self.m, self.lanes, self.peers = d, m, lanes, peers
        self.rows, self.into, self.pack, self.slots, self.part, self.back = rows_ref, into_ref, pack_ref, slots_ref, part_ref, back_ref
        self.stage, self.inbox = stage_ref, inbox_ref
        self.dsend, self.drecv, self.bsend, self.brecv, self.rsend, self.rrecv = dsend, drecv, bsend, brecv, rsend, rrecv
        self.sets = rows_ref.shape[1]
        self.cap = pack_ref.shape[2] // self.sets
        self.width = rows_ref.shape[3]
        self.gather = LineGather(rows_ref, gsend, grecv, d, m, lanes)

    def slot_rows(self, ref, s, i):
        return ref[s, :, i * self.cap : (i + 1) * self.cap, :].reshape(self.peers * self.cap, self.width)

    def set_slot_rows(self, ref, s, i, value):
        ref[s, :, i * self.cap : (i + 1) * self.cap, :] = value.reshape(self.peers, self.cap, self.width)

    def hop(self, src, dst, send, recv, s, k):
        other = lax.rem(self.d + k, self.peers)
        return pltpu.make_async_remote_copy(
            src_ref=src.at[s, other], dst_ref=dst.at[s, self.d], send_sem=send.at[s, k - 1],
            recv_sem=recv.at[s, k - 1], device_id=(other, self.m), device_id_type=MESH,
        )

    def across(self, src, dst, send, recv, s):
        for k in range(1, self.peers):
            self.hop(src, dst, send, recv, s, k).start()
        dst[s, self.d] = src[s, self.d]

    def dispatch(self, s):
        for i in range(self.sets):
            self.set_slot_rows(self.pack, s, i, dot(self.into[s], self.rows[s, i]).astype(BF16))
        self.across(self.pack, self.slots, self.dsend, self.drecv, s)

    def answer(self, s, expert):
        for k in range(1, self.peers):
            self.hop(self.pack, self.slots, self.dsend, self.drecv, s, k).wait_recv()
        for i, value in enumerate(expert(s, [self.slot_rows(self.slots, s, i) for i in range(self.sets)])):
            self.set_slot_rows(self.part, s, i, value.astype(BF16))
        self.across(self.part, self.back, self.bsend, self.brecv, s)

    def home(self, s):
        return pltpu.make_async_remote_copy(
            src_ref=self.stage.at[s], dst_ref=self.inbox.at[self.m], send_sem=self.rsend.at[s], recv_sem=self.rrecv.at[self.m],
            device_id=(self.d, s), device_id_type=MESH,
        )

    def combine(self, s):
        for k in range(1, self.peers):
            self.hop(self.part, self.back, self.bsend, self.brecv, s, k).wait_recv()
        return [dot_tn(self.into[s], self.slot_rows(self.back, s, i)) for i in range(self.sets)]

    def combine_away(self, s):
        for i, value in enumerate(self.combine(s)):
            self.stage[s, i] = value.astype(BF16)
        self.home(s).start()

    def run(self, expert, own_ref, meanwhile):
        one, two, three = self.gather.order
        self.gather.start()
        self.dispatch(self.m)
        self.gather.arrive(0)
        self.dispatch(one)
        self.gather.arrive(1)
        self.dispatch(two)
        self.answer(one, expert)
        self.gather.arrive(2)
        self.dispatch(three)
        self.answer(two, expert)
        self.combine_away(one)
        self.answer(three, expert)
        self.combine_away(two)
        self.answer(self.m, expert)
        self.combine_away(three)
        for i, value in enumerate(self.combine(self.m)):
            own_ref[i] = value
        meanwhile()
        for s in (one, two, three):
            pltpu.make_async_remote_copy(
                src_ref=self.stage.at[s], dst_ref=self.inbox.at[s], send_sem=self.rsend.at[s], recv_sem=self.rrecv.at[s],
                device_id=(self.d, s), device_id_type=MESH,
            ).wait_recv()
            own_ref[...] += self.inbox[s].astype(F32)

    def finish(self):
        self.gather.finish()
        order = [self.m, *self.gather.order]
        for s in order:
            for k in range(1, self.peers):
                self.hop(self.pack, self.slots, self.dsend, self.drecv, s, k).wait_send()
                self.hop(self.part, self.back, self.bsend, self.brecv, s, k).wait_send()
        for s in order[1:]:
            self.home(s).wait_send()


def large(v):
    return v.size * v.dtype.itemsize >= 1 << 17


class Refs(types.SimpleNamespace):
    def need(self, *refs):
        for ref in refs:
            if id(ref) in self.coming:
                self.coming.pop(id(ref)).wait()

    def ship(self, *refs):
        for ref in refs:
            self.gone.append(self.going.pop(id(ref)))
            self.gone[-1].start()


def launch(name, cid, body, inputs, far, outputs, scratch, limit=58):
    near = {k: v for k, v in inputs.items() if not large(v)}
    lazy = {k: v for k, v in inputs.items() if large(v)}
    prompt = {k: v for k, v in outputs.items() if not large(v)}
    late = {k: v for k, v in outputs.items() if large(v)}
    buffers = {k: pltpu.VMEM(v.shape, v.dtype) for k, v in {**lazy, **late}.items()}
    away = [k + "_far" for k in (*lazy, *late)]
    names = [*near, *away[: len(lazy)], *far, *prompt, *away[len(lazy) :], *scratch, *buffers, "moves"]

    def kernel(*refs):
        r = Refs(**dict(zip(names, refs)))
        get = lambda k: getattr(r, k)
        r.gone = []
        r.coming = {id(get(k)): pltpu.make_async_copy(get(k + "_far"), get(k), r.moves.at[i]) for i, k in enumerate(lazy)}
        r.going = {id(get(k)): pltpu.make_async_copy(get(k), get(k + "_far"), r.moves.at[len(lazy) + i]) for i, k in enumerate(late)}
        for copy in r.coming.values():
            copy.start()
        body(r)
        r.need(*map(get, lazy))
        r.ship(*(get(k) for k in late if id(get(k)) in r.going))
        for copy in r.gone:
            copy.wait()

    results = pl.pallas_call(
        kernel,
        out_shape=[*prompt.values(), *late.values()],
        in_specs=vmem(len(near)) + hbm(len(lazy) + len(far)),
        out_specs=vmem(len(prompt)) + hbm(len(late)),
        scratch_shapes=[*scratch.values(), *buffers.values(), dma(max(1, len(lazy) + len(late)))],
        compiler_params=params(cid, limit),
        name=name,
    )(*near.values(), *lazy.values(), *far.values())
    return types.SimpleNamespace(**dict(zip([*prompt, *late], results)))


def convolution(small):
    return dict(norm_in=small.norm_in, conv_w=small.conv_w, conv_b=small.conv_b, since=small.since, x_proj=small.x_proj)


def routing(small):
    return dict(norm_moe=small.norm_moe, router=small.router)


def flat(ref):
    return ref[...].reshape(ref.shape[0] * ref.shape[1], ref.shape[2])


def gate_of(chance, choose):
    return jnp.sum(chance * choose, axis=1, keepdims=True)


class Sizes:
    def __init__(self, lanes, peers, experts, cap, rows, width, channels, hidden):
        self.lanes, self.peers, self.experts, self.cap = lanes, peers, experts, cap
        self.rows, self.width, self.channels, self.hidden = rows, width, channels, hidden
        self.total, self.slots = rows * lanes, experts * cap


def in_outputs(z):
    return dict(whole=bf16(z.lanes, z.rows, z.width), conv=f32(z.total + HEAD, z.channels), zgate=f32(z.total, z.channels),
                xs=f32(z.total, z.channels), proj=bf16(PROJ, z.total))


def sum_scratch(z):
    halves = pltpu.VMEM((2, PARTS, PROJ, z.total // PARTS), BF16)
    return dict(sum_stage=halves, sum_inbox=halves, sum_send=dma(2, PARTS), sum_recv=dma(2, PARTS))


def in_scratch(z):
    return dict(part=pltpu.VMEM((PROJ, z.total), F32), u_send=dma(2, z.lanes), u_recv=dma(z.lanes), **sum_scratch(z))


def in_stage(z, r, l, act, weights):
    d, m = lax.axis_index("dp"), lax.axis_index("mp")
    r.whole[m] = (act * rms_inverse(act) * r.norm_in[l : l + 1, :]).astype(BF16)
    gather = LineGather(r.whole, r.u_send, r.u_recv, d, m, z.lanes)
    gather.start()
    r.conv[:HEAD, :] = jnp.zeros((HEAD, z.channels), F32)
    weights.wait()

    def project(s):
        u = r.whole[s]
        r.conv[pl.ds(pl.multiple_of(s * z.rows + HEAD, 8), z.rows), :] = dot(u, r.win[0])
        r.zgate[pl.ds(pl.multiple_of(s * z.rows, 8), z.rows), :] = dot(u, r.win[1])

    project(m)
    for i in range(z.lanes - 1):
        project(gather.arrive(i))
    r.ship(r.conv, r.zgate, r.whole)
    taps, bias = r.conv_w[l], r.conv_b[l : l + 1, :]

    def conv_step(c, carry):
        base = pl.multiple_of(c * CONV_ROWS, CONV_ROWS)
        pre, _ = conv_window(r.conv, r.since, taps, bias, base)
        xs = pre * sigmoid(pre)
        r.xs[pl.ds(base, CONV_ROWS), :] = xs
        r.part[:, pl.ds(base, CONV_ROWS)] = dot_nt(r.x_proj[l], xs.astype(BF16))
        return carry

    lax.fori_loop(0, z.total // CONV_ROWS, conv_step, 0)
    r.ship(r.xs)
    finish = line_sum(r.part, r.sum_stage, r.sum_inbox, r.sum_send, r.sum_recv, r.proj, d, m, z.lanes)
    gather.finish()
    finish()


def first_block(z, l, act, small, w_in):
    def body(r):
        d, m = lax.axis_index("dp"), lax.axis_index("mp")
        (weights,) = fetch([(r.w_in.at[l], r.win)], r.fetched)
        greet(d, m, z.lanes, 0, False)
        r.need(r.act)
        in_stage(z, r, l, r.act[...].astype(F32), weights)

    inputs = dict(act=act, **convolution(small))
    return launch("mamba_in", 0, body, inputs, dict(w_in=w_in), in_outputs(z),
                  dict(win=pltpu.VMEM(w_in.shape[1:], BF16), fetched=dma(1), **in_scratch(z)))


def expert_refs(r):
    return (r.e_rows, r.e_pack, r.e_slots, r.e_part, r.e_back, r.e_stage, r.e_inbox, r.e_gs, r.e_gr, r.e_ds, r.e_dr, r.e_bs, r.e_br,
            r.e_rs, r.e_rr)


def expert_names(z, sets):
    across = pltpu.VMEM((z.lanes, z.peers, sets * z.cap, z.width), BF16)
    along = pltpu.VMEM((z.lanes, sets, z.rows, z.width), BF16)
    plane, line = dma(z.lanes, z.peers - 1), dma(z.lanes)
    return dict(
        e_rows=along, e_pack=across, e_slots=across, e_part=across, e_back=across, e_stage=along, e_inbox=along, e_gs=dma(2, z.lanes),
        e_gr=line, e_ds=plane, e_dr=plane, e_bs=plane, e_br=plane, e_rs=line, e_rr=line, e_own=pltpu.VMEM((sets, z.rows, z.width), F32))


def weight_scratch(wout, wup, wdown):
    return dict(wout=pltpu.VMEM(wout.shape[1:], BF16), wup=pltpu.VMEM(wup.shape[2:], BF16), wdown=pltpu.VMEM(wdown.shape[2:], BF16))


def out_scratch(z, place):
    stage, inbox, send, recv = reduce_scratch(z.lanes, z.rows, z.width)
    return dict(m_stage=stage, m_inbox=inbox, m_send=send, m_recv=recv, places=pltpu.VMEM((z.lanes, *place.shape), jnp.int32),
                p_send=dma(2, z.lanes), p_recv=dma(z.lanes), m_own=pltpu.VMEM((z.rows, z.width), F32))


def out_stage(z, r, l, wout):
    d, m = lax.axis_index("dp"), lax.axis_index("mp")
    r.places[m] = r.place[...]
    places = LineGather(r.places, r.p_send, r.p_recv, d, m, z.lanes)
    places.start()
    reduce = LineReduce(r.m_stage, r.m_inbox, r.m_send, r.m_recv, d, m, z.lanes)
    wout.wait()
    r.need(r.act, r.gated)
    for s in reduce.order:
        reduce.push(s, dot(r.gated[s], r.wout[...]))
    r.m_own[...] = r.act[...].astype(F32) + dot(r.gated[m], r.wout[...])

    def spread_places(s):
        numbers = lax.broadcasted_iota(jnp.int32, (z.slots, z.rows), 0)
        r.into[s] = (numbers == r.places[s][:1, : z.rows]).astype(F32).astype(BF16)

    spread_places(m)
    owner = lax.broadcasted_iota(jnp.int32, (z.slots, z.experts), 0) // z.cap == lax.broadcasted_iota(jnp.int32, (z.slots, z.experts), 1)
    r.choose[...] = dot_tn(r.into[m], owner.astype(F32).astype(BF16))
    for i in range(z.lanes - 1):
        spread_places(places.arrive(i))
    reduce.total(r.m_own)

    def finish():
        places.finish()
        reduce.finish()

    return finish


def chances(z, normed, table):
    logits = lax.dot_general(normed, table, (((1,), (1,)), ((), ())), precision=highest, preferred_element_type=F32)
    raised = jnp.exp(logits - jnp.max(logits, axis=1, keepdims=True))
    return raised / jnp.sum(raised, axis=1, keepdims=True)


def middle_block(z, l, act, gated, small, weights):
    def body(r):
        d, m = lax.axis_index("dp"), lax.axis_index("mp")
        wout, wup, wdown, win = fetch([(r.w_out.at[l], r.wout), (r.w_up.at[l, 0], r.wup), (r.w_down.at[l, 0], r.wdown),
                                       (r.w_in.at[l + 1], r.win)], r.fetched)
        greet(d, m, z.lanes, z.peers, True)
        finish = out_stage(z, r, l, wout)
        wup.wait()
        wdown.wait()
        middle = r.m_own[...]
        r.middle[...] = middle
        r.e_rows[m, 0] = (middle * rms_inverse(middle) * r.norm_moe[l : l + 1, :]).astype(BF16)
        moe = Experts(d, m, z.lanes, z.peers, r.into, *expert_refs(r))

        def expert(s, rows):
            r.slots[s] = rows[0]
            hidden = dot(rows[0], r.wup[...])
            r.hidden[s] = hidden.astype(BF16)
            active = gelu(hidden).astype(BF16)
            r.active[s] = active
            return [dot(active, r.wdown[...])]

        def meanwhile():
            finish()
            middle = r.middle[...]
            r.chance[...] = chances(z, middle * rms_inverse(middle) * r.norm_moe[l : l + 1, :], r.router[l])

        moe.run(expert, r.e_own, meanwhile)
        r.ship(r.into, r.middle, r.slots, r.hidden, r.active)
        picked = r.e_own[0].astype(BF16)
        r.picked[...] = picked
        following = r.middle[...] + gate_of(r.chance[...], r.choose[...]) * picked.astype(F32)
        r.following[...] = following
        r.ship(r.picked, r.following)
        in_stage(z, r, l + 1, following, win)
        moe.finish()

    w_in, w_out, w_up, w_down = weights
    slots = (z.lanes, z.slots)
    return launch(
        "middle", 1 + l, body, dict(act=act, gated=gated, place=small.place, **routing(small), **convolution(small)),
        dict(w_in=w_in, w_out=w_out, w_up=w_up, w_down=w_down),
        dict(middle=f32(z.rows, z.width), chance=f32(z.rows, z.experts), into=bf16(*slots, z.rows), slots=bf16(*slots, z.width),
             hidden=bf16(*slots, z.hidden), active=bf16(*slots, z.hidden), picked=bf16(z.rows, z.width), choose=f32(z.rows, z.experts), following=f32(z.rows, z.width),
             **in_outputs(z)),
        dict(win=pltpu.VMEM(w_in.shape[1:], BF16), fetched=dma(4), **weight_scratch(w_out, w_up, w_down), **out_scratch(z, small.place),
             **expert_names(z, 1), **in_scratch(z)))


def back_outputs(z):
    return dict(gmid=f32(z.rows, z.width), gup=f32(z.width, z.hidden), gdown=f32(z.hidden, z.width), ggated=f32(z.lanes, z.rows, z.channels),
                gwout=bf16(z.channels, z.width), gshare=f32(z.experts + 8, z.width))


def back_scratch(z):
    return dict(wide=pltpu.VMEM((z.lanes, z.rows, z.width), BF16), w_send=dma(2, z.lanes), w_recv=dma(z.lanes))


def route_back(z, r, l, upstream, middle, chance, choose, picked, returned):
    d, m = lax.axis_index("dp"), lax.axis_index("mp")
    gate = gate_of(chance, choose)
    inverse, gain = rms_inverse(middle), r.norm_moe[l : l + 1, :]
    grad_gate = jnp.sum(upstream * picked.astype(F32), axis=1, keepdims=True)
    grad_logit = gate * grad_gate * (choose - chance)
    grad_normed = returned.astype(BF16).astype(F32) + lax.dot_general(
        grad_logit, r.router[l], (((1,), (0,)), ((), ())), precision=highest, preferred_element_type=F32)
    pulled, grad_gain = norm_back(middle, inverse, gain, grad_normed)
    grad_middle = upstream + pulled
    r.gmid[...] = grad_middle
    r.ship(r.gmid)
    r.wide[m] = grad_middle.astype(BF16)
    gather = LineGather(r.wide, r.w_send, r.w_recv, d, m, z.lanes)
    gather.start()
    grad_router = lax.dot_general(
        grad_logit, middle * inverse * gain, (((0,), (0,)), ((), ())), precision=highest, preferred_element_type=F32)
    r.gshare[: z.experts, :] = grad_router
    r.gshare[z.experts :, :] = jnp.broadcast_to(grad_gain, (8, z.width))

    def gate_back(s):
        r.ggated[s] = dot_nt(r.wide[s], r.wout[...])

    gate_back(m)
    for i in range(z.lanes - 1):
        gate_back(gather.arrive(i))
    r.ship(r.ggated)
    r.need(r.gated)
    r.gwout[...] = dot_tn(flat(r.gated), flat(r.wide)).astype(BF16)
    gather.finish()


def turn_block(z, l, act, gated, cotangent, small, weights):
    def body(r):
        d, m = lax.axis_index("dp"), lax.axis_index("mp")
        wout, wup, wdown = fetch([(r.w_out.at[l], r.wout), (r.w_up.at[l, 0], r.wup), (r.w_down.at[l, 0], r.wdown)], r.fetched)
        greet(d, m, z.lanes, z.peers, True)
        finish = out_stage(z, r, l, wout)
        wup.wait()
        wdown.wait()
        middle = r.m_own[...]
        normed = middle * rms_inverse(middle) * r.norm_moe[l : l + 1, :]
        r.e_rows[m, 0] = normed.astype(BF16)
        chance = chances(z, normed, r.router[l])
        r.chance[...] = chance
        r.need(r.cotangent)
        r.e_rows[m, 1] = (gate_of(chance, r.choose[...]) * r.cotangent[...].astype(F32)).astype(BF16)
        moe = Experts(d, m, z.lanes, z.peers, r.into, *expert_refs(r))

        def expert(s, rows):
            hidden = dot(rows[0], r.wup[...])
            active = gelu(hidden).astype(BF16)
            r.active[s] = active
            grad_hidden = (dot_nt(rows[1], r.wdown[...]) * gelu_slope(hidden)).astype(BF16)
            r.ghid[s] = grad_hidden
            return [dot(active, r.wdown[...]), dot_nt(grad_hidden, r.wup[...])]

        def meanwhile():
            finish()
            for s in range(z.lanes):
                down = dot_tn(r.active[s], moe.slot_rows(moe.slots, s, 1))
                r.gdown[...] = down if s == 0 else r.gdown[...] + down
                up = dot_tn(moe.slot_rows(moe.slots, s, 0), r.ghid[s])
                r.gup[...] = up if s == 0 else r.gup[...] + up
            r.ship(r.gdown, r.gup)

        moe.run(expert, r.e_own, meanwhile)
        picked = r.e_own[0].astype(BF16)
        r.following[...] = r.m_own[...] + gate_of(r.chance[...], r.choose[...]) * picked.astype(F32)
        r.ship(r.following)
        route_back(z, r, l, r.cotangent[...].astype(F32), r.m_own[...], r.chance[...], r.choose[...], picked, r.e_own[1])
        moe.finish()

    w_in, w_out, w_up, w_down = weights
    slots = (z.lanes, z.slots)
    return launch(
        "turn", 8, body, dict(act=act, gated=gated, cotangent=cotangent, place=small.place, **routing(small)),
        dict(w_out=w_out, w_up=w_up, w_down=w_down),
        dict(following=f32(z.rows, z.width), **back_outputs(z)),
        dict(fetched=dma(3), choose=pltpu.VMEM((z.rows, z.experts), F32), chance=pltpu.VMEM((z.rows, z.experts), F32), into=pltpu.VMEM((*slots, z.rows), BF16),
             active=pltpu.VMEM((*slots, z.hidden), BF16), ghid=pltpu.VMEM((*slots, z.hidden), BF16),
             **weight_scratch(w_out, w_up, w_down), **out_scratch(z, small.place), **expert_names(z, 2), **back_scratch(z)),
        58 if z.slots <= 256 else 61)


class PlaneSum:
    def __init__(self, d, m, peers, mine, pair, half, inbox, result, psend, precv, csend, crecv, gsend, grecv):
        self.m, self.mine, self.pair, self.half, self.inbox, self.result = m, mine, pair, half, inbox, result
        self.psend, self.precv, self.csend, self.crecv, self.gsend, self.grecv = psend, precv, csend, crecv, gsend, grecv
        self.chips = peers // 2
        self.chip, self.core = lax.div(d, 2), lax.rem(d, 2)
        self.rows = mine.shape[0] // 2
        self.block = self.rows // self.chips

    def side(self, core):
        return pl.ds(pl.multiple_of(core * self.rows, 16), self.rows)

    def at(self, chip):
        return pl.ds(pl.multiple_of(chip * self.block, 16), self.block)

    def final(self, chip):
        return pl.ds(pl.multiple_of(self.core * self.rows + chip * self.block, 16), self.block)

    def swap(self, src, dst, i):
        return pltpu.make_async_remote_copy(
            src_ref=src, dst_ref=dst, send_sem=self.psend.at[i], recv_sem=self.precv.at[i],
            device_id=(self.chip * 2 + 1 - self.core, self.m), device_id_type=MESH)

    def first_swap(self):
        return self.swap(self.mine.at[self.side(1 - self.core)], self.pair, 0)

    def last_swap(self):
        return self.swap(self.result.at[self.side(self.core)], self.result.at[self.side(self.core)], 1)

    def other(self, k):
        return lax.rem(self.chip + k, self.chips)

    def scatter(self, k):
        return pltpu.make_async_remote_copy(
            src_ref=self.half.at[self.at(self.other(k))], dst_ref=self.inbox.at[k - 1], send_sem=self.csend.at[k - 1],
            recv_sem=self.crecv.at[k - 1], device_id=(self.other(k) * 2 + self.core, self.m), device_id_type=MESH)

    def gather(self, k):
        return pltpu.make_async_remote_copy(
            src_ref=self.result.at[self.final(self.chip)], dst_ref=self.result.at[self.final(self.chip)], send_sem=self.gsend.at[k - 1],
            recv_sem=self.grecv.at[k - 1], device_id=(self.other(k) * 2 + self.core, self.m), device_id_type=MESH)

    def begin(self):
        self.first_swap().start()

    def second(self):
        self.first_swap().wait_recv()
        self.half[...] = (self.mine[self.side(self.core)].astype(F32) + self.pair[...].astype(F32)).astype(BF16)
        for k in range(1, self.chips):
            self.scatter(k).start()

    def third(self):
        for k in range(1, self.chips):
            self.scatter(k).wait_recv()
        summed = self.half[self.at(self.chip)].astype(F32)
        for k in range(1, self.chips):
            summed = summed + self.inbox[k - 1].astype(F32)
        self.result[self.final(self.chip)] = summed.astype(BF16)
        for k in range(1, self.chips):
            self.gather(k).start()

    def fourth(self):
        for k in range(1, self.chips):
            self.gather(k).wait_recv()
        self.last_swap().start()

    def end(self):
        self.last_swap().wait_recv()

    def finish(self):
        self.first_swap().wait_send()
        self.last_swap().wait_send()
        for k in range(1, self.chips):
            self.scatter(k).wait_send()
            self.gather(k).wait_send()


def plane_scratch(peers, rows, width):
    return [
        pltpu.VMEM((rows, width), BF16),
        pltpu.VMEM((rows // 2, width), BF16),
        pltpu.VMEM((rows // 2, width), BF16),
        pltpu.VMEM((peers // 2 - 1, rows // peers, width), BF16),
        dma(2), dma(2), dma(peers // 2 - 1), dma(peers // 2 - 1), dma(peers // 2 - 1), dma(peers // 2 - 1),
    ]


def exchange(targets, buf, inbox, send, recv):
    copies = [
        pltpu.make_async_remote_copy(src_ref=buf, dst_ref=inbox.at[k], send_sem=send.at[k], recv_sem=recv.at[k],
                                     device_id=target, device_id_type=MESH)
        for k, target in enumerate(targets)
    ]
    for copy in copies:
        copy.start()

    def collect():
        total = buf[...].astype(F32)
        for k, copy in enumerate(copies):
            copy.wait()
            total = total + inbox[k].astype(F32)
        return total

    return collect


def early_rows(width, experts):
    sizes = [width, width, DT_RANK, STATE, 16, experts + 8, experts + 8]
    return [sum(sizes[:i]) for i in range(len(sizes) + 1)]


def late_rows(width):
    sizes = [width, PROJ, 16]
    return [sum(sizes[:i]) for i in range(len(sizes) + 1)]


def whole_blocks(rows, peers):
    return -(-rows // (16 * peers)) * 16 * peers


def in_back_scratch(z, win, last):
    early = whole_blocks(early_rows(z.width, z.experts)[-1], z.peers)
    late = whole_blocks(late_rows(z.width)[-1], z.peers)
    shared = 2 * (z.experts + 8)
    small = -(-2 * (z.width // LANES) // 8) * 8
    stage, inbox, send, recv = reduce_scratch(z.lanes, z.rows, z.width)
    found = dict(
        gproj=pltpu.VMEM((PROJ, z.total), BF16), gpre=pltpu.VMEM((z.total + HEAD, z.channels), F32),
        gxi=pltpu.VMEM((z.total, z.channels), BF16), gconv=pltpu.VMEM((16, z.channels), F32), c_own=pltpu.VMEM((z.rows, z.width), F32),
        win=pltpu.VMEM(win.shape[1:], BF16), z_buf=pltpu.VMEM((shared, z.channels), BF16),
        z_in=pltpu.VMEM((z.lanes - 1, shared, z.channels), BF16), z_send=dma(z.lanes - 1), z_recv=dma(z.lanes - 1),
        c_stage=stage, c_inbox=inbox, c_send=send, c_recv=recv,
        **{"e%d" % i: v for i, v in enumerate(plane_scratch(z.peers, early, z.channels))},
        **{"l%d" % i: v for i, v in enumerate(plane_scratch(z.peers, late, z.channels))},
        **sum_scratch(z),
    )
    if last:
        found.update(
            n_buf=pltpu.VMEM((small, LANES), F32), n_in=pltpu.VMEM((z.peers - 1, small, LANES), F32), n_send=dma(z.peers - 1),
            n_recv=dma(z.peers - 1), n_buf2=pltpu.VMEM((small, LANES), F32), n_in2=pltpu.VMEM((z.lanes - 1, small, LANES), F32),
            n_send2=dma(z.lanes - 1), n_recv2=dma(z.lanes - 1))
    return found


def in_back_outputs(z, last):
    early = whole_blocks(early_rows(z.width, z.experts)[-1], z.peers)
    late = whole_blocks(late_rows(z.width)[-1], z.peers)
    return dict(early=bf16(early, z.channels), late=bf16(late, z.channels), share=f32(2 * (z.experts + 8), z.channels),
                gnorm=f32(2 if last else 1, z.width))


def plane_sum(z, r, which, result):
    d, m = lax.axis_index("dp"), lax.axis_index("mp")
    parts = [getattr(r, which + str(i)) for i in range(10)]
    return PlaneSum(d, m, z.peers, *parts[:4], result, *parts[4:])


def in_back_stage(z, r, l, weights, emit):
    d, m = lax.axis_index("dp"), lax.axis_index("mp")
    line = [(d, lax.rem(m + k, z.lanes)) for k in range(1, z.lanes)]
    early, late = plane_sum(z, r, "e", r.early), plane_sum(z, r, "l", r.late)
    emine, lmine = early.mine, late.mine
    ch = z.channels
    at, till = early_rows(z.width, z.experts), late_rows(z.width)

    def early_work():
        r.need(r.b_whole, r.gzg, r.b_gwout, r.b_gshare)
        whole = r.b_whole[...].reshape(z.total, z.width)
        emine[at[0] : at[1], :] = dot_tn(whole, r.gzg[...]).astype(BF16)
        for i in range(z.width // ch):
            emine[at[1] + i * ch : at[1] + (i + 1) * ch, :] = r.b_gwout[:, i * ch : (i + 1) * ch]
            emine[at[5 + i] : at[6 + i], :] = r.b_gshare[:, i * ch : (i + 1) * ch].astype(BF16)
        emine[at[2] : at[3], :] = r.gdtw[...].astype(BF16)
        emine[at[3] : at[4], :] = r.galog[...].astype(BF16)
        emine[at[4] : at[5], :] = jnp.concatenate([r.gdtb[...], r.gskip[...], jnp.zeros((14, ch), F32)], axis=0).astype(BF16)
        if at[7] < emine.shape[0]:
            emine[at[7] :, :] = jnp.zeros((emine.shape[0] - at[7], ch), BF16)
        early.begin()

    r.need(r.gpart)
    finish_sum = line_sum(r.gpart, r.sum_stage, r.sum_inbox, r.sum_send, r.sum_recv, r.gproj, d, m, z.lanes, early_work)
    taps, bias = r.conv_w[l], r.conv_b[l : l + 1, :]
    r.gconv[...] = jnp.zeros_like(r.gconv)
    r.gpre[z.total :, :] = jnp.zeros((HEAD, ch), F32)

    def first(c, carry):
        base = pl.multiple_of(c * CONV_ROWS, CONV_ROWS)
        pre, shifted = conv_window(r.b_conv, r.since, taps, bias, base)
        sig = sigmoid(pre)
        grad = r.gxs[pl.ds(base, CONV_ROWS), :] + dot_tn(r.gproj[:, pl.ds(base, CONV_ROWS)], r.x_proj[l])
        grad = grad * (sig * (1.0 + pre * (1.0 - sig)))
        r.gpre[pl.ds(base, CONV_ROWS), :] = grad
        for j in range(CONV):
            r.gconv[CONV - 1 - j : CONV - j, :] += jnp.sum(grad * shifted[j], axis=0, keepdims=True)
        r.gconv[CONV : CONV + 1, :] += jnp.sum(grad, axis=0, keepdims=True)
        return carry

    r.need(r.b_conv, r.gxs)
    lax.fori_loop(0, z.total // CONV_ROWS, first, 0)

    def second(c, carry):
        base = pl.multiple_of(c * CONV_ROWS, CONV_ROWS)
        window = r.gpre[pl.ds(base, CONV_ROWS + HEAD), :]
        since = r.since[pl.ds(base, CONV_ROWS + HEAD), :]
        grad = taps[CONV - 1 : CONV, :] * window[:CONV_ROWS]
        for j in range(1, CONV):
            grad = grad + taps[CONV - 1 - j : CONV - j, :] * (window * (since >= j).astype(F32))[j : j + CONV_ROWS]
        r.gxi[pl.ds(base, CONV_ROWS), :] = grad.astype(BF16)
        return carry

    lax.fori_loop(0, z.total // CONV_ROWS, second, 0)
    weights.wait()
    reduce = LineReduce(r.c_stage, r.c_inbox, r.c_send, r.c_recv, d, m, z.lanes)

    def term(s):
        part = pl.ds(pl.multiple_of(s * z.rows, 16), z.rows)
        return dot_nt(r.gxi[part, :], r.win[0]) + dot_nt(r.gzg[part, :], r.win[1])

    def push_middle(s):
        @pl.when(reduce.middle)
        def _():
            for p in range(PIECES):
                reduce.push_on(s, p, term(s)[p * reduce.rows : (p + 1) * reduce.rows])

    one, two, three = reduce.order

    @pl.when(reduce.at_end)
    def _():
        for s in reduce.order:
            reduce.push_first(s, term(s))

    early.second()
    r.need(r.b_xs)
    whole = r.b_whole[...].reshape(z.total, z.width)
    lmine[till[0] : till[1], :] = dot_tn(whole, r.gxi[...]).astype(BF16)
    lmine[till[1] : till[2], :] = dot(r.gproj[...], r.b_xs[...].astype(BF16)).astype(BF16)
    lmine[till[2] : till[3], :] = r.gconv[...].astype(BF16)
    if till[3] < lmine.shape[0]:
        lmine[till[3] :, :] = jnp.zeros((lmine.shape[0] - till[3], ch), BF16)
    late.begin()
    push_middle(one)
    late.second()
    r.c_own[...] = term(m)
    early.third()
    push_middle(two)
    late.third()
    early.fourth()
    push_middle(three)
    late.fourth()
    early.end()
    r.ship(r.early)
    r.z_buf[...] = r.early[at[5] : at[7], :]
    shared = exchange(line, r.z_buf, r.z_in, r.z_send, r.z_recv)
    reduce.total(r.c_own)
    r.need(r.b_act, r.b_gmid)
    act = r.b_act[...].astype(F32)
    pulled, grad_gain = norm_back(act, rms_inverse(act), r.norm_in[l : l + 1, :], r.c_own[...])
    emit(r.b_gmid[...] + pulled)

    def finish():
        late.end()
        r.ship(r.late)
        if l == 0:
            both = jnp.concatenate([grad_gain, r.prior[...]], axis=0)
            groups = z.width // LANES
            for g in range(groups):
                r.n_buf[2 * g : 2 * g + 2, :] = both[:, g * LANES : (g + 1) * LANES]
            if 2 * groups < r.n_buf.shape[0]:
                r.n_buf[2 * groups :, :] = jnp.zeros((r.n_buf.shape[0] - 2 * groups, LANES), F32)
            plane = [(lax.rem(d + k, z.peers), m) for k in range(1, z.peers)]
            r.n_buf2[...] = exchange(plane, r.n_buf, r.n_in, r.n_send, r.n_recv)()
            summed = exchange(line, r.n_buf2, r.n_in2, r.n_send2, r.n_recv2)()
            r.gnorm[...] = jnp.concatenate([summed[2 * g : 2 * g + 2, :] for g in range(groups)], axis=1)
        else:
            r.gnorm[...] = grad_gain
        r.share[...] = shared()
        finish_sum()
        reduce.finish()
        early.finish()
        late.finish()

    return finish


def last_block(z, back, prior, small, w_in):
    def body(r):
        d, m = lax.axis_index("dp"), lax.axis_index("mp")
        (win,) = fetch([(r.w_in.at[0], r.win)], r.fetched)
        greet(d, m, z.lanes, z.peers, True)

        def emit(value):
            r.up[...] = value

        in_back_stage(z, r, 0, win, emit)()

    return launch("mamba_in_backward", 9, body, dict(**back, prior=prior, **convolution(small)), dict(w_in=w_in),
                  dict(up=f32(z.rows, z.width), **in_back_outputs(z, True)), dict(fetched=dma(1), **in_back_scratch(z, w_in, True)))


def experts_back(z, r, l, fetched, finish):
    d, m = lax.axis_index("dp"), lax.axis_index("mp")
    for weight in fetched:
        weight.wait()
    r.need(r.into, r.hidden)
    moe = Experts(d, m, z.lanes, z.peers, r.into, *expert_refs(r))

    def expert(s, rows):
        grad_hidden = (dot_nt(rows[0], r.wdown[...]) * gelu_slope(r.hidden[s].astype(F32))).astype(BF16)
        r.ghid[s] = grad_hidden
        return [dot_nt(grad_hidden, r.wup[...])]

    def meanwhile():
        r.need(r.active, r.slots)
        r.gdown[...] = dot_tn(flat(r.active), r.e_slots[...].reshape(z.lanes * z.slots, z.width))
        r.gup[...] = dot_tn(flat(r.slots), flat(r.ghid))
        r.ship(r.gdown, r.gup)
        finish()

    moe.run(expert, r.e_own, meanwhile)
    r.need(r.picked, r.middle)
    route_back(z, r, l, r.upstream[...], r.middle[...], r.chance[...], r.choose[...], r.picked[...], r.e_own[0])
    moe.finish()


def down_blocks(z, l, back, kept, small, weights):
    def upper(r):
        d, m = lax.axis_index("dp"), lax.axis_index("mp")
        (win,) = fetch([(r.w_in.at[l], r.win)], r.fetched)
        greet(d, m, z.lanes, z.peers, True)

        def emit(value):
            r.up[...] = value

        in_back_stage(z, r, l, win, emit)()

    def lower(r):
        d, m = lax.axis_index("dp"), lax.axis_index("mp")
        fetched = fetch([(r.w_down.at[l - 1, 0], r.wdown), (r.w_up.at[l - 1, 0], r.wup), (r.w_out.at[l - 1], r.wout)], r.fetched)
        greet(d, m, z.lanes, z.peers, True)
        r.need(r.upstream)
        r.e_rows[m, 0] = (gate_of(r.chance[...], r.choose[...]) * r.upstream[...]).astype(BF16)
        experts_back(z, r, l - 1, fetched, lambda: None)

    w_in, w_out, w_up, w_down = weights
    slots = (z.lanes, z.slots)
    one = launch("mamba_in_backward", 20 + l, upper, dict(**back, **convolution(small)),
                 dict(w_in=w_in), dict(up=f32(z.rows, z.width), **in_back_outputs(z, False)),
                 dict(fetched=dma(1), **in_back_scratch(z, w_in, False)))
    two = launch("experts_backward", 30 + l, lower, dict(**kept, upstream=one.up, **routing(small)),
                 dict(w_out=w_out, w_up=w_up, w_down=w_down), back_outputs(z),
                 dict(fetched=dma(3), ghid=pltpu.VMEM((*slots, z.hidden), BF16), **weight_scratch(w_out, w_up, w_down),
                      **expert_names(z, 1), **back_scratch(z)))
    return types.SimpleNamespace(**vars(one), **vars(two))


def down_block(z, l, back, kept, small, weights):
    def body(r):
        d, m = lax.axis_index("dp"), lax.axis_index("mp")
        win, wdown, wup, wout = fetch([(r.w_in.at[l], r.win), (r.w_down.at[l - 1, 0], r.wdown), (r.w_up.at[l - 1, 0], r.wup),
                                       (r.w_out.at[l - 1], r.wout)], r.fetched)
        greet(d, m, z.lanes, z.peers, True)

        def emit(value):
            r.upstream[...] = value
            r.e_rows[m, 0] = (gate_of(r.chance[...], r.choose[...]) * value).astype(BF16)

        experts_back(z, r, l - 1, (wdown, wup, wout), in_back_stage(z, r, l, win, emit))

    w_in, w_out, w_up, w_down = weights
    slots = (z.lanes, z.slots)
    return launch(
        "down", 9 + l, body, dict(**back, **kept, **convolution(small), **routing(small)),
        dict(w_in=w_in, w_out=w_out, w_up=w_up, w_down=w_down), dict(**in_back_outputs(z, False), **back_outputs(z)),
        dict(fetched=dma(4), upstream=pltpu.VMEM((z.rows, z.width), F32),
             ghid=pltpu.VMEM((*slots, z.hidden), BF16), **weight_scratch(w_out, w_up, w_down), **in_back_scratch(z, w_in, False),
             **expert_names(z, 1), **back_scratch(z)))


def final_block(z, result, up, gnorm, layers):
    count, ch = len(layers), z.channels
    at, till = early_rows(z.width, z.experts), late_rows(z.width)
    far = dict(result=(z.rows, z.width), tokens=(z.rows, z.width), w_in=(count, 2, z.width, ch), w_out=(count, ch, z.width),
               w_up=(count, 1, z.width, z.hidden), w_down=(count, 1, z.hidden, z.width))
    near = dict(norm_in=(count, z.width), conv_w=(count, CONV, ch), conv_b=(count, ch), x_proj=(count, ch, PROJ), dt_proj=(count, DT_RANK, ch),
                dt_bias=(count, ch), a_log=(count, STATE, ch), skip=(count, ch), norm_moe=(count, z.width), router=(count, z.experts, z.width))
    shapes = {**far, **near}
    sums = [v for layer in layers for v in layer[:2]]
    whole = [result, up, *(v for layer in layers for v in layer[3:])]

    def kernel(*refs):
        small, refs = refs[: 1 + count], refs[1 + count :]
        there, refs = refs[: len(sums) + len(whole)], refs[len(sums) + len(whole) :]
        outs, refs = refs[: len(shapes)], refs[len(shapes) :]
        held, (w_in, w_out, came, went) = refs[: len(there)], refs[len(there) :]
        out = types.SimpleNamespace(**dict(zip(shapes, outs)))
        coming = fetch(list(zip(there, held)), came)
        places = [out.result, out.tokens] + [v.at[l, 0] for l in range(count) for v in (out.w_up, out.w_down)]
        out.norm_in[...] = small[0][...]
        going = []
        for l in range(count):
            early, late, share = held[2 * l], held[2 * l + 1], small[1 + l]
            coming[2 * l].wait()
            coming[2 * l + 1].wait()
            one = slice(l, l + 1)
            w_in[l, 0] = late[till[0] : till[1], :].astype(F32)
            w_in[l, 1] = early[at[0] : at[1], :].astype(F32)
            for i in range(z.width // ch):
                cols = slice(i * ch, (i + 1) * ch)
                w_out[l, :, cols] = early[at[1] + i * ch : at[1] + (i + 1) * ch, :].astype(F32)
                rows = share[i * (z.experts + 8) : (i + 1) * (z.experts + 8), :]
                out.router[l, :, cols] = rows[: z.experts]
                out.norm_moe[one, cols] = rows[z.experts : z.experts + 1]
            for src, dst in ((w_in, out.w_in), (w_out, out.w_out)):
                going.append(pltpu.make_async_copy(src.at[l], dst.at[l], went.at[len(going)]))
                going[-1].start()
            conv = late[till[2] : till[3], :].astype(F32)
            out.conv_w[l] = conv[:CONV]
            out.conv_b[one, :] = conv[CONV : CONV + 1]
            out.x_proj[l] = late[till[1] : till[2], :].astype(F32).T
            out.dt_proj[l] = early[at[2] : at[3], :].astype(F32)
            out.a_log[l] = early[at[3] : at[4], :].astype(F32)
            both = early[at[4] : at[5], :].astype(F32)
            out.dt_bias[one, :] = both[:1]
            out.skip[one, :] = both[1:2]
        for i, place in enumerate(places):
            coming[len(sums) + i].wait()
            going.append(pltpu.make_async_copy(held[len(sums) + i], place, went.at[len(going)]))
            going[-1].start()
        for copy in going:
            copy.wait()

    outputs = pl.pallas_call(
        kernel,
        out_shape=[f32(*shape) for shape in shapes.values()],
        in_specs=vmem(1 + count) + hbm(len(sums) + len(whole)),
        out_specs=hbm(len(far)) + vmem(len(near)),
        scratch_shapes=[pltpu.VMEM(v.shape, v.dtype) for v in (*sums, *whole)]
        + [pltpu.VMEM(far["w_in"], F32), pltpu.VMEM(far["w_out"], F32), dma(len(sums) + len(whole)), dma(2 * count + len(whole))],
        compiler_params=pltpu.CompilerParams(vmem_limit_bytes=60 << 20),
        name="outputs",
    )(gnorm, *(layer[2] for layer in layers), *sums, *whole)
    o = types.SimpleNamespace(**dict(zip(shapes, outputs)))
    return (o.result, o.tokens, o.norm_in, o.w_in, o.conv_w, o.conv_b, o.x_proj, o.dt_proj, o.dt_bias, o.a_log, o.skip, o.w_out, o.norm_moe,
            jnp.swapaxes(o.router, 1, 2), o.w_up, o.w_down)


def on_device(
    tokens, cotangent, lengths, routes, slot_place, norm_in, w_in, conv_w, conv_b, x_proj, dt_proj, dt_bias,
    a_log, d_skip, w_out, norm_moe, router, w_up, w_down,
):
    layers = norm_in.shape[0]
    assert layers == 2
    rows_here, width = tokens.shape
    lanes, peers = lax.axis_size("mp"), lax.axis_size("dp")
    experts, channels = router.shape[2], w_in.shape[3]
    capacity = max(2, (5 * rows_here + 4 * experts - 1) // (4 * experts))
    padded = (capacity + 15) // 16 * 16
    z = Sizes(lanes, peers, experts, padded, rows_here, width, channels, w_up.shape[3])
    position = lax.broadcasted_iota(jnp.int32, (z.total + HEAD, 1), 0)
    since, first = position, 0
    for i in range(lengths.shape[1] - 1):
        first = first + lengths[0, i]
        since = jnp.where(position >= first, position - first, since)
    since = jnp.where(position < z.total, since, 0)
    place = jnp.pad(routes * padded + slot_place, (0, -rows_here % LANES))
    small = types.SimpleNamespace(
        norm_in=norm_in, norm_moe=norm_moe, conv_w=conv_w, conv_b=conv_b, since=since, x_proj=jnp.swapaxes(x_proj, 1, 2),
        router=jnp.swapaxes(router, 1, 2),
        place=jnp.broadcast_to(place[None, :], (8, place.shape[0])),
    )
    weights = (w_in, w_out, w_up, w_down)
    scan_weights = (dt_proj, dt_bias, a_log, d_skip, spread_matrix())

    act, entry = tokens, first_block(z, 0, tokens, small, w_in)
    kept = []
    for l in range(layers):
        gated, ys, marks = scan_fwd(l, entry.xs, entry.zgate, entry.proj, since, *scan_weights)
        gated = gated.reshape(lanes, rows_here, channels)
        if l + 1 < layers:
            out = middle_block(z, l, act, gated, small, weights)
            kept.append((act, entry, gated, ys, marks, out))
            act, entry = out.following, out
        else:
            turn = turn_block(z, l, act, gated, cotangent, small, weights)
            kept.append((act, entry, gated, ys, marks, turn))
    result, above = turn.following, turn
    collected = []
    for l in reversed(range(layers)):
        act, entry, gated, ys, marks, _ = kept[l]
        gxs, gzg, gpart, gdtw, gdtb, galog, gskip = scan_bwd(
            l, entry.xs, entry.zgate, entry.proj, since, ys, above.ggated.reshape(z.total, channels), marks, *scan_weights)
        back = dict(gpart=gpart, gxs=gxs, gzg=gzg, b_conv=entry.conv, b_xs=entry.xs, b_whole=entry.whole, b_act=act, b_gmid=above.gmid,
                    b_gwout=above.gwout, b_gshare=above.gshare, gdtw=gdtw, gdtb=gdtb, galog=galog, gskip=gskip)
        grads = (above.gup, above.gdown)
        if l > 0:
            _, _, below_gated, _, _, below = kept[l - 1]
            forward = dict(gated=below_gated, chance=below.chance, choose=below.choose, into=below.into, slots=below.slots, hidden=below.hidden,
                           active=below.active, picked=below.picked, middle=below.middle)
            above = (down_block if z.slots <= 256 else down_blocks)(z, l, back, forward, small, weights)
            prior = above.gnorm
            collected.append((above.early, above.late, above.share, *grads))
        else:
            end = last_block(z, back, prior, small, w_in)
            collected.append((end.early, end.late, end.share, *grads))
    collected = collected[::-1]
    at, till = early_rows(width, experts), late_rows(width)

    return final_block(z, result, end.up, end.gnorm, collected)


def solution(mesh):
    return jax.shard_map(
        on_device,
        mesh=mesh,
        in_specs=(
            P(("dp", "mp"), None),
            P(("dp", "mp"), None),
            P("dp", None),
            P(("dp", "mp")),
            P(("dp", "mp")),
            P(),
            P(None, None, None, "mp"),
            P(None, None, "mp"),
            P(None, "mp"),
            P(None, "mp", None),
            P(None, None, "mp"),
            P(None, "mp"),
            P(None, None, "mp"),
            P(None, "mp"),
            P(None, "mp", None),
            P(),
            P(),
            P(None, "dp", None, "mp"),
            P(None, "dp", "mp", None),
        ),
        out_specs=(
            P(("dp", "mp"), None),
            P(("dp", "mp"), None),
            P(),
            P(None, None, None, "mp"),
            P(None, None, "mp"),
            P(None, "mp"),
            P(None, "mp", None),
            P(None, None, "mp"),
            P(None, "mp"),
            P(None, None, "mp"),
            P(None, "mp"),
            P(None, "mp", None),
            P(),
            P(),
            P(None, "dp", None, "mp"),
            P(None, "dp", "mp", None),
        ),
        check_vma=False,
    )
```

```python
import functools
import types

import jax
import jax.numpy as jnp
from jax import lax
from jax.experimental import pallas as pl
from jax.experimental.pallas import tpu as pltpu
from jax.sharding import PartitionSpec as P

STATE = 16
DT_RANK = 48
LANES = 128
CHUNK = 128
LOG2E = 1.4426950408889634
RESET = 1.0e6
PROJ = DT_RANK + 2 * STATE
CONV = 4
dt_most = 0.05
epsilon = 1e-05
highest = lax.Precision.HIGHEST
MESH = pl.DeviceIdType.MESH
F32, BF16 = jnp.float32, jnp.bfloat16


def sigmoid(v):
    return 1.0 / (1.0 + jnp.exp(-v))


def dot(a, b):
    return jnp.dot(a, b, preferred_element_type=F32)


def dot_nt(a, b):
    return lax.dot_general(a, b, (((1,), (1,)), ((), ())), preferred_element_type=F32)


def dot_tn(a, b):
    return lax.dot_general(a, b, (((0,), (0,)), ((), ())), preferred_element_type=F32)


def spread_matrix():
    rows = lax.broadcasted_iota(jnp.int32, (STATE, STATE * LANES), 0)
    cols = lax.broadcasted_iota(jnp.int32, (STATE, STATE * LANES), 1)
    return (rows == cols // LANES).astype(BF16)


def put(ref, value):
    for j in range(ref.shape[0]):
        ref[j] = value[:, j * LANES : (j + 1) * LANES]


def spread_rows(proj, spread, out_ref):
    wide = dot_tn(proj, spread)
    for n in range(STATE):
        out_ref[pl.ds(n, CHUNK, stride=STATE), :] = wide[:, n * LANES : (n + 1) * LANES]


def scan_fwd_kernel(l, xs_ref, zg_ref, proj_ref, since_ref, dtw_ref, dtb_ref, alog_ref, skip_ref, spread_ref,
                    gated_ref, ys_ref, hck_ref,
                    h_ref, dm_ref, dx_ref, bx_ref, cx_ref, yq_ref):
    groups = xs_ref.shape[1] // LANES

    @pl.when(pl.program_id(0) == 0)
    def _():
        h_ref[...] = jnp.zeros_like(h_ref)

    hck_ref[0] = h_ref[...]
    proj = proj_ref[...]
    xs = xs_ref[...]
    delta = dt_most * sigmoid(dot_tn(proj[:DT_RANK], dtw_ref[l]) + dtb_ref[l : l + 1, :])
    put(dm_ref, delta + RESET * (since_ref[...] == 0).astype(F32))
    put(dx_ref, delta * xs)
    spread_rows(proj[DT_RANK : DT_RANK + STATE], spread_ref[...], bx_ref)
    spread_rows(proj[DT_RANK + STATE :], spread_ref[...], cx_ref)
    rate = -LOG2E * jnp.exp(alog_ref[l])
    rates = [rate[:, j * LANES : (j + 1) * LANES] for j in range(groups)]

    def step(g, hs):
        hs = list(hs)
        t0 = pl.multiple_of(g * 8, 8)
        for i in range(8):
            t = t0 + i
            r0 = pl.multiple_of(t * STATE, STATE)
            b = bx_ref[pl.ds(r0, STATE), :]
            c = cx_ref[pl.ds(r0, STATE), :]
            q0 = pl.multiple_of(t * 8, 8)
            for j in range(groups):
                lanes = slice(j * LANES, (j + 1) * LANES)
                dec = jnp.exp2(dm_ref[j, pl.ds(t, 1), :] * rates[j])
                hs[j] = dec * hs[j] + dx_ref[j, pl.ds(t, 1), :] * b
                q = c * hs[j]
                yq_ref[j, pl.ds(q0, 8), :] = q[:8] + q[8:]
        return tuple(hs)

    hs = lax.fori_loop(0, CHUNK // 8, step, tuple(h_ref[:, j * LANES : (j + 1) * LANES] for j in range(groups)))
    for j in range(groups):
        h_ref[:, j * LANES : (j + 1) * LANES] = hs[j]
    zg = zg_ref[...]
    for j in range(groups):
        lanes = slice(j * LANES, (j + 1) * LANES)
        y = skip_ref[l : l + 1, lanes] * xs[:, lanes]
        for k in range(8):
            y = y + yq_ref[j, pl.ds(k, CHUNK, stride=8), :]
        ys_ref[:, lanes] = y
        z = zg[:, lanes]
        gated_ref[:, lanes] = (y * z * sigmoid(z)).astype(BF16)


def scan_fwd(l, xs, zg, proj, since, dtw, dtb, alog, skip, spread):
    rows, ch = xs.shape
    steps = rows // CHUNK
    row = lambda w: pl.BlockSpec((CHUNK, w), lambda i: (i, 0))
    full = lambda s: pl.BlockSpec(s, lambda i: (0,) * len(s))
    return pl.pallas_call(
        functools.partial(scan_fwd_kernel, l),
        grid=(steps,),
        out_shape=[
            jax.ShapeDtypeStruct((rows, ch), BF16),
            jax.ShapeDtypeStruct((rows, ch), F32),
            jax.ShapeDtypeStruct((steps, STATE, ch), F32),
        ],
        in_specs=[row(ch), row(ch), pl.BlockSpec((PROJ, CHUNK), lambda i: (0, i)), row(1)]
        + [full(v.shape) for v in (dtw, dtb, alog, skip, spread)],
        out_specs=[row(ch), row(ch), pl.BlockSpec((1, STATE, ch), lambda i: (i, 0, 0))],
        scratch_shapes=[
            pltpu.VMEM((STATE, ch), F32),
            pltpu.VMEM((ch // LANES, CHUNK, LANES), F32),
            pltpu.VMEM((ch // LANES, CHUNK, LANES), F32),
            pltpu.VMEM((CHUNK * STATE, LANES), F32),
            pltpu.VMEM((CHUNK * STATE, LANES), F32),
            pltpu.VMEM((ch // LANES, CHUNK * 8, LANES), F32),
        ],
        compiler_params=pltpu.CompilerParams(vmem_limit_bytes=60 << 20),
        name="scan_fwd",
    )(xs, zg, proj, since, dtw, dtb, alog, skip, spread)


def scan_bwd_kernel(l, xs_ref, zg_ref, proj_ref, since_ref, ys_ref, gg_ref, hck_ref, dtw_ref, dtb_ref, alog_ref, skip_ref, spread_ref,
                    gxs_ref, gzg_ref, gproj_ref, gdtw_ref, gdtb_ref, galog_ref, gskip_ref,
                    a_ref, dm_ref, dx_ref, dl_ref, gy_ref, bx_ref, cx_ref, h_ref, dec_ref, pq_ref, gq_ref, gb_ref, gc_ref):
    groups = xs_ref.shape[1] // LANES
    cols = [slice(j * LANES, (j + 1) * LANES) for j in range(groups)]

    @pl.when(pl.program_id(0) == 0)
    def _():
        a_ref[...] = jnp.zeros_like(a_ref)
        gdtw_ref[...] = jnp.zeros_like(gdtw_ref)
        gdtb_ref[...] = jnp.zeros_like(gdtb_ref)
        galog_ref[...] = jnp.zeros_like(galog_ref)
        gskip_ref[...] = jnp.zeros_like(gskip_ref)

    proj = proj_ref[...]
    xs = xs_ref[...]
    delta = dt_most * sigmoid(dot_tn(proj[:DT_RANK], dtw_ref[l]) + dtb_ref[l : l + 1, :])
    put(dl_ref, delta)
    put(dm_ref, delta + RESET * (since_ref[...] == 0).astype(F32))
    put(dx_ref, delta * xs)
    zg = zg_ref[...]
    sz = sigmoid(zg)
    gg = gg_ref[...]
    gy = gg * (zg * sz)
    put(gy_ref, gy)
    gzg_ref[...] = (gg * ys_ref[...] * (sz * (1.0 + zg * (1.0 - sz)))).astype(BF16)
    gskip_ref[...] += jnp.sum(gy * xs, axis=0, keepdims=True)
    spread_rows(proj[DT_RANK : DT_RANK + STATE], spread_ref[...], bx_ref)
    spread_rows(proj[DT_RANK + STATE :], spread_ref[...], cx_ref)
    rate = -jnp.exp(alog_ref[l])
    rates2 = [LOG2E * rate[:, c] for c in cols]
    rates = [rate[:, c] for c in cols]

    for j in range(groups):
        h_ref[j, :STATE, :] = hck_ref[0][:, cols[j]]

    def again(g, hs):
        hs = list(hs)
        t0 = pl.multiple_of(g * 8, 8)
        for i in range(8):
            t = t0 + i
            r0 = pl.multiple_of(t * STATE, STATE)
            r1 = pl.multiple_of(t * STATE + STATE, STATE)
            b = bx_ref[pl.ds(r0, STATE), :]
            for j in range(groups):
                dec = jnp.exp2(dm_ref[j, pl.ds(t, 1), :] * rates2[j])
                hs[j] = dec * hs[j] + dx_ref[j, pl.ds(t, 1), :] * b
                dec_ref[j, pl.ds(r0, STATE), :] = dec
                h_ref[j, pl.ds(r1, STATE), :] = hs[j]
        return tuple(hs)

    last = lax.fori_loop(0, CHUNK // 8, again, tuple(hck_ref[0][:, c] for c in cols))

    def back(g, carry):
        carry = [list(c) for c in carry]
        aa, hs, acc = carry
        t0 = pl.multiple_of(CHUNK - 8 - g * 8, 8)
        for i in reversed(range(8)):
            t = t0 + i
            r0 = pl.multiple_of(t * STATE, STATE)
            q0 = pl.multiple_of(t * 8, 8)
            b = bx_ref[pl.ds(r0, STATE), :]
            c = cx_ref[pl.ds(r0, STATE), :]
            gb, gc = None, None
            for j in range(groups):
                gyj = gy_ref[j, pl.ds(t, 1), :]
                a = c * gyj + aa[j]
                dec = dec_ref[j, pl.ds(r0, STATE), :]
                before = h_ref[j, pl.ds(r0, STATE), :]
                carry_a = dec * a
                p = carry_a * before * rates[j]
                ab = a * b
                pq_ref[j, pl.ds(q0, 8), :] = p[:8] + p[8:]
                gq_ref[j, pl.ds(q0, 8), :] = ab[:8] + ab[8:]
                acc[j] = acc[j] + p * dl_ref[j, pl.ds(t, 1), :]
                gbj = a * dx_ref[j, pl.ds(t, 1), :]
                gcj = gyj * hs[j]
                gb = gbj if gb is None else gb + gbj
                gc = gcj if gc is None else gc + gcj
                aa[j] = carry_a
                hs[j] = before
            gb_ref[pl.ds(r0, STATE), :] = gb
            gc_ref[pl.ds(r0, STATE), :] = gc
        return tuple(tuple(c) for c in carry)

    aa, _, acc = lax.fori_loop(
        0, CHUNK // 8, back,
        (tuple(a_ref[:, c] for c in cols), last, tuple(jnp.zeros((STATE, LANES), F32) for _ in cols)))
    for j in range(groups):
        a_ref[:, cols[j]] = aa[j]
        galog_ref[:, cols[j]] += acc[j]

    skip = skip_ref[l : l + 1, :]
    gdts = []
    for j in range(groups):
        psum = pq_ref[j, pl.ds(0, CHUNK, stride=8), :]
        gsum = gq_ref[j, pl.ds(0, CHUNK, stride=8), :]
        for k in range(1, 8):
            psum = psum + pq_ref[j, pl.ds(k, CHUNK, stride=8), :]
            gsum = gsum + gq_ref[j, pl.ds(k, CHUNK, stride=8), :]
        dl = delta[:, cols[j]]
        gdelta = psum + xs[:, cols[j]] * gsum
        gxs_ref[:, cols[j]] = dl * gsum + skip[:, cols[j]] * gy[:, cols[j]]
        gdts.append(gdelta * dl * (1.0 - dl * (1.0 / dt_most)))
    gdt = jnp.concatenate(gdts, axis=1)
    gdtb_ref[...] += jnp.sum(gdt, axis=0, keepdims=True)
    gdt_low = gdt.astype(BF16)
    gdtw_ref[...] += dot(proj[:DT_RANK], gdt_low)
    gproj_ref[:DT_RANK, :] = dot_nt(dtw_ref[l], gdt_low)
    wide_b = jnp.concatenate([gb_ref[pl.ds(n, CHUNK, stride=STATE), :].astype(BF16) for n in range(STATE)], axis=1)
    gproj_ref[DT_RANK : DT_RANK + STATE, :] = dot_nt(spread_ref[...], wide_b)
    wide_c = jnp.concatenate([gc_ref[pl.ds(n, CHUNK, stride=STATE), :].astype(BF16) for n in range(STATE)], axis=1)
    gproj_ref[DT_RANK + STATE :, :] = dot_nt(spread_ref[...], wide_c)


def scan_bwd(l, xs, zg, proj, since, ys, gg, hck, dtw, dtb, alog, skip, spread):
    rows, ch = xs.shape
    steps = rows // CHUNK
    row = lambda w: pl.BlockSpec((CHUNK, w), lambda i: (steps - 1 - i, 0))
    full = lambda s: pl.BlockSpec(s, lambda i: (0,) * len(s))
    big = lambda: pltpu.VMEM((CHUNK * STATE, LANES), F32)
    g = ch // LANES
    return pl.pallas_call(
        functools.partial(scan_bwd_kernel, l),
        grid=(steps,),
        out_shape=[
            jax.ShapeDtypeStruct((rows, ch), F32),
            jax.ShapeDtypeStruct((rows, ch), BF16),
            jax.ShapeDtypeStruct((PROJ, rows), F32),
            jax.ShapeDtypeStruct((DT_RANK, ch), F32),
            jax.ShapeDtypeStruct((1, ch), F32),
            jax.ShapeDtypeStruct((STATE, ch), F32),
            jax.ShapeDtypeStruct((1, ch), F32),
        ],
        in_specs=[row(ch), row(ch), pl.BlockSpec((PROJ, CHUNK), lambda i: (0, steps - 1 - i)), row(1), row(ch), row(ch),
                  pl.BlockSpec((1, STATE, ch), lambda i: (steps - 1 - i, 0, 0))]
        + [full(v.shape) for v in (dtw, dtb, alog, skip, spread)],
        out_specs=[row(ch), row(ch), pl.BlockSpec((PROJ, CHUNK), lambda i: (0, steps - 1 - i)), full((DT_RANK, ch)), full((1, ch)), full((STATE, ch)), full((1, ch))],
        scratch_shapes=[
            pltpu.VMEM((STATE, ch), F32),
            pltpu.VMEM((ch // LANES, CHUNK, LANES), F32),
            pltpu.VMEM((ch // LANES, CHUNK, LANES), F32),
            pltpu.VMEM((ch // LANES, CHUNK, LANES), F32),
            pltpu.VMEM((ch // LANES, CHUNK, LANES), F32),
            big(), big(),
            pltpu.VMEM((g, CHUNK * STATE + STATE, LANES), F32),
            pltpu.VMEM((g, CHUNK * STATE, LANES), F32),
            pltpu.VMEM((g, CHUNK * 8, LANES), F32),
            pltpu.VMEM((g, CHUNK * 8, LANES), F32),
            big(), big(),
        ],
        compiler_params=pltpu.CompilerParams(vmem_limit_bytes=60 << 20),
        name="scan_bwd",
    )(xs, zg, proj, since, ys, gg, hck, dtw, dtb, alog, skip, spread)


def rms_inverse(values):
    return lax.rsqrt(jnp.mean(values * values, axis=-1, keepdims=True) + epsilon)


def norm_back(values, inverse, gain, grad):
    scaled = grad * gain
    pulled = inverse * scaled - values * (inverse * inverse * inverse) * jnp.mean(scaled * values, axis=-1, keepdims=True)
    return pulled, jnp.sum(grad * values * inverse, axis=0, keepdims=True)


GELU_A, GELU_B = 0.7978845608028654, 0.044715


def gelu(v):
    return 0.5 * v * (1.0 + jnp.tanh(GELU_A * (v + GELU_B * v * v * v)))


def gelu_slope(v):
    square = v * v
    t = jnp.tanh(GELU_A * v * (1.0 + GELU_B * square))
    return 0.5 * (1.0 + t) + 0.5 * v * (1.0 - t * t) * GELU_A * (1.0 + 3.0 * GELU_B * square)


def by_lane(m, values):
    picked = jnp.int32(values[0])
    for k in range(1, len(values)):
        picked = jnp.where(m == k, jnp.int32(values[k]), picked)
    return picked


def nearest_first(m, lanes):
    orders = [sorted((s for s in range(lanes) if s != k), key=lambda s: (abs(s - k), s)) for k in range(lanes)]
    return [by_lane(m, [order[i] for order in orders]) for i in range(lanes - 1)]


def chain_order(m, lanes):
    def due(k, s):
        return (lanes - 1 - s) + k if s > k else s + (lanes - 1 - k)

    orders = [sorted((s for s in range(lanes) if s != k), key=lambda s: (due(k, s), s)) for k in range(lanes)]
    return [by_lane(m, [order[i] for order in orders]) for i in range(lanes - 1)]


def greet(d, m, lanes, peers, across):
    barrier = pltpu.get_barrier_semaphore()
    if across:
        for k in range(1, lanes):
            pl.semaphore_signal(barrier, inc=1, device_id=(d, lax.rem(m + k, lanes)), device_id_type=MESH)
        for k in range(1, peers):
            pl.semaphore_signal(barrier, inc=1, device_id=(lax.rem(d + k, peers), m), device_id_type=MESH)
        pl.semaphore_wait(barrier, lanes + peers - 2)
    else:

        @pl.when(m > 0)
        def _():
            pl.semaphore_signal(barrier, inc=1, device_id=(d, m - 1), device_id_type=MESH)

        @pl.when(m < lanes - 1)
        def _():
            pl.semaphore_signal(barrier, inc=1, device_id=(d, m + 1), device_id_type=MESH)

        pl.semaphore_wait(barrier, jnp.where(m > 0, 1, 0) + jnp.where(m < lanes - 1, 1, 0))


class LineGather:
    def __init__(self, buf, send, recv, d, m, lanes):
        self.buf, self.send, self.recv, self.d, self.m, self.lanes = buf, send, recv, d, m, lanes
        self.order = nearest_first(m, lanes)

    def copy(self, s, up):
        return pltpu.make_async_remote_copy(
            src_ref=self.buf.at[s], dst_ref=self.buf.at[s], send_sem=self.send.at[0 if up else 1, s],
            recv_sem=self.recv.at[s], device_id=(self.d, self.m + 1 if up else self.m - 1), device_id_type=MESH,
        )

    def start(self):
        @pl.when(self.m < self.lanes - 1)
        def _():
            self.copy(self.m, True).start()

        @pl.when(self.m > 0)
        def _():
            self.copy(self.m, False).start()

    def arrive(self, i):
        s, m = self.order[i], self.m
        self.copy(s, True).wait_recv()

        @pl.when((s < m) & (m < self.lanes - 1))
        def _():
            self.copy(s, True).start()

        @pl.when((s > m) & (m > 0))
        def _():
            self.copy(s, False).start()

        return s

    def finish(self):
        for s in range(self.lanes):

            @pl.when((s <= self.m) & (self.m < self.lanes - 1))
            def _():
                self.copy(s, True).wait_send()

            @pl.when((s >= self.m) & (self.m > 0))
            def _():
                self.copy(s, False).wait_send()


PIECES = 1


class LineReduce:
    def __init__(self, stage, inbox, send, recv, d, m, lanes):
        self.stage, self.inbox, self.send, self.recv = stage, inbox, send, recv
        self.d, self.m, self.lanes = d, m, lanes
        self.rows = stage.shape[1] // PIECES
        self.order = chain_order(m, lanes)
        self.middle = jnp.logical_and(m > 0, m < lanes - 1)
        self.at_end = jnp.logical_not(self.middle)

    def piece(self, p):
        return pl.ds(p * self.rows, self.rows)

    def copy(self, s, p):
        up = s > self.m
        side = jnp.where(up, 0, 1)
        return pltpu.make_async_remote_copy(
            src_ref=self.stage.at[s, self.piece(p)], dst_ref=self.inbox.at[side, s, self.piece(p)], send_sem=self.send.at[s, p],
            recv_sem=self.recv.at[side, s, p], device_id=(self.d, jnp.where(up, self.m + 1, self.m - 1)), device_id_type=MESH,
        )

    def push_first(self, s, term):
        self.stage[s] = term.astype(BF16)
        for p in range(PIECES):
            self.copy(s, p).start()

    def push_on(self, s, p, term):
        side = jnp.where(s > self.m, 0, 1)
        self.copy(s, p).wait_recv()
        self.stage[s, self.piece(p)] = (term + self.inbox[side, s, self.piece(p)].astype(F32)).astype(BF16)
        self.copy(s, p).start()

    def push(self, s, term):
        @pl.when(self.at_end)
        def _():
            self.push_first(s, term)

        @pl.when(self.middle)
        def _():
            for p in range(PIECES):
                self.push_on(s, p, term[p * self.rows : (p + 1) * self.rows])

    def total(self, own_ref):
        m = self.m

        def add(side):
            for p in range(PIECES):
                pltpu.make_async_remote_copy(
                    src_ref=self.stage.at[m, self.piece(p)], dst_ref=self.inbox.at[side, m, self.piece(p)], send_sem=self.send.at[m, p],
                    recv_sem=self.recv.at[side, m, p], device_id=(self.d, m), device_id_type=MESH,
                ).wait_recv()
            own_ref[...] += self.inbox[side, m].astype(F32)

        @pl.when(m > 0)
        def _():
            add(0)

        @pl.when(m < self.lanes - 1)
        def _():
            add(1)

    def finish(self):
        for s in self.order:
            for p in range(PIECES):
                self.copy(s, p).wait_send()


def reduce_scratch(lanes, rows, width):
    return [
        pltpu.VMEM((lanes, rows, width), BF16),
        pltpu.VMEM((2, lanes, rows, width), BF16),
        dma(lanes, PIECES), dma(2, lanes, PIECES),
    ]


PARTS = 3


def line_sum(part, stage, inbox, send, recv, out, d, m, lanes, between=lambda: None):
    width = part.shape[1] // PARTS

    def copy(side, b):
        return pltpu.make_async_remote_copy(
            src_ref=stage.at[side, b], dst_ref=inbox.at[side, b], send_sem=send.at[side, b], recv_sem=recv.at[side, b],
            device_id=(d, m + 1 if side == 0 else m - 1), device_id_type=MESH,
        )

    def step(side, b):
        has_source = m > 0 if side == 0 else m < lanes - 1
        has_target = m < lanes - 1 if side == 0 else m > 0
        cols = slice(b * width, (b + 1) * width)

        @pl.when(has_source)
        def _():
            copy(side, b).wait_recv()

        @pl.when(jnp.logical_not(has_source))
        def _():
            inbox[side, b] = jnp.zeros(inbox.shape[2:], BF16)

        @pl.when(has_target)
        def _():
            stage[side, b] = (part[:, cols] + inbox[side, b].astype(F32)).astype(BF16)
            copy(side, b).start()

    low = 2 * m < lanes

    def both(first):
        def run(side):
            for b in range(PARTS):
                step(side, b)

        @pl.when(low)
        def _():
            run(0 if first else 1)

        @pl.when(jnp.logical_not(low))
        def _():
            run(1 if first else 0)

    both(True)
    between()
    both(False)
    for b in range(PARTS):
        cols = slice(b * width, (b + 1) * width)
        out[:, cols] = (part[:, cols] + inbox[0, b].astype(F32) + inbox[1, b].astype(F32)).astype(BF16)

    def finish():
        for b in range(PARTS):

            @pl.when(m < lanes - 1)
            def _():
                copy(0, b).wait_send()

            @pl.when(m > 0)
            def _():
                copy(1, b).wait_send()

    return finish


def vmem(count):
    return [pl.BlockSpec(memory_space=pltpu.VMEM)] * count


def f32(*shape):
    return jax.ShapeDtypeStruct(shape, F32)


def bf16(*shape):
    return jax.ShapeDtypeStruct(shape, BF16)


def dma(*shape):
    return pltpu.SemaphoreType.DMA(shape)


def hbm(count):
    return [pl.BlockSpec(memory_space=pl.ANY)] * count


def fetch(pairs, sem):
    copies = [pltpu.make_async_copy(src, dst, sem.at[i]) for i, (src, dst) in enumerate(pairs)]
    for copy in copies:
        copy.start()
    return copies


def params(cid, limit=58):
    return pltpu.CompilerParams(collective_id=cid, has_side_effects=True, vmem_limit_bytes=limit << 20)


CONV_ROWS = 128
HEAD = 8


def conv_window(padded_ref, since_ref, taps, bias, base):
    window = padded_ref[pl.ds(base, CONV_ROWS + HEAD), :]
    since = since_ref[pl.ds(base, CONV_ROWS), :]
    shifted = [window[HEAD:]]
    for j in range(1, CONV):
        shifted.append(window[HEAD - j : HEAD - j + CONV_ROWS] * (since >= j).astype(F32))
    pre = bias
    for j in range(CONV):
        pre = pre + taps[CONV - 1 - j : CONV - j, :] * shifted[j]
    return pre, shifted


class Experts:
    def __init__(self, d, m, lanes, peers, into_ref, rows_ref, pack_ref, slots_ref, part_ref, back_ref, stage_ref, inbox_ref,
                 gsend, grecv, dsend, drecv, bsend, brecv, rsend, rrecv):
        self.d, self.m, self.lanes, self.peers = d, m, lanes, peers
        self.rows, self.into, self.pack, self.slots, self.part, self.back = rows_ref, into_ref, pack_ref, slots_ref, part_ref, back_ref
        self.stage, self.inbox = stage_ref, inbox_ref
        self.dsend, self.drecv, self.bsend, self.brecv, self.rsend, self.rrecv = dsend, drecv, bsend, brecv, rsend, rrecv
        self.sets = rows_ref.shape[1]
        self.cap = pack_ref.shape[2] // self.sets
        self.width = rows_ref.shape[3]
        self.gather = LineGather(rows_ref, gsend, grecv, d, m, lanes)

    def slot_rows(self, ref, s, i):
        return ref[s, :, i * self.cap : (i + 1) * self.cap, :].reshape(self.peers * self.cap, self.width)

    def set_slot_rows(self, ref, s, i, value):
        ref[s, :, i * self.cap : (i + 1) * self.cap, :] = value.reshape(self.peers, self.cap, self.width)

    def hop(self, src, dst, send, recv, s, k):
        other = lax.rem(self.d + k, self.peers)
        return pltpu.make_async_remote_copy(
            src_ref=src.at[s, other], dst_ref=dst.at[s, self.d], send_sem=send.at[s, k - 1],
            recv_sem=recv.at[s, k - 1], device_id=(other, self.m), device_id_type=MESH,
        )

    def across(self, src, dst, send, recv, s):
        for k in range(1, self.peers):
            self.hop(src, dst, send, recv, s, k).start()
        dst[s, self.d] = src[s, self.d]

    def dispatch(self, s):
        for i in range(self.sets):
            self.set_slot_rows(self.pack, s, i, dot(self.into[s], self.rows[s, i]).astype(BF16))
        self.across(self.pack, self.slots, self.dsend, self.drecv, s)

    def answer(self, s, expert):
        for k in range(1, self.peers):
            self.hop(self.pack, self.slots, self.dsend, self.drecv, s, k).wait_recv()
        for i, value in enumerate(expert(s, [self.slot_rows(self.slots, s, i) for i in range(self.sets)])):
            self.set_slot_rows(self.part, s, i, value.astype(BF16))
        self.across(self.part, self.back, self.bsend, self.brecv, s)

    def home(self, s):
        return pltpu.make_async_remote_copy(
            src_ref=self.stage.at[s], dst_ref=self.inbox.at[self.m], send_sem=self.rsend.at[s], recv_sem=self.rrecv.at[self.m],
            device_id=(self.d, s), device_id_type=MESH,
        )

    def combine(self, s):
        for k in range(1, self.peers):
            self.hop(self.part, self.back, self.bsend, self.brecv, s, k).wait_recv()
        return [dot_tn(self.into[s], self.slot_rows(self.back, s, i)) for i in range(self.sets)]

    def combine_away(self, s):
        for i, value in enumerate(self.combine(s)):
            self.stage[s, i] = value.astype(BF16)
        self.home(s).start()

    def steps(self, expert, own_ref):
        one, two, three = self.gather.order
        self.dispatch(self.m)
        yield
        self.gather.arrive(0)
        self.dispatch(one)
        yield
        self.gather.arrive(1)
        self.dispatch(two)
        self.answer(one, expert)
        yield
        self.gather.arrive(2)
        self.dispatch(three)
        self.answer(two, expert)
        self.combine_away(one)
        yield
        self.answer(three, expert)
        self.combine_away(two)
        yield
        self.answer(self.m, expert)
        self.combine_away(three)
        yield
        for i, value in enumerate(self.combine(self.m)):
            own_ref[i] = value
        yield

    def settle(self, own_ref):
        for s in self.gather.order:
            pltpu.make_async_remote_copy(
                src_ref=self.stage.at[s], dst_ref=self.inbox.at[s], send_sem=self.rsend.at[s], recv_sem=self.rrecv.at[s],
                device_id=(self.d, s), device_id_type=MESH,
            ).wait_recv()
            own_ref[...] += self.inbox[s].astype(F32)

    def run(self, expert, own_ref, meanwhile):
        self.gather.start()
        for _ in self.steps(expert, own_ref):
            pass
        meanwhile()
        self.settle(own_ref)

    def finish(self):
        self.gather.finish()
        order = [self.m, *self.gather.order]
        for s in order:
            for k in range(1, self.peers):
                self.hop(self.pack, self.slots, self.dsend, self.drecv, s, k).wait_send()
                self.hop(self.part, self.back, self.bsend, self.brecv, s, k).wait_send()
        for s in order[1:]:
            self.home(s).wait_send()


def large(v):
    return v.size * v.dtype.itemsize >= 1 << 17


class Refs(types.SimpleNamespace):
    def need(self, *refs):
        for ref in refs:
            if id(ref) in self.coming:
                self.coming.pop(id(ref)).wait()

    def ship(self, *refs):
        for ref in refs:
            self.gone.append(self.going.pop(id(ref)))
            self.gone[-1].start()


def launch(name, cid, body, inputs, far, outputs, scratch, limit=58):
    near = {k: v for k, v in inputs.items() if not large(v)}
    lazy = {k: v for k, v in inputs.items() if large(v)}
    prompt = {k: v for k, v in outputs.items() if not large(v)}
    late = {k: v for k, v in outputs.items() if large(v)}
    buffers = {k: pltpu.VMEM(v.shape, v.dtype) for k, v in {**lazy, **late}.items()}
    away = [k + "_far" for k in (*lazy, *late)]
    names = [*near, *away[: len(lazy)], *far, *prompt, *away[len(lazy) :], *scratch, *buffers, "moves"]

    def kernel(*refs):
        r = Refs(**dict(zip(names, refs)))
        get = lambda k: getattr(r, k)
        r.gone = []
        r.coming = {id(get(k)): pltpu.make_async_copy(get(k + "_far"), get(k), r.moves.at[i]) for i, k in enumerate(lazy)}
        r.going = {id(get(k)): pltpu.make_async_copy(get(k), get(k + "_far"), r.moves.at[len(lazy) + i]) for i, k in enumerate(late)}
        for copy in r.coming.values():
            copy.start()
        body(r)
        r.need(*map(get, lazy))
        r.ship(*(get(k) for k in late if id(get(k)) in r.going))
        for copy in r.gone:
            copy.wait()

    results = pl.pallas_call(
        kernel,
        out_shape=[*prompt.values(), *late.values()],
        in_specs=vmem(len(near)) + hbm(len(lazy) + len(far)),
        out_specs=vmem(len(prompt)) + hbm(len(late)),
        scratch_shapes=[*scratch.values(), *buffers.values(), dma(max(1, len(lazy) + len(late)))],
        compiler_params=params(cid, limit),
        name=name,
    )(*near.values(), *lazy.values(), *far.values())
    return types.SimpleNamespace(**dict(zip([*prompt, *late], results)))


def convolution(small):
    return dict(norm_in=small.norm_in, conv_w=small.conv_w, conv_b=small.conv_b, since=small.since, x_proj=small.x_proj)


def routing(small):
    return dict(norm_moe=small.norm_moe, router=small.router)


def flat(ref):
    return ref[...].reshape(ref.shape[0] * ref.shape[1], ref.shape[2])


def gate_of(chance, choose):
    return jnp.sum(chance * choose, axis=1, keepdims=True)


class Sizes:
    def __init__(self, lanes, peers, experts, cap, rows, width, channels, hidden):
        self.lanes, self.peers, self.experts, self.cap = lanes, peers, experts, cap
        self.rows, self.width, self.channels, self.hidden = rows, width, channels, hidden
        self.total, self.slots = rows * lanes, experts * cap


def in_outputs(z):
    return dict(whole=bf16(z.lanes, z.rows, z.width), conv=f32(z.total + HEAD, z.channels), zgate=f32(z.total, z.channels),
                xs=f32(z.total, z.channels), proj=bf16(PROJ, z.total))


def sum_scratch(z):
    halves = pltpu.VMEM((2, PARTS, PROJ, z.total // PARTS), BF16)
    return dict(sum_stage=halves, sum_inbox=halves, sum_send=dma(2, PARTS), sum_recv=dma(2, PARTS))


def in_scratch(z):
    return dict(part=pltpu.VMEM((PROJ, z.total), F32), u_send=dma(2, z.lanes), u_recv=dma(z.lanes), **sum_scratch(z))


def in_stage(z, r, l, act, weights):
    d, m = lax.axis_index("dp"), lax.axis_index("mp")
    r.whole[m] = (act * rms_inverse(act) * r.norm_in[l : l + 1, :]).astype(BF16)
    gather = LineGather(r.whole, r.u_send, r.u_recv, d, m, z.lanes)
    gather.start()
    r.conv[:HEAD, :] = jnp.zeros((HEAD, z.channels), F32)
    weights.wait()

    def project(s):
        u = r.whole[s]
        r.conv[pl.ds(pl.multiple_of(s * z.rows + HEAD, 8), z.rows), :] = dot(u, r.win[0])
        r.zgate[pl.ds(pl.multiple_of(s * z.rows, 8), z.rows), :] = dot(u, r.win[1])

    project(m)
    for i in range(z.lanes - 1):
        project(gather.arrive(i))
    r.ship(r.conv, r.zgate, r.whole)
    taps, bias = r.conv_w[l], r.conv_b[l : l + 1, :]

    def conv_step(c, carry):
        base = pl.multiple_of(c * CONV_ROWS, CONV_ROWS)
        pre, _ = conv_window(r.conv, r.since, taps, bias, base)
        xs = pre * sigmoid(pre)
        r.xs[pl.ds(base, CONV_ROWS), :] = xs
        r.part[:, pl.ds(base, CONV_ROWS)] = dot_nt(r.x_proj[l], xs.astype(BF16))
        return carry

    lax.fori_loop(0, z.total // CONV_ROWS, conv_step, 0)
    r.ship(r.xs)
    finish = line_sum(r.part, r.sum_stage, r.sum_inbox, r.sum_send, r.sum_recv, r.proj, d, m, z.lanes)
    gather.finish()
    finish()


def first_block(z, l, act, small, w_in):
    def body(r):
        d, m = lax.axis_index("dp"), lax.axis_index("mp")
        (weights,) = fetch([(r.w_in.at[l], r.win)], r.fetched)
        greet(d, m, z.lanes, 0, False)
        r.need(r.act)
        in_stage(z, r, l, r.act[...].astype(F32), weights)

    inputs = dict(act=act, **convolution(small))
    return launch("mamba_in", 0, body, inputs, dict(w_in=w_in), in_outputs(z),
                  dict(win=pltpu.VMEM(w_in.shape[1:], BF16), fetched=dma(1), **in_scratch(z)))


def expert_refs(r):
    return (r.e_rows, r.e_pack, r.e_slots, r.e_part, r.e_back, r.e_stage, r.e_inbox, r.e_gs, r.e_gr, r.e_ds, r.e_dr, r.e_bs, r.e_br,
            r.e_rs, r.e_rr)


def expert_names(z, sets):
    across = pltpu.VMEM((z.lanes, z.peers, sets * z.cap, z.width), BF16)
    along = pltpu.VMEM((z.lanes, sets, z.rows, z.width), BF16)
    plane, line = dma(z.lanes, z.peers - 1), dma(z.lanes)
    return dict(
        e_rows=along, e_pack=across, e_slots=across, e_part=across, e_back=across, e_stage=along, e_inbox=along, e_gs=dma(2, z.lanes),
        e_gr=line, e_ds=plane, e_dr=plane, e_bs=plane, e_br=plane, e_rs=line, e_rr=line, e_own=pltpu.VMEM((sets, z.rows, z.width), F32))


def weight_scratch(wout, wup, wdown):
    return dict(wout=pltpu.VMEM(wout.shape[1:], BF16), wup=pltpu.VMEM(wup.shape[2:], BF16), wdown=pltpu.VMEM(wdown.shape[2:], BF16))


def out_scratch(z, place):
    stage, inbox, send, recv = reduce_scratch(z.lanes, z.rows, z.width)
    return dict(m_stage=stage, m_inbox=inbox, m_send=send, m_recv=recv, places=pltpu.VMEM((z.lanes, *place.shape), jnp.int32),
                p_send=dma(2, z.lanes), p_recv=dma(z.lanes), m_own=pltpu.VMEM((z.rows, z.width), F32))


def out_stage(z, r, l, wout):
    d, m = lax.axis_index("dp"), lax.axis_index("mp")
    r.places[m] = r.place[...]
    places = LineGather(r.places, r.p_send, r.p_recv, d, m, z.lanes)
    places.start()
    reduce = LineReduce(r.m_stage, r.m_inbox, r.m_send, r.m_recv, d, m, z.lanes)
    wout.wait()
    r.need(r.act, r.gated)
    for s in reduce.order:
        reduce.push(s, dot(r.gated[s], r.wout[...]))
    r.m_own[...] = r.act[...].astype(F32) + dot(r.gated[m], r.wout[...])

    def spread_places(s):
        numbers = lax.broadcasted_iota(jnp.int32, (z.slots, z.rows), 0)
        r.into[s] = (numbers == r.places[s][:1, : z.rows]).astype(F32).astype(BF16)

    spread_places(m)
    owner = lax.broadcasted_iota(jnp.int32, (z.slots, z.experts), 0) // z.cap == lax.broadcasted_iota(jnp.int32, (z.slots, z.experts), 1)
    r.choose[...] = dot_tn(r.into[m], owner.astype(F32).astype(BF16))
    for i in range(z.lanes - 1):
        spread_places(places.arrive(i))
    reduce.total(r.m_own)

    def finish():
        places.finish()
        reduce.finish()

    return finish


def chances(z, normed, table):
    logits = lax.dot_general(normed, table, (((1,), (1,)), ((), ())), precision=highest, preferred_element_type=F32)
    raised = jnp.exp(logits - jnp.max(logits, axis=1, keepdims=True))
    return raised / jnp.sum(raised, axis=1, keepdims=True)


def middle_block(z, l, act, gated, small, weights):
    def body(r):
        d, m = lax.axis_index("dp"), lax.axis_index("mp")
        wout, wup, wdown, win = fetch([(r.w_out.at[l], r.wout), (r.w_up.at[l, 0], r.wup), (r.w_down.at[l, 0], r.wdown),
                                       (r.w_in.at[l + 1], r.win)], r.fetched)
        greet(d, m, z.lanes, z.peers, True)
        finish = out_stage(z, r, l, wout)
        wup.wait()
        wdown.wait()
        middle = r.m_own[...]
        r.middle[...] = middle
        r.e_rows[m, 0] = (middle * rms_inverse(middle) * r.norm_moe[l : l + 1, :]).astype(BF16)
        moe = Experts(d, m, z.lanes, z.peers, r.into, *expert_refs(r))

        def expert(s, rows):
            r.slots[s] = rows[0]
            hidden = dot(rows[0], r.wup[...])
            r.hidden[s] = hidden.astype(BF16)
            active = gelu(hidden).astype(BF16)
            r.active[s] = active
            return [dot(active, r.wdown[...])]

        def meanwhile():
            finish()
            middle = r.middle[...]
            r.chance[...] = chances(z, middle * rms_inverse(middle) * r.norm_moe[l : l + 1, :], r.router[l])

        moe.run(expert, r.e_own, meanwhile)
        r.ship(r.into, r.middle, r.slots, r.hidden, r.active)
        picked = r.e_own[0].astype(BF16)
        r.picked[...] = picked
        following = r.middle[...] + gate_of(r.chance[...], r.choose[...]) * picked.astype(F32)
        r.following[...] = following
        r.ship(r.picked, r.following)
        in_stage(z, r, l + 1, following, win)
        moe.finish()

    w_in, w_out, w_up, w_down = weights
    slots = (z.lanes, z.slots)
    return launch(
        "middle", 1 + l, body, dict(act=act, gated=gated, place=small.place, **routing(small), **convolution(small)),
        dict(w_in=w_in, w_out=w_out, w_up=w_up, w_down=w_down),
        dict(middle=f32(z.rows, z.width), chance=f32(z.rows, z.experts), into=bf16(*slots, z.rows), slots=bf16(*slots, z.width),
             hidden=bf16(*slots, z.hidden), active=bf16(*slots, z.hidden), picked=bf16(z.rows, z.width), choose=f32(z.rows, z.experts), following=f32(z.rows, z.width),
             **in_outputs(z)),
        dict(win=pltpu.VMEM(w_in.shape[1:], BF16), fetched=dma(4), **weight_scratch(w_out, w_up, w_down), **out_scratch(z, small.place),
             **expert_names(z, 1), **in_scratch(z)))


def back_outputs(z):
    return dict(gmid=f32(z.rows, z.width), gup=f32(z.width, z.hidden), gdown=f32(z.hidden, z.width), ggated=f32(z.lanes, z.rows, z.channels),
                gwout=bf16(z.channels, z.width), gshare=f32(z.experts + 8, z.width))


def back_scratch(z):
    return dict(wide=pltpu.VMEM((z.lanes, z.rows, z.width), BF16), w_send=dma(2, z.lanes), w_recv=dma(z.lanes))


def route_back(z, r, l, upstream, middle, chance, choose, picked, returned):
    d, m = lax.axis_index("dp"), lax.axis_index("mp")
    gate = gate_of(chance, choose)
    inverse, gain = rms_inverse(middle), r.norm_moe[l : l + 1, :]
    grad_gate = jnp.sum(upstream * picked.astype(F32), axis=1, keepdims=True)
    grad_logit = gate * grad_gate * (choose - chance)
    grad_normed = returned.astype(BF16).astype(F32) + lax.dot_general(
        grad_logit, r.router[l], (((1,), (0,)), ((), ())), precision=highest, preferred_element_type=F32)
    pulled, grad_gain = norm_back(middle, inverse, gain, grad_normed)
    grad_middle = upstream + pulled
    r.gmid[...] = grad_middle
    r.ship(r.gmid)
    r.wide[m] = grad_middle.astype(BF16)
    gather = LineGather(r.wide, r.w_send, r.w_recv, d, m, z.lanes)
    gather.start()
    grad_router = lax.dot_general(
        grad_logit, middle * inverse * gain, (((0,), (0,)), ((), ())), precision=highest, preferred_element_type=F32)
    r.gshare[: z.experts, :] = grad_router
    r.gshare[z.experts :, :] = jnp.broadcast_to(grad_gain, (8, z.width))

    def gate_back(s):
        r.ggated[s] = dot_nt(r.wide[s], r.wout[...])

    gate_back(m)
    for i in range(z.lanes - 1):
        gate_back(gather.arrive(i))
    r.ship(r.ggated)
    r.need(r.gated)
    r.gwout[...] = dot_tn(flat(r.gated), flat(r.wide)).astype(BF16)
    gather.finish()


def turn_block(z, l, act, gated, cotangent, small, weights):
    def body(r):
        d, m = lax.axis_index("dp"), lax.axis_index("mp")
        wout, wup, wdown = fetch([(r.w_out.at[l], r.wout), (r.w_up.at[l, 0], r.wup), (r.w_down.at[l, 0], r.wdown)], r.fetched)
        greet(d, m, z.lanes, z.peers, True)
        finish = out_stage(z, r, l, wout)
        wup.wait()
        wdown.wait()
        middle = r.m_own[...]
        normed = middle * rms_inverse(middle) * r.norm_moe[l : l + 1, :]
        forth = Experts(d, m, z.lanes, z.peers, r.into, *expert_refs(r))
        back = Experts(d, m, z.lanes, z.peers, r.into, *(getattr(r, "f" + k[1:]) for k in list(expert_names(z, 1))[:-1]))
        r.e_rows[m, 0] = normed.astype(BF16)
        forth.gather.start()
        chance = chances(z, normed, r.router[l])
        r.chance[...] = chance
        r.need(r.cotangent)
        r.f_rows[m, 0] = (gate_of(chance, r.choose[...]) * r.cotangent[...].astype(F32)).astype(BF16)
        back.gather.start()

        def expert_forth(s, rows):
            active = gelu(dot(rows[0], r.wup[...])).astype(BF16)
            r.active[s] = active
            return [dot(active, r.wdown[...])]

        def expert_back(s, rows):
            slope = gelu_slope(dot(forth.slot_rows(forth.slots, s, 0), r.wup[...]))
            grad_hidden = (dot_nt(rows[0], r.wdown[...]) * slope).astype(BF16)
            r.ghid[s] = grad_hidden
            return [dot_nt(grad_hidden, r.wup[...])]

        for _ in zip(forth.steps(expert_forth, r.e_own), back.steps(expert_back, r.f_own)):
            pass
        finish()
        r.gdown[...] = dot_tn(flat(r.active), r.f_slots[...].reshape(z.lanes * z.slots, z.width))
        r.gup[...] = dot_tn(r.e_slots[...].reshape(z.lanes * z.slots, z.width), flat(r.ghid))
        r.ship(r.gdown, r.gup)
        forth.settle(r.e_own)
        back.settle(r.f_own)
        picked = r.e_own[0].astype(BF16)
        r.following[...] = r.m_own[...] + gate_of(r.chance[...], r.choose[...]) * picked.astype(F32)
        r.ship(r.following)
        route_back(z, r, l, r.cotangent[...].astype(F32), r.m_own[...], r.chance[...], r.choose[...], picked, r.f_own[0])
        forth.finish()
        back.finish()

    w_in, w_out, w_up, w_down = weights
    slots = (z.lanes, z.slots)
    return launch(
        "turn", 8, body, dict(act=act, gated=gated, cotangent=cotangent, place=small.place, **routing(small)),
        dict(w_out=w_out, w_up=w_up, w_down=w_down),
        dict(following=f32(z.rows, z.width), **back_outputs(z)),
        dict(fetched=dma(3), choose=pltpu.VMEM((z.rows, z.experts), F32), chance=pltpu.VMEM((z.rows, z.experts), F32), into=pltpu.VMEM((*slots, z.rows), BF16),
             active=pltpu.VMEM((*slots, z.hidden), BF16), ghid=pltpu.VMEM((*slots, z.hidden), BF16),
             **weight_scratch(w_out, w_up, w_down), **out_scratch(z, small.place), **expert_names(z, 1),
             **{"f" + k[1:]: v for k, v in expert_names(z, 1).items()}, **back_scratch(z)),
        58 if z.slots <= 256 else 61)


class PlaneSum:
    def __init__(self, d, m, peers, mine, pair, half, inbox, result, psend, precv, csend, crecv, gsend, grecv):
        self.m, self.mine, self.pair, self.half, self.inbox, self.result = m, mine, pair, half, inbox, result
        self.psend, self.precv, self.csend, self.crecv, self.gsend, self.grecv = psend, precv, csend, crecv, gsend, grecv
        self.chips = peers // 2
        self.chip, self.core = lax.div(d, 2), lax.rem(d, 2)
        self.rows = mine.shape[0] // 2
        self.block = self.rows // self.chips

    def side(self, core):
        return pl.ds(pl.multiple_of(core * self.rows, 16), self.rows)

    def at(self, chip):
        return pl.ds(pl.multiple_of(chip * self.block, 16), self.block)

    def final(self, chip):
        return pl.ds(pl.multiple_of(self.core * self.rows + chip * self.block, 16), self.block)

    def swap(self, src, dst, i):
        return pltpu.make_async_remote_copy(
            src_ref=src, dst_ref=dst, send_sem=self.psend.at[i], recv_sem=self.precv.at[i],
            device_id=(self.chip * 2 + 1 - self.core, self.m), device_id_type=MESH)

    def first_swap(self):
        return self.swap(self.mine.at[self.side(1 - self.core)], self.pair, 0)

    def last_swap(self):
        return self.swap(self.result.at[self.side(self.core)], self.result.at[self.side(self.core)], 1)

    def other(self, k):
        return lax.rem(self.chip + k, self.chips)

    def scatter(self, k):
        return pltpu.make_async_remote_copy(
            src_ref=self.half.at[self.at(self.other(k))], dst_ref=self.inbox.at[k - 1], send_sem=self.csend.at[k - 1],
            recv_sem=self.crecv.at[k - 1], device_id=(self.other(k) * 2 + self.core, self.m), device_id_type=MESH)

    def gather(self, k):
        return pltpu.make_async_remote_copy(
            src_ref=self.result.at[self.final(self.chip)], dst_ref=self.result.at[self.final(self.chip)], send_sem=self.gsend.at[k - 1],
            recv_sem=self.grecv.at[k - 1], device_id=(self.other(k) * 2 + self.core, self.m), device_id_type=MESH)

    def begin(self):
        self.first_swap().start()

    def second(self):
        self.first_swap().wait_recv()
        self.half[...] = (self.mine[self.side(self.core)].astype(F32) + self.pair[...].astype(F32)).astype(BF16)
        for k in range(1, self.chips):
            self.scatter(k).start()

    def third(self):
        for k in range(1, self.chips):
            self.scatter(k).wait_recv()
        summed = self.half[self.at(self.chip)].astype(F32)
        for k in range(1, self.chips):
            summed = summed + self.inbox[k - 1].astype(F32)
        self.result[self.final(self.chip)] = summed.astype(BF16)
        for k in range(1, self.chips):
            self.gather(k).start()

    def fourth(self):
        for k in range(1, self.chips):
            self.gather(k).wait_recv()
        self.last_swap().start()

    def end(self):
        self.last_swap().wait_recv()

    def finish(self):
        self.first_swap().wait_send()
        self.last_swap().wait_send()
        for k in range(1, self.chips):
            self.scatter(k).wait_send()
            self.gather(k).wait_send()


def plane_scratch(peers, rows, width):
    return [
        pltpu.VMEM((rows, width), BF16),
        pltpu.VMEM((rows // 2, width), BF16),
        pltpu.VMEM((rows // 2, width), BF16),
        pltpu.VMEM((peers // 2 - 1, rows // peers, width), BF16),
        dma(2), dma(2), dma(peers // 2 - 1), dma(peers // 2 - 1), dma(peers // 2 - 1), dma(peers // 2 - 1),
    ]


def exchange(targets, buf, inbox, send, recv):
    copies = [
        pltpu.make_async_remote_copy(src_ref=buf, dst_ref=inbox.at[k], send_sem=send.at[k], recv_sem=recv.at[k],
                                     device_id=target, device_id_type=MESH)
        for k, target in enumerate(targets)
    ]
    for copy in copies:
        copy.start()

    def collect():
        total = buf[...].astype(F32)
        for k, copy in enumerate(copies):
            copy.wait()
            total = total + inbox[k].astype(F32)
        return total

    return collect


def early_rows(width, experts):
    sizes = [width, width, DT_RANK, STATE, 16, experts + 8, experts + 8]
    return [sum(sizes[:i]) for i in range(len(sizes) + 1)]


def late_rows(width):
    sizes = [width, PROJ, 16]
    return [sum(sizes[:i]) for i in range(len(sizes) + 1)]


def whole_blocks(rows, peers):
    return -(-rows // (16 * peers)) * 16 * peers


def in_back_scratch(z, win, last):
    early = whole_blocks(early_rows(z.width, z.experts)[-1], z.peers)
    late = whole_blocks(late_rows(z.width)[-1], z.peers)
    shared = 2 * (z.experts + 8)
    small = -(-2 * (z.width // LANES) // 8) * 8
    stage, inbox, send, recv = reduce_scratch(z.lanes, z.rows, z.width)
    found = dict(
        gproj=pltpu.VMEM((PROJ, z.total), BF16), gpre=pltpu.VMEM((z.total + HEAD, z.channels), F32),
        gxi=pltpu.VMEM((z.total, z.channels), BF16), gconv=pltpu.VMEM((16, z.channels), F32), c_own=pltpu.VMEM((z.rows, z.width), F32),
        win=pltpu.VMEM(win.shape[1:], BF16), z_buf=pltpu.VMEM((shared, z.channels), BF16),
        z_in=pltpu.VMEM((z.lanes - 1, shared, z.channels), BF16), z_send=dma(z.lanes - 1), z_recv=dma(z.lanes - 1),
        c_stage=stage, c_inbox=inbox, c_send=send, c_recv=recv,
        **{"e%d" % i: v for i, v in enumerate(plane_scratch(z.peers, early, z.channels))},
        **{"l%d" % i: v for i, v in enumerate(plane_scratch(z.peers, late, z.channels))},
        **sum_scratch(z),
    )
    if last:
        found.update(
            n_buf=pltpu.VMEM((small, LANES), F32), n_in=pltpu.VMEM((z.peers - 1, small, LANES), F32), n_send=dma(z.peers - 1),
            n_recv=dma(z.peers - 1), n_buf2=pltpu.VMEM((small, LANES), F32), n_in2=pltpu.VMEM((z.lanes - 1, small, LANES), F32),
            n_send2=dma(z.lanes - 1), n_recv2=dma(z.lanes - 1))
    return found


def in_back_outputs(z, last):
    early = whole_blocks(early_rows(z.width, z.experts)[-1], z.peers)
    late = whole_blocks(late_rows(z.width)[-1], z.peers)
    return dict(early=bf16(early, z.channels), late=bf16(late, z.channels), share=f32(2 * (z.experts + 8), z.channels),
                gnorm=f32(2 if last else 1, z.width))


def plane_sum(z, r, which, result):
    d, m = lax.axis_index("dp"), lax.axis_index("mp")
    parts = [getattr(r, which + str(i)) for i in range(10)]
    return PlaneSum(d, m, z.peers, *parts[:4], result, *parts[4:])


def in_back_stage(z, r, l, weights, emit):
    d, m = lax.axis_index("dp"), lax.axis_index("mp")
    line = [(d, lax.rem(m + k, z.lanes)) for k in range(1, z.lanes)]
    early, late = plane_sum(z, r, "e", r.early), plane_sum(z, r, "l", r.late)
    emine, lmine = early.mine, late.mine
    ch = z.channels
    at, till = early_rows(z.width, z.experts), late_rows(z.width)

    def early_work():
        r.need(r.b_whole, r.gzg, r.b_gwout, r.b_gshare)
        whole = r.b_whole[...].reshape(z.total, z.width)
        emine[at[0] : at[1], :] = dot_tn(whole, r.gzg[...]).astype(BF16)
        for i in range(z.width // ch):
            emine[at[1] + i * ch : at[1] + (i + 1) * ch, :] = r.b_gwout[:, i * ch : (i + 1) * ch]
            emine[at[5 + i] : at[6 + i], :] = r.b_gshare[:, i * ch : (i + 1) * ch].astype(BF16)
        emine[at[2] : at[3], :] = r.gdtw[...].astype(BF16)
        emine[at[3] : at[4], :] = r.galog[...].astype(BF16)
        emine[at[4] : at[5], :] = jnp.concatenate([r.gdtb[...], r.gskip[...], jnp.zeros((14, ch), F32)], axis=0).astype(BF16)
        if at[7] < emine.shape[0]:
            emine[at[7] :, :] = jnp.zeros((emine.shape[0] - at[7], ch), BF16)
        early.begin()

    r.need(r.gpart)
    finish_sum = line_sum(r.gpart, r.sum_stage, r.sum_inbox, r.sum_send, r.sum_recv, r.gproj, d, m, z.lanes, early_work)
    taps, bias = r.conv_w[l], r.conv_b[l : l + 1, :]
    r.gconv[...] = jnp.zeros_like(r.gconv)
    r.gpre[z.total :, :] = jnp.zeros((HEAD, ch), F32)

    def first(c, carry):
        base = pl.multiple_of(c * CONV_ROWS, CONV_ROWS)
        pre, shifted = conv_window(r.b_conv, r.since, taps, bias, base)
        sig = sigmoid(pre)
        grad = r.gxs[pl.ds(base, CONV_ROWS), :] + dot_tn(r.gproj[:, pl.ds(base, CONV_ROWS)], r.x_proj[l])
        grad = grad * (sig * (1.0 + pre * (1.0 - sig)))
        r.gpre[pl.ds(base, CONV_ROWS), :] = grad
        for j in range(CONV):
            r.gconv[CONV - 1 - j : CONV - j, :] += jnp.sum(grad * shifted[j], axis=0, keepdims=True)
        r.gconv[CONV : CONV + 1, :] += jnp.sum(grad, axis=0, keepdims=True)
        return carry

    r.need(r.b_conv, r.gxs)
    lax.fori_loop(0, z.total // CONV_ROWS, first, 0)

    def second(c, carry):
        base = pl.multiple_of(c * CONV_ROWS, CONV_ROWS)
        window = r.gpre[pl.ds(base, CONV_ROWS + HEAD), :]
        since = r.since[pl.ds(base, CONV_ROWS + HEAD), :]
        grad = taps[CONV - 1 : CONV, :] * window[:CONV_ROWS]
        for j in range(1, CONV):
            grad = grad + taps[CONV - 1 - j : CONV - j, :] * (window * (since >= j).astype(F32))[j : j + CONV_ROWS]
        r.gxi[pl.ds(base, CONV_ROWS), :] = grad.astype(BF16)
        return carry

    lax.fori_loop(0, z.total // CONV_ROWS, second, 0)
    weights.wait()
    reduce = LineReduce(r.c_stage, r.c_inbox, r.c_send, r.c_recv, d, m, z.lanes)

    def term(s):
        part = pl.ds(pl.multiple_of(s * z.rows, 16), z.rows)
        return dot_nt(r.gxi[part, :], r.win[0]) + dot_nt(r.gzg[part, :], r.win[1])

    def push_middle(s):
        @pl.when(reduce.middle)
        def _():
            for p in range(PIECES):
                reduce.push_on(s, p, term(s)[p * reduce.rows : (p + 1) * reduce.rows])

    one, two, three = reduce.order

    @pl.when(reduce.at_end)
    def _():
        for s in reduce.order:
            reduce.push_first(s, term(s))

    early.second()
    r.need(r.b_xs)
    whole = r.b_whole[...].reshape(z.total, z.width)
    lmine[till[0] : till[1], :] = dot_tn(whole, r.gxi[...]).astype(BF16)
    lmine[till[1] : till[2], :] = dot(r.gproj[...], r.b_xs[...].astype(BF16)).astype(BF16)
    lmine[till[2] : till[3], :] = r.gconv[...].astype(BF16)
    if till[3] < lmine.shape[0]:
        lmine[till[3] :, :] = jnp.zeros((lmine.shape[0] - till[3], ch), BF16)
    late.begin()
    push_middle(one)
    late.second()
    r.c_own[...] = term(m)
    early.third()
    push_middle(two)
    late.third()
    early.fourth()
    push_middle(three)
    late.fourth()
    early.end()
    r.ship(r.early)
    r.z_buf[...] = r.early[at[5] : at[7], :]
    shared = exchange(line, r.z_buf, r.z_in, r.z_send, r.z_recv)
    reduce.total(r.c_own)
    r.need(r.b_act, r.b_gmid)
    act = r.b_act[...].astype(F32)
    pulled, grad_gain = norm_back(act, rms_inverse(act), r.norm_in[l : l + 1, :], r.c_own[...])
    emit(r.b_gmid[...] + pulled)

    def finish():
        late.end()
        r.ship(r.late)
        if l == 0:
            both = jnp.concatenate([grad_gain, r.prior[...]], axis=0)
            groups = z.width // LANES
            for g in range(groups):
                r.n_buf[2 * g : 2 * g + 2, :] = both[:, g * LANES : (g + 1) * LANES]
            if 2 * groups < r.n_buf.shape[0]:
                r.n_buf[2 * groups :, :] = jnp.zeros((r.n_buf.shape[0] - 2 * groups, LANES), F32)
            plane = [(lax.rem(d + k, z.peers), m) for k in range(1, z.peers)]
            r.n_buf2[...] = exchange(plane, r.n_buf, r.n_in, r.n_send, r.n_recv)()
            summed = exchange(line, r.n_buf2, r.n_in2, r.n_send2, r.n_recv2)()
            r.gnorm[...] = jnp.concatenate([summed[2 * g : 2 * g + 2, :] for g in range(groups)], axis=1)
        else:
            r.gnorm[...] = grad_gain
        r.share[...] = shared()
        finish_sum()
        reduce.finish()
        early.finish()
        late.finish()

    return finish


def last_block(z, back, prior, small, w_in):
    def body(r):
        d, m = lax.axis_index("dp"), lax.axis_index("mp")
        (win,) = fetch([(r.w_in.at[0], r.win)], r.fetched)
        greet(d, m, z.lanes, z.peers, True)

        def emit(value):
            r.up[...] = value

        in_back_stage(z, r, 0, win, emit)()

    return launch("mamba_in_backward", 9, body, dict(**back, prior=prior, **convolution(small)), dict(w_in=w_in),
                  dict(up=f32(z.rows, z.width), **in_back_outputs(z, True)), dict(fetched=dma(1), **in_back_scratch(z, w_in, True)))


def experts_back(z, r, l, fetched, finish):
    d, m = lax.axis_index("dp"), lax.axis_index("mp")
    for weight in fetched:
        weight.wait()
    r.need(r.into, r.hidden)
    moe = Experts(d, m, z.lanes, z.peers, r.into, *expert_refs(r))

    def expert(s, rows):
        grad_hidden = (dot_nt(rows[0], r.wdown[...]) * gelu_slope(r.hidden[s].astype(F32))).astype(BF16)
        r.ghid[s] = grad_hidden
        return [dot_nt(grad_hidden, r.wup[...])]

    def meanwhile():
        r.need(r.active, r.slots)
        r.gdown[...] = dot_tn(flat(r.active), r.e_slots[...].reshape(z.lanes * z.slots, z.width))
        r.gup[...] = dot_tn(flat(r.slots), flat(r.ghid))
        r.ship(r.gdown, r.gup)
        finish()

    moe.run(expert, r.e_own, meanwhile)
    r.need(r.picked, r.middle)
    route_back(z, r, l, r.upstream[...], r.middle[...], r.chance[...], r.choose[...], r.picked[...], r.e_own[0])
    moe.finish()


def down_blocks(z, l, back, kept, small, weights):
    def upper(r):
        d, m = lax.axis_index("dp"), lax.axis_index("mp")
        (win,) = fetch([(r.w_in.at[l], r.win)], r.fetched)
        greet(d, m, z.lanes, z.peers, True)

        def emit(value):
            r.up[...] = value

        in_back_stage(z, r, l, win, emit)()

    def lower(r):
        d, m = lax.axis_index("dp"), lax.axis_index("mp")
        fetched = fetch([(r.w_down.at[l - 1, 0], r.wdown), (r.w_up.at[l - 1, 0], r.wup), (r.w_out.at[l - 1], r.wout)], r.fetched)
        greet(d, m, z.lanes, z.peers, True)
        r.need(r.upstream)
        r.e_rows[m, 0] = (gate_of(r.chance[...], r.choose[...]) * r.upstream[...]).astype(BF16)
        experts_back(z, r, l - 1, fetched, lambda: None)

    w_in, w_out, w_up, w_down = weights
    slots = (z.lanes, z.slots)
    one = launch("mamba_in_backward", 20 + l, upper, dict(**back, **convolution(small)),
                 dict(w_in=w_in), dict(up=f32(z.rows, z.width), **in_back_outputs(z, False)),
                 dict(fetched=dma(1), **in_back_scratch(z, w_in, False)))
    two = launch("experts_backward", 30 + l, lower, dict(**kept, upstream=one.up, **routing(small)),
                 dict(w_out=w_out, w_up=w_up, w_down=w_down), back_outputs(z),
                 dict(fetched=dma(3), ghid=pltpu.VMEM((*slots, z.hidden), BF16), **weight_scratch(w_out, w_up, w_down),
                      **expert_names(z, 1), **back_scratch(z)))
    return types.SimpleNamespace(**vars(one), **vars(two))


def down_block(z, l, back, kept, small, weights):
    def body(r):
        d, m = lax.axis_index("dp"), lax.axis_index("mp")
        win, wdown, wup, wout = fetch([(r.w_in.at[l], r.win), (r.w_down.at[l - 1, 0], r.wdown), (r.w_up.at[l - 1, 0], r.wup),
                                       (r.w_out.at[l - 1], r.wout)], r.fetched)
        greet(d, m, z.lanes, z.peers, True)

        def emit(value):
            r.upstream[...] = value
            r.e_rows[m, 0] = (gate_of(r.chance[...], r.choose[...]) * value).astype(BF16)

        experts_back(z, r, l - 1, (wdown, wup, wout), in_back_stage(z, r, l, win, emit))

    w_in, w_out, w_up, w_down = weights
    slots = (z.lanes, z.slots)
    return launch(
        "down", 9 + l, body, dict(**back, **kept, **convolution(small), **routing(small)),
        dict(w_in=w_in, w_out=w_out, w_up=w_up, w_down=w_down), dict(**in_back_outputs(z, False), **back_outputs(z)),
        dict(fetched=dma(4), upstream=pltpu.VMEM((z.rows, z.width), F32),
             ghid=pltpu.VMEM((*slots, z.hidden), BF16), **weight_scratch(w_out, w_up, w_down), **in_back_scratch(z, w_in, False),
             **expert_names(z, 1), **back_scratch(z)))


def final_block(z, result, up, gnorm, layers):
    count, ch = len(layers), z.channels
    at, till = early_rows(z.width, z.experts), late_rows(z.width)
    far = dict(result=(z.rows, z.width), tokens=(z.rows, z.width), w_in=(count, 2, z.width, ch), w_out=(count, ch, z.width),
               w_up=(count, 1, z.width, z.hidden), w_down=(count, 1, z.hidden, z.width))
    near = dict(norm_in=(count, z.width), conv_w=(count, CONV, ch), conv_b=(count, ch), x_proj=(count, PROJ, ch), dt_proj=(count, DT_RANK, ch),
                dt_bias=(count, ch), a_log=(count, STATE, ch), skip=(count, ch), norm_moe=(count, z.width), router=(count, z.experts, z.width))
    shapes = {**far, **near}
    sums = [v for layer in layers for v in layer[:2]]
    whole = [result, up, *(v for layer in layers for v in layer[3:])]

    def kernel(*refs):
        small, refs = refs[: 1 + count], refs[1 + count :]
        there, refs = refs[: len(sums) + len(whole)], refs[len(sums) + len(whole) :]
        outs, refs = refs[: len(shapes)], refs[len(shapes) :]
        held, (w_in, w_out, came, went) = refs[: len(there)], refs[len(there) :]
        out = types.SimpleNamespace(**dict(zip(shapes, outs)))
        coming = fetch(list(zip(there, held)), came)
        places = [out.result, out.tokens] + [v.at[l, 0] for l in range(count) for v in (out.w_up, out.w_down)]
        out.norm_in[...] = small[0][...]
        going = []
        for l in range(count):
            early, late, share = held[2 * l], held[2 * l + 1], small[1 + l]
            coming[2 * l].wait()
            coming[2 * l + 1].wait()
            one = slice(l, l + 1)
            w_in[l, 0] = late[till[0] : till[1], :].astype(F32)
            w_in[l, 1] = early[at[0] : at[1], :].astype(F32)
            for i in range(z.width // ch):
                cols = slice(i * ch, (i + 1) * ch)
                w_out[l, :, cols] = early[at[1] + i * ch : at[1] + (i + 1) * ch, :].astype(F32)
                rows = share[i * (z.experts + 8) : (i + 1) * (z.experts + 8), :]
                out.router[l, :, cols] = rows[: z.experts]
                out.norm_moe[one, cols] = rows[z.experts : z.experts + 1]
            for src, dst in ((w_in, out.w_in), (w_out, out.w_out)):
                going.append(pltpu.make_async_copy(src.at[l], dst.at[l], went.at[len(going)]))
                going[-1].start()
            conv = late[till[2] : till[3], :].astype(F32)
            out.conv_w[l] = conv[:CONV]
            out.conv_b[one, :] = conv[CONV : CONV + 1]
            out.x_proj[l] = late[till[1] : till[2], :].astype(F32)
            out.dt_proj[l] = early[at[2] : at[3], :].astype(F32)
            out.a_log[l] = early[at[3] : at[4], :].astype(F32)
            both = early[at[4] : at[5], :].astype(F32)
            out.dt_bias[one, :] = both[:1]
            out.skip[one, :] = both[1:2]
        for i, place in enumerate(places):
            coming[len(sums) + i].wait()
            going.append(pltpu.make_async_copy(held[len(sums) + i], place, went.at[len(going)]))
            going[-1].start()
        for copy in going:
            copy.wait()

    outputs = pl.pallas_call(
        kernel,
        out_shape=[f32(*shape) for shape in shapes.values()],
        in_specs=vmem(1 + count) + hbm(len(sums) + len(whole)),
        out_specs=hbm(len(far)) + vmem(len(near)),
        scratch_shapes=[pltpu.VMEM(v.shape, v.dtype) for v in (*sums, *whole)]
        + [pltpu.VMEM(far["w_in"], F32), pltpu.VMEM(far["w_out"], F32), dma(len(sums) + len(whole)), dma(2 * count + len(whole))],
        compiler_params=pltpu.CompilerParams(vmem_limit_bytes=60 << 20),
        name="outputs",
    )(gnorm, *(layer[2] for layer in layers), *sums, *whole)
    o = types.SimpleNamespace(**dict(zip(shapes, outputs)))
    return (o.result, o.tokens, o.norm_in, o.w_in, o.conv_w, o.conv_b, jnp.swapaxes(o.x_proj, 1, 2), o.dt_proj, o.dt_bias, o.a_log, o.skip, o.w_out, o.norm_moe,
            jnp.swapaxes(o.router, 1, 2), o.w_up, o.w_down)


def on_device(
    tokens, cotangent, lengths, routes, slot_place, norm_in, w_in, conv_w, conv_b, x_proj, dt_proj, dt_bias,
    a_log, d_skip, w_out, norm_moe, router, w_up, w_down,
):
    layers = norm_in.shape[0]
    assert layers == 2
    rows_here, width = tokens.shape
    lanes, peers = lax.axis_size("mp"), lax.axis_size("dp")
    experts, channels = router.shape[2], w_in.shape[3]
    capacity = max(2, (5 * rows_here + 4 * experts - 1) // (4 * experts))
    padded = (capacity + 15) // 16 * 16
    z = Sizes(lanes, peers, experts, padded, rows_here, width, channels, w_up.shape[3])
    position = lax.broadcasted_iota(jnp.int32, (z.total + HEAD, 1), 0)
    since, first = position, 0
    for i in range(lengths.shape[1] - 1):
        first = first + lengths[0, i]
        since = jnp.where(position >= first, position - first, since)
    since = jnp.where(position < z.total, since, 0)
    place = jnp.pad(routes * padded + slot_place, (0, -rows_here % LANES))
    small = types.SimpleNamespace(
        norm_in=norm_in, norm_moe=norm_moe, conv_w=conv_w, conv_b=conv_b, since=since, x_proj=jnp.swapaxes(x_proj, 1, 2),
        router=jnp.swapaxes(router, 1, 2),
        place=jnp.broadcast_to(place[None, :], (8, place.shape[0])),
    )
    weights = (w_in, w_out, w_up, w_down)
    scan_weights = (dt_proj, dt_bias, a_log, d_skip, spread_matrix())

    act, entry = tokens, first_block(z, 0, tokens, small, w_in)
    kept = []
    for l in range(layers):
        gated, ys, marks = scan_fwd(l, entry.xs, entry.zgate, entry.proj, since, *scan_weights)
        gated = gated.reshape(lanes, rows_here, channels)
        if l + 1 < layers:
            out = middle_block(z, l, act, gated, small, weights)
            kept.append((act, entry, gated, ys, marks, out))
            act, entry = out.following, out
        else:
            turn = turn_block(z, l, act, gated, cotangent, small, weights)
            kept.append((act, entry, gated, ys, marks, turn))
    result, above = turn.following, turn
    collected = []
    for l in reversed(range(layers)):
        act, entry, gated, ys, marks, _ = kept[l]
        gxs, gzg, gpart, gdtw, gdtb, galog, gskip = scan_bwd(
            l, entry.xs, entry.zgate, entry.proj, since, ys, above.ggated.reshape(z.total, channels), marks, *scan_weights)
        back = dict(gpart=gpart, gxs=gxs, gzg=gzg, b_conv=entry.conv, b_xs=entry.xs, b_whole=entry.whole, b_act=act, b_gmid=above.gmid,
                    b_gwout=above.gwout, b_gshare=above.gshare, gdtw=gdtw, gdtb=gdtb, galog=galog, gskip=gskip)
        grads = (above.gup, above.gdown)
        if l > 0:
            _, _, below_gated, _, _, below = kept[l - 1]
            forward = dict(gated=below_gated, chance=below.chance, choose=below.choose, into=below.into, slots=below.slots, hidden=below.hidden,
                           active=below.active, picked=below.picked, middle=below.middle)
            above = (down_block if z.slots <= 256 else down_blocks)(z, l, back, forward, small, weights)
            prior = above.gnorm
            collected.append((above.early, above.late, above.share, *grads))
        else:
            end = last_block(z, back, prior, small, w_in)
            collected.append((end.early, end.late, end.share, *grads))
    collected = collected[::-1]
    at, till = early_rows(width, experts), late_rows(width)

    return final_block(z, result, end.up, end.gnorm, collected)


def solution(mesh):
    return jax.shard_map(
        on_device,
        mesh=mesh,
        in_specs=(
            P(("dp", "mp"), None),
            P(("dp", "mp"), None),
            P("dp", None),
            P(("dp", "mp")),
            P(("dp", "mp")),
            P(),
            P(None, None, None, "mp"),
            P(None, None, "mp"),
            P(None, "mp"),
            P(None, "mp", None),
            P(None, None, "mp"),
            P(None, "mp"),
            P(None, None, "mp"),
            P(None, "mp"),
            P(None, "mp", None),
            P(),
            P(),
            P(None, "dp", None, "mp"),
            P(None, "dp", "mp", None),
        ),
        out_specs=(
            P(("dp", "mp"), None),
            P(("dp", "mp"), None),
            P(),
            P(None, None, None, "mp"),
            P(None, None, "mp"),
            P(None, "mp"),
            P(None, "mp", None),
            P(None, None, "mp"),
            P(None, "mp"),
            P(None, None, "mp"),
            P(None, "mp"),
            P(None, "mp", None),
            P(),
            P(),
            P(None, "dp", None, "mp"),
            P(None, "dp", "mp", None),
        ),
        check_vma=False,
    )
```

```python
import functools
import types

import jax
import jax.numpy as jnp
from jax import lax
from jax.experimental import pallas as pl
from jax.experimental.pallas import tpu as pltpu
from jax.sharding import PartitionSpec as P

STATE = 16
DT_RANK = 48
LANES = 128
CHUNK = 128
LOG2E = 1.4426950408889634
RESET = 1.0e6
PROJ = DT_RANK + 2 * STATE
CONV = 4
dt_most = 0.05
epsilon = 1e-05
highest = lax.Precision.HIGHEST
MESH = pl.DeviceIdType.MESH
F32, BF16 = jnp.float32, jnp.bfloat16


def sigmoid(v):
    return 1.0 / (1.0 + jnp.exp(-v))


def dot(a, b):
    return jnp.dot(a, b, preferred_element_type=F32)


def dot_nt(a, b):
    return lax.dot_general(a, b, (((1,), (1,)), ((), ())), preferred_element_type=F32)


def dot_tn(a, b):
    return lax.dot_general(a, b, (((0,), (0,)), ((), ())), preferred_element_type=F32)


def spread_matrix():
    rows = lax.broadcasted_iota(jnp.int32, (STATE, STATE * LANES), 0)
    cols = lax.broadcasted_iota(jnp.int32, (STATE, STATE * LANES), 1)
    return (rows == cols // LANES).astype(BF16)


def put(ref, value):
    for j in range(ref.shape[0]):
        ref[j] = value[:, j * LANES : (j + 1) * LANES]


def spread_rows(proj, spread, out_ref):
    wide = dot_tn(proj, spread)
    for n in range(STATE):
        out_ref[pl.ds(n, CHUNK, stride=STATE), :] = wide[:, n * LANES : (n + 1) * LANES]


def scan_fwd_kernel(l, xs_ref, zg_ref, proj_ref, since_ref, dtw_ref, dtb_ref, alog_ref, skip_ref, spread_ref,
                    gated_ref, ys_ref, hck_ref,
                    h_ref, dm_ref, dx_ref, bx_ref, cx_ref, yq_ref):
    groups = xs_ref.shape[1] // LANES

    @pl.when(pl.program_id(0) == 0)
    def _():
        h_ref[...] = jnp.zeros_like(h_ref)

    hck_ref[0] = h_ref[...]
    proj = proj_ref[...]
    xs = xs_ref[...]
    delta = dt_most * sigmoid(dot_tn(proj[:DT_RANK], dtw_ref[l]) + dtb_ref[l : l + 1, :])
    put(dm_ref, delta + RESET * (since_ref[...] == 0).astype(F32))
    put(dx_ref, delta * xs)
    spread_rows(proj[DT_RANK : DT_RANK + STATE], spread_ref[...], bx_ref)
    spread_rows(proj[DT_RANK + STATE :], spread_ref[...], cx_ref)
    rate = -LOG2E * jnp.exp(alog_ref[l])
    rates = [rate[:, j * LANES : (j + 1) * LANES] for j in range(groups)]

    def step(g, hs):
        hs = list(hs)
        t0 = pl.multiple_of(g * 32, 32)
        for i in range(32):
            t = t0 + i
            r0 = pl.multiple_of(t * STATE, STATE)
            b = bx_ref[pl.ds(r0, STATE), :]
            c = cx_ref[pl.ds(r0, STATE), :]
            q0 = pl.multiple_of(t * 8, 8)
            for j in range(groups):
                lanes = slice(j * LANES, (j + 1) * LANES)
                dec = jnp.exp2(dm_ref[j, pl.ds(t, 1), :] * rates[j])
                hs[j] = dec * hs[j] + dx_ref[j, pl.ds(t, 1), :] * b
                q = c * hs[j]
                yq_ref[j, pl.ds(q0, 8), :] = q[:8] + q[8:]
        return tuple(hs)

    hs = lax.fori_loop(0, CHUNK // 32, step, tuple(h_ref[:, j * LANES : (j + 1) * LANES] for j in range(groups)))
    for j in range(groups):
        h_ref[:, j * LANES : (j + 1) * LANES] = hs[j]
    zg = zg_ref[...]
    for j in range(groups):
        lanes = slice(j * LANES, (j + 1) * LANES)
        y = skip_ref[l : l + 1, lanes] * xs[:, lanes]
        for k in range(8):
            y = y + yq_ref[j, pl.ds(k, CHUNK, stride=8), :]
        ys_ref[:, lanes] = y
        z = zg[:, lanes]
        gated_ref[:, lanes] = (y * z * sigmoid(z)).astype(BF16)


def scan_fwd(l, xs, zg, proj, since, dtw, dtb, alog, skip, spread):
    rows, ch = xs.shape
    steps = rows // CHUNK
    row = lambda w: pl.BlockSpec((CHUNK, w), lambda i: (i, 0))
    full = lambda s: pl.BlockSpec(s, lambda i: (0,) * len(s))
    return pl.pallas_call(
        functools.partial(scan_fwd_kernel, l),
        grid=(steps,),
        out_shape=[
            jax.ShapeDtypeStruct((rows, ch), BF16),
            jax.ShapeDtypeStruct((rows, ch), F32),
            jax.ShapeDtypeStruct((steps, STATE, ch), F32),
        ],
        in_specs=[row(ch), row(ch), pl.BlockSpec((PROJ, CHUNK), lambda i: (0, i)), row(1)]
        + [full(v.shape) for v in (dtw, dtb, alog, skip, spread)],
        out_specs=[row(ch), row(ch), pl.BlockSpec((1, STATE, ch), lambda i: (i, 0, 0))],
        scratch_shapes=[
            pltpu.VMEM((STATE, ch), F32),
            pltpu.VMEM((ch // LANES, CHUNK, LANES), F32),
            pltpu.VMEM((ch // LANES, CHUNK, LANES), F32),
            pltpu.VMEM((CHUNK * STATE, LANES), F32),
            pltpu.VMEM((CHUNK * STATE, LANES), F32),
            pltpu.VMEM((ch // LANES, CHUNK * 8, LANES), F32),
        ],
        compiler_params=pltpu.CompilerParams(vmem_limit_bytes=60 << 20),
        name="scan_fwd",
    )(xs, zg, proj, since, dtw, dtb, alog, skip, spread)


def scan_bwd_kernel(l, xs_ref, zg_ref, proj_ref, since_ref, ys_ref, gg_ref, hck_ref, dtw_ref, dtb_ref, alog_ref, skip_ref, spread_ref,
                    gxs_ref, gzg_ref, gproj_ref, gdtw_ref, gdtb_ref, galog_ref, gskip_ref,
                    a_ref, dm_ref, dx_ref, dl_ref, gy_ref, bx_ref, cx_ref, h_ref, dec_ref, pq_ref, gq_ref, gb_ref, gc_ref):
    groups = xs_ref.shape[1] // LANES
    cols = [slice(j * LANES, (j + 1) * LANES) for j in range(groups)]

    @pl.when(pl.program_id(0) == 0)
    def _():
        a_ref[...] = jnp.zeros_like(a_ref)
        gdtw_ref[...] = jnp.zeros_like(gdtw_ref)
        gdtb_ref[...] = jnp.zeros_like(gdtb_ref)
        galog_ref[...] = jnp.zeros_like(galog_ref)
        gskip_ref[...] = jnp.zeros_like(gskip_ref)

    proj = proj_ref[...]
    xs = xs_ref[...]
    delta = dt_most * sigmoid(dot_tn(proj[:DT_RANK], dtw_ref[l]) + dtb_ref[l : l + 1, :])
    put(dl_ref, delta)
    put(dm_ref, delta + RESET * (since_ref[...] == 0).astype(F32))
    put(dx_ref, delta * xs)
    zg = zg_ref[...]
    sz = sigmoid(zg)
    gg = gg_ref[...]
    gy = gg * (zg * sz)
    put(gy_ref, gy)
    gzg_ref[...] = (gg * ys_ref[...] * (sz * (1.0 + zg * (1.0 - sz)))).astype(BF16)
    gskip_ref[...] += jnp.sum(gy * xs, axis=0, keepdims=True)
    spread_rows(proj[DT_RANK : DT_RANK + STATE], spread_ref[...], bx_ref)
    spread_rows(proj[DT_RANK + STATE :], spread_ref[...], cx_ref)
    rate = -jnp.exp(alog_ref[l])
    rates2 = [LOG2E * rate[:, c] for c in cols]
    rates = [rate[:, c] for c in cols]

    for j in range(groups):
        h_ref[j, :STATE, :] = hck_ref[0][:, cols[j]]

    def again(g, hs):
        hs = list(hs)
        t0 = pl.multiple_of(g * 32, 32)
        for i in range(32):
            t = t0 + i
            r0 = pl.multiple_of(t * STATE, STATE)
            r1 = pl.multiple_of(t * STATE + STATE, STATE)
            b = bx_ref[pl.ds(r0, STATE), :]
            for j in range(groups):
                dec = jnp.exp2(dm_ref[j, pl.ds(t, 1), :] * rates2[j])
                hs[j] = dec * hs[j] + dx_ref[j, pl.ds(t, 1), :] * b
                dec_ref[j, pl.ds(r0, STATE), :] = dec
                h_ref[j, pl.ds(r1, STATE), :] = hs[j]
        return tuple(hs)

    last = lax.fori_loop(0, CHUNK // 32, again, tuple(hck_ref[0][:, c] for c in cols))

    def back(g, carry):
        carry = [list(c) for c in carry]
        aa, hs, acc = carry
        t0 = pl.multiple_of(CHUNK - 32 - g * 32, 32)
        for i in reversed(range(32)):
            t = t0 + i
            r0 = pl.multiple_of(t * STATE, STATE)
            q0 = pl.multiple_of(t * 8, 8)
            b = bx_ref[pl.ds(r0, STATE), :]
            c = cx_ref[pl.ds(r0, STATE), :]
            gb, gc = None, None
            for j in range(groups):
                gyj = gy_ref[j, pl.ds(t, 1), :]
                a = c * gyj + aa[j]
                dec = dec_ref[j, pl.ds(r0, STATE), :]
                before = h_ref[j, pl.ds(r0, STATE), :]
                carry_a = dec * a
                p = carry_a * before * rates[j]
                ab = a * b
                pq_ref[j, pl.ds(q0, 8), :] = p[:8] + p[8:]
                gq_ref[j, pl.ds(q0, 8), :] = ab[:8] + ab[8:]
                acc[j] = acc[j] + p * dl_ref[j, pl.ds(t, 1), :]
                gbj = a * dx_ref[j, pl.ds(t, 1), :]
                gcj = gyj * hs[j]
                gb = gbj if gb is None else gb + gbj
                gc = gcj if gc is None else gc + gcj
                aa[j] = carry_a
                hs[j] = before
            gb_ref[pl.ds(r0, STATE), :] = gb
            gc_ref[pl.ds(r0, STATE), :] = gc
        return tuple(tuple(c) for c in carry)

    aa, _, acc = lax.fori_loop(
        0, CHUNK // 32, back,
        (tuple(a_ref[:, c] for c in cols), last, tuple(jnp.zeros((STATE, LANES), F32) for _ in cols)))
    for j in range(groups):
        a_ref[:, cols[j]] = aa[j]
        galog_ref[:, cols[j]] += acc[j]

    skip = skip_ref[l : l + 1, :]
    gdts = []
    for j in range(groups):
        psum = pq_ref[j, pl.ds(0, CHUNK, stride=8), :]
        gsum = gq_ref[j, pl.ds(0, CHUNK, stride=8), :]
        for k in range(1, 8):
            psum = psum + pq_ref[j, pl.ds(k, CHUNK, stride=8), :]
            gsum = gsum + gq_ref[j, pl.ds(k, CHUNK, stride=8), :]
        dl = delta[:, cols[j]]
        gdelta = psum + xs[:, cols[j]] * gsum
        gxs_ref[:, cols[j]] = dl * gsum + skip[:, cols[j]] * gy[:, cols[j]]
        gdts.append(gdelta * dl * (1.0 - dl * (1.0 / dt_most)))
    gdt = jnp.concatenate(gdts, axis=1)
    gdtb_ref[...] += jnp.sum(gdt, axis=0, keepdims=True)
    gdt_low = gdt.astype(BF16)
    gdtw_ref[...] += dot(proj[:DT_RANK], gdt_low)
    gproj_ref[:DT_RANK, :] = dot_nt(dtw_ref[l], gdt_low)
    wide_b = jnp.concatenate([gb_ref[pl.ds(n, CHUNK, stride=STATE), :].astype(BF16) for n in range(STATE)], axis=1)
    gproj_ref[DT_RANK : DT_RANK + STATE, :] = dot_nt(spread_ref[...], wide_b)
    wide_c = jnp.concatenate([gc_ref[pl.ds(n, CHUNK, stride=STATE), :].astype(BF16) for n in range(STATE)], axis=1)
    gproj_ref[DT_RANK + STATE :, :] = dot_nt(spread_ref[...], wide_c)


def scan_bwd(l, xs, zg, proj, since, ys, gg, hck, dtw, dtb, alog, skip, spread, beside=None):
    work, far, made, room = beside or (None, [], [], [])
    rows, ch = xs.shape
    steps = rows // CHUNK
    row = lambda w: pl.BlockSpec((CHUNK, w), lambda i: (steps - 1 - i, 0))
    full = lambda s: pl.BlockSpec(s, lambda i: (0,) * len(s))
    big = lambda: pltpu.VMEM((CHUNK * STATE, LANES), F32)
    g = ch // LANES

    def kernel(*refs):
        cuts = [12, len(far), 7, len(made), 13, len(room)]
        at = [sum(cuts[:i]) for i in range(7)]
        ins, xin, outs, xout, held, xheld = (refs[at[i] : at[i + 1]] for i in range(6))
        if work is not None:
            work(steps, xin, xout, xheld)
        scan_bwd_kernel(l, *ins, *outs, *held)

    anywhere = pl.BlockSpec(memory_space=pl.ANY)
    return pl.pallas_call(
        kernel,
        grid=(steps,),
        out_shape=[
            jax.ShapeDtypeStruct((rows, ch), F32),
            jax.ShapeDtypeStruct((rows, ch), BF16),
            jax.ShapeDtypeStruct((PROJ, rows), F32),
            jax.ShapeDtypeStruct((DT_RANK, ch), F32),
            jax.ShapeDtypeStruct((1, ch), F32),
            jax.ShapeDtypeStruct((STATE, ch), F32),
            jax.ShapeDtypeStruct((1, ch), F32),
            *made,
        ],
        in_specs=[row(ch), row(ch), pl.BlockSpec((PROJ, CHUNK), lambda i: (0, steps - 1 - i)), row(1), row(ch), row(ch),
                  pl.BlockSpec((1, STATE, ch), lambda i: (steps - 1 - i, 0, 0))]
        + [full(v.shape) for v in (dtw, dtb, alog, skip, spread)]
        + [anywhere] * len(far),
        out_specs=[row(ch), row(ch), pl.BlockSpec((PROJ, CHUNK), lambda i: (0, steps - 1 - i)), full((DT_RANK, ch)), full((1, ch)), full((STATE, ch)), full((1, ch))]
        + [anywhere] * len(made),
        scratch_shapes=[
            pltpu.VMEM((STATE, ch), F32),
            pltpu.VMEM((ch // LANES, CHUNK, LANES), F32),
            pltpu.VMEM((ch // LANES, CHUNK, LANES), F32),
            pltpu.VMEM((ch // LANES, CHUNK, LANES), F32),
            pltpu.VMEM((ch // LANES, CHUNK, LANES), F32),
            big(), big(),
            pltpu.VMEM((g, CHUNK * STATE + STATE, LANES), F32),
            pltpu.VMEM((g, CHUNK * STATE, LANES), F32),
            pltpu.VMEM((g, CHUNK * 8, LANES), F32),
            pltpu.VMEM((g, CHUNK * 8, LANES), F32),
            big(), big(),
            *room,
        ],
        compiler_params=pltpu.CompilerParams(vmem_limit_bytes=60 << 20),
        name="scan_bwd",
    )(xs, zg, proj, since, ys, gg, hck, dtw, dtb, alog, skip, spread, *far)


def rms_inverse(values):
    return lax.rsqrt(jnp.mean(values * values, axis=-1, keepdims=True) + epsilon)


def norm_back(values, inverse, gain, grad):
    scaled = grad * gain
    pulled = inverse * scaled - values * (inverse * inverse * inverse) * jnp.mean(scaled * values, axis=-1, keepdims=True)
    return pulled, jnp.sum(grad * values * inverse, axis=0, keepdims=True)


GELU_A, GELU_B = 0.7978845608028654, 0.044715


def gelu(v):
    return 0.5 * v * (1.0 + jnp.tanh(GELU_A * (v + GELU_B * v * v * v)))


def gelu_slope(v):
    square = v * v
    t = jnp.tanh(GELU_A * v * (1.0 + GELU_B * square))
    return 0.5 * (1.0 + t) + 0.5 * v * (1.0 - t * t) * GELU_A * (1.0 + 3.0 * GELU_B * square)


def by_lane(m, values):
    picked = jnp.int32(values[0])
    for k in range(1, len(values)):
        picked = jnp.where(m == k, jnp.int32(values[k]), picked)
    return picked


def nearest_first(m, lanes):
    orders = [sorted((s for s in range(lanes) if s != k), key=lambda s: (abs(s - k), s)) for k in range(lanes)]
    return [by_lane(m, [order[i] for order in orders]) for i in range(lanes - 1)]


def chain_order(m, lanes):
    def due(k, s):
        return (lanes - 1 - s) + k if s > k else s + (lanes - 1 - k)

    orders = [sorted((s for s in range(lanes) if s != k), key=lambda s: (due(k, s), s)) for k in range(lanes)]
    return [by_lane(m, [order[i] for order in orders]) for i in range(lanes - 1)]


def greet(d, m, lanes, peers, across):
    barrier = pltpu.get_barrier_semaphore()
    if across:
        for k in range(1, lanes):
            pl.semaphore_signal(barrier, inc=1, device_id=(d, lax.rem(m + k, lanes)), device_id_type=MESH)
        for k in range(1, peers):
            pl.semaphore_signal(barrier, inc=1, device_id=(lax.rem(d + k, peers), m), device_id_type=MESH)
        pl.semaphore_wait(barrier, lanes + peers - 2)
    else:

        @pl.when(m > 0)
        def _():
            pl.semaphore_signal(barrier, inc=1, device_id=(d, m - 1), device_id_type=MESH)

        @pl.when(m < lanes - 1)
        def _():
            pl.semaphore_signal(barrier, inc=1, device_id=(d, m + 1), device_id_type=MESH)

        pl.semaphore_wait(barrier, jnp.where(m > 0, 1, 0) + jnp.where(m < lanes - 1, 1, 0))


class LineGather:
    def __init__(self, buf, send, recv, d, m, lanes):
        self.buf, self.send, self.recv, self.d, self.m, self.lanes = buf, send, recv, d, m, lanes
        self.order = nearest_first(m, lanes)

    def copy(self, s, up):
        return pltpu.make_async_remote_copy(
            src_ref=self.buf.at[s], dst_ref=self.buf.at[s], send_sem=self.send.at[0 if up else 1, s],
            recv_sem=self.recv.at[s], device_id=(self.d, self.m + 1 if up else self.m - 1), device_id_type=MESH,
        )

    def start(self):
        @pl.when(self.m < self.lanes - 1)
        def _():
            self.copy(self.m, True).start()

        @pl.when(self.m > 0)
        def _():
            self.copy(self.m, False).start()

    def arrive(self, i):
        s, m = self.order[i], self.m
        self.copy(s, True).wait_recv()

        @pl.when((s < m) & (m < self.lanes - 1))
        def _():
            self.copy(s, True).start()

        @pl.when((s > m) & (m > 0))
        def _():
            self.copy(s, False).start()

        return s

    def finish(self):
        for s in range(self.lanes):

            @pl.when((s <= self.m) & (self.m < self.lanes - 1))
            def _():
                self.copy(s, True).wait_send()

            @pl.when((s >= self.m) & (self.m > 0))
            def _():
                self.copy(s, False).wait_send()


PIECES = 1


class LineReduce:
    def __init__(self, stage, inbox, send, recv, d, m, lanes):
        self.stage, self.inbox, self.send, self.recv = stage, inbox, send, recv
        self.d, self.m, self.lanes = d, m, lanes
        self.rows = stage.shape[1] // PIECES
        self.order = chain_order(m, lanes)
        self.middle = jnp.logical_and(m > 0, m < lanes - 1)
        self.at_end = jnp.logical_not(self.middle)

    def piece(self, p):
        return pl.ds(p * self.rows, self.rows)

    def copy(self, s, p):
        up = s > self.m
        side = jnp.where(up, 0, 1)
        return pltpu.make_async_remote_copy(
            src_ref=self.stage.at[s, self.piece(p)], dst_ref=self.inbox.at[side, s, self.piece(p)], send_sem=self.send.at[s, p],
            recv_sem=self.recv.at[side, s, p], device_id=(self.d, jnp.where(up, self.m + 1, self.m - 1)), device_id_type=MESH,
        )

    def push_first(self, s, term):
        self.stage[s] = term.astype(BF16)
        for p in range(PIECES):
            self.copy(s, p).start()

    def push_on(self, s, p, term):
        side = jnp.where(s > self.m, 0, 1)
        self.copy(s, p).wait_recv()
        self.stage[s, self.piece(p)] = (term + self.inbox[side, s, self.piece(p)].astype(F32)).astype(BF16)
        self.copy(s, p).start()

    def push(self, s, term):
        @pl.when(self.at_end)
        def _():
            self.push_first(s, term)

        @pl.when(self.middle)
        def _():
            for p in range(PIECES):
                self.push_on(s, p, term[p * self.rows : (p + 1) * self.rows])

    def total(self, own_ref):
        m = self.m

        def add(side):
            for p in range(PIECES):
                pltpu.make_async_remote_copy(
                    src_ref=self.stage.at[m, self.piece(p)], dst_ref=self.inbox.at[side, m, self.piece(p)], send_sem=self.send.at[m, p],
                    recv_sem=self.recv.at[side, m, p], device_id=(self.d, m), device_id_type=MESH,
                ).wait_recv()
            own_ref[...] += self.inbox[side, m].astype(F32)

        @pl.when(m > 0)
        def _():
            add(0)

        @pl.when(m < self.lanes - 1)
        def _():
            add(1)

    def finish(self):
        for s in self.order:
            for p in range(PIECES):
                self.copy(s, p).wait_send()


def reduce_scratch(lanes, rows, width):
    return [
        pltpu.VMEM((lanes, rows, width), BF16),
        pltpu.VMEM((2, lanes, rows, width), BF16),
        dma(lanes, PIECES), dma(2, lanes, PIECES),
    ]


PARTS = 3


def line_sum(part, stage, inbox, send, recv, out, d, m, lanes, between=lambda: None):
    width = part.shape[1] // PARTS

    def copy(side, b):
        return pltpu.make_async_remote_copy(
            src_ref=stage.at[side, b], dst_ref=inbox.at[side, b], send_sem=send.at[side, b], recv_sem=recv.at[side, b],
            device_id=(d, m + 1 if side == 0 else m - 1), device_id_type=MESH,
        )

    def step(side, b):
        has_source = m > 0 if side == 0 else m < lanes - 1
        has_target = m < lanes - 1 if side == 0 else m > 0
        cols = slice(b * width, (b + 1) * width)

        @pl.when(has_source)
        def _():
            copy(side, b).wait_recv()

        @pl.when(jnp.logical_not(has_source))
        def _():
            inbox[side, b] = jnp.zeros(inbox.shape[2:], BF16)

        @pl.when(has_target)
        def _():
            stage[side, b] = (part[:, cols] + inbox[side, b].astype(F32)).astype(BF16)
            copy(side, b).start()

    low = 2 * m < lanes

    def both(first):
        def run(side):
            for b in range(PARTS):
                step(side, b)

        @pl.when(low)
        def _():
            run(0 if first else 1)

        @pl.when(jnp.logical_not(low))
        def _():
            run(1 if first else 0)

    both(True)
    between()
    both(False)
    for b in range(PARTS):
        cols = slice(b * width, (b + 1) * width)
        out[:, cols] = (part[:, cols] + inbox[0, b].astype(F32) + inbox[1, b].astype(F32)).astype(BF16)

    def finish():
        for b in range(PARTS):

            @pl.when(m < lanes - 1)
            def _():
                copy(0, b).wait_send()

            @pl.when(m > 0)
            def _():
                copy(1, b).wait_send()

    return finish


def vmem(count):
    return [pl.BlockSpec(memory_space=pltpu.VMEM)] * count


def f32(*shape):
    return jax.ShapeDtypeStruct(shape, F32)


def bf16(*shape):
    return jax.ShapeDtypeStruct(shape, BF16)


def dma(*shape):
    return pltpu.SemaphoreType.DMA(shape)


def hbm(count):
    return [pl.BlockSpec(memory_space=pl.ANY)] * count


def fetch(pairs, sem):
    copies = [pltpu.make_async_copy(src, dst, sem.at[i]) for i, (src, dst) in enumerate(pairs)]
    for copy in copies:
        copy.start()
    return copies


def params(cid, limit=58):
    return pltpu.CompilerParams(collective_id=cid, has_side_effects=True, vmem_limit_bytes=limit << 20)


CONV_ROWS = 128
HEAD = 8


def conv_window(padded_ref, since_ref, taps, bias, base):
    window = padded_ref[pl.ds(base, CONV_ROWS + HEAD), :]
    since = since_ref[pl.ds(base, CONV_ROWS), :]
    shifted = [window[HEAD:]]
    for j in range(1, CONV):
        shifted.append(window[HEAD - j : HEAD - j + CONV_ROWS] * (since >= j).astype(F32))
    pre = bias
    for j in range(CONV):
        pre = pre + taps[CONV - 1 - j : CONV - j, :] * shifted[j]
    return pre, shifted


class Experts:
    def __init__(self, d, m, lanes, peers, into_ref, rows_ref, pack_ref, slots_ref, part_ref, back_ref, stage_ref, inbox_ref,
                 gsend, grecv, dsend, drecv, bsend, brecv, rsend, rrecv):
        self.d, self.m, self.lanes, self.peers = d, m, lanes, peers
        self.rows, self.into, self.pack, self.slots, self.part, self.back = rows_ref, into_ref, pack_ref, slots_ref, part_ref, back_ref
        self.stage, self.inbox = stage_ref, inbox_ref
        self.dsend, self.drecv, self.bsend, self.brecv, self.rsend, self.rrecv = dsend, drecv, bsend, brecv, rsend, rrecv
        self.sets = rows_ref.shape[1]
        self.cap = pack_ref.shape[2] // self.sets
        self.width = rows_ref.shape[3]
        self.gather = LineGather(rows_ref, gsend, grecv, d, m, lanes)

    def slot_rows(self, ref, s, i):
        return ref[s, :, i * self.cap : (i + 1) * self.cap, :].reshape(self.peers * self.cap, self.width)

    def set_slot_rows(self, ref, s, i, value):
        ref[s, :, i * self.cap : (i + 1) * self.cap, :] = value.reshape(self.peers, self.cap, self.width)

    def hop(self, src, dst, send, recv, s, k):
        other = lax.rem(self.d + k, self.peers)
        return pltpu.make_async_remote_copy(
            src_ref=src.at[s, other], dst_ref=dst.at[s, self.d], send_sem=send.at[s, k - 1],
            recv_sem=recv.at[s, k - 1], device_id=(other, self.m), device_id_type=MESH,
        )

    def across(self, src, dst, send, recv, s):
        for k in range(1, self.peers):
            self.hop(src, dst, send, recv, s, k).start()
        dst[s, self.d] = src[s, self.d]

    def dispatch(self, s):
        for i in range(self.sets):
            self.set_slot_rows(self.pack, s, i, dot(self.into[s], self.rows[s, i]).astype(BF16))
        self.across(self.pack, self.slots, self.dsend, self.drecv, s)

    def answer(self, s, expert):
        for k in range(1, self.peers):
            self.hop(self.pack, self.slots, self.dsend, self.drecv, s, k).wait_recv()
        for i, value in enumerate(expert(s, [self.slot_rows(self.slots, s, i) for i in range(self.sets)])):
            self.set_slot_rows(self.part, s, i, value.astype(BF16))
        self.across(self.part, self.back, self.bsend, self.brecv, s)

    def home(self, s):
        return pltpu.make_async_remote_copy(
            src_ref=self.stage.at[s], dst_ref=self.inbox.at[self.m], send_sem=self.rsend.at[s], recv_sem=self.rrecv.at[self.m],
            device_id=(self.d, s), device_id_type=MESH,
        )

    def combine(self, s):
        for k in range(1, self.peers):
            self.hop(self.part, self.back, self.bsend, self.brecv, s, k).wait_recv()
        return [dot_tn(self.into[s], self.slot_rows(self.back, s, i)) for i in range(self.sets)]

    def combine_away(self, s):
        for i, value in enumerate(self.combine(s)):
            self.stage[s, i] = value.astype(BF16)
        self.home(s).start()

    def steps(self, expert, own_ref):
        one, two, three = self.gather.order
        self.dispatch(self.m)
        yield
        self.gather.arrive(0)
        self.dispatch(one)
        yield
        self.gather.arrive(1)
        self.dispatch(two)
        self.answer(one, expert)
        yield
        self.gather.arrive(2)
        self.dispatch(three)
        self.answer(two, expert)
        self.combine_away(one)
        yield
        self.answer(three, expert)
        self.combine_away(two)
        yield
        self.answer(self.m, expert)
        self.combine_away(three)
        yield
        for i, value in enumerate(self.combine(self.m)):
            own_ref[i] = value
        yield

    def settle(self, own_ref):
        for s in self.gather.order:
            pltpu.make_async_remote_copy(
                src_ref=self.stage.at[s], dst_ref=self.inbox.at[s], send_sem=self.rsend.at[s], recv_sem=self.rrecv.at[s],
                device_id=(self.d, s), device_id_type=MESH,
            ).wait_recv()
            own_ref[...] += self.inbox[s].astype(F32)

    def run(self, expert, own_ref, meanwhile):
        self.gather.start()
        for _ in self.steps(expert, own_ref):
            pass
        meanwhile()
        self.settle(own_ref)

    def finish(self):
        self.gather.finish()
        order = [self.m, *self.gather.order]
        for s in order:
            for k in range(1, self.peers):
                self.hop(self.pack, self.slots, self.dsend, self.drecv, s, k).wait_send()
                self.hop(self.part, self.back, self.bsend, self.brecv, s, k).wait_send()
        for s in order[1:]:
            self.home(s).wait_send()


def large(v):
    return v.size * v.dtype.itemsize >= 1 << 17


class Refs(types.SimpleNamespace):
    def need(self, *refs):
        for ref in refs:
            if id(ref) in self.coming:
                self.coming.pop(id(ref)).wait()

    def ship(self, *refs):
        for ref in refs:
            self.gone.append(self.going.pop(id(ref)))
            self.gone[-1].start()


def launch(name, cid, body, inputs, far, outputs, scratch, limit=58):
    near = {k: v for k, v in inputs.items() if not large(v)}
    lazy = {k: v for k, v in inputs.items() if large(v)}
    prompt = {k: v for k, v in outputs.items() if not large(v)}
    late = {k: v for k, v in outputs.items() if large(v)}
    buffers = {k: pltpu.VMEM(v.shape, v.dtype) for k, v in {**lazy, **late}.items()}
    away = [k + "_far" for k in (*lazy, *late)]
    names = [*near, *away[: len(lazy)], *far, *prompt, *away[len(lazy) :], *scratch, *buffers, "moves"]

    def kernel(*refs):
        r = Refs(**dict(zip(names, refs)))
        get = lambda k: getattr(r, k)
        r.gone = []
        r.coming = {id(get(k)): pltpu.make_async_copy(get(k + "_far"), get(k), r.moves.at[i]) for i, k in enumerate(lazy)}
        r.going = {id(get(k)): pltpu.make_async_copy(get(k), get(k + "_far"), r.moves.at[len(lazy) + i]) for i, k in enumerate(late)}
        for copy in r.coming.values():
            copy.start()
        body(r)
        r.need(*map(get, lazy))
        r.ship(*(get(k) for k in late if id(get(k)) in r.going))
        for copy in r.gone:
            copy.wait()

    results = pl.pallas_call(
        kernel,
        out_shape=[*prompt.values(), *late.values()],
        in_specs=vmem(len(near)) + hbm(len(lazy) + len(far)),
        out_specs=vmem(len(prompt)) + hbm(len(late)),
        scratch_shapes=[*scratch.values(), *buffers.values(), dma(max(1, len(lazy) + len(late)))],
        compiler_params=params(cid, limit),
        name=name,
    )(*near.values(), *lazy.values(), *far.values())
    return types.SimpleNamespace(**dict(zip([*prompt, *late], results)))


def convolution(small):
    return dict(norm_in=small.norm_in, conv_w=small.conv_w, conv_b=small.conv_b, since=small.since, x_proj=small.x_proj)


def routing(small):
    return dict(norm_moe=small.norm_moe, router=small.router)


def flat(ref):
    return ref[...].reshape(ref.shape[0] * ref.shape[1], ref.shape[2])


def gate_of(chance, choose):
    return jnp.sum(chance * choose, axis=1, keepdims=True)


class Sizes:
    def __init__(self, lanes, peers, experts, cap, rows, width, channels, hidden):
        self.lanes, self.peers, self.experts, self.cap = lanes, peers, experts, cap
        self.rows, self.width, self.channels, self.hidden = rows, width, channels, hidden
        self.total, self.slots = rows * lanes, experts * cap


def in_outputs(z):
    return dict(whole=bf16(z.lanes, z.rows, z.width), conv=f32(z.total + HEAD, z.channels), zgate=f32(z.total, z.channels),
                xs=f32(z.total, z.channels), proj=bf16(PROJ, z.total))


def sum_scratch(z):
    halves = pltpu.VMEM((2, PARTS, PROJ, z.total // PARTS), BF16)
    return dict(sum_stage=halves, sum_inbox=halves, sum_send=dma(2, PARTS), sum_recv=dma(2, PARTS))


def in_scratch(z):
    return dict(part=pltpu.VMEM((PROJ, z.total), F32), u_send=dma(2, z.lanes), u_recv=dma(z.lanes), **sum_scratch(z))


def in_stage(z, r, l, act, weights):
    d, m = lax.axis_index("dp"), lax.axis_index("mp")
    r.whole[m] = (act * rms_inverse(act) * r.norm_in[l : l + 1, :]).astype(BF16)
    gather = LineGather(r.whole, r.u_send, r.u_recv, d, m, z.lanes)
    gather.start()
    r.conv[:HEAD, :] = jnp.zeros((HEAD, z.channels), F32)
    weights.wait()

    def project(s):
        u = r.whole[s]
        r.conv[pl.ds(pl.multiple_of(s * z.rows + HEAD, 8), z.rows), :] = dot(u, r.win[0])
        r.zgate[pl.ds(pl.multiple_of(s * z.rows, 8), z.rows), :] = dot(u, r.win[1])

    project(m)
    for i in range(z.lanes - 1):
        project(gather.arrive(i))
    r.ship(r.conv, r.zgate, r.whole)
    taps, bias = r.conv_w[l], r.conv_b[l : l + 1, :]

    def conv_step(c, carry):
        base = pl.multiple_of(c * CONV_ROWS, CONV_ROWS)
        pre, _ = conv_window(r.conv, r.since, taps, bias, base)
        xs = pre * sigmoid(pre)
        r.xs[pl.ds(base, CONV_ROWS), :] = xs
        r.part[:, pl.ds(base, CONV_ROWS)] = dot_nt(r.x_proj[l], xs.astype(BF16))
        return carry

    lax.fori_loop(0, z.total // CONV_ROWS, conv_step, 0)
    r.ship(r.xs)
    finish = line_sum(r.part, r.sum_stage, r.sum_inbox, r.sum_send, r.sum_recv, r.proj, d, m, z.lanes)
    gather.finish()
    finish()


def first_block(z, l, act, small, w_in):
    def body(r):
        d, m = lax.axis_index("dp"), lax.axis_index("mp")
        (weights,) = fetch([(r.w_in.at[l], r.win)], r.fetched)
        greet(d, m, z.lanes, 0, False)
        r.need(r.act)
        in_stage(z, r, l, r.act[...].astype(F32), weights)

    inputs = dict(act=act, **convolution(small))
    return launch("mamba_in", 0, body, inputs, dict(w_in=w_in), in_outputs(z),
                  dict(win=pltpu.VMEM(w_in.shape[1:], BF16), fetched=dma(1), **in_scratch(z)))


def expert_refs(r):
    return (r.e_rows, r.e_pack, r.e_slots, r.e_part, r.e_back, r.e_stage, r.e_inbox, r.e_gs, r.e_gr, r.e_ds, r.e_dr, r.e_bs, r.e_br,
            r.e_rs, r.e_rr)


def expert_names(z, sets):
    across = pltpu.VMEM((z.lanes, z.peers, sets * z.cap, z.width), BF16)
    along = pltpu.VMEM((z.lanes, sets, z.rows, z.width), BF16)
    plane, line = dma(z.lanes, z.peers - 1), dma(z.lanes)
    return dict(
        e_rows=along, e_pack=across, e_slots=across, e_part=across, e_back=across, e_stage=along, e_inbox=along, e_gs=dma(2, z.lanes),
        e_gr=line, e_ds=plane, e_dr=plane, e_bs=plane, e_br=plane, e_rs=line, e_rr=line, e_own=pltpu.VMEM((sets, z.rows, z.width), F32))


def weight_scratch(wout, wup, wdown):
    return dict(wout=pltpu.VMEM(wout.shape[1:], BF16), wup=pltpu.VMEM(wup.shape[2:], BF16), wdown=pltpu.VMEM(wdown.shape[2:], BF16))


def out_scratch(z, place):
    stage, inbox, send, recv = reduce_scratch(z.lanes, z.rows, z.width)
    return dict(m_stage=stage, m_inbox=inbox, m_send=send, m_recv=recv, places=pltpu.VMEM((z.lanes, *place.shape), jnp.int32),
                p_send=dma(2, z.lanes), p_recv=dma(z.lanes), m_own=pltpu.VMEM((z.rows, z.width), F32))


def out_stage(z, r, l, wout):
    d, m = lax.axis_index("dp"), lax.axis_index("mp")
    r.places[m] = r.place[...]
    places = LineGather(r.places, r.p_send, r.p_recv, d, m, z.lanes)
    places.start()
    reduce = LineReduce(r.m_stage, r.m_inbox, r.m_send, r.m_recv, d, m, z.lanes)
    wout.wait()
    r.need(r.act, r.gated)
    for s in reduce.order:
        reduce.push(s, dot(r.gated[s], r.wout[...]))
    r.m_own[...] = r.act[...].astype(F32) + dot(r.gated[m], r.wout[...])

    def spread_places(s):
        numbers = lax.broadcasted_iota(jnp.int32, (z.slots, z.rows), 0)
        r.into[s] = (numbers == r.places[s][:1, : z.rows]).astype(F32).astype(BF16)

    spread_places(m)
    owner = lax.broadcasted_iota(jnp.int32, (z.slots, z.experts), 0) // z.cap == lax.broadcasted_iota(jnp.int32, (z.slots, z.experts), 1)
    r.choose[...] = dot_tn(r.into[m], owner.astype(F32).astype(BF16))
    for i in range(z.lanes - 1):
        spread_places(places.arrive(i))
    reduce.total(r.m_own)

    def finish():
        places.finish()
        reduce.finish()

    return finish


def chances(z, normed, table):
    logits = lax.dot_general(normed, table, (((1,), (1,)), ((), ())), precision=highest, preferred_element_type=F32)
    raised = jnp.exp(logits - jnp.max(logits, axis=1, keepdims=True))
    return raised / jnp.sum(raised, axis=1, keepdims=True)


def middle_block(z, l, act, gated, small, weights):
    def body(r):
        d, m = lax.axis_index("dp"), lax.axis_index("mp")
        wout, wup, wdown, win = fetch([(r.w_out.at[l], r.wout), (r.w_up.at[l, 0], r.wup), (r.w_down.at[l, 0], r.wdown),
                                       (r.w_in.at[l + 1], r.win)], r.fetched)
        greet(d, m, z.lanes, z.peers, True)
        finish = out_stage(z, r, l, wout)
        wup.wait()
        wdown.wait()
        middle = r.m_own[...]
        r.middle[...] = middle
        r.e_rows[m, 0] = (middle * rms_inverse(middle) * r.norm_moe[l : l + 1, :]).astype(BF16)
        moe = Experts(d, m, z.lanes, z.peers, r.into, *expert_refs(r))

        def expert(s, rows):
            r.slots[s] = rows[0]
            hidden = dot(rows[0], r.wup[...])
            r.hidden[s] = hidden.astype(BF16)
            active = gelu(hidden).astype(BF16)
            r.active[s] = active
            return [dot(active, r.wdown[...])]

        def meanwhile():
            finish()
            middle = r.middle[...]
            r.chance[...] = chances(z, middle * rms_inverse(middle) * r.norm_moe[l : l + 1, :], r.router[l])

        moe.run(expert, r.e_own, meanwhile)
        r.ship(r.into, r.middle, r.slots, r.hidden, r.active)
        picked = r.e_own[0].astype(BF16)
        r.picked[...] = picked
        following = r.middle[...] + gate_of(r.chance[...], r.choose[...]) * picked.astype(F32)
        r.following[...] = following
        r.ship(r.picked, r.following)
        in_stage(z, r, l + 1, following, win)
        moe.finish()

    w_in, w_out, w_up, w_down = weights
    slots = (z.lanes, z.slots)
    return launch(
        "middle", 1 + l, body, dict(act=act, gated=gated, place=small.place, **routing(small), **convolution(small)),
        dict(w_in=w_in, w_out=w_out, w_up=w_up, w_down=w_down),
        dict(middle=f32(z.rows, z.width), chance=f32(z.rows, z.experts), into=bf16(*slots, z.rows), slots=bf16(*slots, z.width),
             hidden=bf16(*slots, z.hidden), active=bf16(*slots, z.hidden), picked=bf16(z.rows, z.width), choose=f32(z.rows, z.experts), following=f32(z.rows, z.width),
             **in_outputs(z)),
        dict(win=pltpu.VMEM(w_in.shape[1:], BF16), fetched=dma(4), **weight_scratch(w_out, w_up, w_down), **out_scratch(z, small.place),
             **expert_names(z, 1), **in_scratch(z)))


def back_outputs(z):
    return dict(gmid=f32(z.rows, z.width), gup=f32(z.width, z.hidden), gdown=f32(z.hidden, z.width), ggated=f32(z.lanes, z.rows, z.channels),
                gwout=bf16(z.channels, z.width), gshare=f32(z.experts + 8, z.width))


def back_scratch(z):
    return dict(wide=pltpu.VMEM((z.lanes, z.rows, z.width), BF16), w_send=dma(2, z.lanes), w_recv=dma(z.lanes))


def route_back(z, r, l, upstream, middle, chance, choose, picked, returned):
    d, m = lax.axis_index("dp"), lax.axis_index("mp")
    gate = gate_of(chance, choose)
    inverse, gain = rms_inverse(middle), r.norm_moe[l : l + 1, :]
    grad_gate = jnp.sum(upstream * picked.astype(F32), axis=1, keepdims=True)
    grad_logit = gate * grad_gate * (choose - chance)
    grad_normed = returned.astype(BF16).astype(F32) + lax.dot_general(
        grad_logit, r.router[l], (((1,), (0,)), ((), ())), precision=highest, preferred_element_type=F32)
    pulled, grad_gain = norm_back(middle, inverse, gain, grad_normed)
    grad_middle = upstream + pulled
    r.gmid[...] = grad_middle
    r.ship(r.gmid)
    r.wide[m] = grad_middle.astype(BF16)
    gather = LineGather(r.wide, r.w_send, r.w_recv, d, m, z.lanes)
    gather.start()
    grad_router = lax.dot_general(
        grad_logit, middle * inverse * gain, (((0,), (0,)), ((), ())), precision=highest, preferred_element_type=F32)
    r.gshare[: z.experts, :] = grad_router
    r.gshare[z.experts :, :] = jnp.broadcast_to(grad_gain, (8, z.width))

    def gate_back(s):
        r.ggated[s] = dot_nt(r.wide[s], r.wout[...])

    gate_back(m)
    for i in range(z.lanes - 1):
        gate_back(gather.arrive(i))
    r.ship(r.ggated)
    r.need(r.gated)
    r.gwout[...] = dot_tn(flat(r.gated), flat(r.wide)).astype(BF16)
    gather.finish()


def turn_block(z, l, act, gated, cotangent, small, weights):
    def body(r):
        d, m = lax.axis_index("dp"), lax.axis_index("mp")
        wout, wup, wdown = fetch([(r.w_out.at[l], r.wout), (r.w_up.at[l, 0], r.wup), (r.w_down.at[l, 0], r.wdown)], r.fetched)
        greet(d, m, z.lanes, z.peers, True)
        finish = out_stage(z, r, l, wout)
        wup.wait()
        wdown.wait()
        middle = r.m_own[...]
        normed = middle * rms_inverse(middle) * r.norm_moe[l : l + 1, :]
        forth = Experts(d, m, z.lanes, z.peers, r.into, *expert_refs(r))
        back = Experts(d, m, z.lanes, z.peers, r.into, *(getattr(r, "f" + k[1:]) for k in list(expert_names(z, 1))[:-1]))
        r.e_rows[m, 0] = normed.astype(BF16)
        forth.gather.start()
        chance = chances(z, normed, r.router[l])
        r.chance[...] = chance
        r.need(r.cotangent)
        r.f_rows[m, 0] = (gate_of(chance, r.choose[...]) * r.cotangent[...].astype(F32)).astype(BF16)
        back.gather.start()

        def expert_forth(s, rows):
            active = gelu(dot(rows[0], r.wup[...])).astype(BF16)
            r.active[s] = active
            return [dot(active, r.wdown[...])]

        def expert_back(s, rows):
            slope = gelu_slope(dot(forth.slot_rows(forth.slots, s, 0), r.wup[...]))
            grad_hidden = (dot_nt(rows[0], r.wdown[...]) * slope).astype(BF16)
            r.ghid[s] = grad_hidden
            return [dot_nt(grad_hidden, r.wup[...])]

        for _ in zip(forth.steps(expert_forth, r.e_own), back.steps(expert_back, r.f_own)):
            pass
        finish()
        r.gdown[...] = dot_tn(flat(r.active), r.f_slots[...].reshape(z.lanes * z.slots, z.width))
        r.gup[...] = dot_tn(r.e_slots[...].reshape(z.lanes * z.slots, z.width), flat(r.ghid))
        r.ship(r.gdown, r.gup)
        forth.settle(r.e_own)
        back.settle(r.f_own)
        picked = r.e_own[0].astype(BF16)
        r.following[...] = r.m_own[...] + gate_of(r.chance[...], r.choose[...]) * picked.astype(F32)
        r.ship(r.following)
        route_back(z, r, l, r.cotangent[...].astype(F32), r.m_own[...], r.chance[...], r.choose[...], picked, r.f_own[0])
        forth.finish()
        back.finish()

    w_in, w_out, w_up, w_down = weights
    slots = (z.lanes, z.slots)
    return launch(
        "turn", 8, body, dict(act=act, gated=gated, cotangent=cotangent, place=small.place, **routing(small)),
        dict(w_out=w_out, w_up=w_up, w_down=w_down),
        dict(following=f32(z.rows, z.width), **back_outputs(z)),
        dict(fetched=dma(3), choose=pltpu.VMEM((z.rows, z.experts), F32), chance=pltpu.VMEM((z.rows, z.experts), F32), into=pltpu.VMEM((*slots, z.rows), BF16),
             active=pltpu.VMEM((*slots, z.hidden), BF16), ghid=pltpu.VMEM((*slots, z.hidden), BF16),
             **weight_scratch(w_out, w_up, w_down), **out_scratch(z, small.place), **expert_names(z, 1),
             **{"f" + k[1:]: v for k, v in expert_names(z, 1).items()}, **back_scratch(z)),
        58 if z.slots <= 256 else 61)


class PlaneSum:
    def __init__(self, d, m, peers, mine, pair, half, inbox, result, psend, precv, csend, crecv, gsend, grecv):
        self.m, self.mine, self.pair, self.half, self.inbox, self.result = m, mine, pair, half, inbox, result
        self.psend, self.precv, self.csend, self.crecv, self.gsend, self.grecv = psend, precv, csend, crecv, gsend, grecv
        self.chips = peers // 2
        self.chip, self.core = lax.div(d, 2), lax.rem(d, 2)
        self.rows = mine.shape[0] // 2
        self.block = self.rows // self.chips

    def side(self, core):
        return pl.ds(pl.multiple_of(core * self.rows, 16), self.rows)

    def at(self, chip):
        return pl.ds(pl.multiple_of(chip * self.block, 16), self.block)

    def final(self, chip):
        return pl.ds(pl.multiple_of(self.core * self.rows + chip * self.block, 16), self.block)

    def swap(self, src, dst, i):
        return pltpu.make_async_remote_copy(
            src_ref=src, dst_ref=dst, send_sem=self.psend.at[i], recv_sem=self.precv.at[i],
            device_id=(self.chip * 2 + 1 - self.core, self.m), device_id_type=MESH)

    def first_swap(self):
        return self.swap(self.mine.at[self.side(1 - self.core)], self.pair, 0)

    def last_swap(self):
        return self.swap(self.result.at[self.side(self.core)], self.result.at[self.side(self.core)], 1)

    def other(self, k):
        return lax.rem(self.chip + k, self.chips)

    def scatter(self, k):
        return pltpu.make_async_remote_copy(
            src_ref=self.half.at[self.at(self.other(k))], dst_ref=self.inbox.at[k - 1], send_sem=self.csend.at[k - 1],
            recv_sem=self.crecv.at[k - 1], device_id=(self.other(k) * 2 + self.core, self.m), device_id_type=MESH)

    def gather(self, k):
        return pltpu.make_async_remote_copy(
            src_ref=self.result.at[self.final(self.chip)], dst_ref=self.result.at[self.final(self.chip)], send_sem=self.gsend.at[k - 1],
            recv_sem=self.grecv.at[k - 1], device_id=(self.other(k) * 2 + self.core, self.m), device_id_type=MESH)

    def begin(self):
        self.first_swap().start()

    def second(self):
        self.first_swap().wait_recv()
        self.half[...] = (self.mine[self.side(self.core)].astype(F32) + self.pair[...].astype(F32)).astype(BF16)
        for k in range(1, self.chips):
            self.scatter(k).start()

    def third(self):
        for k in range(1, self.chips):
            self.scatter(k).wait_recv()
        summed = self.half[self.at(self.chip)].astype(F32)
        for k in range(1, self.chips):
            summed = summed + self.inbox[k - 1].astype(F32)
        self.result[self.final(self.chip)] = summed.astype(BF16)
        for k in range(1, self.chips):
            self.gather(k).start()

    def fourth(self):
        for k in range(1, self.chips):
            self.gather(k).wait_recv()
        self.last_swap().start()

    def end(self):
        self.last_swap().wait_recv()

    def finish(self):
        self.first_swap().wait_send()
        self.last_swap().wait_send()
        for k in range(1, self.chips):
            self.scatter(k).wait_send()
            self.gather(k).wait_send()


def plane_scratch(peers, rows, width):
    return [
        pltpu.VMEM((rows, width), BF16),
        pltpu.VMEM((rows // 2, width), BF16),
        pltpu.VMEM((rows // 2, width), BF16),
        pltpu.VMEM((peers // 2 - 1, rows // peers, width), BF16),
        dma(2), dma(2), dma(peers // 2 - 1), dma(peers // 2 - 1), dma(peers // 2 - 1), dma(peers // 2 - 1),
    ]


def exchange(targets, buf, inbox, send, recv):
    copies = [
        pltpu.make_async_remote_copy(src_ref=buf, dst_ref=inbox.at[k], send_sem=send.at[k], recv_sem=recv.at[k],
                                     device_id=target, device_id_type=MESH)
        for k, target in enumerate(targets)
    ]
    for copy in copies:
        copy.start()

    def collect():
        total = buf[...].astype(F32)
        for k, copy in enumerate(copies):
            copy.wait()
            total = total + inbox[k].astype(F32)
        return total

    return collect


def early_rows(width, experts):
    sizes = [width, width, DT_RANK, STATE, 16, experts + 8, experts + 8]
    return [sum(sizes[:i]) for i in range(len(sizes) + 1)]


def late_rows(width):
    sizes = [width, PROJ, 16]
    return [sum(sizes[:i]) for i in range(len(sizes) + 1)]


def whole_blocks(rows, peers):
    return -(-rows // (16 * peers)) * 16 * peers


def in_back_scratch(z, win, last):
    early = whole_blocks(early_rows(z.width, z.experts)[-1], z.peers)
    late = whole_blocks(late_rows(z.width)[-1], z.peers)
    shared = 2 * (z.experts + 8)
    small = -(-2 * (z.width // LANES) // 8) * 8
    stage, inbox, send, recv = reduce_scratch(z.lanes, z.rows, z.width)
    found = dict(
        gproj=pltpu.VMEM((PROJ, z.total), BF16), gpre=pltpu.VMEM((z.total + HEAD, z.channels), F32),
        gxi=pltpu.VMEM((z.total, z.channels), BF16), gconv=pltpu.VMEM((16, z.channels), F32), c_own=pltpu.VMEM((z.rows, z.width), F32),
        win=pltpu.VMEM(win.shape[1:], BF16), z_buf=pltpu.VMEM((shared, z.channels), BF16),
        z_in=pltpu.VMEM((z.lanes - 1, shared, z.channels), BF16), z_send=dma(z.lanes - 1), z_recv=dma(z.lanes - 1),
        c_stage=stage, c_inbox=inbox, c_send=send, c_recv=recv,
        **{"e%d" % i: v for i, v in enumerate(plane_scratch(z.peers, early, z.channels))},
        **{"l%d" % i: v for i, v in enumerate(plane_scratch(z.peers, late, z.channels))},
        **sum_scratch(z),
    )
    if last:
        found.update(
            n_buf=pltpu.VMEM((small, LANES), F32), n_in=pltpu.VMEM((z.peers - 1, small, LANES), F32), n_send=dma(z.peers - 1),
            n_recv=dma(z.peers - 1), n_buf2=pltpu.VMEM((small, LANES), F32), n_in2=pltpu.VMEM((z.lanes - 1, small, LANES), F32),
            n_send2=dma(z.lanes - 1), n_recv2=dma(z.lanes - 1))
    return found


def in_back_outputs(z, last):
    early = whole_blocks(early_rows(z.width, z.experts)[-1], z.peers)
    late = whole_blocks(late_rows(z.width)[-1], z.peers)
    return dict(early=bf16(early, z.channels), late=bf16(late, z.channels), share=f32(2 * (z.experts + 8), z.channels),
                gnorm=f32(2 if last else 1, z.width))


def plane_sum(z, r, which, result):
    d, m = lax.axis_index("dp"), lax.axis_index("mp")
    parts = [getattr(r, which + str(i)) for i in range(10)]
    return PlaneSum(d, m, z.peers, *parts[:4], result, *parts[4:])


def in_back_stage(z, r, l, weights, emit):
    d, m = lax.axis_index("dp"), lax.axis_index("mp")
    line = [(d, lax.rem(m + k, z.lanes)) for k in range(1, z.lanes)]
    early, late = plane_sum(z, r, "e", r.early), plane_sum(z, r, "l", r.late)
    emine, lmine = early.mine, late.mine
    ch = z.channels
    at, till = early_rows(z.width, z.experts), late_rows(z.width)

    def early_work():
        r.need(r.b_whole, r.gzg, r.b_gwout, r.b_gshare)
        whole = r.b_whole[...].reshape(z.total, z.width)
        emine[at[0] : at[1], :] = dot_tn(whole, r.gzg[...]).astype(BF16)
        for i in range(z.width // ch):
            emine[at[1] + i * ch : at[1] + (i + 1) * ch, :] = r.b_gwout[:, i * ch : (i + 1) * ch]
            emine[at[5 + i] : at[6 + i], :] = r.b_gshare[:, i * ch : (i + 1) * ch].astype(BF16)
        emine[at[2] : at[3], :] = r.gdtw[...].astype(BF16)
        emine[at[3] : at[4], :] = r.galog[...].astype(BF16)
        emine[at[4] : at[5], :] = jnp.concatenate([r.gdtb[...], r.gskip[...], jnp.zeros((14, ch), F32)], axis=0).astype(BF16)
        if at[7] < emine.shape[0]:
            emine[at[7] :, :] = jnp.zeros((emine.shape[0] - at[7], ch), BF16)
        early.begin()

    r.need(r.gpart)
    finish_sum = line_sum(r.gpart, r.sum_stage, r.sum_inbox, r.sum_send, r.sum_recv, r.gproj, d, m, z.lanes, early_work)
    taps, bias = r.conv_w[l], r.conv_b[l : l + 1, :]
    r.gconv[...] = jnp.zeros_like(r.gconv)
    r.gpre[z.total :, :] = jnp.zeros((HEAD, ch), F32)

    def first(c, carry):
        base = pl.multiple_of(c * CONV_ROWS, CONV_ROWS)
        pre, shifted = conv_window(r.b_conv, r.since, taps, bias, base)
        sig = sigmoid(pre)
        grad = r.gxs[pl.ds(base, CONV_ROWS), :] + dot_tn(r.gproj[:, pl.ds(base, CONV_ROWS)], r.x_proj[l])
        grad = grad * (sig * (1.0 + pre * (1.0 - sig)))
        r.gpre[pl.ds(base, CONV_ROWS), :] = grad
        for j in range(CONV):
            r.gconv[CONV - 1 - j : CONV - j, :] += jnp.sum(grad * shifted[j], axis=0, keepdims=True)
        r.gconv[CONV : CONV + 1, :] += jnp.sum(grad, axis=0, keepdims=True)
        return carry

    r.need(r.b_conv, r.gxs)
    lax.fori_loop(0, z.total // CONV_ROWS, first, 0)

    def second(c, carry):
        base = pl.multiple_of(c * CONV_ROWS, CONV_ROWS)
        window = r.gpre[pl.ds(base, CONV_ROWS + HEAD), :]
        since = r.since[pl.ds(base, CONV_ROWS + HEAD), :]
        grad = taps[CONV - 1 : CONV, :] * window[:CONV_ROWS]
        for j in range(1, CONV):
            grad = grad + taps[CONV - 1 - j : CONV - j, :] * (window * (since >= j).astype(F32))[j : j + CONV_ROWS]
        r.gxi[pl.ds(base, CONV_ROWS), :] = grad.astype(BF16)
        return carry

    lax.fori_loop(0, z.total // CONV_ROWS, second, 0)
    weights.wait()
    reduce = LineReduce(r.c_stage, r.c_inbox, r.c_send, r.c_recv, d, m, z.lanes)

    def term(s):
        part = pl.ds(pl.multiple_of(s * z.rows, 16), z.rows)
        return dot_nt(r.gxi[part, :], r.win[0]) + dot_nt(r.gzg[part, :], r.win[1])

    def push_middle(s):
        @pl.when(reduce.middle)
        def _():
            for p in range(PIECES):
                reduce.push_on(s, p, term(s)[p * reduce.rows : (p + 1) * reduce.rows])

    one, two, three = reduce.order

    @pl.when(reduce.at_end)
    def _():
        for s in reduce.order:
            reduce.push_first(s, term(s))

    early.second()
    r.need(r.b_xs)
    whole = r.b_whole[...].reshape(z.total, z.width)
    lmine[till[0] : till[1], :] = dot_tn(whole, r.gxi[...]).astype(BF16)
    lmine[till[1] : till[2], :] = dot(r.gproj[...], r.b_xs[...].astype(BF16)).astype(BF16)
    lmine[till[2] : till[3], :] = r.gconv[...].astype(BF16)
    if till[3] < lmine.shape[0]:
        lmine[till[3] :, :] = jnp.zeros((lmine.shape[0] - till[3], ch), BF16)
    late.begin()
    push_middle(one)
    late.second()
    r.c_own[...] = term(m)
    early.third()
    push_middle(two)
    late.third()
    early.fourth()
    push_middle(three)
    late.fourth()
    early.end()
    r.ship(r.early)
    r.z_buf[...] = r.early[at[5] : at[7], :]
    shared = exchange(line, r.z_buf, r.z_in, r.z_send, r.z_recv)
    reduce.total(r.c_own)
    r.need(r.b_act, r.b_gmid)
    act = r.b_act[...].astype(F32)
    pulled, grad_gain = norm_back(act, rms_inverse(act), r.norm_in[l : l + 1, :], r.c_own[...])
    emit(r.b_gmid[...] + pulled)

    def finish():
        late.end()
        r.ship(r.late)
        if l == 0:
            both = jnp.concatenate([grad_gain, r.prior[...]], axis=0)
            groups = z.width // LANES
            for g in range(groups):
                r.n_buf[2 * g : 2 * g + 2, :] = both[:, g * LANES : (g + 1) * LANES]
            if 2 * groups < r.n_buf.shape[0]:
                r.n_buf[2 * groups :, :] = jnp.zeros((r.n_buf.shape[0] - 2 * groups, LANES), F32)
            plane = [(lax.rem(d + k, z.peers), m) for k in range(1, z.peers)]
            r.n_buf2[...] = exchange(plane, r.n_buf, r.n_in, r.n_send, r.n_recv)()
            summed = exchange(line, r.n_buf2, r.n_in2, r.n_send2, r.n_recv2)()
            r.gnorm[...] = jnp.concatenate([summed[2 * g : 2 * g + 2, :] for g in range(groups)], axis=1)
        else:
            r.gnorm[...] = grad_gain
        r.share[...] = shared()
        finish_sum()
        reduce.finish()
        early.finish()
        late.finish()

    return finish


def last_block(z, back, prior, small, w_in):
    def body(r):
        d, m = lax.axis_index("dp"), lax.axis_index("mp")
        (win,) = fetch([(r.w_in.at[0], r.win)], r.fetched)
        greet(d, m, z.lanes, z.peers, True)

        def emit(value):
            r.up[...] = value

        in_back_stage(z, r, 0, win, emit)()

    return launch("mamba_in_backward", 9, body, dict(**back, prior=prior, **convolution(small)), dict(w_in=w_in),
                  dict(up=f32(z.rows, z.width), **in_back_outputs(z, True)), dict(fetched=dma(1), **in_back_scratch(z, w_in, True)))


def experts_back(z, r, l, fetched, finish):
    d, m = lax.axis_index("dp"), lax.axis_index("mp")
    for weight in fetched:
        weight.wait()
    r.need(r.into, r.hidden)
    moe = Experts(d, m, z.lanes, z.peers, r.into, *expert_refs(r))

    def expert(s, rows):
        grad_hidden = (dot_nt(rows[0], r.wdown[...]) * gelu_slope(r.hidden[s].astype(F32))).astype(BF16)
        r.ghid[s] = grad_hidden
        return [dot_nt(grad_hidden, r.wup[...])]

    def meanwhile():
        r.need(r.active, r.slots)
        r.gdown[...] = dot_tn(flat(r.active), r.e_slots[...].reshape(z.lanes * z.slots, z.width))
        r.gup[...] = dot_tn(flat(r.slots), flat(r.ghid))
        r.ship(r.gdown, r.gup)
        finish()

    moe.run(expert, r.e_own, meanwhile)
    r.need(r.picked, r.middle)
    route_back(z, r, l, r.upstream[...], r.middle[...], r.chance[...], r.choose[...], r.picked[...], r.e_own[0])
    moe.finish()


def down_blocks(z, l, back, kept, small, weights):
    def upper(r):
        d, m = lax.axis_index("dp"), lax.axis_index("mp")
        (win,) = fetch([(r.w_in.at[l], r.win)], r.fetched)
        greet(d, m, z.lanes, z.peers, True)

        def emit(value):
            r.up[...] = value

        in_back_stage(z, r, l, win, emit)()

    def lower(r):
        d, m = lax.axis_index("dp"), lax.axis_index("mp")
        fetched = fetch([(r.w_down.at[l - 1, 0], r.wdown), (r.w_up.at[l - 1, 0], r.wup), (r.w_out.at[l - 1], r.wout)], r.fetched)
        greet(d, m, z.lanes, z.peers, True)
        r.need(r.upstream)
        r.e_rows[m, 0] = (gate_of(r.chance[...], r.choose[...]) * r.upstream[...]).astype(BF16)
        experts_back(z, r, l - 1, fetched, lambda: None)

    w_in, w_out, w_up, w_down = weights
    slots = (z.lanes, z.slots)
    one = launch("mamba_in_backward", 20 + l, upper, dict(**back, **convolution(small)),
                 dict(w_in=w_in), dict(up=f32(z.rows, z.width), **in_back_outputs(z, False)),
                 dict(fetched=dma(1), **in_back_scratch(z, w_in, False)))
    two = launch("experts_backward", 30 + l, lower, dict(**kept, upstream=one.up, **routing(small)),
                 dict(w_out=w_out, w_up=w_up, w_down=w_down), back_outputs(z),
                 dict(fetched=dma(3), ghid=pltpu.VMEM((*slots, z.hidden), BF16), **weight_scratch(w_out, w_up, w_down),
                      **expert_names(z, 1), **back_scratch(z)))
    return types.SimpleNamespace(**vars(one), **vars(two))


def down_block(z, l, back, kept, small, weights):
    def body(r):
        d, m = lax.axis_index("dp"), lax.axis_index("mp")
        win, wdown, wup, wout = fetch([(r.w_in.at[l], r.win), (r.w_down.at[l - 1, 0], r.wdown), (r.w_up.at[l - 1, 0], r.wup),
                                       (r.w_out.at[l - 1], r.wout)], r.fetched)
        greet(d, m, z.lanes, z.peers, True)

        def emit(value):
            r.upstream[...] = value
            r.e_rows[m, 0] = (gate_of(r.chance[...], r.choose[...]) * value).astype(BF16)

        experts_back(z, r, l - 1, (wdown, wup, wout), in_back_stage(z, r, l, win, emit))

    w_in, w_out, w_up, w_down = weights
    slots = (z.lanes, z.slots)
    return launch(
        "down", 9 + l, body, dict(**back, **kept, **convolution(small), **routing(small)),
        dict(w_in=w_in, w_out=w_out, w_up=w_up, w_down=w_down), dict(**in_back_outputs(z, False), **back_outputs(z)),
        dict(fetched=dma(4), upstream=pltpu.VMEM((z.rows, z.width), F32),
             ghid=pltpu.VMEM((*slots, z.hidden), BF16), **weight_scratch(w_out, w_up, w_down), **in_back_scratch(z, w_in, False),
             **expert_names(z, 1), **back_scratch(z)))


def big_outputs(z, count):
    return dict(w_in=(count, 2, z.width, z.channels), w_out=(count, z.channels, z.width), w_up=(count, 1, z.width, z.hidden),
                w_down=(count, 1, z.hidden, z.width))


def widen(z, early, late, w_in, w_out):
    at, till, ch = early_rows(z.width, z.experts), late_rows(z.width), z.channels
    w_in[0] = late[till[0] : till[1], :].astype(F32)
    w_in[1] = early[at[0] : at[1], :].astype(F32)
    for i in range(z.width // ch):
        w_out[:, i * ch : (i + 1) * ch] = early[at[1] + i * ch : at[1] + (i + 1) * ch, :].astype(F32)


def upper_outputs(z, count, layer):
    early, late, _, up, down = layer
    far = [early, late, up, down]
    shapes = big_outputs(z, count)
    room = [pltpu.VMEM(v.shape, v.dtype) for v in far]
    room += [pltpu.VMEM(shapes["w_in"][1:], F32), pltpu.VMEM(shapes["w_out"][1:], F32), dma(4), dma(4)]

    def work(steps, there, outs, held):
        e, l, u, v, w_in, w_out, came, went = held
        coming = [pltpu.make_async_copy(src, dst, came.at[i]) for i, (src, dst) in enumerate(zip(there, (e, l, u, v)))]
        out_in, out_out, out_up, out_down = outs
        pairs = [(w_in, out_in.at[1]), (w_out, out_out.at[1]), (u, out_up.at[1, 0]), (v, out_down.at[1, 0])]
        going = [pltpu.make_async_copy(src, dst, went.at[i]) for i, (src, dst) in enumerate(pairs)]

        @pl.when(pl.program_id(0) == 0)
        def _():
            for copy in coming:
                copy.start()

        @pl.when(pl.program_id(0) == 1)
        def _():
            for copy in coming:
                copy.wait()
            widen(z, e, l, w_in, w_out)
            for copy in going:
                copy.start()

        @pl.when(pl.program_id(0) == steps - 1)
        def _():
            for copy in going:
                copy.wait()

    return work, far, [f32(*shape) for shape in shapes.values()], room


def final_block(z, result, up, gnorm, layers, large_ones):
    count, ch = len(layers), z.channels
    assert count == 2
    at, till = early_rows(z.width, z.experts), late_rows(z.width)
    far = dict(result=(z.rows, z.width), tokens=(z.rows, z.width), **big_outputs(z, count))
    near = dict(norm_in=(count, z.width), conv_w=(count, CONV, ch), conv_b=(count, ch), x_proj=(count, PROJ, ch), dt_proj=(count, DT_RANK, ch),
                dt_bias=(count, ch), a_log=(count, STATE, ch), skip=(count, ch), norm_moe=(count, z.width), router=(count, z.experts, z.width))
    shapes = {**far, **near}
    sums = [v for layer in layers for v in layer[:2]]
    whole = [*layers[0][3:], result, up]

    def kernel(*refs):
        small, refs = refs[: 1 + count], refs[1 + count :]
        there, refs = refs[: len(sums) + len(whole)], refs[len(sums) + len(whole) + len(large_ones) :]
        outs, refs = refs[: len(shapes)], refs[len(shapes) :]
        held, (w_in, w_out, came, went) = refs[: len(there)], refs[len(there) :]
        out = types.SimpleNamespace(**dict(zip(shapes, outs)))
        coming = fetch(list(zip(there, held)), came)
        out.norm_in[...] = small[0][...]
        going = []

        def send(src, dst):
            going.append(pltpu.make_async_copy(src, dst, went.at[len(going)]))
            going[-1].start()

        for l in range(count):
            early, late, share = held[2 * l], held[2 * l + 1], small[1 + l]
            coming[2 * l].wait()
            coming[2 * l + 1].wait()
            one = slice(l, l + 1)
            if l == 0:
                widen(z, early, late, w_in, w_out)
                send(w_in, out.w_in.at[0])
                send(w_out, out.w_out.at[0])
            for i in range(z.width // ch):
                cols = slice(i * ch, (i + 1) * ch)
                rows = share[i * (z.experts + 8) : (i + 1) * (z.experts + 8), :]
                out.router[l, :, cols] = rows[: z.experts]
                out.norm_moe[one, cols] = rows[z.experts : z.experts + 1]
            conv = late[till[2] : till[3], :].astype(F32)
            out.conv_w[l] = conv[:CONV]
            out.conv_b[one, :] = conv[CONV : CONV + 1]
            out.x_proj[l] = late[till[1] : till[2], :].astype(F32)
            out.dt_proj[l] = early[at[2] : at[3], :].astype(F32)
            out.a_log[l] = early[at[3] : at[4], :].astype(F32)
            both = early[at[4] : at[5], :].astype(F32)
            out.dt_bias[one, :] = both[:1]
            out.skip[one, :] = both[1:2]
        for i, place in enumerate((out.w_up.at[0, 0], out.w_down.at[0, 0], out.result, out.tokens)):
            coming[len(sums) + i].wait()
            send(held[len(sums) + i], place)
        for copy in going:
            copy.wait()

    before = 1 + count + len(sums) + len(whole)
    outputs = pl.pallas_call(
        kernel,
        out_shape=[f32(*shape) for shape in shapes.values()],
        in_specs=vmem(1 + count) + hbm(len(sums) + len(whole) + len(large_ones)),
        out_specs=hbm(len(far)) + vmem(len(near)),
        scratch_shapes=[pltpu.VMEM(v.shape, v.dtype) for v in (*sums, *whole)]
        + [pltpu.VMEM(far["w_in"][1:], F32), pltpu.VMEM(far["w_out"][1:], F32), dma(len(sums) + len(whole)), dma(2 + len(whole))],
        input_output_aliases={before + i: 2 + i for i in range(len(large_ones))},
        compiler_params=pltpu.CompilerParams(vmem_limit_bytes=60 << 20),
        name="outputs",
    )(gnorm, *(layer[2] for layer in layers), *sums, *whole, *large_ones)
    o = types.SimpleNamespace(**dict(zip(shapes, outputs)))
    return (o.result, o.tokens, o.norm_in, o.w_in, o.conv_w, o.conv_b, jnp.swapaxes(o.x_proj, 1, 2), o.dt_proj, o.dt_bias, o.a_log, o.skip, o.w_out, o.norm_moe,
            jnp.swapaxes(o.router, 1, 2), o.w_up, o.w_down)


def on_device(
    tokens, cotangent, lengths, routes, slot_place, norm_in, w_in, conv_w, conv_b, x_proj, dt_proj, dt_bias,
    a_log, d_skip, w_out, norm_moe, router, w_up, w_down,
):
    layers = norm_in.shape[0]
    assert layers == 2
    rows_here, width = tokens.shape
    lanes, peers = lax.axis_size("mp"), lax.axis_size("dp")
    experts, channels = router.shape[2], w_in.shape[3]
    capacity = max(2, (5 * rows_here + 4 * experts - 1) // (4 * experts))
    padded = (capacity + 15) // 16 * 16
    z = Sizes(lanes, peers, experts, padded, rows_here, width, channels, w_up.shape[3])
    position = lax.broadcasted_iota(jnp.int32, (z.total + HEAD, 1), 0)
    sequences = lengths.shape[1]
    earlier = jnp.arange(sequences)[:, None] < jnp.arange(sequences)[None, :]
    starts = jnp.sum(jnp.where(earlier, lengths[0][:, None], 0), axis=0)
    since = position - jnp.max(jnp.where(position >= starts[None, :], starts[None, :], 0), axis=1, keepdims=True)
    since = jnp.where(position < z.total, since, 0)
    place = jnp.pad(routes * padded + slot_place, (0, -rows_here % LANES))
    small = types.SimpleNamespace(
        norm_in=norm_in, norm_moe=norm_moe, conv_w=conv_w, conv_b=conv_b, since=since, x_proj=jnp.swapaxes(x_proj, 1, 2),
        router=jnp.swapaxes(router, 1, 2),
        place=jnp.broadcast_to(place[None, :], (8, place.shape[0])),
    )
    weights = (w_in, w_out, w_up, w_down)
    scan_weights = (dt_proj, dt_bias, a_log, d_skip, spread_matrix())

    act, entry = tokens, first_block(z, 0, tokens, small, w_in)
    kept = []
    for l in range(layers):
        gated, ys, marks = scan_fwd(l, entry.xs, entry.zgate, entry.proj, since, *scan_weights)
        gated = gated.reshape(lanes, rows_here, channels)
        if l + 1 < layers:
            out = middle_block(z, l, act, gated, small, weights)
            kept.append((act, entry, gated, ys, marks, out))
            act, entry = out.following, out
        else:
            turn = turn_block(z, l, act, gated, cotangent, small, weights)
            kept.append((act, entry, gated, ys, marks, turn))
    result, above = turn.following, turn
    collected = []
    for l in reversed(range(layers)):
        act, entry, gated, ys, marks, _ = kept[l]
        gxs, gzg, gpart, gdtw, gdtb, galog, gskip, *large_ones = scan_bwd(
            l, entry.xs, entry.zgate, entry.proj, since, ys, above.ggated.reshape(z.total, channels), marks, *scan_weights,
            beside=upper_outputs(z, layers, collected[-1]) if l == 0 else None)
        back = dict(gpart=gpart, gxs=gxs, gzg=gzg, b_conv=entry.conv, b_xs=entry.xs, b_whole=entry.whole, b_act=act, b_gmid=above.gmid,
                    b_gwout=above.gwout, b_gshare=above.gshare, gdtw=gdtw, gdtb=gdtb, galog=galog, gskip=gskip)
        grads = (above.gup, above.gdown)
        if l > 0:
            _, _, below_gated, _, _, below = kept[l - 1]
            forward = dict(gated=below_gated, chance=below.chance, choose=below.choose, into=below.into, slots=below.slots, hidden=below.hidden,
                           active=below.active, picked=below.picked, middle=below.middle)
            above = (down_block if z.slots <= 256 else down_blocks)(z, l, back, forward, small, weights)
            prior = above.gnorm
            collected.append((above.early, above.late, above.share, *grads))
        else:
            end = last_block(z, back, prior, small, w_in)
            collected.append((end.early, end.late, end.share, *grads))
    collected = collected[::-1]
    at, till = early_rows(width, experts), late_rows(width)

    return final_block(z, result, end.up, end.gnorm, collected, large_ones)


def solution(mesh):
    return jax.shard_map(
        on_device,
        mesh=mesh,
        in_specs=(
            P(("dp", "mp"), None),
            P(("dp", "mp"), None),
            P("dp", None),
            P(("dp", "mp")),
            P(("dp", "mp")),
            P(),
            P(None, None, None, "mp"),
            P(None, None, "mp"),
            P(None, "mp"),
            P(None, "mp", None),
            P(None, None, "mp"),
            P(None, "mp"),
            P(None, None, "mp"),
            P(None, "mp"),
            P(None, "mp", None),
            P(),
            P(),
            P(None, "dp", None, "mp"),
            P(None, "dp", "mp", None),
        ),
        out_specs=(
            P(("dp", "mp"), None),
            P(("dp", "mp"), None),
            P(),
            P(None, None, None, "mp"),
            P(None, None, "mp"),
            P(None, "mp"),
            P(None, "mp", None),
            P(None, None, "mp"),
            P(None, "mp"),
            P(None, None, "mp"),
            P(None, "mp"),
            P(None, "mp", None),
            P(),
            P(),
            P(None, "dp", None, "mp"),
            P(None, "dp", "mp", None),
        ),
        check_vma=False,
    )
```

```python
import functools
import types

import jax
import jax.numpy as jnp
from jax import lax
from jax.experimental import pallas as pl
from jax.experimental.pallas import tpu as pltpu
from jax.sharding import PartitionSpec as P

STATE = 16
DT_RANK = 48
LANES = 128
CHUNK = 128
LOG2E = 1.4426950408889634
RESET = 1.0e6
PROJ = DT_RANK + 2 * STATE
CONV = 4
dt_most = 0.05
epsilon = 1e-05
highest = lax.Precision.HIGHEST
MESH = pl.DeviceIdType.MESH
F32, BF16 = jnp.float32, jnp.bfloat16


def sigmoid(v):
    return 1.0 / (1.0 + jnp.exp(-v))


def dot(a, b):
    return jnp.dot(a, b, preferred_element_type=F32)


def dot_nt(a, b):
    return lax.dot_general(a, b, (((1,), (1,)), ((), ())), preferred_element_type=F32)


def dot_tn(a, b):
    return lax.dot_general(a, b, (((0,), (0,)), ((), ())), preferred_element_type=F32)


def spread_matrix():
    rows = lax.broadcasted_iota(jnp.int32, (STATE, STATE * LANES), 0)
    cols = lax.broadcasted_iota(jnp.int32, (STATE, STATE * LANES), 1)
    return (rows == cols // LANES).astype(BF16)


def put(ref, value):
    for j in range(ref.shape[0]):
        ref[j] = value[:, j * LANES : (j + 1) * LANES]


def spread_rows(proj, spread, out_ref):
    wide = dot_tn(proj, spread)
    for n in range(STATE):
        out_ref[pl.ds(n, CHUNK, stride=STATE), :] = wide[:, n * LANES : (n + 1) * LANES]


def scan_fwd_kernel(l, xs_ref, zg_ref, proj_ref, since_ref, dtw_ref, dtb_ref, alog_ref, skip_ref, spread_ref,
                    gated_ref, ys_ref, hck_ref,
                    h_ref, dm_ref, dx_ref, bx_ref, cx_ref, yq_ref):
    groups = xs_ref.shape[1] // LANES

    @pl.when(pl.program_id(0) == 0)
    def _():
        h_ref[...] = jnp.zeros_like(h_ref)

    hck_ref[0] = h_ref[...]
    proj = proj_ref[...]
    xs = xs_ref[...]
    delta = dt_most * sigmoid(dot_tn(proj[:DT_RANK], dtw_ref[l]) + dtb_ref[l : l + 1, :])
    put(dm_ref, delta + RESET * (since_ref[...] == 0).astype(F32))
    put(dx_ref, delta * xs)
    spread_rows(proj[DT_RANK : DT_RANK + STATE], spread_ref[...], bx_ref)
    spread_rows(proj[DT_RANK + STATE :], spread_ref[...], cx_ref)
    rate = -LOG2E * jnp.exp(alog_ref[l])
    rates = [rate[:, j * LANES : (j + 1) * LANES] for j in range(groups)]

    def step(g, hs):
        hs = list(hs)
        t0 = pl.multiple_of(g * 32, 32)
        for i in range(32):
            t = t0 + i
            r0 = pl.multiple_of(t * STATE, STATE)
            b = bx_ref[pl.ds(r0, STATE), :]
            c = cx_ref[pl.ds(r0, STATE), :]
            q0 = pl.multiple_of(t * 8, 8)
            for j in range(groups):
                lanes = slice(j * LANES, (j + 1) * LANES)
                dec = jnp.exp2(dm_ref[j, pl.ds(t, 1), :] * rates[j])
                hs[j] = dec * hs[j] + dx_ref[j, pl.ds(t, 1), :] * b
                q = c * hs[j]
                yq_ref[j, pl.ds(q0, 8), :] = q[:8] + q[8:]
        return tuple(hs)

    hs = lax.fori_loop(0, CHUNK // 32, step, tuple(h_ref[:, j * LANES : (j + 1) * LANES] for j in range(groups)))
    for j in range(groups):
        h_ref[:, j * LANES : (j + 1) * LANES] = hs[j]
    zg = zg_ref[...]
    for j in range(groups):
        lanes = slice(j * LANES, (j + 1) * LANES)
        y = skip_ref[l : l + 1, lanes] * xs[:, lanes]
        for k in range(8):
            y = y + yq_ref[j, pl.ds(k, CHUNK, stride=8), :]
        ys_ref[:, lanes] = y
        z = zg[:, lanes]
        gated_ref[:, lanes] = (y * z * sigmoid(z)).astype(BF16)


def scan_fwd(l, xs, zg, proj, since, dtw, dtb, alog, skip, spread):
    rows, ch = xs.shape
    steps = rows // CHUNK
    row = lambda w: pl.BlockSpec((CHUNK, w), lambda i: (i, 0))
    full = lambda s: pl.BlockSpec(s, lambda i: (0,) * len(s))
    return pl.pallas_call(
        functools.partial(scan_fwd_kernel, l),
        grid=(steps,),
        out_shape=[
            jax.ShapeDtypeStruct((rows, ch), BF16),
            jax.ShapeDtypeStruct((rows, ch), F32),
            jax.ShapeDtypeStruct((steps, STATE, ch), F32),
        ],
        in_specs=[row(ch), row(ch), pl.BlockSpec((PROJ, CHUNK), lambda i: (0, i)), row(1)]
        + [full(v.shape) for v in (dtw, dtb, alog, skip, spread)],
        out_specs=[row(ch), row(ch), pl.BlockSpec((1, STATE, ch), lambda i: (i, 0, 0))],
        scratch_shapes=[
            pltpu.VMEM((STATE, ch), F32),
            pltpu.VMEM((ch // LANES, CHUNK, LANES), F32),
            pltpu.VMEM((ch // LANES, CHUNK, LANES), F32),
            pltpu.VMEM((CHUNK * STATE, LANES), F32),
            pltpu.VMEM((CHUNK * STATE, LANES), F32),
            pltpu.VMEM((ch // LANES, CHUNK * 8, LANES), F32),
        ],
        compiler_params=pltpu.CompilerParams(vmem_limit_bytes=60 << 20),
        name="scan_fwd",
    )(xs, zg, proj, since, dtw, dtb, alog, skip, spread)


def scan_bwd_kernel(l, xs_ref, zg_ref, proj_ref, since_ref, ys_ref, gg_ref, hck_ref, dtw_ref, dtb_ref, alog_ref, skip_ref, spread_ref,
                    gxs_ref, gzg_ref, gproj_ref, gdtw_ref, gdtb_ref, galog_ref, gskip_ref,
                    a_ref, dm_ref, dx_ref, dl_ref, gy_ref, bx_ref, cx_ref, h_ref, dec_ref, pq_ref, gq_ref, gb_ref, gc_ref):
    groups = xs_ref.shape[1] // LANES
    cols = [slice(j * LANES, (j + 1) * LANES) for j in range(groups)]

    @pl.when(pl.program_id(0) == 0)
    def _():
        a_ref[...] = jnp.zeros_like(a_ref)
        gdtw_ref[...] = jnp.zeros_like(gdtw_ref)
        gdtb_ref[...] = jnp.zeros_like(gdtb_ref)
        galog_ref[...] = jnp.zeros_like(galog_ref)
        gskip_ref[...] = jnp.zeros_like(gskip_ref)

    proj = proj_ref[...]
    xs = xs_ref[...]
    delta = dt_most * sigmoid(dot_tn(proj[:DT_RANK], dtw_ref[l]) + dtb_ref[l : l + 1, :])
    put(dl_ref, delta)
    put(dm_ref, delta + RESET * (since_ref[...] == 0).astype(F32))
    put(dx_ref, delta * xs)
    zg = zg_ref[...]
    sz = sigmoid(zg)
    gg = gg_ref[...]
    gy = gg * (zg * sz)
    put(gy_ref, gy)
    gzg_ref[...] = (gg * ys_ref[...] * (sz * (1.0 + zg * (1.0 - sz)))).astype(BF16)
    gskip_ref[...] += jnp.sum(gy * xs, axis=0, keepdims=True)
    spread_rows(proj[DT_RANK : DT_RANK + STATE], spread_ref[...], bx_ref)
    spread_rows(proj[DT_RANK + STATE :], spread_ref[...], cx_ref)
    rate = -jnp.exp(alog_ref[l])
    rates2 = [LOG2E * rate[:, c] for c in cols]
    rates = [rate[:, c] for c in cols]

    for j in range(groups):
        h_ref[j, :STATE, :] = hck_ref[0][:, cols[j]]

    def again(g, hs):
        hs = list(hs)
        t0 = pl.multiple_of(g * 32, 32)
        for i in range(32):
            t = t0 + i
            r0 = pl.multiple_of(t * STATE, STATE)
            r1 = pl.multiple_of(t * STATE + STATE, STATE)
            b = bx_ref[pl.ds(r0, STATE), :]
            for j in range(groups):
                dec = jnp.exp2(dm_ref[j, pl.ds(t, 1), :] * rates2[j])
                hs[j] = dec * hs[j] + dx_ref[j, pl.ds(t, 1), :] * b
                dec_ref[j, pl.ds(r0, STATE), :] = dec
                h_ref[j, pl.ds(r1, STATE), :] = hs[j]
        return tuple(hs)

    last = lax.fori_loop(0, CHUNK // 32, again, tuple(hck_ref[0][:, c] for c in cols))

    def back(g, carry):
        carry = [list(c) for c in carry]
        aa, hs, acc = carry
        t0 = pl.multiple_of(CHUNK - 32 - g * 32, 32)
        for i in reversed(range(32)):
            t = t0 + i
            r0 = pl.multiple_of(t * STATE, STATE)
            q0 = pl.multiple_of(t * 8, 8)
            b = bx_ref[pl.ds(r0, STATE), :]
            c = cx_ref[pl.ds(r0, STATE), :]
            gb, gc = None, None
            for j in range(groups):
                gyj = gy_ref[j, pl.ds(t, 1), :]
                a = c * gyj + aa[j]
                dec = dec_ref[j, pl.ds(r0, STATE), :]
                before = h_ref[j, pl.ds(r0, STATE), :]
                carry_a = dec * a
                p = carry_a * before * rates[j]
                ab = a * b
                pq_ref[j, pl.ds(q0, 8), :] = p[:8] + p[8:]
                gq_ref[j, pl.ds(q0, 8), :] = ab[:8] + ab[8:]
                acc[j] = acc[j] + p * dl_ref[j, pl.ds(t, 1), :]
                gbj = a * dx_ref[j, pl.ds(t, 1), :]
                gcj = gyj * hs[j]
                gb = gbj if gb is None else gb + gbj
                gc = gcj if gc is None else gc + gcj
                aa[j] = carry_a
                hs[j] = before
            gb_ref[pl.ds(r0, STATE), :] = gb
            gc_ref[pl.ds(r0, STATE), :] = gc
        return tuple(tuple(c) for c in carry)

    aa, _, acc = lax.fori_loop(
        0, CHUNK // 32, back,
        (tuple(a_ref[:, c] for c in cols), last, tuple(jnp.zeros((STATE, LANES), F32) for _ in cols)))
    for j in range(groups):
        a_ref[:, cols[j]] = aa[j]
        galog_ref[:, cols[j]] += acc[j]

    skip = skip_ref[l : l + 1, :]
    gdts = []
    for j in range(groups):
        psum = pq_ref[j, pl.ds(0, CHUNK, stride=8), :]
        gsum = gq_ref[j, pl.ds(0, CHUNK, stride=8), :]
        for k in range(1, 8):
            psum = psum + pq_ref[j, pl.ds(k, CHUNK, stride=8), :]
            gsum = gsum + gq_ref[j, pl.ds(k, CHUNK, stride=8), :]
        dl = delta[:, cols[j]]
        gdelta = psum + xs[:, cols[j]] * gsum
        gxs_ref[:, cols[j]] = dl * gsum + skip[:, cols[j]] * gy[:, cols[j]]
        gdts.append(gdelta * dl * (1.0 - dl * (1.0 / dt_most)))
    gdt = jnp.concatenate(gdts, axis=1)
    gdtb_ref[...] += jnp.sum(gdt, axis=0, keepdims=True)
    gdt_low = gdt.astype(BF16)
    gdtw_ref[...] += dot(proj[:DT_RANK], gdt_low)
    gproj_ref[:DT_RANK, :] = dot_nt(dtw_ref[l], gdt_low)
    wide_b = jnp.concatenate([gb_ref[pl.ds(n, CHUNK, stride=STATE), :].astype(BF16) for n in range(STATE)], axis=1)
    gproj_ref[DT_RANK : DT_RANK + STATE, :] = dot_nt(spread_ref[...], wide_b)
    wide_c = jnp.concatenate([gc_ref[pl.ds(n, CHUNK, stride=STATE), :].astype(BF16) for n in range(STATE)], axis=1)
    gproj_ref[DT_RANK + STATE :, :] = dot_nt(spread_ref[...], wide_c)


def scan_bwd(l, xs, zg, proj, since, ys, gg, hck, dtw, dtb, alog, skip, spread, beside=None):
    work, far, made, room = beside or (None, [], [], [])
    rows, ch = xs.shape
    steps = rows // CHUNK
    row = lambda w: pl.BlockSpec((CHUNK, w), lambda i: (steps - 1 - i, 0))
    full = lambda s: pl.BlockSpec(s, lambda i: (0,) * len(s))
    big = lambda: pltpu.VMEM((CHUNK * STATE, LANES), F32)
    g = ch // LANES

    def kernel(*refs):
        cuts = [12, len(far), 7, len(made), 13, len(room)]
        at = [sum(cuts[:i]) for i in range(7)]
        ins, xin, outs, xout, held, xheld = (refs[at[i] : at[i + 1]] for i in range(6))
        if work is not None:
            work(steps, xin, xout, xheld)
        scan_bwd_kernel(l, *ins, *outs, *held)

    anywhere = pl.BlockSpec(memory_space=pl.ANY)
    return pl.pallas_call(
        kernel,
        grid=(steps,),
        out_shape=[
            jax.ShapeDtypeStruct((rows, ch), F32),
            jax.ShapeDtypeStruct((rows, ch), BF16),
            jax.ShapeDtypeStruct((PROJ, rows), F32),
            jax.ShapeDtypeStruct((DT_RANK, ch), F32),
            jax.ShapeDtypeStruct((1, ch), F32),
            jax.ShapeDtypeStruct((STATE, ch), F32),
            jax.ShapeDtypeStruct((1, ch), F32),
            *made,
        ],
        in_specs=[row(ch), row(ch), pl.BlockSpec((PROJ, CHUNK), lambda i: (0, steps - 1 - i)), row(1), row(ch), row(ch),
                  pl.BlockSpec((1, STATE, ch), lambda i: (steps - 1 - i, 0, 0))]
        + [full(v.shape) for v in (dtw, dtb, alog, skip, spread)]
        + [anywhere] * len(far),
        out_specs=[row(ch), row(ch), pl.BlockSpec((PROJ, CHUNK), lambda i: (0, steps - 1 - i)), full((DT_RANK, ch)), full((1, ch)), full((STATE, ch)), full((1, ch))]
        + [anywhere] * len(made),
        scratch_shapes=[
            pltpu.VMEM((STATE, ch), F32),
            pltpu.VMEM((ch // LANES, CHUNK, LANES), F32),
            pltpu.VMEM((ch // LANES, CHUNK, LANES), F32),
            pltpu.VMEM((ch // LANES, CHUNK, LANES), F32),
            pltpu.VMEM((ch // LANES, CHUNK, LANES), F32),
            big(), big(),
            pltpu.VMEM((g, CHUNK * STATE + STATE, LANES), F32),
            pltpu.VMEM((g, CHUNK * STATE, LANES), F32),
            pltpu.VMEM((g, CHUNK * 8, LANES), F32),
            pltpu.VMEM((g, CHUNK * 8, LANES), F32),
            big(), big(),
            *room,
        ],
        compiler_params=pltpu.CompilerParams(vmem_limit_bytes=60 << 20),
        name="scan_bwd",
    )(xs, zg, proj, since, ys, gg, hck, dtw, dtb, alog, skip, spread, *far)


def rms_inverse(values):
    return lax.rsqrt(jnp.mean(values * values, axis=-1, keepdims=True) + epsilon)


def norm_back(values, inverse, gain, grad):
    scaled = grad * gain
    pulled = inverse * scaled - values * (inverse * inverse * inverse) * jnp.mean(scaled * values, axis=-1, keepdims=True)
    return pulled, jnp.sum(grad * values * inverse, axis=0, keepdims=True)


GELU_A, GELU_B = 0.7978845608028654, 0.044715


def gelu(v):
    return 0.5 * v * (1.0 + jnp.tanh(GELU_A * (v + GELU_B * v * v * v)))


def gelu_slope(v):
    square = v * v
    t = jnp.tanh(GELU_A * v * (1.0 + GELU_B * square))
    return 0.5 * (1.0 + t) + 0.5 * v * (1.0 - t * t) * GELU_A * (1.0 + 3.0 * GELU_B * square)


def by_lane(m, values):
    picked = jnp.int32(values[0])
    for k in range(1, len(values)):
        picked = jnp.where(m == k, jnp.int32(values[k]), picked)
    return picked


def nearest_first(m, lanes):
    orders = [sorted((s for s in range(lanes) if s != k), key=lambda s: (abs(s - k), s)) for k in range(lanes)]
    return [by_lane(m, [order[i] for order in orders]) for i in range(lanes - 1)]


def chain_order(m, lanes):
    def due(k, s):
        return (lanes - 1 - s) + k if s > k else s + (lanes - 1 - k)

    orders = [sorted((s for s in range(lanes) if s != k), key=lambda s: (due(k, s), s)) for k in range(lanes)]
    return [by_lane(m, [order[i] for order in orders]) for i in range(lanes - 1)]


def greet(d, m, lanes, peers, across):
    barrier = pltpu.get_barrier_semaphore()
    if across:
        for k in range(1, lanes):
            pl.semaphore_signal(barrier, inc=1, device_id=(d, lax.rem(m + k, lanes)), device_id_type=MESH)
        for k in range(1, peers):
            pl.semaphore_signal(barrier, inc=1, device_id=(lax.rem(d + k, peers), m), device_id_type=MESH)
        pl.semaphore_wait(barrier, lanes + peers - 2)
    else:

        @pl.when(m > 0)
        def _():
            pl.semaphore_signal(barrier, inc=1, device_id=(d, m - 1), device_id_type=MESH)

        @pl.when(m < lanes - 1)
        def _():
            pl.semaphore_signal(barrier, inc=1, device_id=(d, m + 1), device_id_type=MESH)

        pl.semaphore_wait(barrier, jnp.where(m > 0, 1, 0) + jnp.where(m < lanes - 1, 1, 0))


class LineGather:
    def __init__(self, buf, send, recv, d, m, lanes):
        self.buf, self.send, self.recv, self.d, self.m, self.lanes = buf, send, recv, d, m, lanes
        self.order = nearest_first(m, lanes)

    def copy(self, s, up):
        return pltpu.make_async_remote_copy(
            src_ref=self.buf.at[s], dst_ref=self.buf.at[s], send_sem=self.send.at[0 if up else 1, s],
            recv_sem=self.recv.at[s], device_id=(self.d, self.m + 1 if up else self.m - 1), device_id_type=MESH,
        )

    def start(self):
        @pl.when(self.m < self.lanes - 1)
        def _():
            self.copy(self.m, True).start()

        @pl.when(self.m > 0)
        def _():
            self.copy(self.m, False).start()

    def arrive(self, i):
        s, m = self.order[i], self.m
        self.copy(s, True).wait_recv()

        @pl.when((s < m) & (m < self.lanes - 1))
        def _():
            self.copy(s, True).start()

        @pl.when((s > m) & (m > 0))
        def _():
            self.copy(s, False).start()

        return s

    def finish(self):
        for s in range(self.lanes):

            @pl.when((s <= self.m) & (self.m < self.lanes - 1))
            def _():
                self.copy(s, True).wait_send()

            @pl.when((s >= self.m) & (self.m > 0))
            def _():
                self.copy(s, False).wait_send()


PIECES = 1


class LineReduce:
    def __init__(self, stage, inbox, send, recv, d, m, lanes):
        self.stage, self.inbox, self.send, self.recv = stage, inbox, send, recv
        self.d, self.m, self.lanes = d, m, lanes
        self.rows = stage.shape[1] // PIECES
        self.order = chain_order(m, lanes)
        self.middle = jnp.logical_and(m > 0, m < lanes - 1)
        self.at_end = jnp.logical_not(self.middle)

    def piece(self, p):
        return pl.ds(p * self.rows, self.rows)

    def copy(self, s, p):
        up = s > self.m
        side = jnp.where(up, 0, 1)
        return pltpu.make_async_remote_copy(
            src_ref=self.stage.at[s, self.piece(p)], dst_ref=self.inbox.at[side, s, self.piece(p)], send_sem=self.send.at[s, p],
            recv_sem=self.recv.at[side, s, p], device_id=(self.d, jnp.where(up, self.m + 1, self.m - 1)), device_id_type=MESH,
        )

    def push_first(self, s, term):
        self.stage[s] = term.astype(BF16)
        for p in range(PIECES):
            self.copy(s, p).start()

    def push_on(self, s, p, term):
        side = jnp.where(s > self.m, 0, 1)
        self.copy(s, p).wait_recv()
        self.stage[s, self.piece(p)] = (term + self.inbox[side, s, self.piece(p)].astype(F32)).astype(BF16)
        self.copy(s, p).start()

    def push(self, s, term):
        @pl.when(self.at_end)
        def _():
            self.push_first(s, term)

        @pl.when(self.middle)
        def _():
            for p in range(PIECES):
                self.push_on(s, p, term[p * self.rows : (p + 1) * self.rows])

    def total(self, own_ref):
        m = self.m

        def add(side):
            for p in range(PIECES):
                pltpu.make_async_remote_copy(
                    src_ref=self.stage.at[m, self.piece(p)], dst_ref=self.inbox.at[side, m, self.piece(p)], send_sem=self.send.at[m, p],
                    recv_sem=self.recv.at[side, m, p], device_id=(self.d, m), device_id_type=MESH,
                ).wait_recv()
            own_ref[...] += self.inbox[side, m].astype(F32)

        @pl.when(m > 0)
        def _():
            add(0)

        @pl.when(m < self.lanes - 1)
        def _():
            add(1)

    def finish(self):
        for s in self.order:
            for p in range(PIECES):
                self.copy(s, p).wait_send()


def reduce_scratch(lanes, rows, width):
    return [
        pltpu.VMEM((lanes, rows, width), BF16),
        pltpu.VMEM((2, lanes, rows, width), BF16),
        dma(lanes, PIECES), dma(2, lanes, PIECES),
    ]


PARTS = 3


def line_sum(part, stage, inbox, send, recv, out, d, m, lanes, between=lambda: None, produce=lambda b: None):
    width = part.shape[1] // PARTS

    def copy(side, b):
        return pltpu.make_async_remote_copy(
            src_ref=stage.at[side, b], dst_ref=inbox.at[side, b], send_sem=send.at[side, b], recv_sem=recv.at[side, b],
            device_id=(d, m + 1 if side == 0 else m - 1), device_id_type=MESH,
        )

    def step(side, b):
        has_source = m > 0 if side == 0 else m < lanes - 1
        has_target = m < lanes - 1 if side == 0 else m > 0
        cols = slice(b * width, (b + 1) * width)

        @pl.when(has_source)
        def _():
            copy(side, b).wait_recv()

        @pl.when(jnp.logical_not(has_source))
        def _():
            inbox[side, b] = jnp.zeros(inbox.shape[2:], BF16)

        @pl.when(has_target)
        def _():
            stage[side, b] = (part[:, cols] + inbox[side, b].astype(F32)).astype(BF16)
            copy(side, b).start()

    low = 2 * m < lanes

    def either(side, b):
        @pl.when(low)
        def _():
            step(side, b)

        @pl.when(jnp.logical_not(low))
        def _():
            step(1 - side, b)

    for b in range(PARTS):
        produce(b)
        either(0, b)
    between()
    for b in range(PARTS):
        either(1, b)
    for b in range(PARTS):
        cols = slice(b * width, (b + 1) * width)
        out[:, cols] = (part[:, cols] + inbox[0, b].astype(F32) + inbox[1, b].astype(F32)).astype(BF16)

    def finish():
        for b in range(PARTS):

            @pl.when(m < lanes - 1)
            def _():
                copy(0, b).wait_send()

            @pl.when(m > 0)
            def _():
                copy(1, b).wait_send()

    return finish


def vmem(count):
    return [pl.BlockSpec(memory_space=pltpu.VMEM)] * count


def f32(*shape):
    return jax.ShapeDtypeStruct(shape, F32)


def bf16(*shape):
    return jax.ShapeDtypeStruct(shape, BF16)


def dma(*shape):
    return pltpu.SemaphoreType.DMA(shape)


def hbm(count):
    return [pl.BlockSpec(memory_space=pl.ANY)] * count


def fetch(pairs, sem):
    copies = [pltpu.make_async_copy(src, dst, sem.at[i]) for i, (src, dst) in enumerate(pairs)]
    for copy in copies:
        copy.start()
    return copies


def params(cid, limit=58):
    return pltpu.CompilerParams(collective_id=cid, has_side_effects=True, vmem_limit_bytes=limit << 20)


CONV_ROWS = 128
HEAD = 8


def conv_window(padded_ref, since_ref, taps, bias, base):
    window = padded_ref[pl.ds(base, CONV_ROWS + HEAD), :]
    since = since_ref[pl.ds(base, CONV_ROWS), :]
    shifted = [window[HEAD:]]
    for j in range(1, CONV):
        shifted.append(window[HEAD - j : HEAD - j + CONV_ROWS] * (since >= j).astype(F32))
    pre = bias
    for j in range(CONV):
        pre = pre + taps[CONV - 1 - j : CONV - j, :] * shifted[j]
    return pre, shifted


class Experts:
    def __init__(self, d, m, lanes, peers, into_ref, rows_ref, pack_ref, slots_ref, part_ref, back_ref, stage_ref, inbox_ref,
                 gsend, grecv, dsend, drecv, bsend, brecv, rsend, rrecv):
        self.d, self.m, self.lanes, self.peers = d, m, lanes, peers
        self.rows, self.into, self.pack, self.slots, self.part, self.back = rows_ref, into_ref, pack_ref, slots_ref, part_ref, back_ref
        self.stage, self.inbox = stage_ref, inbox_ref
        self.dsend, self.drecv, self.bsend, self.brecv, self.rsend, self.rrecv = dsend, drecv, bsend, brecv, rsend, rrecv
        self.sets = rows_ref.shape[1]
        self.cap = pack_ref.shape[2] // self.sets
        self.width = rows_ref.shape[3]
        self.gather = LineGather(rows_ref, gsend, grecv, d, m, lanes)

    def slot_rows(self, ref, s, i):
        return ref[s, :, i * self.cap : (i + 1) * self.cap, :].reshape(self.peers * self.cap, self.width)

    def set_slot_rows(self, ref, s, i, value):
        ref[s, :, i * self.cap : (i + 1) * self.cap, :] = value.reshape(self.peers, self.cap, self.width)

    def hop(self, src, dst, send, recv, s, k):
        other = lax.rem(self.d + k, self.peers)
        return pltpu.make_async_remote_copy(
            src_ref=src.at[s, other], dst_ref=dst.at[s, self.d], send_sem=send.at[s, k - 1],
            recv_sem=recv.at[s, k - 1], device_id=(other, self.m), device_id_type=MESH,
        )

    def across(self, src, dst, send, recv, s):
        for k in range(1, self.peers):
            self.hop(src, dst, send, recv, s, k).start()
        dst[s, self.d] = src[s, self.d]

    def dispatch(self, s):
        for i in range(self.sets):
            self.set_slot_rows(self.pack, s, i, dot(self.into[s], self.rows[s, i]).astype(BF16))
        self.across(self.pack, self.slots, self.dsend, self.drecv, s)

    def answer(self, s, expert):
        for k in range(1, self.peers):
            self.hop(self.pack, self.slots, self.dsend, self.drecv, s, k).wait_recv()
        for i, value in enumerate(expert(s, [self.slot_rows(self.slots, s, i) for i in range(self.sets)])):
            self.set_slot_rows(self.part, s, i, value.astype(BF16))
        self.across(self.part, self.back, self.bsend, self.brecv, s)

    def home(self, s):
        return pltpu.make_async_remote_copy(
            src_ref=self.stage.at[s], dst_ref=self.inbox.at[self.m], send_sem=self.rsend.at[s], recv_sem=self.rrecv.at[self.m],
            device_id=(self.d, s), device_id_type=MESH,
        )

    def combine(self, s):
        for k in range(1, self.peers):
            self.hop(self.part, self.back, self.bsend, self.brecv, s, k).wait_recv()
        return [dot_tn(self.into[s], self.slot_rows(self.back, s, i)) for i in range(self.sets)]

    def combine_away(self, s):
        for i, value in enumerate(self.combine(s)):
            self.stage[s, i] = value.astype(BF16)
        self.home(s).start()

    def steps(self, expert, own_ref):
        one, two, three = self.gather.order
        self.dispatch(self.m)
        yield
        self.gather.arrive(0)
        self.dispatch(one)
        yield
        self.gather.arrive(1)
        self.dispatch(two)
        self.answer(one, expert)
        yield
        self.gather.arrive(2)
        self.dispatch(three)
        self.answer(two, expert)
        self.combine_away(one)
        yield
        self.answer(three, expert)
        self.combine_away(two)
        yield
        self.combine_away(three)
        yield
        self.answer(self.m, expert)
        yield
        for i, value in enumerate(self.combine(self.m)):
            own_ref[i] = value
        yield

    def settle(self, own_ref):
        for s in self.gather.order:
            pltpu.make_async_remote_copy(
                src_ref=self.stage.at[s], dst_ref=self.inbox.at[s], send_sem=self.rsend.at[s], recv_sem=self.rrecv.at[s],
                device_id=(self.d, s), device_id_type=MESH,
            ).wait_recv()
            own_ref[...] += self.inbox[s].astype(F32)

    def run(self, expert, own_ref, meanwhile):
        self.gather.start()
        for _ in self.steps(expert, own_ref):
            pass
        meanwhile()
        self.settle(own_ref)

    def finish(self):
        self.gather.finish()
        order = [self.m, *self.gather.order]
        for s in order:
            for k in range(1, self.peers):
                self.hop(self.pack, self.slots, self.dsend, self.drecv, s, k).wait_send()
                self.hop(self.part, self.back, self.bsend, self.brecv, s, k).wait_send()
        for s in order[1:]:
            self.home(s).wait_send()


def large(v):
    return v.size * v.dtype.itemsize >= 1 << 17


class Refs(types.SimpleNamespace):
    def need(self, *refs):
        for ref in refs:
            if id(ref) in self.coming:
                self.coming.pop(id(ref)).wait()

    def ship(self, *refs):
        for ref in refs:
            self.gone.append(self.going.pop(id(ref)))
            self.gone[-1].start()


def launch(name, cid, body, inputs, far, outputs, scratch, limit=58):
    near = {k: v for k, v in inputs.items() if not large(v)}
    lazy = {k: v for k, v in inputs.items() if large(v)}
    prompt = {k: v for k, v in outputs.items() if not large(v)}
    late = {k: v for k, v in outputs.items() if large(v)}
    buffers = {k: pltpu.VMEM(v.shape, v.dtype) for k, v in {**lazy, **late}.items()}
    away = [k + "_far" for k in (*lazy, *late)]
    names = [*near, *away[: len(lazy)], *far, *prompt, *away[len(lazy) :], *scratch, *buffers, "moves"]

    def kernel(*refs):
        r = Refs(**dict(zip(names, refs)))
        get = lambda k: getattr(r, k)
        r.gone = []
        r.coming = {id(get(k)): pltpu.make_async_copy(get(k + "_far"), get(k), r.moves.at[i]) for i, k in enumerate(lazy)}
        r.going = {id(get(k)): pltpu.make_async_copy(get(k), get(k + "_far"), r.moves.at[len(lazy) + i]) for i, k in enumerate(late)}
        for copy in r.coming.values():
            copy.start()
        body(r)
        r.need(*map(get, lazy))
        r.ship(*(get(k) for k in late if id(get(k)) in r.going))
        for copy in r.gone:
            copy.wait()

    results = pl.pallas_call(
        kernel,
        out_shape=[*prompt.values(), *late.values()],
        in_specs=vmem(len(near)) + hbm(len(lazy) + len(far)),
        out_specs=vmem(len(prompt)) + hbm(len(late)),
        scratch_shapes=[*scratch.values(), *buffers.values(), dma(max(1, len(lazy) + len(late)))],
        compiler_params=params(cid, limit),
        name=name,
    )(*near.values(), *lazy.values(), *far.values())
    return types.SimpleNamespace(**dict(zip([*prompt, *late], results)))


def convolution(small):
    return dict(norm_in=small.norm_in, conv_w=small.conv_w, conv_b=small.conv_b, since=small.since, x_proj=small.x_proj)


def routing(small):
    return dict(norm_moe=small.norm_moe, router=small.router)


def flat(ref):
    return ref[...].reshape(ref.shape[0] * ref.shape[1], ref.shape[2])


def gate_of(chance, choose):
    return jnp.sum(chance * choose, axis=1, keepdims=True)


class Sizes:
    def __init__(self, lanes, peers, experts, cap, rows, width, channels, hidden):
        self.lanes, self.peers, self.experts, self.cap = lanes, peers, experts, cap
        self.rows, self.width, self.channels, self.hidden = rows, width, channels, hidden
        self.total, self.slots = rows * lanes, experts * cap


def in_outputs(z):
    return dict(whole=bf16(z.lanes, z.rows, z.width), conv=f32(z.total + HEAD, z.channels), zgate=f32(z.total, z.channels),
                xs=f32(z.total, z.channels), proj=bf16(PROJ, z.total))


def sum_scratch(z):
    halves = pltpu.VMEM((2, PARTS, PROJ, z.total // PARTS), BF16)
    return dict(sum_stage=halves, sum_inbox=halves, sum_send=dma(2, PARTS), sum_recv=dma(2, PARTS))


def in_scratch(z):
    return dict(part=pltpu.VMEM((PROJ, z.total), F32), u_send=dma(2, z.lanes), u_recv=dma(z.lanes), **sum_scratch(z))


def in_stage(z, r, l, act, weights):
    d, m = lax.axis_index("dp"), lax.axis_index("mp")
    r.whole[m] = (act * rms_inverse(act) * r.norm_in[l : l + 1, :]).astype(BF16)
    gather = LineGather(r.whole, r.u_send, r.u_recv, d, m, z.lanes)
    gather.start()
    r.conv[:HEAD, :] = jnp.zeros((HEAD, z.channels), F32)
    weights.wait()

    def project(s):
        u = r.whole[s]
        r.conv[pl.ds(pl.multiple_of(s * z.rows + HEAD, 8), z.rows), :] = dot(u, r.win[0])
        r.zgate[pl.ds(pl.multiple_of(s * z.rows, 8), z.rows), :] = dot(u, r.win[1])

    project(m)
    for i in range(z.lanes - 1):
        project(gather.arrive(i))
    r.ship(r.conv, r.zgate, r.whole)
    taps, bias = r.conv_w[l], r.conv_b[l : l + 1, :]

    def conv_step(c, carry):
        base = pl.multiple_of(c * CONV_ROWS, CONV_ROWS)
        pre, _ = conv_window(r.conv, r.since, taps, bias, base)
        xs = pre * sigmoid(pre)
        r.xs[pl.ds(base, CONV_ROWS), :] = xs
        r.part[:, pl.ds(base, CONV_ROWS)] = dot_nt(r.x_proj[l], xs.astype(BF16))
        return carry

    chunks = z.total // CONV_ROWS // PARTS

    def produce(b):
        lax.fori_loop(b * chunks, (b + 1) * chunks, conv_step, 0)

    finish = line_sum(r.part, r.sum_stage, r.sum_inbox, r.sum_send, r.sum_recv, r.proj, d, m, z.lanes, lambda: r.ship(r.xs), produce)
    gather.finish()
    finish()


def first_block(z, l, act, small, w_in):
    def body(r):
        d, m = lax.axis_index("dp"), lax.axis_index("mp")
        (weights,) = fetch([(r.w_in.at[l], r.win)], r.fetched)
        greet(d, m, z.lanes, 0, False)
        r.need(r.act)
        in_stage(z, r, l, r.act[...].astype(F32), weights)

    inputs = dict(act=act, **convolution(small))
    return launch("mamba_in", 0, body, inputs, dict(w_in=w_in), in_outputs(z),
                  dict(win=pltpu.VMEM(w_in.shape[1:], BF16), fetched=dma(1), **in_scratch(z)))


def expert_refs(r):
    return (r.e_rows, r.e_pack, r.e_slots, r.e_part, r.e_back, r.e_stage, r.e_inbox, r.e_gs, r.e_gr, r.e_ds, r.e_dr, r.e_bs, r.e_br,
            r.e_rs, r.e_rr)


def expert_names(z, sets):
    across = pltpu.VMEM((z.lanes, z.peers, sets * z.cap, z.width), BF16)
    along = pltpu.VMEM((z.lanes, sets, z.rows, z.width), BF16)
    plane, line = dma(z.lanes, z.peers - 1), dma(z.lanes)
    return dict(
        e_rows=along, e_pack=across, e_slots=across, e_part=across, e_back=across, e_stage=along, e_inbox=along, e_gs=dma(2, z.lanes),
        e_gr=line, e_ds=plane, e_dr=plane, e_bs=plane, e_br=plane, e_rs=line, e_rr=line, e_own=pltpu.VMEM((sets, z.rows, z.width), F32))


def weight_scratch(wout, wup, wdown):
    return dict(wout=pltpu.VMEM(wout.shape[1:], BF16), wup=pltpu.VMEM(wup.shape[2:], BF16), wdown=pltpu.VMEM(wdown.shape[2:], BF16))


def out_scratch(z, place):
    stage, inbox, send, recv = reduce_scratch(z.lanes, z.rows, z.width)
    return dict(m_stage=stage, m_inbox=inbox, m_send=send, m_recv=recv, places=pltpu.VMEM((z.lanes, *place.shape), jnp.int32),
                p_send=dma(2, z.lanes), p_recv=dma(z.lanes), m_own=pltpu.VMEM((z.rows, z.width), F32))


def out_stage(z, r, l, wout):
    d, m = lax.axis_index("dp"), lax.axis_index("mp")
    r.places[m] = r.place[...]
    places = LineGather(r.places, r.p_send, r.p_recv, d, m, z.lanes)
    places.start()
    reduce = LineReduce(r.m_stage, r.m_inbox, r.m_send, r.m_recv, d, m, z.lanes)
    wout.wait()
    r.need(r.act, r.gated)
    for s in reduce.order:
        reduce.push(s, dot(r.gated[s], r.wout[...]))
    r.m_own[...] = r.act[...].astype(F32) + dot(r.gated[m], r.wout[...])

    def spread_places(s):
        numbers = lax.broadcasted_iota(jnp.int32, (z.slots, z.rows), 0)
        r.into[s] = (numbers == r.places[s][:1, : z.rows]).astype(F32).astype(BF16)

    spread_places(m)
    owner = lax.broadcasted_iota(jnp.int32, (z.slots, z.experts), 0) // z.cap == lax.broadcasted_iota(jnp.int32, (z.slots, z.experts), 1)
    r.choose[...] = dot_tn(r.into[m], owner.astype(F32).astype(BF16))
    for i in range(z.lanes - 1):
        spread_places(places.arrive(i))
    reduce.total(r.m_own)

    def finish():
        places.finish()
        reduce.finish()

    return finish


def chances(z, normed, table):
    logits = lax.dot_general(normed, table, (((1,), (1,)), ((), ())), precision=highest, preferred_element_type=F32)
    raised = jnp.exp(logits - jnp.max(logits, axis=1, keepdims=True))
    return raised / jnp.sum(raised, axis=1, keepdims=True)


def middle_block(z, l, act, gated, small, weights):
    def body(r):
        d, m = lax.axis_index("dp"), lax.axis_index("mp")
        wout, wup, wdown, win = fetch([(r.w_out.at[l], r.wout), (r.w_up.at[l, 0], r.wup), (r.w_down.at[l, 0], r.wdown),
                                       (r.w_in.at[l + 1], r.win)], r.fetched)
        greet(d, m, z.lanes, z.peers, True)
        finish = out_stage(z, r, l, wout)
        wup.wait()
        wdown.wait()
        middle = r.m_own[...]
        r.middle[...] = middle
        r.e_rows[m, 0] = (middle * rms_inverse(middle) * r.norm_moe[l : l + 1, :]).astype(BF16)
        moe = Experts(d, m, z.lanes, z.peers, r.into, *expert_refs(r))

        def expert(s, rows):
            r.slots[s] = rows[0]
            hidden = dot(rows[0], r.wup[...])
            r.hidden[s] = hidden.astype(BF16)
            active = gelu(hidden).astype(BF16)
            r.active[s] = active
            return [dot(active, r.wdown[...])]

        def meanwhile():
            finish()
            middle = r.middle[...]
            r.chance[...] = chances(z, middle * rms_inverse(middle) * r.norm_moe[l : l + 1, :], r.router[l])

        moe.run(expert, r.e_own, meanwhile)
        r.ship(r.into, r.middle, r.slots, r.hidden, r.active)
        picked = r.e_own[0].astype(BF16)
        r.picked[...] = picked
        following = r.middle[...] + gate_of(r.chance[...], r.choose[...]) * picked.astype(F32)
        r.following[...] = following
        r.ship(r.picked, r.following)
        in_stage(z, r, l + 1, following, win)
        moe.finish()

    w_in, w_out, w_up, w_down = weights
    slots = (z.lanes, z.slots)
    return launch(
        "middle", 1 + l, body, dict(act=act, gated=gated, place=small.place, **routing(small), **convolution(small)),
        dict(w_in=w_in, w_out=w_out, w_up=w_up, w_down=w_down),
        dict(middle=f32(z.rows, z.width), chance=f32(z.rows, z.experts), into=bf16(*slots, z.rows), slots=bf16(*slots, z.width),
             hidden=bf16(*slots, z.hidden), active=bf16(*slots, z.hidden), picked=bf16(z.rows, z.width), choose=f32(z.rows, z.experts), following=f32(z.rows, z.width),
             **in_outputs(z)),
        dict(win=pltpu.VMEM(w_in.shape[1:], BF16), fetched=dma(4), **weight_scratch(w_out, w_up, w_down), **out_scratch(z, small.place),
             **expert_names(z, 1), **in_scratch(z)))


def back_outputs(z):
    return dict(gmid=f32(z.rows, z.width), gup=f32(z.width, z.hidden), gdown=f32(z.hidden, z.width), ggated=f32(z.lanes, z.rows, z.channels),
                gwout=bf16(z.channels, z.width), gshare=f32(z.experts + 8, z.width))


def back_scratch(z):
    return dict(wide=pltpu.VMEM((z.lanes, z.rows, z.width), BF16), w_send=dma(2, z.lanes), w_recv=dma(z.lanes))


def route_back(z, r, l, upstream, middle, chance, choose, picked, returned):
    d, m = lax.axis_index("dp"), lax.axis_index("mp")
    gate = gate_of(chance, choose)
    inverse, gain = rms_inverse(middle), r.norm_moe[l : l + 1, :]
    grad_gate = jnp.sum(upstream * picked.astype(F32), axis=1, keepdims=True)
    grad_logit = gate * grad_gate * (choose - chance)
    grad_normed = returned.astype(BF16).astype(F32) + lax.dot_general(
        grad_logit, r.router[l], (((1,), (0,)), ((), ())), precision=highest, preferred_element_type=F32)
    pulled, grad_gain = norm_back(middle, inverse, gain, grad_normed)
    grad_middle = upstream + pulled
    r.gmid[...] = grad_middle
    r.ship(r.gmid)
    r.wide[m] = grad_middle.astype(BF16)
    gather = LineGather(r.wide, r.w_send, r.w_recv, d, m, z.lanes)
    gather.start()
    grad_router = lax.dot_general(
        grad_logit, middle * inverse * gain, (((0,), (0,)), ((), ())), precision=highest, preferred_element_type=F32)
    r.gshare[: z.experts, :] = grad_router
    r.gshare[z.experts :, :] = jnp.broadcast_to(grad_gain, (8, z.width))

    def gate_back(s):
        r.ggated[s] = dot_nt(r.wide[s], r.wout[...])

    gate_back(m)
    for i in range(z.lanes - 1):
        gate_back(gather.arrive(i))
    r.ship(r.ggated)
    r.need(r.gated)
    r.gwout[...] = dot_tn(flat(r.gated), flat(r.wide)).astype(BF16)
    gather.finish()


def turn_block(z, l, act, gated, cotangent, small, weights):
    def body(r):
        d, m = lax.axis_index("dp"), lax.axis_index("mp")
        wout, wup, wdown = fetch([(r.w_out.at[l], r.wout), (r.w_up.at[l, 0], r.wup), (r.w_down.at[l, 0], r.wdown)], r.fetched)
        greet(d, m, z.lanes, z.peers, True)
        finish = out_stage(z, r, l, wout)
        wup.wait()
        wdown.wait()
        middle = r.m_own[...]
        normed = middle * rms_inverse(middle) * r.norm_moe[l : l + 1, :]
        forth = Experts(d, m, z.lanes, z.peers, r.into, *expert_refs(r))
        back = Experts(d, m, z.lanes, z.peers, r.into, *(getattr(r, "f" + k[1:]) for k in list(expert_names(z, 1))[:-1]))
        r.e_rows[m, 0] = normed.astype(BF16)
        forth.gather.start()
        chance = chances(z, normed, r.router[l])
        r.chance[...] = chance
        r.need(r.cotangent)
        r.f_rows[m, 0] = (gate_of(chance, r.choose[...]) * r.cotangent[...].astype(F32)).astype(BF16)
        back.gather.start()

        def expert_forth(s, rows):
            active = gelu(dot(rows[0], r.wup[...])).astype(BF16)
            r.active[s] = active
            return [dot(active, r.wdown[...])]

        def expert_back(s, rows):
            slope = gelu_slope(dot(forth.slot_rows(forth.slots, s, 0), r.wup[...]))
            grad_hidden = (dot_nt(rows[0], r.wdown[...]) * slope).astype(BF16)
            r.ghid[s] = grad_hidden
            return [dot_nt(grad_hidden, r.wup[...])]

        for _ in zip(forth.steps(expert_forth, r.e_own), back.steps(expert_back, r.f_own)):
            pass
        finish()
        r.gdown[...] = dot_tn(flat(r.active), r.f_slots[...].reshape(z.lanes * z.slots, z.width))
        r.gup[...] = dot_tn(r.e_slots[...].reshape(z.lanes * z.slots, z.width), flat(r.ghid))
        r.ship(r.gdown, r.gup)
        forth.settle(r.e_own)
        back.settle(r.f_own)
        picked = r.e_own[0].astype(BF16)
        r.following[...] = r.m_own[...] + gate_of(r.chance[...], r.choose[...]) * picked.astype(F32)
        r.ship(r.following)
        route_back(z, r, l, r.cotangent[...].astype(F32), r.m_own[...], r.chance[...], r.choose[...], picked, r.f_own[0])
        forth.finish()
        back.finish()

    w_in, w_out, w_up, w_down = weights
    slots = (z.lanes, z.slots)
    return launch(
        "turn", 8, body, dict(act=act, gated=gated, cotangent=cotangent, place=small.place, **routing(small)),
        dict(w_out=w_out, w_up=w_up, w_down=w_down),
        dict(following=f32(z.rows, z.width), **back_outputs(z)),
        dict(fetched=dma(3), choose=pltpu.VMEM((z.rows, z.experts), F32), chance=pltpu.VMEM((z.rows, z.experts), F32), into=pltpu.VMEM((*slots, z.rows), BF16),
             active=pltpu.VMEM((*slots, z.hidden), BF16), ghid=pltpu.VMEM((*slots, z.hidden), BF16),
             **weight_scratch(w_out, w_up, w_down), **out_scratch(z, small.place), **expert_names(z, 1),
             **{"f" + k[1:]: v for k, v in expert_names(z, 1).items()}, **back_scratch(z)),
        58 if z.slots <= 256 else 61)


class PlaneSum:
    def __init__(self, d, m, peers, mine, pair, half, inbox, result, psend, precv, csend, crecv, gsend, grecv):
        self.m, self.mine, self.pair, self.half, self.inbox, self.result = m, mine, pair, half, inbox, result
        self.psend, self.precv, self.csend, self.crecv, self.gsend, self.grecv = psend, precv, csend, crecv, gsend, grecv
        self.chips = peers // 2
        self.chip, self.core = lax.div(d, 2), lax.rem(d, 2)
        self.rows = mine.shape[0] // 2
        self.block = self.rows // self.chips

    def side(self, core):
        return pl.ds(pl.multiple_of(core * self.rows, 16), self.rows)

    def at(self, chip):
        return pl.ds(pl.multiple_of(chip * self.block, 16), self.block)

    def final(self, chip):
        return pl.ds(pl.multiple_of(self.core * self.rows + chip * self.block, 16), self.block)

    def swap(self, src, dst, i):
        return pltpu.make_async_remote_copy(
            src_ref=src, dst_ref=dst, send_sem=self.psend.at[i], recv_sem=self.precv.at[i],
            device_id=(self.chip * 2 + 1 - self.core, self.m), device_id_type=MESH)

    def first_swap(self):
        return self.swap(self.mine.at[self.side(1 - self.core)], self.pair, 0)

    def last_swap(self):
        return self.swap(self.result.at[self.side(self.core)], self.result.at[self.side(self.core)], 1)

    def other(self, k):
        return lax.rem(self.chip + k, self.chips)

    def scatter(self, k):
        return pltpu.make_async_remote_copy(
            src_ref=self.half.at[self.at(self.other(k))], dst_ref=self.inbox.at[k - 1], send_sem=self.csend.at[k - 1],
            recv_sem=self.crecv.at[k - 1], device_id=(self.other(k) * 2 + self.core, self.m), device_id_type=MESH)

    def gather(self, k):
        return pltpu.make_async_remote_copy(
            src_ref=self.result.at[self.final(self.chip)], dst_ref=self.result.at[self.final(self.chip)], send_sem=self.gsend.at[k - 1],
            recv_sem=self.grecv.at[k - 1], device_id=(self.other(k) * 2 + self.core, self.m), device_id_type=MESH)

    def begin(self):
        self.first_swap().start()

    def second(self):
        self.first_swap().wait_recv()
        self.half[...] = (self.mine[self.side(self.core)].astype(F32) + self.pair[...].astype(F32)).astype(BF16)
        for k in range(1, self.chips):
            self.scatter(k).start()

    def third(self):
        for k in range(1, self.chips):
            self.scatter(k).wait_recv()
        summed = self.half[self.at(self.chip)].astype(F32)
        for k in range(1, self.chips):
            summed = summed + self.inbox[k - 1].astype(F32)
        self.result[self.final(self.chip)] = summed.astype(BF16)
        for k in range(1, self.chips):
            self.gather(k).start()

    def fourth(self):
        for k in range(1, self.chips):
            self.gather(k).wait_recv()
        self.last_swap().start()

    def end(self):
        self.last_swap().wait_recv()

    def finish(self):
        self.first_swap().wait_send()
        self.last_swap().wait_send()
        for k in range(1, self.chips):
            self.scatter(k).wait_send()
            self.gather(k).wait_send()


def plane_scratch(peers, rows, width):
    return [
        pltpu.VMEM((rows, width), BF16),
        pltpu.VMEM((rows // 2, width), BF16),
        pltpu.VMEM((rows // 2, width), BF16),
        pltpu.VMEM((peers // 2 - 1, rows // peers, width), BF16),
        dma(2), dma(2), dma(peers // 2 - 1), dma(peers // 2 - 1), dma(peers // 2 - 1), dma(peers // 2 - 1),
    ]


def exchange(targets, buf, inbox, send, recv):
    copies = [
        pltpu.make_async_remote_copy(src_ref=buf, dst_ref=inbox.at[k], send_sem=send.at[k], recv_sem=recv.at[k],
                                     device_id=target, device_id_type=MESH)
        for k, target in enumerate(targets)
    ]
    for copy in copies:
        copy.start()

    def collect():
        total = buf[...].astype(F32)
        for k, copy in enumerate(copies):
            copy.wait()
            total = total + inbox[k].astype(F32)
        return total

    return collect


def early_rows(width, experts):
    sizes = [width, width, DT_RANK, STATE, 16, experts + 8, experts + 8]
    return [sum(sizes[:i]) for i in range(len(sizes) + 1)]


def late_rows(width):
    sizes = [width, PROJ, 16]
    return [sum(sizes[:i]) for i in range(len(sizes) + 1)]


def whole_blocks(rows, peers):
    return -(-rows // (16 * peers)) * 16 * peers


def in_back_scratch(z, win, last):
    early = whole_blocks(early_rows(z.width, z.experts)[-1], z.peers)
    late = whole_blocks(late_rows(z.width)[-1], z.peers)
    shared = 2 * (z.experts + 8)
    small = -(-2 * (z.width // LANES) // 8) * 8
    stage, inbox, send, recv = reduce_scratch(z.lanes, z.rows, z.width)
    found = dict(
        gproj=pltpu.VMEM((PROJ, z.total), BF16), gpre=pltpu.VMEM((z.total + HEAD, z.channels), F32),
        gxi=pltpu.VMEM((z.total, z.channels), BF16), gconv=pltpu.VMEM((16, z.channels), F32), c_own=pltpu.VMEM((z.rows, z.width), F32),
        win=pltpu.VMEM(win.shape[1:], BF16), z_buf=pltpu.VMEM((shared, z.channels), BF16),
        z_in=pltpu.VMEM((z.lanes - 1, shared, z.channels), BF16), z_send=dma(z.lanes - 1), z_recv=dma(z.lanes - 1),
        c_stage=stage, c_inbox=inbox, c_send=send, c_recv=recv,
        **{"e%d" % i: v for i, v in enumerate(plane_scratch(z.peers, early, z.channels))},
        **{"l%d" % i: v for i, v in enumerate(plane_scratch(z.peers, late, z.channels))},
        **sum_scratch(z),
    )
    if last:
        found.update(
            n_buf=pltpu.VMEM((small, LANES), F32), n_in=pltpu.VMEM((z.peers - 1, small, LANES), F32), n_send=dma(z.peers - 1),
            n_recv=dma(z.peers - 1), n_buf2=pltpu.VMEM((small, LANES), F32), n_in2=pltpu.VMEM((z.lanes - 1, small, LANES), F32),
            n_send2=dma(z.lanes - 1), n_recv2=dma(z.lanes - 1))
    return found


def in_back_outputs(z, last):
    early = whole_blocks(early_rows(z.width, z.experts)[-1], z.peers)
    late = whole_blocks(late_rows(z.width)[-1], z.peers)
    return dict(early=bf16(early, z.channels), late=bf16(late, z.channels), share=f32(2 * (z.experts + 8), z.channels),
                gnorm=f32(2 if last else 1, z.width))


def plane_sum(z, r, which, result):
    d, m = lax.axis_index("dp"), lax.axis_index("mp")
    parts = [getattr(r, which + str(i)) for i in range(10)]
    return PlaneSum(d, m, z.peers, *parts[:4], result, *parts[4:])


def in_back_stage(z, r, l, weights, emit):
    d, m = lax.axis_index("dp"), lax.axis_index("mp")
    line = [(d, lax.rem(m + k, z.lanes)) for k in range(1, z.lanes)]
    early, late = plane_sum(z, r, "e", r.early), plane_sum(z, r, "l", r.late)
    emine, lmine = early.mine, late.mine
    ch = z.channels
    at, till = early_rows(z.width, z.experts), late_rows(z.width)

    def early_work():
        r.need(r.b_whole, r.gzg, r.b_gwout, r.b_gshare)
        whole = r.b_whole[...].reshape(z.total, z.width)
        emine[at[0] : at[1], :] = dot_tn(whole, r.gzg[...]).astype(BF16)
        for i in range(z.width // ch):
            emine[at[1] + i * ch : at[1] + (i + 1) * ch, :] = r.b_gwout[:, i * ch : (i + 1) * ch]
            emine[at[5 + i] : at[6 + i], :] = r.b_gshare[:, i * ch : (i + 1) * ch].astype(BF16)
        emine[at[2] : at[3], :] = r.gdtw[...].astype(BF16)
        emine[at[3] : at[4], :] = r.galog[...].astype(BF16)
        emine[at[4] : at[5], :] = jnp.concatenate([r.gdtb[...], r.gskip[...], jnp.zeros((14, ch), F32)], axis=0).astype(BF16)
        if at[7] < emine.shape[0]:
            emine[at[7] :, :] = jnp.zeros((emine.shape[0] - at[7], ch), BF16)
        early.begin()

    r.need(r.gpart)
    finish_sum = line_sum(r.gpart, r.sum_stage, r.sum_inbox, r.sum_send, r.sum_recv, r.gproj, d, m, z.lanes, early_work)
    taps, bias = r.conv_w[l], r.conv_b[l : l + 1, :]
    r.gconv[...] = jnp.zeros_like(r.gconv)
    r.gpre[z.total :, :] = jnp.zeros((HEAD, ch), F32)

    def first(c, carry):
        base = pl.multiple_of(c * CONV_ROWS, CONV_ROWS)
        pre, shifted = conv_window(r.b_conv, r.since, taps, bias, base)
        sig = sigmoid(pre)
        grad = r.gxs[pl.ds(base, CONV_ROWS), :] + dot_tn(r.gproj[:, pl.ds(base, CONV_ROWS)], r.x_proj[l])
        grad = grad * (sig * (1.0 + pre * (1.0 - sig)))
        r.gpre[pl.ds(base, CONV_ROWS), :] = grad
        for j in range(CONV):
            r.gconv[CONV - 1 - j : CONV - j, :] += jnp.sum(grad * shifted[j], axis=0, keepdims=True)
        r.gconv[CONV : CONV + 1, :] += jnp.sum(grad, axis=0, keepdims=True)
        return carry

    r.need(r.b_conv, r.gxs)
    lax.fori_loop(0, z.total // CONV_ROWS, first, 0)

    def second(c, carry):
        base = pl.multiple_of(c * CONV_ROWS, CONV_ROWS)
        window = r.gpre[pl.ds(base, CONV_ROWS + HEAD), :]
        since = r.since[pl.ds(base, CONV_ROWS + HEAD), :]
        grad = taps[CONV - 1 : CONV, :] * window[:CONV_ROWS]
        for j in range(1, CONV):
            grad = grad + taps[CONV - 1 - j : CONV - j, :] * (window * (since >= j).astype(F32))[j : j + CONV_ROWS]
        r.gxi[pl.ds(base, CONV_ROWS), :] = grad.astype(BF16)
        return carry

    lax.fori_loop(0, z.total // CONV_ROWS, second, 0)
    weights.wait()
    reduce = LineReduce(r.c_stage, r.c_inbox, r.c_send, r.c_recv, d, m, z.lanes)

    def term(s):
        part = pl.ds(pl.multiple_of(s * z.rows, 16), z.rows)
        return dot_nt(r.gxi[part, :], r.win[0]) + dot_nt(r.gzg[part, :], r.win[1])

    def push_middle(s):
        @pl.when(reduce.middle)
        def _():
            for p in range(PIECES):
                reduce.push_on(s, p, term(s)[p * reduce.rows : (p + 1) * reduce.rows])

    one, two, three = reduce.order

    @pl.when(reduce.at_end)
    def _():
        for s in reduce.order:
            reduce.push_first(s, term(s))

    early.second()
    r.need(r.b_xs)
    whole = r.b_whole[...].reshape(z.total, z.width)
    lmine[till[0] : till[1], :] = dot_tn(whole, r.gxi[...]).astype(BF16)
    lmine[till[1] : till[2], :] = dot(r.gproj[...], r.b_xs[...].astype(BF16)).astype(BF16)
    lmine[till[2] : till[3], :] = r.gconv[...].astype(BF16)
    if till[3] < lmine.shape[0]:
        lmine[till[3] :, :] = jnp.zeros((lmine.shape[0] - till[3], ch), BF16)
    late.begin()
    push_middle(one)
    late.second()
    r.c_own[...] = term(m)
    early.third()
    push_middle(two)
    late.third()
    early.fourth()
    push_middle(three)
    late.fourth()
    early.end()
    r.ship(r.early)
    r.z_buf[...] = r.early[at[5] : at[7], :]
    shared = exchange(line, r.z_buf, r.z_in, r.z_send, r.z_recv)
    reduce.total(r.c_own)
    r.need(r.b_act, r.b_gmid)
    act = r.b_act[...].astype(F32)
    pulled, grad_gain = norm_back(act, rms_inverse(act), r.norm_in[l : l + 1, :], r.c_own[...])
    emit(r.b_gmid[...] + pulled)

    def finish():
        late.end()
        r.ship(r.late)
        if l == 0:
            both = jnp.concatenate([grad_gain, r.prior[...]], axis=0)
            groups = z.width // LANES
            for g in range(groups):
                r.n_buf[2 * g : 2 * g + 2, :] = both[:, g * LANES : (g + 1) * LANES]
            if 2 * groups < r.n_buf.shape[0]:
                r.n_buf[2 * groups :, :] = jnp.zeros((r.n_buf.shape[0] - 2 * groups, LANES), F32)
            plane = [(lax.rem(d + k, z.peers), m) for k in range(1, z.peers)]
            r.n_buf2[...] = exchange(plane, r.n_buf, r.n_in, r.n_send, r.n_recv)()
            summed = exchange(line, r.n_buf2, r.n_in2, r.n_send2, r.n_recv2)()
            r.gnorm[...] = jnp.concatenate([summed[2 * g : 2 * g + 2, :] for g in range(groups)], axis=1)
        else:
            r.gnorm[...] = grad_gain
        r.share[...] = shared()
        finish_sum()
        reduce.finish()
        early.finish()
        late.finish()

    return finish


def last_block(z, back, prior, small, w_in):
    def body(r):
        d, m = lax.axis_index("dp"), lax.axis_index("mp")
        (win,) = fetch([(r.w_in.at[0], r.win)], r.fetched)
        greet(d, m, z.lanes, z.peers, True)

        def emit(value):
            r.up[...] = value

        in_back_stage(z, r, 0, win, emit)()

    return launch("mamba_in_backward", 9, body, dict(**back, prior=prior, **convolution(small)), dict(w_in=w_in),
                  dict(up=f32(z.rows, z.width), **in_back_outputs(z, True)), dict(fetched=dma(1), **in_back_scratch(z, w_in, True)))


def experts_back(z, r, l, fetched, finish):
    d, m = lax.axis_index("dp"), lax.axis_index("mp")
    for weight in fetched:
        weight.wait()
    r.need(r.into, r.hidden)
    moe = Experts(d, m, z.lanes, z.peers, r.into, *expert_refs(r))

    def expert(s, rows):
        grad_hidden = (dot_nt(rows[0], r.wdown[...]) * gelu_slope(r.hidden[s].astype(F32))).astype(BF16)
        r.ghid[s] = grad_hidden
        return [dot_nt(grad_hidden, r.wup[...])]

    def meanwhile():
        r.need(r.active, r.slots)
        r.gdown[...] = dot_tn(flat(r.active), r.e_slots[...].reshape(z.lanes * z.slots, z.width))
        r.gup[...] = dot_tn(flat(r.slots), flat(r.ghid))
        r.ship(r.gdown, r.gup)
        finish()

    moe.run(expert, r.e_own, meanwhile)
    r.need(r.picked, r.middle)
    route_back(z, r, l, r.upstream[...], r.middle[...], r.chance[...], r.choose[...], r.picked[...], r.e_own[0])
    moe.finish()


def down_blocks(z, l, back, kept, small, weights):
    def upper(r):
        d, m = lax.axis_index("dp"), lax.axis_index("mp")
        (win,) = fetch([(r.w_in.at[l], r.win)], r.fetched)
        greet(d, m, z.lanes, z.peers, True)

        def emit(value):
            r.up[...] = value

        in_back_stage(z, r, l, win, emit)()

    def lower(r):
        d, m = lax.axis_index("dp"), lax.axis_index("mp")
        fetched = fetch([(r.w_down.at[l - 1, 0], r.wdown), (r.w_up.at[l - 1, 0], r.wup), (r.w_out.at[l - 1], r.wout)], r.fetched)
        greet(d, m, z.lanes, z.peers, True)
        r.need(r.upstream)
        r.e_rows[m, 0] = (gate_of(r.chance[...], r.choose[...]) * r.upstream[...]).astype(BF16)
        experts_back(z, r, l - 1, fetched, lambda: None)

    w_in, w_out, w_up, w_down = weights
    slots = (z.lanes, z.slots)
    one = launch("mamba_in_backward", 20 + l, upper, dict(**back, **convolution(small)),
                 dict(w_in=w_in), dict(up=f32(z.rows, z.width), **in_back_outputs(z, False)),
                 dict(fetched=dma(1), **in_back_scratch(z, w_in, False)))
    two = launch("experts_backward", 30 + l, lower, dict(**kept, upstream=one.up, **routing(small)),
                 dict(w_out=w_out, w_up=w_up, w_down=w_down), back_outputs(z),
                 dict(fetched=dma(3), ghid=pltpu.VMEM((*slots, z.hidden), BF16), **weight_scratch(w_out, w_up, w_down),
                      **expert_names(z, 1), **back_scratch(z)))
    return types.SimpleNamespace(**vars(one), **vars(two))


def down_block(z, l, back, kept, small, weights):
    def body(r):
        d, m = lax.axis_index("dp"), lax.axis_index("mp")
        win, wdown, wup, wout = fetch([(r.w_in.at[l], r.win), (r.w_down.at[l - 1, 0], r.wdown), (r.w_up.at[l - 1, 0], r.wup),
                                       (r.w_out.at[l - 1], r.wout)], r.fetched)
        greet(d, m, z.lanes, z.peers, True)

        def emit(value):
            r.upstream[...] = value
            r.e_rows[m, 0] = (gate_of(r.chance[...], r.choose[...]) * value).astype(BF16)

        experts_back(z, r, l - 1, (wdown, wup, wout), in_back_stage(z, r, l, win, emit))

    w_in, w_out, w_up, w_down = weights
    slots = (z.lanes, z.slots)
    return launch(
        "down", 9 + l, body, dict(**back, **kept, **convolution(small), **routing(small)),
        dict(w_in=w_in, w_out=w_out, w_up=w_up, w_down=w_down), dict(**in_back_outputs(z, False), **back_outputs(z)),
        dict(fetched=dma(4), upstream=pltpu.VMEM((z.rows, z.width), F32),
             ghid=pltpu.VMEM((*slots, z.hidden), BF16), **weight_scratch(w_out, w_up, w_down), **in_back_scratch(z, w_in, False),
             **expert_names(z, 1), **back_scratch(z)))


def big_outputs(z, count):
    return dict(w_in=(count, 2, z.width, z.channels), w_out=(count, z.channels, z.width), w_up=(count, 1, z.width, z.hidden),
                w_down=(count, 1, z.hidden, z.width))


def widen(z, early, late, w_in, w_out):
    at, till, ch = early_rows(z.width, z.experts), late_rows(z.width), z.channels
    w_in[0] = late[till[0] : till[1], :].astype(F32)
    w_in[1] = early[at[0] : at[1], :].astype(F32)
    for i in range(z.width // ch):
        w_out[:, i * ch : (i + 1) * ch] = early[at[1] + i * ch : at[1] + (i + 1) * ch, :].astype(F32)


def upper_outputs(z, count, layer):
    early, late, _, up, down = layer
    far = [early, late, up, down]
    shapes = big_outputs(z, count)
    room = [pltpu.VMEM(v.shape, v.dtype) for v in far]
    room += [pltpu.VMEM(shapes["w_in"][1:], F32), pltpu.VMEM(shapes["w_out"][1:], F32), dma(4), dma(4)]

    def work(steps, there, outs, held):
        e, l, u, v, w_in, w_out, came, went = held
        coming = [pltpu.make_async_copy(src, dst, came.at[i]) for i, (src, dst) in enumerate(zip(there, (e, l, u, v)))]
        out_in, out_out, out_up, out_down = outs
        pairs = [(w_in, out_in.at[1]), (w_out, out_out.at[1]), (u, out_up.at[1, 0]), (v, out_down.at[1, 0])]
        going = [pltpu.make_async_copy(src, dst, went.at[i]) for i, (src, dst) in enumerate(pairs)]

        @pl.when(pl.program_id(0) == 0)
        def _():
            for copy in coming:
                copy.start()

        @pl.when(pl.program_id(0) == 1)
        def _():
            for copy in coming:
                copy.wait()
            widen(z, e, l, w_in, w_out)
            for copy in going:
                copy.start()

        @pl.when(pl.program_id(0) == steps - 1)
        def _():
            for copy in going:
                copy.wait()

    return work, far, [f32(*shape) for shape in shapes.values()], room


def final_block(z, result, up, gnorm, layers, large_ones):
    count, ch = len(layers), z.channels
    assert count == 2
    at, till = early_rows(z.width, z.experts), late_rows(z.width)
    far = dict(result=(z.rows, z.width), tokens=(z.rows, z.width), **big_outputs(z, count))
    near = dict(norm_in=(count, z.width), conv_w=(count, CONV, ch), conv_b=(count, ch), x_proj=(count, PROJ, ch), dt_proj=(count, DT_RANK, ch),
                dt_bias=(count, ch), a_log=(count, STATE, ch), skip=(count, ch), norm_moe=(count, z.width), router=(count, z.experts, z.width))
    shapes = {**far, **near}
    sums = [v for layer in layers for v in layer[:2]]
    whole = [*layers[0][3:], result, up]

    def kernel(*refs):
        small, refs = refs[: 1 + count], refs[1 + count :]
        there, refs = refs[: len(sums) + len(whole)], refs[len(sums) + len(whole) + len(large_ones) :]
        outs, refs = refs[: len(shapes)], refs[len(shapes) :]
        held, (w_in, w_out, came, went) = refs[: len(there)], refs[len(there) :]
        out = types.SimpleNamespace(**dict(zip(shapes, outs)))
        coming = fetch(list(zip(there, held)), came)
        out.norm_in[...] = small[0][...]
        going = []

        def send(src, dst):
            going.append(pltpu.make_async_copy(src, dst, went.at[len(going)]))
            going[-1].start()

        for l in range(count):
            early, late, share = held[2 * l], held[2 * l + 1], small[1 + l]
            coming[2 * l].wait()
            coming[2 * l + 1].wait()
            one = slice(l, l + 1)
            if l == 0:
                widen(z, early, late, w_in, w_out)
                send(w_in, out.w_in.at[0])
                send(w_out, out.w_out.at[0])
            for i in range(z.width // ch):
                cols = slice(i * ch, (i + 1) * ch)
                rows = share[i * (z.experts + 8) : (i + 1) * (z.experts + 8), :]
                out.router[l, :, cols] = rows[: z.experts]
                out.norm_moe[one, cols] = rows[z.experts : z.experts + 1]
            conv = late[till[2] : till[3], :].astype(F32)
            out.conv_w[l] = conv[:CONV]
            out.conv_b[one, :] = conv[CONV : CONV + 1]
            out.x_proj[l] = late[till[1] : till[2], :].astype(F32)
            out.dt_proj[l] = early[at[2] : at[3], :].astype(F32)
            out.a_log[l] = early[at[3] : at[4], :].astype(F32)
            both = early[at[4] : at[5], :].astype(F32)
            out.dt_bias[one, :] = both[:1]
            out.skip[one, :] = both[1:2]
        for i, place in enumerate((out.w_up.at[0, 0], out.w_down.at[0, 0], out.result, out.tokens)):
            coming[len(sums) + i].wait()
            send(held[len(sums) + i], place)
        for copy in going:
            copy.wait()

    before = 1 + count + len(sums) + len(whole)
    outputs = pl.pallas_call(
        kernel,
        out_shape=[f32(*shape) for shape in shapes.values()],
        in_specs=vmem(1 + count) + hbm(len(sums) + len(whole) + len(large_ones)),
        out_specs=hbm(len(far)) + vmem(len(near)),
        scratch_shapes=[pltpu.VMEM(v.shape, v.dtype) for v in (*sums, *whole)]
        + [pltpu.VMEM(far["w_in"][1:], F32), pltpu.VMEM(far["w_out"][1:], F32), dma(len(sums) + len(whole)), dma(2 + len(whole))],
        input_output_aliases={before + i: 2 + i for i in range(len(large_ones))},
        compiler_params=pltpu.CompilerParams(vmem_limit_bytes=60 << 20),
        name="outputs",
    )(gnorm, *(layer[2] for layer in layers), *sums, *whole, *large_ones)
    o = types.SimpleNamespace(**dict(zip(shapes, outputs)))
    return (o.result, o.tokens, o.norm_in, o.w_in, o.conv_w, o.conv_b, jnp.swapaxes(o.x_proj, 1, 2), o.dt_proj, o.dt_bias, o.a_log, o.skip, o.w_out, o.norm_moe,
            jnp.swapaxes(o.router, 1, 2), o.w_up, o.w_down)


def on_device(
    tokens, cotangent, lengths, routes, slot_place, norm_in, w_in, conv_w, conv_b, x_proj, dt_proj, dt_bias,
    a_log, d_skip, w_out, norm_moe, router, w_up, w_down,
):
    layers = norm_in.shape[0]
    assert layers == 2
    rows_here, width = tokens.shape
    lanes, peers = lax.axis_size("mp"), lax.axis_size("dp")
    experts, channels = router.shape[2], w_in.shape[3]
    capacity = max(2, (5 * rows_here + 4 * experts - 1) // (4 * experts))
    padded = (capacity + 15) // 16 * 16
    z = Sizes(lanes, peers, experts, padded, rows_here, width, channels, w_up.shape[3])
    position = lax.broadcasted_iota(jnp.int32, (z.total + HEAD, 1), 0)
    sequences = lengths.shape[1]
    earlier = jnp.arange(sequences)[:, None] < jnp.arange(sequences)[None, :]
    starts = jnp.sum(jnp.where(earlier, lengths[0][:, None], 0), axis=0)
    since = position - jnp.max(jnp.where(position >= starts[None, :], starts[None, :], 0), axis=1, keepdims=True)
    since = jnp.where(position < z.total, since, 0)
    place = jnp.pad(routes * padded + slot_place, (0, -rows_here % LANES))
    small = types.SimpleNamespace(
        norm_in=norm_in, norm_moe=norm_moe, conv_w=conv_w, conv_b=conv_b, since=since, x_proj=jnp.swapaxes(x_proj, 1, 2),
        router=jnp.swapaxes(router, 1, 2),
        place=jnp.broadcast_to(place[None, :], (8, place.shape[0])),
    )
    weights = (w_in, w_out, w_up, w_down)
    scan_weights = (dt_proj, dt_bias, a_log, d_skip, spread_matrix())

    act, entry = tokens, first_block(z, 0, tokens, small, w_in)
    kept = []
    for l in range(layers):
        gated, ys, marks = scan_fwd(l, entry.xs, entry.zgate, entry.proj, since, *scan_weights)
        gated = gated.reshape(lanes, rows_here, channels)
        if l + 1 < layers:
            out = middle_block(z, l, act, gated, small, weights)
            kept.append((act, entry, gated, ys, marks, out))
            act, entry = out.following, out
        else:
            turn = turn_block(z, l, act, gated, cotangent, small, weights)
            kept.append((act, entry, gated, ys, marks, turn))
    result, above = turn.following, turn
    collected = []
    for l in reversed(range(layers)):
        act, entry, gated, ys, marks, _ = kept[l]
        gxs, gzg, gpart, gdtw, gdtb, galog, gskip, *large_ones = scan_bwd(
            l, entry.xs, entry.zgate, entry.proj, since, ys, above.ggated.reshape(z.total, channels), marks, *scan_weights,
            beside=upper_outputs(z, layers, collected[-1]) if l == 0 else None)
        back = dict(gpart=gpart, gxs=gxs, gzg=gzg, b_conv=entry.conv, b_xs=entry.xs, b_whole=entry.whole, b_act=act, b_gmid=above.gmid,
                    b_gwout=above.gwout, b_gshare=above.gshare, gdtw=gdtw, gdtb=gdtb, galog=galog, gskip=gskip)
        grads = (above.gup, above.gdown)
        if l > 0:
            _, _, below_gated, _, _, below = kept[l - 1]
            forward = dict(gated=below_gated, chance=below.chance, choose=below.choose, into=below.into, slots=below.slots, hidden=below.hidden,
                           active=below.active, picked=below.picked, middle=below.middle)
            above = (down_block if z.slots <= 256 else down_blocks)(z, l, back, forward, small, weights)
            prior = above.gnorm
            collected.append((above.early, above.late, above.share, *grads))
        else:
            end = last_block(z, back, prior, small, w_in)
            collected.append((end.early, end.late, end.share, *grads))
    collected = collected[::-1]
    at, till = early_rows(width, experts), late_rows(width)

    return final_block(z, result, end.up, end.gnorm, collected, large_ones)


def solution(mesh):
    return jax.shard_map(
        on_device,
        mesh=mesh,
        in_specs=(
            P(("dp", "mp"), None),
            P(("dp", "mp"), None),
            P("dp", None),
            P(("dp", "mp")),
            P(("dp", "mp")),
            P(),
            P(None, None, None, "mp"),
            P(None, None, "mp"),
            P(None, "mp"),
            P(None, "mp", None),
            P(None, None, "mp"),
            P(None, "mp"),
            P(None, None, "mp"),
            P(None, "mp"),
            P(None, "mp", None),
            P(),
            P(),
            P(None, "dp", None, "mp"),
            P(None, "dp", "mp", None),
        ),
        out_specs=(
            P(("dp", "mp"), None),
            P(("dp", "mp"), None),
            P(),
            P(None, None, None, "mp"),
            P(None, None, "mp"),
            P(None, "mp"),
            P(None, "mp", None),
            P(None, None, "mp"),
            P(None, "mp"),
            P(None, None, "mp"),
            P(None, "mp"),
            P(None, "mp", None),
            P(),
            P(),
            P(None, "dp", None, "mp"),
            P(None, "dp", "mp", None),
        ),
        check_vma=False,
    )
```
